32 devices in a mesh: grp: 2 (over x), lat: 16 (over z, y, core).
Axes of the slice: x: 2, y: 2, z: 4, core: 2. Of those that a mesh axis runs over, the one named last changes fastest.
Arguments:
- inputs: bfloat16 [192, 108, 512], P(('grp', 'lat')), parts along dimension 0, may hold values from -24 to 24
- cotangent: bfloat16 [192, 108, 512], P(('grp', 'lat')), parts along dimension 0, may hold values from -6 to 6
- idents: int32 [192, 108], P(('grp', 'lat')), parts along dimension 0, may hold values from 0 to 3, as said below
- w_qkv: bfloat16 [512, 1536], P('lat'), may hold values from -0.25 to 0.25
- w_out: bfloat16 [512, 512], P('lat'), may hold values from -0.25 to 0.25
- gain: float32 [512], replicated, may hold values from 0.1 to 1.9
Outputs:
- output: bfloat16 [192, 108, 512], P(('grp', 'lat')), parts along dimension 0
- grad_in: bfloat16 [192, 108, 512], P(('grp', 'lat')), parts along dimension 0
- grad_qkv: float32 [1024, 1536], P(('grp', 'lat')), parts along dimension 0
- grad_out: float32 [1024, 512], P(('grp', 'lat')), parts along dimension 0
The draws below stay inside these ranges and needn't reach their ends.
There are 2 independent parts, one for each index of `grp`. The reference program is written for one: setup_inputs(seed, part) draws one part's arguments, and reference() takes and returns one part's arrays. A program takes and returns all parts, laid end to end along the dimension named above; an argument that names none is the same for every part. Nothing has to cross between parts.
Inputs may be any that keep to these rules, and one draw needn't show every extreme that they name: `idents`: within a window only cells of equal id see each other; in the last 6 rows the last 3 rows never share an id with the rows below them.
All inputs are finite; a program needn't handle non-finite values.
Results may differ from the reference program's by a relative error of at most 0.012.
The reference program's roundings to bfloat16 on the way count: a program that leaves them out, or rounds other values in their place, can miss the bound.
Values may be sent and summed in bfloat16 or wider, within the bound.
No kernel may reach another device: no remote copies, remote signals or barrier semaphores. Data moves between devices by JAX's collectives and lax.ppermute only.
A program may use at most 64 MiB of HBM per device.

```python
import jax
import jax.numpy as jnp
from jax import lax

D = 512
HEADS = 8
WIN_R = 6
WIN_C = 12
LON = 108
LAT = 96


def draw_inputs(key, part):
    key = jax.random.fold_in(key, 11)
    key_list = jax.random.split(key, 1)
    full_shape = (LAT, LON, D)
    values = jnp.clip(jax.random.normal(key_list[0], full_shape, jnp.float32), -6.0, 6.0)
    values = jnp.clip(values, -24.0, 24.0)
    values = jnp.roll(values, (WIN_R // 2, WIN_C // 2), (0, 1))
    return values.astype(jnp.bfloat16)


def draw_idents(key, part):
    key = jax.random.fold_in(key, 23)
    first_key, second_key = jax.random.split(key)
    blocks_lat = LAT // WIN_R
    blocks_lon = LON // WIN_C
    row_cut = jax.random.randint(first_key, (blocks_lat, blocks_lon), 0, WIN_R)
    col_cut = jax.random.randint(second_key, (blocks_lat, blocks_lon), 0, WIN_C)
    row_cut = row_cut.at[0, 0].set(WIN_R // 2)
    col_cut = col_cut.at[0, 0].set(WIN_C // 2)
    row_cut = row_cut.at[blocks_lat - 1, :].set(WIN_R // 2)
    row_pos = jnp.arange(WIN_R, dtype=jnp.int32)[None, :, None, None]
    col_pos = jnp.arange(WIN_C, dtype=jnp.int32)[None, None, None, :]
    upper = (row_pos >= row_cut[:, None, :, None]).astype(jnp.int32)
    right = (col_pos >= col_cut[:, None, :, None]).astype(jnp.int32)
    labels = 2 * upper + right
    return labels.reshape(LAT, LON)


def block_scale(own_key, extent, shards, low, top_value):
    level = 1.0
    for axis_at, shards_of in shards:
        steps = jax.random.uniform(jax.random.fold_in(jax.random.fold_in(own_key, 6), axis_at), (shards_of,), jnp.float32, low / len(shards), top_value / len(shards))
        level = level * jnp.repeat(jnp.exp(steps), extent[axis_at] // shards_of).reshape((-1,) + (1,) * (len(extent) - 1 - axis_at))
    return level


def gaussian(rng, dims, spread, most, cuts=(), kind=jnp.bfloat16):
    array = jax.random.normal(rng, dims, jnp.float32) * spread
    if len(cuts) > 0:
        array = block_scale(rng, dims, cuts, -0.22, 0.18) * array
    return jnp.clip(array, min=-most, max=most).astype(kind)


def setup_inputs(seed: int = 0, part: int = 0) -> dict:
    streams_of = jax.random.split(jax.random.key(seed), 7)
    part_splits = jax.random.split(jax.random.fold_in(streams_of[6], part), 7)
    inputs = draw_inputs(jax.random.fold_in(jax.random.fold_in(streams_of[6], part), 71), part)
    cotangent = gaussian(part_splits[1], (LAT, LON, D), 1.0, 6.0, ((0, 16),))
    idents = draw_idents(jax.random.fold_in(jax.random.fold_in(streams_of[6], part), 71), part)
    w_qkv = gaussian(streams_of[3], (D, 3 * D), D ** -0.5, 0.25, ((0, 16),))
    w_out = gaussian(streams_of[4], (D, D), D ** -0.5, 0.25, ((0, 16),))
    gain = jnp.clip(1.0 + 0.18 * jax.random.normal(streams_of[5], (D,), jnp.float32), 0.1, 1.9)
    return {"inputs": inputs, "cotangent": cotangent, "idents": idents, "w_qkv": w_qkv, "w_out": w_out, "gain": gain}


EPS = 1e-05

def to_windows(field, win_rows, win_cols):
    lat_cells, lon_cells, depth = field.shape
    field = field.reshape(lat_cells // win_rows, win_rows, lon_cells // win_cols, win_cols, depth)
    field = field.transpose(0, 2, 1, 3, 4)
    return field.reshape(-1, win_rows * win_cols, depth)

def from_windows(tiles, lat_cells, lon_cells, win_rows, win_cols):
    depth = tiles.shape[-1]
    tiles = tiles.reshape(lat_cells // win_rows, lon_cells // win_cols, win_rows, win_cols, depth)
    return tiles.transpose(0, 2, 1, 3, 4).reshape(lat_cells, lon_cells, depth)

def window_pass(shifted, cot_shift, idents, w_qkv, w_out, gain):
    lat_cells, lon_cells, model_width = shifted.shape
    head_dim = model_width // HEADS
    window_len = WIN_R * WIN_C
    factor = head_dim ** (-0.5)
    tokens_flat = shifted.reshape(-1, model_width)
    qkv_tok = jnp.dot(tokens_flat, w_qkv, preferred_element_type=jnp.float32).astype(jnp.bfloat16)
    qkv_tiles = to_windows(qkv_tok.reshape(lat_cells, lon_cells, 3 * model_width), WIN_R, WIN_C)
    number_win = qkv_tiles.shape[0]
    queries = qkv_tiles[:, :, :model_width].reshape(number_win, window_len, HEADS, head_dim)
    key_tiles = qkv_tiles[:, :, model_width:2 * model_width].reshape(number_win, window_len, HEADS, head_dim)
    values = qkv_tiles[:, :, 2 * model_width:].reshape(number_win, window_len, HEADS, head_dim)
    id_tiles = to_windows(idents[:, :, None], WIN_R, WIN_C)[:, :, 0]
    visible = (id_tiles[:, :, None] == id_tiles[:, None, :])[:, None]
    scores = jnp.einsum('wphd,wqhd->whpq', queries.astype(jnp.float32), key_tiles.astype(jnp.float32)) * factor
    masked = jnp.where(visible, scores, -1e+30)
    row_top = lax.optimization_barrier(jnp.max(masked, axis=-1, keepdims=True))
    lifted = jnp.where(visible, jnp.exp(masked - row_top), 0.0)
    probs = (lifted / lax.optimization_barrier(jnp.sum(lifted, axis=-1, keepdims=True))).astype(jnp.bfloat16)
    mixed_tile = jnp.einsum('whpq,wqhd->wphd', probs.astype(jnp.float32), values.astype(jnp.float32)).astype(jnp.bfloat16)
    mixed_tok = from_windows(mixed_tile.reshape(number_win, window_len, model_width), lat_cells, lon_cells, WIN_R, WIN_C).reshape(-1, model_width)
    projected = jnp.dot(mixed_tok, w_out, preferred_element_type=jnp.float32)
    center = projected - lax.optimization_barrier(jnp.mean(projected, axis=-1, keepdims=True))
    inverse = lax.rsqrt(lax.optimization_barrier(jnp.mean(center * center, axis=-1, keepdims=True)) + EPS)
    normal = center * inverse
    normed = (normal * gain).astype(jnp.bfloat16)
    scaled = cot_shift.reshape(-1, model_width).astype(jnp.float32) * gain
    grad_proj = ((scaled - lax.optimization_barrier(jnp.mean(scaled, axis=-1, keepdims=True)) - normal * lax.optimization_barrier(jnp.mean(scaled * normal, axis=-1, keepdims=True))) * inverse).astype(jnp.bfloat16)
    out_term = jnp.dot(mixed_tok.T, grad_proj, preferred_element_type=jnp.float32)
    grad_mix = jnp.dot(grad_proj, w_out.T, preferred_element_type=jnp.float32).astype(jnp.bfloat16)
    mix_tiles = to_windows(grad_mix.reshape(lat_cells, lon_cells, model_width), WIN_R, WIN_C).reshape(number_win, window_len, HEADS, head_dim)
    grad_probs = jnp.einsum('wphd,wqhd->whpq', mix_tiles.astype(jnp.float32), values.astype(jnp.float32))
    float_probs = probs.astype(jnp.float32)
    grad_values = jnp.einsum('whpq,wphd->wqhd', float_probs, mix_tiles.astype(jnp.float32)).astype(jnp.bfloat16)
    grad_scores = (factor * float_probs * (grad_probs - lax.optimization_barrier(jnp.sum(float_probs * grad_probs, axis=-1, keepdims=True)))).astype(jnp.bfloat16)
    grad_queries = jnp.einsum('whpq,wqhd->wphd', grad_scores.astype(jnp.float32), key_tiles.astype(jnp.float32)).astype(jnp.bfloat16)
    grad_keys = jnp.einsum('whpq,wphd->wqhd', grad_scores.astype(jnp.float32), queries.astype(jnp.float32)).astype(jnp.bfloat16)
    joined = jnp.concatenate([grad_queries.reshape(number_win, window_len, model_width), grad_keys.reshape(number_win, window_len, model_width), grad_values.reshape(number_win, window_len, model_width)], axis=-1)
    grad_cells = from_windows(joined, lat_cells, lon_cells, WIN_R, WIN_C).reshape(-1, 3 * model_width)
    qkv_term = jnp.dot(tokens_flat.T, grad_cells, preferred_element_type=jnp.float32)
    grad_shift = jnp.dot(grad_cells, w_qkv.T, preferred_element_type=jnp.float32).astype(jnp.bfloat16)
    return (normed.reshape(lat_cells, lon_cells, model_width), grad_shift.reshape(lat_cells, lon_cells, model_width), qkv_term, out_term)

def move_forward(field, half_rows, half_cols):
    rolled = jnp.roll(field, -half_cols, 1)
    pad_rows = jnp.zeros((half_rows,) + field.shape[1:], field.dtype)
    return jnp.concatenate([rolled[half_rows:], pad_rows], axis=0)

def move_back(field, half_rows, half_cols):
    rolled = jnp.roll(field, half_cols, 1)
    pad_rows = jnp.zeros((half_rows,) + field.shape[1:], field.dtype)
    return jnp.concatenate([pad_rows, rolled[:-half_rows]], axis=0)

def reference(inputs, cotangent, idents, w_qkv, w_out, gain):
    half_rows = WIN_R // 2
    half_cols = WIN_C // 2
    shifted = move_forward(inputs, half_rows, half_cols)
    cot_shift = move_forward(cotangent, half_rows, half_cols)
    blocks_lat = LAT // WIN_R
    pieces = (shifted.reshape(blocks_lat, WIN_R, LON, D), cot_shift.reshape(blocks_lat, WIN_R, LON, D), idents.reshape(blocks_lat, WIN_R, LON))

    def advance(carry, piece):
        normed, grad_shift, qkv_term, out_term = window_pass(piece[0], piece[1], piece[2], w_qkv, w_out, gain)
        return ((carry[0] + qkv_term, carry[1] + out_term), (normed, grad_shift))
    start_carry = (jnp.zeros((D, 3 * D), jnp.float32), jnp.zeros((D, D), jnp.float32))
    (grad_qkv, grad_out), (normed, grad_shift) = lax.scan(advance, start_carry, pieces)
    normed = move_back(normed.reshape(LAT, LON, D), half_rows, half_cols)
    grad_shift = move_back(grad_shift.reshape(LAT, LON, D), half_rows, half_cols)
    output = (inputs.astype(jnp.float32) + normed.astype(jnp.float32)).astype(jnp.bfloat16)
    grad_in = (cotangent.astype(jnp.float32) + grad_shift.astype(jnp.float32)).astype(jnp.bfloat16)
    return (output, grad_in, grad_qkv, grad_out)
```

```python
import jax
import jax.numpy as jnp
from jax import lax
from jax.sharding import PartitionSpec as P

HEADS = 8
WIN_R = 6
WIN_C = 12


EPS = 1e-05


def passed_along(value, axis, steps):
    count = lax.axis_size(axis)
    first, last = (max(0, -steps), min(count, count - steps))
    return lax.ppermute(value, axis, [(source, source + steps) for source in range(first, last)])


def lat_split():
    count = lax.axis_size("lat")
    core = 2 if count % 2 == 0 else 1
    rest = count // core
    inner = 1
    while inner * inner * 2 <= rest:
        inner *= 2
    while rest % inner:
        inner //= 2
    return rest // inner, inner, core


def line_gather(block, stride, count):
    total = lax.axis_size("lat")
    if count == 1:
        return block[None]
    place = lax.rem(lax.axis_index("lat") // stride, count)

    def position(index):
        return (index // stride) % count

    after, before = [], []
    from_low = from_high = block
    for step in range(1, count):
        up = [(i, i + stride) for i in range(total) if step - 1 <= position(i) < count - 1]
        down = [(i, i - stride) for i in range(total) if 1 <= position(i) <= count - step]
        from_low = lax.ppermute(from_low, "lat", up)
        from_high = lax.ppermute(from_high, "lat", down)
        before.insert(0, from_low)
        after.append(from_high)
    around = jnp.stack(before + [block] + after)
    return lax.dynamic_slice_in_dim(around, count - 1 - place, count, 0)


def gather_rows(block):
    outer, inner, core = lat_split()
    rows, columns = block.shape
    part = line_gather(block, core, inner)
    part = line_gather(part, core * inner, outer)
    part = line_gather(part, 1, core)
    part = part.reshape(core, outer * inner, rows, columns).transpose(1, 0, 2, 3)
    return part.reshape(-1, columns)


def halve(part, stride, count):
    total = lax.axis_size("lat")
    place = lax.rem(lax.axis_index("lat") // stride, count)
    bit = 1
    while bit < count:
        mine = lax.rem(place // bit, 2)
        pairs = [(i, i ^ (stride * bit)) for i in range(total)]
        view = part.reshape((part.shape[0] // 2, 2) + part.shape[1:])
        sent = lax.dynamic_index_in_dim(view, 1 - mine, 1, keepdims=False)
        kept = lax.dynamic_index_in_dim(view, mine, 1, keepdims=False)
        part = kept + lax.ppermute(sent, "lat", pairs)
        bit *= 2
    return part[0]


def scatter_rows(partial):
    outer, inner, core = lat_split()
    columns = partial.shape[1]
    part = partial.reshape(outer * inner, core, -1, columns).transpose(1, 0, 2, 3)
    part = halve(part, 1, core)
    part = part.reshape((outer, inner) + part.shape[1:]).transpose(1, 0, 2, 3)
    part = halve(part, core, inner)
    return halve(part, core * inner, outer)


def to_windows(field, win_rows, win_cols):
    lat_cells, lon_cells, depth = field.shape
    field = field.reshape(lat_cells // win_rows, win_rows, lon_cells // win_cols, win_cols, depth)
    field = field.transpose(0, 2, 1, 3, 4)
    return field.reshape(-1, win_rows * win_cols, depth)


def from_windows(tiles, lat_cells, lon_cells, win_rows, win_cols):
    depth = tiles.shape[-1]
    tiles = tiles.reshape(lat_cells // win_rows, lon_cells // win_cols, win_rows, win_cols, depth)
    return tiles.transpose(0, 2, 1, 3, 4).reshape(lat_cells, lon_cells, depth)


def attend_forward(qkv_tok, idents, lat_cells, lon_cells):
    model_width = qkv_tok.shape[1] // 3
    head_dim = model_width // HEADS
    window_len = WIN_R * WIN_C
    factor = head_dim ** (-0.5)
    qkv_tiles = to_windows(qkv_tok.reshape(lat_cells, lon_cells, 3 * model_width), WIN_R, WIN_C)
    number_win = qkv_tiles.shape[0]
    queries = qkv_tiles[:, :, :model_width].reshape(number_win, window_len, HEADS, head_dim)
    key_tiles = qkv_tiles[:, :, model_width : 2 * model_width].reshape(
        number_win, window_len, HEADS, head_dim
    )
    values = qkv_tiles[:, :, 2 * model_width :].reshape(number_win, window_len, HEADS, head_dim)
    id_tiles = to_windows(idents[:, :, None], WIN_R, WIN_C)[:, :, 0]
    visible = (id_tiles[:, :, None] == id_tiles[:, None, :])[:, None]
    scores = (
        jnp.einsum("wphd,wqhd->whpq", queries, key_tiles, preferred_element_type=jnp.float32)
        * factor
    )
    masked = jnp.where(visible, scores, -1e30)
    row_top = jnp.max(masked, axis=-1, keepdims=True)
    lifted = jnp.where(visible, jnp.exp(masked - row_top), 0.0)
    probs = (lifted / jnp.sum(lifted, axis=-1, keepdims=True)).astype(jnp.bfloat16)
    mixed_tile = jnp.einsum(
        "whpq,wqhd->wphd", probs, values, preferred_element_type=jnp.float32
    ).astype(jnp.bfloat16)
    mixed_tok = from_windows(
        mixed_tile.reshape(number_win, window_len, model_width), lat_cells, lon_cells, WIN_R, WIN_C
    ).reshape(-1, model_width)
    return (mixed_tok, (queries, key_tiles, values, probs))


def attend_backward(grad_mix, saved, lat_cells, lon_cells):
    queries, key_tiles, values, probs = saved
    model_width = grad_mix.shape[1]
    head_dim = model_width // HEADS
    window_len = WIN_R * WIN_C
    factor = head_dim ** (-0.5)
    number_win = queries.shape[0]
    mix_tiles = to_windows(
        grad_mix.reshape(lat_cells, lon_cells, model_width), WIN_R, WIN_C
    ).reshape(number_win, window_len, HEADS, head_dim)
    grad_probs = jnp.einsum(
        "wphd,wqhd->whpq", mix_tiles, values, preferred_element_type=jnp.float32
    )
    grad_values = jnp.einsum(
        "whpq,wphd->wqhd", probs, mix_tiles, preferred_element_type=jnp.float32
    ).astype(jnp.bfloat16)
    float_probs = probs.astype(jnp.float32)
    grad_scores = (
        factor
        * float_probs
        * (grad_probs - jnp.sum(float_probs * grad_probs, axis=-1, keepdims=True))
    ).astype(jnp.bfloat16)
    grad_queries = jnp.einsum(
        "whpq,wqhd->wphd", grad_scores, key_tiles, preferred_element_type=jnp.float32
    ).astype(jnp.bfloat16)
    grad_keys = jnp.einsum(
        "whpq,wphd->wqhd", grad_scores, queries, preferred_element_type=jnp.float32
    ).astype(jnp.bfloat16)
    joined = jnp.concatenate(
        [
            grad_queries.reshape(number_win, window_len, model_width),
            grad_keys.reshape(number_win, window_len, model_width),
            grad_values.reshape(number_win, window_len, model_width),
        ],
        axis=-1,
    )
    return from_windows(joined, lat_cells, lon_cells, WIN_R, WIN_C).reshape(-1, 3 * model_width)


def norm_forward(projected, gain):
    center = projected - jnp.mean(projected, axis=-1, keepdims=True)
    inverse = lax.rsqrt(jnp.mean(center * center, axis=-1, keepdims=True) + EPS)
    normal = center * inverse
    return ((normal * gain).astype(jnp.bfloat16), (normal, inverse))


def norm_backward(cot_flat, gain, saved):
    normal, inverse = saved
    scaled = cot_flat.astype(jnp.float32) * gain
    return (
        (
            scaled
            - jnp.mean(scaled, axis=-1, keepdims=True)
            - normal * jnp.mean(scaled * normal, axis=-1, keepdims=True)
        )
        * inverse
    ).astype(jnp.bfloat16)


def per_device(inputs, cotangent, idents, w_qkv, w_out, gain):
    lat_cells, lon_cells, model_width = inputs.shape
    half_rows = WIN_R // 2
    half_cols = WIN_C // 2
    upper_in = passed_along(inputs[:half_rows], "lat", -1)
    shifted = jnp.roll(jnp.concatenate([inputs[half_rows:], upper_in], axis=0), -half_cols, 1)
    tokens_flat = shifted.reshape(-1, model_width)
    qkv_full = gather_rows(w_qkv)
    out_full = gather_rows(w_out)
    qkv_tok = jnp.dot(
        tokens_flat,
        qkv_full,
        preferred_element_type=jnp.float32,
    ).astype(jnp.bfloat16)
    mixed_tok, saved = attend_forward(qkv_tok, idents, lat_cells, lon_cells)
    projected = jnp.dot(
        mixed_tok,
        out_full,
        preferred_element_type=jnp.float32,
    )
    normed, norm_saved = norm_forward(projected, gain)
    normed_grid = jnp.roll(normed.reshape(lat_cells, lon_cells, model_width), half_cols, 1)
    lower_out = passed_along(normed_grid[-half_rows:], "lat", 1)
    upper_cot = passed_along(cotangent[:half_rows], "lat", -1)
    cot_shift = jnp.roll(jnp.concatenate([cotangent[half_rows:], upper_cot], axis=0), -half_cols, 1)
    grad_proj = norm_backward(cot_shift.reshape(-1, model_width), gain, norm_saved)
    grad_mix = jnp.dot(
        grad_proj,
        out_full.T,
        preferred_element_type=jnp.float32,
    ).astype(jnp.bfloat16)
    grad_cells = attend_backward(grad_mix, saved, lat_cells, lon_cells)
    first_part = jnp.dot(mixed_tok.T, grad_proj, preferred_element_type=jnp.float32)
    second_part = jnp.dot(tokens_flat.T, grad_cells, preferred_element_type=jnp.float32)
    grad_out = scatter_rows(first_part)
    grad_qkv = scatter_rows(second_part)
    grad_shift = jnp.dot(
        grad_cells,
        qkv_full.T,
        preferred_element_type=jnp.float32,
    ).astype(jnp.bfloat16)
    grad_grid = jnp.roll(grad_shift.reshape(lat_cells, lon_cells, model_width), half_cols, 1)
    lower_grad = passed_along(grad_grid[-half_rows:], "lat", 1)
    back_out_grid = jnp.concatenate([lower_out, normed_grid[:-half_rows]], axis=0)
    back_grad_grid = jnp.concatenate([lower_grad, grad_grid[:-half_rows]], axis=0)
    output = (inputs.astype(jnp.float32) + back_out_grid.astype(jnp.float32)).astype(jnp.bfloat16)
    grad_in = (cotangent.astype(jnp.float32) + back_grad_grid.astype(jnp.float32)).astype(
        jnp.bfloat16
    )
    return (output, grad_in, grad_qkv, grad_out)


def solution(mesh):
    in_specs = (
        P(("grp", "lat"), None, None),
        P(("grp", "lat"), None, None),
        P(("grp", "lat"), None),
        P("lat", None),
        P("lat", None),
        P(),
    )
    out_specs = (
        P(("grp", "lat"), None, None),
        P(("grp", "lat"), None, None),
        P(("grp", "lat"), None),
        P(("grp", "lat"), None),
    )
    return jax.shard_map(
        per_device, mesh=mesh, in_specs=in_specs, out_specs=out_specs, check_vma=False
    )
```

```python
import functools
import math

import jax
import jax.numpy as jnp
from jax import lax
from jax.experimental import pallas as pl
from jax.experimental.pallas import tpu as pltpu
from jax.sharding import PartitionSpec as P

HEADS = 8
WIN_R = 6
WIN_C = 12
EPS = 1e-05
HIDDEN = -1e30
VMEM_BYTES = 40 * 1024 * 1024

NN = (((1,), (0,)), ((), ()))
NT = (((1,), (1,)), ((), ()))
TN = (((0,), (0,)), ((), ()))


def mxu(left, right, dims=NN):
    return lax.dot_general(left, right, dims, preferred_element_type=jnp.float32)


def passed_along(value, axis, steps):
    count = lax.axis_size(axis)
    first, last = (max(0, -steps), min(count, count - steps))
    return lax.ppermute(value, axis, [(source, source + steps) for source in range(first, last)])


def padded_rows():
    return -(-WIN_R * WIN_C // 16) * 16


def to_windows(field):
    lat_cells, lon_cells, depth = field.shape
    field = field.reshape(lat_cells // WIN_R, WIN_R, lon_cells // WIN_C, WIN_C, depth)
    field = field.transpose(0, 2, 1, 3, 4).reshape(-1, WIN_R * WIN_C, depth)
    return jnp.pad(field, ((0, 0), (0, padded_rows() - WIN_R * WIN_C), (0, 0)))


def from_windows(tiles, lat_cells, lon_cells):
    depth = tiles.shape[-1]
    tiles = tiles.reshape(-1, padded_rows(), depth)[:, : WIN_R * WIN_C]
    tiles = tiles.reshape(lat_cells // WIN_R, lon_cells // WIN_C, WIN_R, WIN_C, depth)
    return tiles.transpose(0, 2, 1, 3, 4).reshape(lat_cells, lon_cells, depth)


def head_halves(value):
    lane = lax.broadcasted_iota(jnp.int32, value.shape, 1)
    zero = jnp.zeros_like(value)
    low = jnp.where(lane < value.shape[1] // 2, value, zero)
    high = jnp.where(lane < value.shape[1] // 2, zero, value)
    return low, high


def forward_kernel(
    x_ref, w_qkv_ref, w_out_ref, cot_ref, bias_ref, gain_ref,
    qkv_ref, probs_ref, normed_ref, grad_mix_ref, grad_out_ref,
    mixed_ref, grad_proj_ref,
):
    windows, win = bias_ref.shape[:2]
    width = x_ref.shape[1]
    pair = 2 * width // HEADS
    factor = (width // HEADS) ** (-0.5) * math.log2(math.e)

    for part in range(3):
        columns = slice(part * width, (part + 1) * width)
        qkv_ref[:, columns] = mxu(x_ref[...], w_qkv_ref[:, columns]).astype(jnp.bfloat16)

    def attend(window, carry):
        rows = pl.ds(pl.multiple_of(window * win, 16), win)
        bias = bias_ref[window]
        for at in range(HEADS // 2):
            columns = slice(at * pair, (at + 1) * pair)
            keys = qkv_ref[rows, width + at * pair : width + (at + 1) * pair]
            values = qkv_ref[rows, 2 * width + at * pair : 2 * width + (at + 1) * pair]
            both = []
            for head, queries in enumerate(head_halves(qkv_ref[rows, columns])):
                scores = mxu(keys, queries, NT) * factor + bias
                lifted = jnp.exp2(scores - jnp.max(scores, axis=0, keepdims=True))
                total = jnp.sum(lifted, axis=0, keepdims=True)
                probs = (lifted * (1.0 / total)).astype(jnp.bfloat16)
                probs_ref[window, 2 * at + head] = probs
                both.append(probs)
            mixed = mxu(
                jnp.concatenate(both, axis=0), jnp.concatenate(head_halves(values), axis=0), TN
            )
            mixed_ref[rows, columns] = mixed.astype(jnp.bfloat16)
        return carry

    lax.fori_loop(0, windows, attend, 0)

    gain = gain_ref[...]

    def normalise(window, carry):
        rows = pl.ds(pl.multiple_of(window * win, 16), win)
        projected = mxu(mixed_ref[rows, :], w_out_ref[...])
        center = projected - jnp.mean(projected, axis=-1, keepdims=True)
        inverse = lax.rsqrt(jnp.mean(center * center, axis=-1, keepdims=True) + EPS)
        normal = center * inverse
        normed_ref[rows, :] = (normal * gain).astype(jnp.bfloat16)
        scaled = cot_ref[rows, :].astype(jnp.float32) * gain
        grad_proj = (
            scaled
            - jnp.mean(scaled, axis=-1, keepdims=True)
            - normal * jnp.mean(scaled * normal, axis=-1, keepdims=True)
        ) * inverse
        grad_proj_ref[rows, :] = grad_proj.astype(jnp.bfloat16)
        return carry

    lax.fori_loop(0, windows, normalise, 0)
    grad_out_ref[...] = mxu(mixed_ref[...], grad_proj_ref[...], TN)
    grad_mix_ref[...] = mxu(grad_proj_ref[...], w_out_ref[...], NT).astype(jnp.bfloat16)


def backward_kernel(
    qkv_ref, probs_ref, grad_mix_ref, turned_ref, cells_ref, grad_qkv_ref
):
    windows, _, win = probs_ref.shape[:3]
    width = grad_mix_ref.shape[1]
    pair = 2 * width // HEADS
    factor = (width // HEADS) ** (-0.5)

    def attend(window, carry):
        rows = pl.ds(pl.multiple_of(window * win, 16), win)
        for at in range(HEADS // 2):
            columns = slice(at * pair, (at + 1) * pair)
            key_columns = slice(width + at * pair, width + (at + 1) * pair)
            value_columns = slice(2 * width + at * pair, 2 * width + (at + 1) * pair)
            queries = head_halves(qkv_ref[rows, columns])
            keys = head_halves(qkv_ref[rows, key_columns])
            values = qkv_ref[rows, value_columns]
            grad_keys = grad_values = None
            both = []
            for head, mix in enumerate(head_halves(grad_mix_ref[rows, columns])):
                probs = probs_ref[window, 2 * at + head]
                float_probs = probs.astype(jnp.float32)
                grad_probs = mxu(values, mix, NT)
                center = jnp.sum(float_probs * grad_probs, axis=0, keepdims=True)
                grad_scores = (factor * float_probs * (grad_probs - center)).astype(jnp.bfloat16)
                both.append(grad_scores)
                value_term = mxu(probs, mix)
                key_term = mxu(grad_scores, queries[head])
                grad_values = value_term if head == 0 else grad_values + value_term
                grad_keys = key_term if head == 0 else grad_keys + key_term
            grad_queries = mxu(jnp.concatenate(both, axis=0), jnp.concatenate(keys, axis=0), TN)
            cells_ref[rows, columns] = grad_queries.astype(jnp.bfloat16)
            cells_ref[rows, key_columns] = grad_keys.astype(jnp.bfloat16)
            cells_ref[rows, value_columns] = grad_values.astype(jnp.bfloat16)
        return carry

    lax.fori_loop(0, windows, attend, 0)
    for part in range(3):
        columns = slice(part * width, (part + 1) * width)
        grad_qkv_ref[:, columns] = mxu(turned_ref[...], cells_ref[:, columns])


def call(kernel, name, outs, operands, scratch=(), flops=0):
    size = sum(math.prod(o.shape) * o.dtype.itemsize for o in (*outs, *operands))
    return pl.pallas_call(
        kernel,
        out_shape=outs,
        in_specs=[pl.BlockSpec(memory_space=pltpu.VMEM)] * len(operands),
        out_specs=[pl.BlockSpec(memory_space=pltpu.VMEM)] * len(outs),
        scratch_shapes=list(scratch),
        compiler_params=pltpu.CompilerParams(vmem_limit_bytes=VMEM_BYTES),
        cost_estimate=pl.CostEstimate(flops=flops, bytes_accessed=size, transcendentals=0),
        name=name,
    )(*operands)


def per_device(inputs, cotangent, idents, w_qkv, w_out, gain):
    lat_cells, lon_cells, width = inputs.shape
    half_rows = WIN_R // 2
    half_cols = WIN_C // 2
    win = padded_rows()
    weights = lax.all_gather(jnp.concatenate([w_qkv, w_out], axis=1), "lat", axis=0, tiled=True)
    qkv_full, out_full = weights[:, : 3 * width], weights[:, 3 * width :]

    upper_in = passed_along(inputs[:half_rows], "lat", -1)
    upper_cot = passed_along(cotangent[:half_rows], "lat", -1)
    shifted = jnp.roll(jnp.concatenate([inputs[half_rows:], upper_in], axis=0), -half_cols, 1)
    cot_shift = jnp.roll(jnp.concatenate([cotangent[half_rows:], upper_cot], axis=0), -half_cols, 1)
    tokens = to_windows(shifted).reshape(-1, width)
    cot = to_windows(cot_shift).reshape(-1, width)
    labels = to_windows(idents[:, :, None] + 1)[:, :, 0]
    bias = jnp.where(labels[:, :, None] == labels[:, None, :], 0.0, HIDDEN).astype(jnp.float32)
    windows = labels.shape[0]
    cells = windows * win

    def shape(*dims, dtype=jnp.bfloat16):
        return jax.ShapeDtypeStruct(dims, dtype)

    qkv, probs, normed, grad_mix, grad_out = call(
        forward_kernel,
        "forward",
        (
            shape(cells, 3 * width),
            shape(windows, HEADS, win, win),
            shape(cells, width),
            shape(cells, width),
            shape(width, width, dtype=jnp.float32),
        ),
        (tokens, qkv_full, out_full, cot, bias, gain[None]),
        (pltpu.VMEM((cells, width), jnp.bfloat16), pltpu.VMEM((cells, width), jnp.bfloat16)),
        flops=2 * cells * width * width * 10,
    )
    grad_out = lax.psum_scatter(grad_out, "lat", scatter_dimension=0, tiled=True)
    grad_cells, grad_qkv = call(
        backward_kernel,
        "backward",
        (shape(cells, 3 * width), shape(width, 3 * width, dtype=jnp.float32)),
        (qkv, probs, grad_mix, tokens.T),
        flops=2 * cells * width * width * 10,
    )
    grad_qkv = lax.psum_scatter(grad_qkv, "lat", scatter_dimension=0, tiled=True)
    grad_shift = mxu(grad_cells, qkv_full, NT).astype(jnp.bfloat16)

    def moved_back(field, base):
        grid = jnp.roll(from_windows(field, lat_cells, lon_cells), half_cols, 1)
        lower = passed_along(grid[-half_rows:], "lat", 1)
        back = jnp.concatenate([lower, grid[:-half_rows]], axis=0)
        return (base.astype(jnp.float32) + back.astype(jnp.float32)).astype(jnp.bfloat16)

    return (moved_back(normed, inputs), moved_back(grad_shift, cotangent), grad_qkv, grad_out)


def solution(mesh):
    in_specs = (
        P(("grp", "lat"), None, None),
        P(("grp", "lat"), None, None),
        P(("grp", "lat"), None),
        P("lat", None),
        P("lat", None),
        P(),
    )
    out_specs = (
        P(("grp", "lat"), None, None),
        P(("grp", "lat"), None, None),
        P(("grp", "lat"), None),
        P(("grp", "lat"), None),
    )
    return jax.shard_map(
        per_device, mesh=mesh, in_specs=in_specs, out_specs=out_specs, check_vma=False
    )
```

```python
import functools
import math

import jax
import jax.numpy as jnp
from jax import lax
from jax.experimental import pallas as pl
from jax.experimental.pallas import tpu as pltpu
from jax.sharding import PartitionSpec as P

HEADS = 8
WIN_R = 6
WIN_C = 12
EPS = 1e-05
HIDDEN = -1e30
VMEM_BYTES = 40 * 1024 * 1024

NN = (((1,), (0,)), ((), ()))
NT = (((1,), (1,)), ((), ()))
TN = (((0,), (0,)), ((), ()))


def mxu(left, right, dims=NN):
    return lax.dot_general(left, right, dims, preferred_element_type=jnp.float32)


def passed_along(value, axis, steps):
    count = lax.axis_size(axis)
    first, last = (max(0, -steps), min(count, count - steps))
    return lax.ppermute(value, axis, [(source, source + steps) for source in range(first, last)])


def padded_rows():
    return -(-WIN_R * WIN_C // 16) * 16


def to_windows(field):
    lat_cells, lon_cells, depth = field.shape
    field = field.reshape(lat_cells // WIN_R, WIN_R, lon_cells // WIN_C, WIN_C, depth)
    field = field.transpose(0, 2, 1, 3, 4).reshape(-1, WIN_R * WIN_C, depth)
    return jnp.pad(field, ((0, 0), (0, padded_rows() - WIN_R * WIN_C), (0, 0)))


def from_windows(tiles, lat_cells, lon_cells):
    depth = tiles.shape[-1]
    tiles = tiles.reshape(-1, padded_rows(), depth)[:, : WIN_R * WIN_C]
    tiles = tiles.reshape(lat_cells // WIN_R, lon_cells // WIN_C, WIN_R, WIN_C, depth)
    return tiles.transpose(0, 2, 1, 3, 4).reshape(lat_cells, lon_cells, depth)


def head_halves(value):
    lane = lax.broadcasted_iota(jnp.int32, value.shape, 1)
    zero = jnp.zeros_like(value)
    low = jnp.where(lane < value.shape[1] // 2, value, zero)
    high = jnp.where(lane < value.shape[1] // 2, zero, value)
    return low, high


def block_kernel(
    into_ref, from_ref, x_ref, near_ref, near_other_ref, far_ref, far_other_ref, cot_ref, bias_ref, gain_ref,
    normed_ref, cells_ref, w_qkv_ref, grad_out_ref,
    w_out_ref, qkv_ref, probs_ref, mixed_ref, grad_proj_ref, grad_mix_ref,
):
    windows, win = bias_ref.shape[:2]
    width = x_ref.shape[1]
    pair = 2 * width // HEADS
    scale = (width // HEADS) ** (-0.5)
    factor = scale * math.log2(math.e)

    blocks = into_ref.shape[0]
    depth = width // blocks
    place = 0
    for part_ref in (near_ref, near_other_ref, far_ref, far_other_ref):
        for at in range(part_ref.shape[0]):
            rows = pl.ds(pl.multiple_of(into_ref[place] * depth, depth), depth)
            w_qkv_ref[rows, :] = part_ref[at, :, : 3 * width]
            w_out_ref[rows, :] = part_ref[at, :, 3 * width :]
            place += 1

    for part in range(3):
        columns = slice(part * width, (part + 1) * width)
        qkv_ref[:, columns] = mxu(x_ref[...], w_qkv_ref[:, columns]).astype(jnp.bfloat16)

    def attend(window, carry):
        rows = pl.ds(pl.multiple_of(window * win, 16), win)
        bias = bias_ref[window]
        for at in range(HEADS // 2):
            columns = slice(at * pair, (at + 1) * pair)
            keys = qkv_ref[rows, width + at * pair : width + (at + 1) * pair]
            values = qkv_ref[rows, 2 * width + at * pair : 2 * width + (at + 1) * pair]
            both = []
            for head, queries in enumerate(head_halves(qkv_ref[rows, columns])):
                scores = mxu(keys, queries, NT) * factor + bias
                lifted = jnp.exp2(scores - jnp.max(scores, axis=0, keepdims=True))
                total = jnp.sum(lifted, axis=0, keepdims=True)
                probs = (lifted * (1.0 / total)).astype(jnp.bfloat16)
                probs_ref[window, 2 * at + head] = probs
                both.append(probs)
            mixed = mxu(
                jnp.concatenate(both, axis=0), jnp.concatenate(head_halves(values), axis=0), TN
            )
            mixed_ref[rows, columns] = mixed.astype(jnp.bfloat16)
        return carry

    lax.fori_loop(0, windows, attend, 0)

    gain = gain_ref[...]

    def normalise(window, carry):
        rows = pl.ds(pl.multiple_of(window * win, 16), win)
        projected = mxu(mixed_ref[rows, :], w_out_ref[...])
        center = projected - jnp.mean(projected, axis=-1, keepdims=True)
        inverse = lax.rsqrt(jnp.mean(center * center, axis=-1, keepdims=True) + EPS)
        normal = center * inverse
        normed_ref[rows, :] = (normal * gain).astype(jnp.bfloat16)
        scaled = cot_ref[rows, :].astype(jnp.float32) * gain
        grad_proj = (
            scaled
            - jnp.mean(scaled, axis=-1, keepdims=True)
            - normal * jnp.mean(scaled * normal, axis=-1, keepdims=True)
        ) * inverse
        grad_proj_ref[rows, :] = grad_proj.astype(jnp.bfloat16)
        return carry

    lax.fori_loop(0, windows, normalise, 0)
    grad_out = mxu(mixed_ref[...], grad_proj_ref[...], TN)
    for block in range(blocks):
        rows = pl.ds(pl.multiple_of(from_ref[block] * depth, depth), depth)
        grad_out_ref[rows, :] = grad_out[block * depth : (block + 1) * depth, :]
    grad_mix_ref[...] = mxu(grad_proj_ref[...], w_out_ref[...], NT).astype(jnp.bfloat16)

    def attend_back(window, carry):
        rows = pl.ds(pl.multiple_of(window * win, 16), win)
        for at in range(HEADS // 2):
            columns = slice(at * pair, (at + 1) * pair)
            key_columns = slice(width + at * pair, width + (at + 1) * pair)
            value_columns = slice(2 * width + at * pair, 2 * width + (at + 1) * pair)
            queries = head_halves(qkv_ref[rows, columns])
            keys = head_halves(qkv_ref[rows, key_columns])
            values = qkv_ref[rows, value_columns]
            grad_keys = grad_values = None
            both = []
            for head, mix in enumerate(head_halves(grad_mix_ref[rows, columns])):
                probs = probs_ref[window, 2 * at + head]
                float_probs = probs.astype(jnp.float32)
                grad_probs = mxu(values, mix, NT)
                center = jnp.sum(float_probs * grad_probs, axis=0, keepdims=True)
                grad_scores = (scale * float_probs * (grad_probs - center)).astype(jnp.bfloat16)
                both.append(grad_scores)
                value_term = mxu(probs, mix)
                key_term = mxu(grad_scores, queries[head])
                grad_values = value_term if head == 0 else grad_values + value_term
                grad_keys = key_term if head == 0 else grad_keys + key_term
            grad_queries = mxu(jnp.concatenate(both, axis=0), jnp.concatenate(keys, axis=0), TN)
            cells_ref[rows, columns] = grad_queries.astype(jnp.bfloat16)
            cells_ref[rows, key_columns] = grad_keys.astype(jnp.bfloat16)
            cells_ref[rows, value_columns] = grad_values.astype(jnp.bfloat16)
        return carry

    lax.fori_loop(0, windows, attend_back, 0)


def exchanged(value, distance):
    count = lax.axis_size("lat")
    return lax.ppermute(value, "lat", [(i, i ^ distance) for i in range(count)])


def gathered(block):
    count = lax.axis_size("lat")
    outer = [exchanged(block, 4 * step) for step in range(count // 4 - 1, 0, -1)]
    distances = [4 * step for step in range(count // 4 - 1, 0, -1)]
    early = jnp.stack([block, outer[-1]])
    early = jnp.concatenate([early, exchanged(early, 2)])
    early_at = [0, distances[-1], 2, distances[-1] + 2]
    late = jnp.stack(outer[:-1] + [exchanged(value, 2) for value in outer[:-1]])
    late_at = distances[:-1] + [distance + 2 for distance in distances[:-1]]
    early_other, late_other = exchanged(early, 1), exchanged(late, 1)
    order = early_at + [at + 1 for at in early_at] + late_at + [at + 1 for at in late_at]
    return (early, early_other, late, late_other), order


def reversed_bits(value, count):
    result = 0
    bit = 1
    while bit < count:
        result = 2 * result + (value & 1)
        value = value >> 1
        bit *= 2
    return result


def summed(sent, kept):
    count = lax.axis_size("lat")
    distance = 1
    while True:
        kept = kept + exchanged(sent, distance)
        distance *= 2
        if distance >= count:
            return kept
        half = kept.shape[0] // 2
        kept, sent = kept[:half], kept[half:]


def call(kernel, name, outs, tables, operands, scratch=(), flops=0):
    size = sum(math.prod(o.shape) * o.dtype.itemsize for o in (*outs, *operands))
    return pl.pallas_call(
        kernel,
        out_shape=outs,
        in_specs=[pl.BlockSpec(memory_space=pltpu.SMEM)] * len(tables)
        + [pl.BlockSpec(memory_space=pltpu.VMEM)] * len(operands),
        out_specs=[pl.BlockSpec(memory_space=pltpu.VMEM)] * len(outs),
        scratch_shapes=list(scratch),
        compiler_params=pltpu.CompilerParams(vmem_limit_bytes=VMEM_BYTES),
        cost_estimate=pl.CostEstimate(flops=flops, bytes_accessed=size, transcendentals=0),
        name=name,
    )(*tables, *operands)


def per_device(inputs, cotangent, idents, w_qkv, w_out, gain):
    lat_cells, lon_cells, width = inputs.shape
    half_rows = WIN_R // 2
    half_cols = WIN_C // 2
    win = padded_rows()
    count = lax.axis_size("lat")
    me = lax.axis_index("lat")
    weights = jnp.concatenate([w_qkv, w_out], axis=1)
    direct = count >= 16 and count & (count - 1) == 0 and width % (16 * count) == 0
    if direct:
        shards, order = gathered(weights)
        blocks = jnp.arange(count, dtype=jnp.int32)
        into = jnp.array(order, jnp.int32) ^ me
        to_slot = reversed_bits(blocks ^ me, count)
        of_slot = reversed_bits(blocks, count) ^ me
    else:
        weights = lax.all_gather(weights, "lat", axis=0, tiled=True)
        shards = tuple(weights.reshape(4, 4, width // 16, 4 * width))
        into = to_slot = of_slot = jnp.arange(16, dtype=jnp.int32)

    upper_in = passed_along(inputs[:half_rows], "lat", -1)
    upper_cot = passed_along(cotangent[:half_rows], "lat", -1)
    shifted = jnp.roll(jnp.concatenate([inputs[half_rows:], upper_in], axis=0), -half_cols, 1)
    cot_shift = jnp.roll(jnp.concatenate([cotangent[half_rows:], upper_cot], axis=0), -half_cols, 1)
    tokens = to_windows(shifted).reshape(-1, width)
    cot = to_windows(cot_shift).reshape(-1, width)
    labels = to_windows(idents[:, :, None] + 1)[:, :, 0]
    bias = jnp.where(labels[:, :, None] == labels[:, None, :], 0.0, HIDDEN).astype(jnp.float32)
    windows = labels.shape[0]
    cells = windows * win

    def shape(*dims, dtype=jnp.bfloat16):
        return jax.ShapeDtypeStruct(dims, dtype)

    normed, grad_cells, qkv_full, grad_out = call(
        block_kernel,
        "block",
        (
            shape(cells, width),
            shape(cells, 3 * width),
            shape(width, 3 * width),
            shape(width, width, dtype=jnp.float32),
        ),
        (into, to_slot),
        (tokens, *shards, cot, bias, gain[None]),
        (
            pltpu.VMEM((width, width), jnp.bfloat16),
            pltpu.VMEM((cells, 3 * width), jnp.bfloat16),
            pltpu.VMEM((windows, HEADS, win, win), jnp.bfloat16),
            pltpu.VMEM((cells, width), jnp.bfloat16),
            pltpu.VMEM((cells, width), jnp.bfloat16),
            pltpu.VMEM((cells, width), jnp.bfloat16),
        ),
        flops=2 * cells * width * width * 10,
    )
    turned = jnp.take(tokens.T.reshape(of_slot.size, -1, cells), of_slot, axis=0)
    turned = turned.reshape(width, cells)
    if direct:
        half = width // 2
        grad_out = summed(grad_out[half:], grad_out[:half])
        parts = []
        for part in range(3):
            columns = grad_cells[:, part * width : (part + 1) * width]
            parts.append(summed(mxu(turned[half:], columns), mxu(turned[:half], columns)))
        grad_qkv = jnp.concatenate(parts, axis=1)
    else:
        both = jnp.concatenate([mxu(turned, grad_cells), grad_out], axis=1)
        both = lax.psum_scatter(both, "lat", scatter_dimension=0, tiled=True)
        grad_qkv, grad_out = both[:, : 3 * width], both[:, 3 * width :]
    grad_shift = mxu(grad_cells, qkv_full, NT).astype(jnp.bfloat16)

    def moved_back(field, base):
        grid = jnp.roll(from_windows(field, lat_cells, lon_cells), half_cols, 1)
        lower = passed_along(grid[-half_rows:], "lat", 1)
        back = jnp.concatenate([lower, grid[:-half_rows]], axis=0)
        return (base.astype(jnp.float32) + back.astype(jnp.float32)).astype(jnp.bfloat16)

    return (moved_back(normed, inputs), moved_back(grad_shift, cotangent), grad_qkv, grad_out)


def solution(mesh):
    in_specs = (
        P(("grp", "lat"), None, None),
        P(("grp", "lat"), None, None),
        P(("grp", "lat"), None),
        P("lat", None),
        P("lat", None),
        P(),
    )
    out_specs = (
        P(("grp", "lat"), None, None),
        P(("grp", "lat"), None, None),
        P(("grp", "lat"), None),
        P(("grp", "lat"), None),
    )
    return jax.shard_map(
        per_device, mesh=mesh, in_specs=in_specs, out_specs=out_specs, check_vma=False
    )
```

```python
import math

import jax
import jax.numpy as jnp
import numpy as np
from jax import lax
from jax.experimental import pallas as pl
from jax.experimental.pallas import tpu as pltpu
from jax.sharding import PartitionSpec as P

HEADS = 8
WIN_R = 6
WIN_C = 12
EPS = 1e-05
HIDDEN = -1e30
GROUP = 2
VMEM_BYTES = 40 * 1024 * 1024

NN = (((1,), (0,)), ((), ()))
NT = (((1,), (1,)), ((), ()))
TN = (((0,), (0,)), ((), ()))


def mxu(left, right, dims=NN):
    return lax.dot_general(left, right, dims, preferred_element_type=jnp.float32)


def passed_along(value, axis, steps):
    count = lax.axis_size(axis)
    first, last = (max(0, -steps), min(count, count - steps))
    return lax.ppermute(value, axis, [(source, source + steps) for source in range(first, last)])


def padded_rows():
    return -(-WIN_R * WIN_C // 16) * 16


def to_windows(field):
    lat_cells, lon_cells = field.shape
    field = field.reshape(lat_cells // WIN_R, WIN_R, lon_cells // WIN_C, WIN_C)
    field = field.transpose(0, 2, 1, 3).reshape(-1, WIN_R * WIN_C)
    return jnp.pad(field, ((0, 0), (0, padded_rows() - WIN_R * WIN_C)))


def window_places(lon_cells):
    win = padded_rows()
    places = np.zeros((WIN_R, lon_cells // WIN_C, win, lon_cells), np.float32)
    for row in range(WIN_R):
        for window in range(lon_cells // WIN_C):
            for column in range(WIN_C):
                source = (window * WIN_C + column + WIN_C // 2) % lon_cells
                places[row, window, row * WIN_C + column, source] = 1
    return places.reshape(WIN_R, -1, lon_cells)


def masked_heads(value, head_dim):
    head = lax.broadcasted_iota(jnp.int32, value.shape, 1) // head_dim
    zero = jnp.zeros_like(value)
    count = value.shape[1] // head_dim
    return jnp.concatenate([jnp.where(head == at, value, zero) for at in range(count)], axis=0)


def own_heads(stacked, head_dim):
    count = stacked.shape[1] // head_dim
    rows = stacked.shape[0] // count
    head = lax.broadcasted_iota(jnp.int32, (rows, stacked.shape[1]), 1) // head_dim
    result = stacked[:rows]
    for at in range(1, count):
        result = jnp.where(head == at, stacked[at * rows : (at + 1) * rows], result)
    return result


def turned_heads(stacked, count):
    rows = stacked.shape[0] // count
    return jnp.concatenate(
        [stacked[at * rows : (at + 1) * rows].T for at in range(count)], axis=0
    )


def prepare_kernel(
    to_slot_ref, inputs_ref, upper_in_ref, cot_ref, upper_cot_ref, places_ref,
    tokens_ref, cot_tokens_ref, turned_ref,
):
    half = upper_in_ref.shape[0]
    lat_cells = inputs_ref.shape[0]
    cells = places_ref.shape[1]
    blocks = to_slot_ref.shape[0]
    for band in range(lat_cells // WIN_R):
        rows = slice(band * cells, (band + 1) * cells)
        for own_ref, upper_ref, result_ref in (
            (inputs_ref, upper_in_ref, tokens_ref),
            (cot_ref, upper_cot_ref, cot_tokens_ref),
        ):
            total = None
            for row in range(WIN_R):
                source = band * WIN_R + row + half
                field = own_ref[source] if source < lat_cells else upper_ref[source - lat_cells]
                term = mxu(places_ref[row], field)
                total = term if total is None else total + term
            result_ref[rows, :] = total.astype(jnp.bfloat16)
    depth = tokens_ref.shape[1] // blocks
    turned = tokens_ref[...].T
    for block in range(blocks):
        rows = pl.ds(pl.multiple_of(to_slot_ref[block] * depth, depth), depth)
        turned_ref[rows, :] = turned[block * depth : (block + 1) * depth, :]


def finish_kernel(
    cells_ref, w_qkv_ref, normed_ref, inputs_ref, cot_ref, places_ref,
    output_ref, lower_out_ref, grad_in_ref, lower_grad_ref, shift_ref,
):
    lat_cells = inputs_ref.shape[0]
    half = lower_out_ref.shape[0]
    count = places_ref.shape[1]
    shift_ref[...] = mxu(cells_ref[...], w_qkv_ref[...], NT).astype(jnp.bfloat16)
    for value_ref, base_ref, result_ref, lower_ref in (
        (normed_ref, inputs_ref, output_ref, lower_out_ref),
        (shift_ref, cot_ref, grad_in_ref, lower_grad_ref),
    ):
        result_ref[:half] = base_ref[:half]
        for band in range(lat_cells // WIN_R):
            value = value_ref[band * count : (band + 1) * count, :]
            for row in range(WIN_R):
                back = mxu(places_ref[row], value, TN)
                target = band * WIN_R + row + half
                if target < lat_cells:
                    base = base_ref[target].astype(jnp.float32)
                    result_ref[target] = (base + back).astype(jnp.bfloat16)
                else:
                    lower_ref[target - lat_cells] = back.astype(jnp.bfloat16)


def block_kernel(
    into_ref, to_slot_ref, x_ref, turned_ref, near_ref, near_other_ref, far_ref, far_other_ref,
    cot_ref, bias_ref, gain_ref,
    normed_ref, cells_ref, w_qkv_ref, *rest,
):
    grad_refs, (w_out_ref, qkv_ref, probs_ref, mixed_ref, grad_proj_ref, grad_mix_ref) = rest[:8], rest[8:]
    windows, win = bias_ref.shape[:2]
    width = x_ref.shape[1]
    head_dim = width // HEADS
    group = GROUP * head_dim
    scale = head_dim ** (-0.5)
    factor = scale * math.log2(math.e)

    blocks = into_ref.shape[0]
    depth = width // blocks
    place = 0
    for part_ref in (near_ref, near_other_ref, far_ref, far_other_ref):
        for at in range(part_ref.shape[0]):
            rows = pl.ds(pl.multiple_of(into_ref[place] * depth, depth), depth)
            w_qkv_ref[rows, :] = part_ref[at, :, : 3 * width]
            w_out_ref[rows, :] = part_ref[at, :, 3 * width :]
            place += 1

    for part in range(3):
        columns = slice(part * width, (part + 1) * width)
        qkv_ref[:, columns] = mxu(x_ref[...], w_qkv_ref[:, columns]).astype(jnp.bfloat16)

    def attend(window, carry):
        rows = pl.ds(pl.multiple_of(window * win, 16), win)
        bias = bias_ref[window]
        for at in range(HEADS // GROUP):
            columns = slice(at * group, (at + 1) * group)
            queries = qkv_ref[rows, columns]
            keys = qkv_ref[rows, width + at * group : width + (at + 1) * group]
            values = qkv_ref[rows, 2 * width + at * group : 2 * width + (at + 1) * group]
            scores = mxu(masked_heads(keys, head_dim), queries, NT)
            scores = scores.reshape(GROUP, win, win) * factor + bias
            lifted = jnp.exp2(scores - jnp.max(scores, axis=1, keepdims=True))
            total = jnp.sum(lifted, axis=1, keepdims=True)
            probs = (lifted * (1.0 / total)).astype(jnp.bfloat16)
            probs = probs.reshape(GROUP * win, win)
            probs_ref[window, at] = probs
            mixed = own_heads(mxu(turned_heads(probs, GROUP), values), head_dim)
            mixed_ref[rows, columns] = mixed.astype(jnp.bfloat16)
        return carry

    lax.fori_loop(0, windows, attend, 0)

    gain = gain_ref[...]

    def normalise(window, carry):
        rows = pl.ds(pl.multiple_of(window * win, 16), win)
        projected = mxu(mixed_ref[rows, :], w_out_ref[...])
        center = projected - jnp.mean(projected, axis=-1, keepdims=True)
        inverse = lax.rsqrt(jnp.mean(center * center, axis=-1, keepdims=True) + EPS)
        normal = center * inverse
        normed_ref[rows, :] = (normal * gain).astype(jnp.bfloat16)
        scaled = cot_ref[rows, :].astype(jnp.float32) * gain
        grad_proj = (
            scaled
            - jnp.mean(scaled, axis=-1, keepdims=True)
            - normal * jnp.mean(scaled * normal, axis=-1, keepdims=True)
        ) * inverse
        grad_proj_ref[rows, :] = grad_proj.astype(jnp.bfloat16)
        return carry

    lax.fori_loop(0, windows, normalise, 0)
    sent_ref, kept_ref = grad_refs[:2]
    half = kept_ref.shape[0]
    grad_out = mxu(mixed_ref[...], grad_proj_ref[...], TN)
    for block in range(blocks):
        slot = to_slot_ref[block]
        value = grad_out[block * depth : (block + 1) * depth, :]
        rows = pl.ds(pl.multiple_of(lax.rem(slot, blocks // 2) * depth, depth), depth)

        @pl.when(slot < blocks // 2)
        def _():
            kept_ref[rows, :] = value

        @pl.when(slot >= blocks // 2)
        def _():
            sent_ref[rows, :] = value

    grad_mix_ref[...] = mxu(grad_proj_ref[...], w_out_ref[...], NT).astype(jnp.bfloat16)

    def attend_back(window, carry):
        rows = pl.ds(pl.multiple_of(window * win, 16), win)
        for at in range(HEADS // GROUP):
            columns = slice(at * group, (at + 1) * group)
            key_columns = slice(width + at * group, width + (at + 1) * group)
            value_columns = slice(2 * width + at * group, 2 * width + (at + 1) * group)
            mix = grad_mix_ref[rows, columns]
            probs = probs_ref[window, at]
            float_probs = probs.astype(jnp.float32)
            grad_probs = mxu(masked_heads(qkv_ref[rows, value_columns], head_dim), mix, NT)
            product = (float_probs * grad_probs).reshape(GROUP, win, win)
            center = jnp.sum(product, axis=1, keepdims=True)
            grad_scores = scale * (product - float_probs.reshape(GROUP, win, win) * center)
            grad_scores = grad_scores.astype(jnp.bfloat16).reshape(GROUP * win, win)
            grad_values = own_heads(mxu(probs, mix), head_dim)
            grad_keys = own_heads(mxu(grad_scores, qkv_ref[rows, columns]), head_dim)
            turned = turned_heads(grad_scores, GROUP)
            grad_queries = own_heads(mxu(turned, qkv_ref[rows, key_columns]), head_dim)
            cells_ref[rows, columns] = grad_queries.astype(jnp.bfloat16)
            cells_ref[rows, key_columns] = grad_keys.astype(jnp.bfloat16)
            cells_ref[rows, value_columns] = grad_values.astype(jnp.bfloat16)
        return carry

    lax.fori_loop(0, windows, attend_back, 0)

    for part in range(3):
        columns = slice(part * width, (part + 1) * width)
        sent_ref, kept_ref = grad_refs[2 + 2 * part : 4 + 2 * part]
        sent_ref[...] = mxu(turned_ref[half:, :], cells_ref[:, columns])
        kept_ref[...] = mxu(turned_ref[:half, :], cells_ref[:, columns])


def exchanged(value, distance):
    count = lax.axis_size("lat")
    return lax.ppermute(value, "lat", [(i, i ^ distance) for i in range(count)])


def gathered(block, prepare):
    count = lax.axis_size("lat")
    outer = [exchanged(block, 4 * step) for step in range(count // 4 - 1, 0, -1)]
    distances = [4 * step for step in range(count // 4 - 1, 0, -1)]
    early = jnp.stack([block, outer[-1]])
    early = jnp.concatenate([early, exchanged(early, 2)])
    early_at = [0, distances[-1], 2, distances[-1] + 2]
    late = jnp.stack(outer[:-1] + [exchanged(value, 2) for value in outer[:-1]])
    late_at = distances[:-1] + [distance + 2 for distance in distances[:-1]]
    early, late, *prepared = lax.optimization_barrier((early, late, *prepare()))
    early_other, late_other = exchanged(early, 1), exchanged(late, 1)
    order = early_at + [at + 1 for at in early_at] + late_at + [at + 1 for at in late_at]
    return (early, early_other, late, late_other), order, prepared


def reversed_bits(value, count):
    result = 0
    bit = 1
    while bit < count:
        result = 2 * result + (value & 1)
        value = value >> 1
        bit *= 2
    return result


def summed(sent, kept, distances):
    for at, distance in enumerate(distances):
        if at > 0:
            half = kept.shape[0] // 2
            kept, sent = kept[:half], kept[half:]
        kept = kept + exchanged(sent, distance)
    return kept


def call(kernel, name, outs, tables, operands, scratch=(), flops=0):
    size = sum(math.prod(o.shape) * o.dtype.itemsize for o in (*outs, *operands))
    return pl.pallas_call(
        kernel,
        out_shape=outs,
        in_specs=[pl.BlockSpec(memory_space=pltpu.SMEM)] * len(tables)
        + [pl.BlockSpec(memory_space=pltpu.VMEM)] * len(operands),
        out_specs=[pl.BlockSpec(memory_space=pltpu.VMEM)] * len(outs),
        scratch_shapes=list(scratch),
        compiler_params=pltpu.CompilerParams(vmem_limit_bytes=VMEM_BYTES),
        cost_estimate=pl.CostEstimate(flops=flops, bytes_accessed=size, transcendentals=0),
        name=name,
    )(*tables, *operands)


def per_device(inputs, cotangent, idents, w_qkv, w_out, gain):
    lat_cells, lon_cells, width = inputs.shape
    half_rows = WIN_R // 2
    win = padded_rows()
    windows = (lat_cells // WIN_R) * (lon_cells // WIN_C)
    cells = windows * win
    places = jnp.asarray(window_places(lon_cells), jnp.bfloat16)

    def shape(*dims, dtype=jnp.bfloat16):
        return jax.ShapeDtypeStruct(dims, dtype)

    count = lax.axis_size("lat")
    me = lax.axis_index("lat")
    direct = count >= 16 and count & (count - 1) == 0 and width % (16 * count) == 0
    if direct:
        blocks = jnp.arange(count, dtype=jnp.int32)
        to_slot = reversed_bits(blocks ^ me, count)
    else:
        to_slot = jnp.arange(16, dtype=jnp.int32)

    def prepare():
        upper_in = passed_along(inputs[:half_rows], "lat", -1)
        upper_cot = passed_along(cotangent[:half_rows], "lat", -1)
        return call(
            prepare_kernel,
            "prepare",
            (shape(cells, width), shape(cells, width), shape(width, cells)),
            (to_slot,),
            (inputs, upper_in, cotangent, upper_cot, places),
            flops=4 * cells * width * lon_cells * WIN_R,
        )

    weights = jnp.concatenate([w_qkv, w_out], axis=1)
    if direct:
        shards, order, (tokens, cot, turned) = gathered(weights, prepare)
        into = jnp.array(order, jnp.int32) ^ me
    else:
        weights = lax.all_gather(weights, "lat", axis=0, tiled=True)
        shards = tuple(weights.reshape(4, 4, width // 16, 4 * width))
        into = to_slot
        tokens, cot, turned = prepare()

    labels = to_windows(idents + 1)
    bias = jnp.where(labels[:, :, None] == labels[:, None, :], 0.0, HIDDEN).astype(jnp.float32)

    normed, grad_cells, qkv_full, *grads = call(
        block_kernel,
        "block",
        (
            shape(cells, width),
            shape(cells, 3 * width),
            shape(width, 3 * width),
            *[shape(width // 2, width, dtype=jnp.float32)] * 8,
        ),
        (into, to_slot),
        (tokens, turned, *shards, cot, bias, gain[None]),
        (
            pltpu.VMEM((width, width), jnp.bfloat16),
            pltpu.VMEM((cells, 3 * width), jnp.bfloat16),
            pltpu.VMEM((windows, HEADS // GROUP, GROUP * win, win), jnp.bfloat16),
            pltpu.VMEM((cells, width), jnp.bfloat16),
            pltpu.VMEM((cells, width), jnp.bfloat16),
            pltpu.VMEM((cells, width), jnp.bfloat16),
        ),
        flops=2 * cells * width * width * 10,
    )
    if direct:
        distances = [2**bit for bit in range(count.bit_length() - 1)]
        sums = [summed(sent, kept, distances[:2]) for sent, kept in zip(grads[::2], grads[1::2])]
        sums[0], normed, grad_cells = lax.optimization_barrier((sums[0], normed, grad_cells))
        half = sums[0].shape[0] // 2
        grad_out, *parts = [summed(kept[half:], kept[:half], distances[2:]) for kept in sums]
        grad_qkv = jnp.concatenate(parts, axis=1)
    else:
        whole = [jnp.concatenate([kept, sent]) for sent, kept in zip(grads[::2], grads[1::2])]
        both = lax.psum_scatter(jnp.concatenate(whole, axis=1), "lat", scatter_dimension=0, tiled=True)
        grad_out, grad_qkv = both[:, :width], both[:, width:]

    output, lower_out, grad_in, lower_grad = call(
        finish_kernel,
        "finish",
        (
            shape(*inputs.shape),
            shape(half_rows, lon_cells, width),
            shape(*inputs.shape),
            shape(half_rows, lon_cells, width),
        ),
        (),
        (grad_cells, qkv_full, normed, inputs, cotangent, places),
        (pltpu.VMEM((cells, width), jnp.bfloat16),),
        flops=2 * cells * width * (3 * width + 2 * lon_cells * WIN_R),
    )

    def completed(result, lower):
        lower = passed_along(lower, "lat", 1)
        top = result[:half_rows].astype(jnp.float32) + lower.astype(jnp.float32)
        return result.at[:half_rows].set(top.astype(jnp.bfloat16))

    return (completed(output, lower_out), completed(grad_in, lower_grad), grad_qkv, grad_out)


def solution(mesh):
    in_specs = (
        P(("grp", "lat"), None, None),
        P(("grp", "lat"), None, None),
        P(("grp", "lat"), None),
        P("lat", None),
        P("lat", None),
        P(),
    )
    out_specs = (
        P(("grp", "lat"), None, None),
        P(("grp", "lat"), None, None),
        P(("grp", "lat"), None),
        P(("grp", "lat"), None),
    )
    return jax.shard_map(
        per_device, mesh=mesh, in_specs=in_specs, out_specs=out_specs, check_vma=False
    )
```

```python
import math

import jax
import jax.numpy as jnp
import numpy as np
from jax import lax
from jax.experimental import pallas as pl
from jax.experimental.pallas import tpu as pltpu
from jax.sharding import PartitionSpec as P

HEADS = 8
WIN_R = 6
WIN_C = 12
EPS = 1e-05
HIDDEN = -1e30
GROUP = 2
VMEM_BYTES = 40 * 1024 * 1024

NN = (((1,), (0,)), ((), ()))
NT = (((1,), (1,)), ((), ()))
TN = (((0,), (0,)), ((), ()))


def mxu(left, right, dims=NN):
    return lax.dot_general(left, right, dims, preferred_element_type=jnp.float32)


def passed_along(value, axis, steps):
    count = lax.axis_size(axis)
    first, last = (max(0, -steps), min(count, count - steps))
    return lax.ppermute(value, axis, [(source, source + steps) for source in range(first, last)])


def padded_rows():
    return -(-WIN_R * WIN_C // 16) * 16


def to_windows(field):
    lat_cells, lon_cells = field.shape
    field = field.reshape(lat_cells // WIN_R, WIN_R, lon_cells // WIN_C, WIN_C)
    field = field.transpose(0, 2, 1, 3).reshape(-1, WIN_R * WIN_C)
    return jnp.pad(field, ((0, 0), (0, padded_rows() - WIN_R * WIN_C)))


def window_places(lon_cells):
    win = padded_rows()
    places = np.zeros((WIN_R, lon_cells // WIN_C, win, lon_cells), np.float32)
    for row in range(WIN_R):
        for window in range(lon_cells // WIN_C):
            for column in range(WIN_C):
                source = (window * WIN_C + column + WIN_C // 2) % lon_cells
                places[row, window, row * WIN_C + column, source] = 1
    return places.reshape(WIN_R, -1, lon_cells)


def masked_heads(value, head_dim):
    head = lax.broadcasted_iota(jnp.int32, value.shape, 1) // head_dim
    zero = jnp.zeros_like(value)
    count = value.shape[1] // head_dim
    return jnp.concatenate([jnp.where(head == at, value, zero) for at in range(count)], axis=0)


def own_heads(stacked, head_dim):
    count = stacked.shape[1] // head_dim
    rows = stacked.shape[0] // count
    head = lax.broadcasted_iota(jnp.int32, (rows, stacked.shape[1]), 1) // head_dim
    result = stacked[:rows]
    for at in range(1, count):
        result = jnp.where(head == at, stacked[at * rows : (at + 1) * rows], result)
    return result


def turned_heads(stacked, count):
    rows = stacked.shape[0] // count
    return jnp.concatenate(
        [stacked[at * rows : (at + 1) * rows].T for at in range(count)], axis=0
    )


def prepare_kernel(
    to_slot_ref, inputs_ref, upper_in_ref, cot_ref, upper_cot_ref, places_ref,
    tokens_ref, cot_tokens_ref, turned_ref,
):
    half = upper_in_ref.shape[0]
    lat_cells = inputs_ref.shape[0]
    cells = places_ref.shape[1]
    blocks = to_slot_ref.shape[0]
    for band in range(lat_cells // WIN_R):
        rows = slice(band * cells, (band + 1) * cells)
        for own_ref, upper_ref, result_ref in (
            (inputs_ref, upper_in_ref, tokens_ref),
            (cot_ref, upper_cot_ref, cot_tokens_ref),
        ):
            total = None
            for row in range(WIN_R):
                source = band * WIN_R + row + half
                field = own_ref[source] if source < lat_cells else upper_ref[source - lat_cells]
                term = mxu(places_ref[row], field)
                total = term if total is None else total + term
            result_ref[rows, :] = total.astype(jnp.bfloat16)
    depth = tokens_ref.shape[1] // blocks
    turned = tokens_ref[...].T
    for block in range(blocks):
        rows = pl.ds(pl.multiple_of(to_slot_ref[block] * depth, depth), depth)
        turned_ref[rows, :] = turned[block * depth : (block + 1) * depth, :]


def finish_kernel(
    cells_ref, w_qkv_ref, normed_ref, inputs_ref, cot_ref, places_ref,
    output_ref, lower_out_ref, grad_in_ref, lower_grad_ref, shift_ref,
):
    lat_cells = inputs_ref.shape[0]
    half = lower_out_ref.shape[0]
    count = places_ref.shape[1]
    shift_ref[...] = mxu(cells_ref[...], w_qkv_ref[...], NT).astype(jnp.bfloat16)
    for value_ref, base_ref, result_ref, lower_ref in (
        (normed_ref, inputs_ref, output_ref, lower_out_ref),
        (shift_ref, cot_ref, grad_in_ref, lower_grad_ref),
    ):
        result_ref[:half] = base_ref[:half]
        for band in range(lat_cells // WIN_R):
            value = value_ref[band * count : (band + 1) * count, :]
            for row in range(WIN_R):
                back = mxu(places_ref[row], value, TN)
                target = band * WIN_R + row + half
                if target < lat_cells:
                    base = base_ref[target].astype(jnp.float32)
                    result_ref[target] = (base + back).astype(jnp.bfloat16)
                else:
                    lower_ref[target - lat_cells] = back.astype(jnp.bfloat16)


def block_kernel(into_ref, to_slot_ref, gain_ref, x_hbm, turned_hbm, cot_hbm, bias_hbm, *rest):
    shard_refs, rest = rest[: into_ref.shape[0]], rest[into_ref.shape[0] :]
    normed_hbm, cells_hbm, w_qkv_hbm, *grad_hbms = rest[:11]
    x_ref, turned_ref, cot_ref, bias_ref, normed_ref, cells_ref, w_qkv_ref, grads_ref = rest[11:19]
    w_out_ref, qkv_ref, probs_ref, mixed_ref, grad_proj_ref, grad_mix_ref = rest[19:25]
    weight_sems, in_sems, out_sems = rest[25:]
    windows, win = bias_ref.shape[:2]
    width = x_ref.shape[1]
    head_dim = width // HEADS
    group = GROUP * head_dim
    scale = head_dim ** (-0.5)
    factor = scale * math.log2(math.e)

    blocks = into_ref.shape[0]
    depth = width // blocks
    weight_copies = []
    for at, shard in enumerate(shard_refs):
        rows = pl.ds(pl.multiple_of(into_ref[at] * depth, depth), depth)
        weight_copies.append((shard.at[:, : 3 * width], w_qkv_ref.at[rows, :]))
        weight_copies.append((shard.at[:, 3 * width :], w_out_ref.at[rows, :]))
    weight_copies = [
        pltpu.make_async_copy(source, target, weight_sems.at[at])
        for at, (source, target) in enumerate(weight_copies)
    ]
    pairs = ((x_hbm, x_ref), (bias_hbm, bias_ref), (cot_hbm, cot_ref), (turned_hbm, turned_ref))
    x_copy, bias_copy, cot_copy, turned_copy = [
        pltpu.make_async_copy(source, target, in_sems.at[at])
        for at, (source, target) in enumerate(pairs)
    ]
    results = ((w_qkv_ref, w_qkv_hbm), (normed_ref, normed_hbm), (cells_ref, cells_hbm))
    results += tuple((grads_ref.at[at], grad_hbms[at]) for at in range(8))
    w_copy, normed_copy, cells_copy, *grad_copies = [
        pltpu.make_async_copy(source, target, out_sems.at[at])
        for at, (source, target) in enumerate(results)
    ]
    for copy in (*weight_copies, x_copy, bias_copy, cot_copy, turned_copy):
        copy.start()
    for copy in (*weight_copies, x_copy):
        copy.wait()
    w_copy.start()

    for part in range(3):
        columns = slice(part * width, (part + 1) * width)
        qkv_ref[:, columns] = mxu(x_ref[...], w_qkv_ref[:, columns]).astype(jnp.bfloat16)

    def attend(window, carry):
        rows = pl.ds(pl.multiple_of(window * win, 16), win)
        bias = bias_ref[window]
        for at in range(HEADS // GROUP):
            columns = slice(at * group, (at + 1) * group)
            queries = qkv_ref[rows, columns]
            keys = qkv_ref[rows, width + at * group : width + (at + 1) * group]
            values = qkv_ref[rows, 2 * width + at * group : 2 * width + (at + 1) * group]
            scores = mxu(masked_heads(keys, head_dim), queries, NT)
            scores = scores.reshape(GROUP, win, win) * factor + bias
            lifted = jnp.exp2(scores - jnp.max(scores, axis=1, keepdims=True))
            total = jnp.sum(lifted, axis=1, keepdims=True)
            probs = (lifted * (1.0 / total)).astype(jnp.bfloat16)
            probs = probs.reshape(GROUP * win, win)
            probs_ref[window, at] = probs
            mixed = own_heads(mxu(turned_heads(probs, GROUP), values), head_dim)
            mixed_ref[rows, columns] = mixed.astype(jnp.bfloat16)
        return carry

    bias_copy.wait()
    lax.fori_loop(0, windows, attend, 0)

    cot_copy.wait()
    gain = gain_ref[...]

    def normalise(window, carry):
        rows = pl.ds(pl.multiple_of(window * win, 16), win)
        projected = mxu(mixed_ref[rows, :], w_out_ref[...])
        center = projected - jnp.mean(projected, axis=-1, keepdims=True)
        inverse = lax.rsqrt(jnp.mean(center * center, axis=-1, keepdims=True) + EPS)
        normal = center * inverse
        normed_ref[rows, :] = (normal * gain).astype(jnp.bfloat16)
        scaled = cot_ref[rows, :].astype(jnp.float32) * gain
        grad_proj = (
            scaled
            - jnp.mean(scaled, axis=-1, keepdims=True)
            - normal * jnp.mean(scaled * normal, axis=-1, keepdims=True)
        ) * inverse
        grad_proj_ref[rows, :] = grad_proj.astype(jnp.bfloat16)
        return carry

    lax.fori_loop(0, windows, normalise, 0)
    normed_copy.start()
    sent_ref, kept_ref = grads_ref.at[0], grads_ref.at[1]
    half = width // 2
    grad_out = mxu(mixed_ref[...], grad_proj_ref[...], TN)
    for block in range(blocks):
        slot = to_slot_ref[block]
        value = grad_out[block * depth : (block + 1) * depth, :]
        rows = pl.ds(pl.multiple_of(lax.rem(slot, blocks // 2) * depth, depth), depth)

        @pl.when(slot < blocks // 2)
        def _():
            kept_ref[rows, :] = value

        @pl.when(slot >= blocks // 2)
        def _():
            sent_ref[rows, :] = value

    grad_copies[0].start()
    grad_copies[1].start()
    grad_mix_ref[...] = mxu(grad_proj_ref[...], w_out_ref[...], NT).astype(jnp.bfloat16)

    def attend_back(window, carry):
        rows = pl.ds(pl.multiple_of(window * win, 16), win)
        for at in range(HEADS // GROUP):
            columns = slice(at * group, (at + 1) * group)
            key_columns = slice(width + at * group, width + (at + 1) * group)
            value_columns = slice(2 * width + at * group, 2 * width + (at + 1) * group)
            mix = grad_mix_ref[rows, columns]
            probs = probs_ref[window, at]
            float_probs = probs.astype(jnp.float32)
            grad_probs = mxu(masked_heads(qkv_ref[rows, value_columns], head_dim), mix, NT)
            product = (float_probs * grad_probs).reshape(GROUP, win, win)
            center = jnp.sum(product, axis=1, keepdims=True)
            grad_scores = scale * (product - float_probs.reshape(GROUP, win, win) * center)
            grad_scores = grad_scores.astype(jnp.bfloat16).reshape(GROUP * win, win)
            grad_values = own_heads(mxu(probs, mix), head_dim)
            grad_keys = own_heads(mxu(grad_scores, qkv_ref[rows, columns]), head_dim)
            turned = turned_heads(grad_scores, GROUP)
            grad_queries = own_heads(mxu(turned, qkv_ref[rows, key_columns]), head_dim)
            cells_ref[rows, columns] = grad_queries.astype(jnp.bfloat16)
            cells_ref[rows, key_columns] = grad_keys.astype(jnp.bfloat16)
            cells_ref[rows, value_columns] = grad_values.astype(jnp.bfloat16)
        return carry

    lax.fori_loop(0, windows, attend_back, 0)

    cells_copy.start()
    turned_copy.wait()
    for part in range(3):
        columns = slice(part * width, (part + 1) * width)
        for at, rows in enumerate((slice(half, width), slice(0, half))):
            grads_ref[2 + 2 * part + at] = mxu(turned_ref[rows, :], cells_ref[:, columns])
            grad_copies[2 + 2 * part + at].start()
    for copy in (w_copy, normed_copy, cells_copy, *grad_copies):
        copy.wait()


def exchanged(value, distance):
    count = lax.axis_size("lat")
    return lax.ppermute(value, "lat", [(i, i ^ distance) for i in range(count)])


def gathered(block, prepare, bias):
    count = lax.axis_size("lat")
    distances = [4 * step for step in range(count // 4 - 1, 0, -1)]
    shards = {distance: exchanged(block, distance) for distance in distances}
    shards[0] = block
    shards[2] = exchanged(block, 2)
    near = distances[-1]
    shards[near], bias = lax.optimization_barrier((shards[near], bias))
    for distance in [near] + distances[:-1]:
        shards[distance + 2] = exchanged(shards[distance], 2)
    last = distances[-2] + 2
    shards[last], *prepared = lax.optimization_barrier((shards[last], *prepare(shards[near])))
    for distance in list(shards):
        shards[distance + 1] = exchanged(shards[distance], 1)
    return tuple(shards.values()), list(shards), prepared, bias


def reversed_bits(value, count):
    result = 0
    bit = 1
    while bit < count:
        result = 2 * result + (value & 1)
        value = value >> 1
        bit *= 2
    return result


def summed(sent, kept, distances):
    for at, distance in enumerate(distances):
        if at > 0:
            half = kept.shape[0] // 2
            kept, sent = kept[:half], kept[half:]
        kept = kept + exchanged(sent, distance)
    return kept


def call(kernel, name, outs, tables, operands, scratch=(), far=(), flops=0):
    size = sum(math.prod(o.shape) * o.dtype.itemsize for o in (*outs, *operands, *far))
    vmem = pl.BlockSpec(memory_space=pltpu.VMEM)
    hbm = pl.BlockSpec(memory_space=pl.ANY)
    return pl.pallas_call(
        kernel,
        out_shape=outs,
        in_specs=[pl.BlockSpec(memory_space=pltpu.SMEM)] * len(tables)
        + [vmem] * len(operands)
        + [hbm] * len(far),
        out_specs=[hbm if far else vmem] * len(outs),
        scratch_shapes=list(scratch),
        compiler_params=pltpu.CompilerParams(vmem_limit_bytes=VMEM_BYTES),
        cost_estimate=pl.CostEstimate(flops=flops, bytes_accessed=size, transcendentals=0),
        name=name,
    )(*tables, *operands, *far)


def per_device(inputs, cotangent, idents, w_qkv, w_out, gain):
    lat_cells, lon_cells, width = inputs.shape
    half_rows = WIN_R // 2
    win = padded_rows()
    windows = (lat_cells // WIN_R) * (lon_cells // WIN_C)
    cells = windows * win
    places = jnp.asarray(window_places(lon_cells), jnp.bfloat16)

    def shape(*dims, dtype=jnp.bfloat16):
        return jax.ShapeDtypeStruct(dims, dtype)

    count = lax.axis_size("lat")
    me = lax.axis_index("lat")
    direct = count >= 16 and count & (count - 1) == 0 and width % (16 * count) == 0
    if direct:
        blocks = jnp.arange(count, dtype=jnp.int32)
        to_slot = reversed_bits(blocks ^ me, count)
    else:
        to_slot = jnp.arange(16, dtype=jnp.int32)

    def prepare(first=None):
        upper_in = passed_along(inputs[:half_rows], "lat", -1)
        upper_cot = cotangent[:half_rows]
        if first is not None:
            _, upper_cot = lax.optimization_barrier((first, upper_cot))
        upper_cot = passed_along(upper_cot, "lat", -1)
        return call(
            prepare_kernel,
            "prepare",
            (shape(cells, width), shape(cells, width), shape(width, cells)),
            (to_slot,),
            (inputs, upper_in, cotangent, upper_cot, places),
            flops=4 * cells * width * lon_cells * WIN_R,
        )

    weights = jnp.concatenate([w_qkv, w_out], axis=1)
    labels = to_windows(idents + 1)
    bias = jnp.where(labels[:, :, None] == labels[:, None, :], 0.0, HIDDEN).astype(jnp.float32)
    if direct:
        shards, order, (tokens, cot, turned), bias = gathered(weights, prepare, bias)
        into = jnp.array(order, jnp.int32) ^ me
    else:
        weights = lax.all_gather(weights, "lat", axis=0, tiled=True)
        shards = tuple(weights.reshape(16, width // 16, 4 * width))
        into = to_slot
        tokens, cot, turned = prepare()

    normed, grad_cells, qkv_full, *grads = call(
        block_kernel,
        "block",
        (
            shape(cells, width),
            shape(cells, 3 * width),
            shape(width, 3 * width),
            *[shape(width // 2, width, dtype=jnp.float32)] * 8,
        ),
        (into, to_slot),
        (gain[None],),
        (
            pltpu.VMEM((cells, width), jnp.bfloat16),
            pltpu.VMEM((width, cells), jnp.bfloat16),
            pltpu.VMEM((cells, width), jnp.bfloat16),
            pltpu.VMEM((windows, win, win), jnp.float32),
            pltpu.VMEM((cells, width), jnp.bfloat16),
            pltpu.VMEM((cells, 3 * width), jnp.bfloat16),
            pltpu.VMEM((width, 3 * width), jnp.bfloat16),
            pltpu.VMEM((8, width // 2, width), jnp.float32),
            pltpu.VMEM((width, width), jnp.bfloat16),
            pltpu.VMEM((cells, 3 * width), jnp.bfloat16),
            pltpu.VMEM((windows, HEADS // GROUP, GROUP * win, win), jnp.bfloat16),
            pltpu.VMEM((cells, width), jnp.bfloat16),
            pltpu.VMEM((cells, width), jnp.bfloat16),
            pltpu.VMEM((cells, width), jnp.bfloat16),
            pltpu.SemaphoreType.DMA((2 * len(shards),)),
            pltpu.SemaphoreType.DMA((4,)),
            pltpu.SemaphoreType.DMA((11,)),
        ),
        far=(tokens, turned, cot, bias, *shards),
        flops=2 * cells * width * width * 10,
    )
    if direct:
        distances = [2**bit for bit in range(count.bit_length() - 1)]
        sums = [summed(sent, kept, distances[:2]) for sent, kept in zip(grads[::2], grads[1::2])]
        sums[0], normed, grad_cells = lax.optimization_barrier((sums[0], normed, grad_cells))
        half = sums[0].shape[0] // 2
        grad_out, *parts = [summed(kept[half:], kept[:half], distances[2:]) for kept in sums]
        grad_qkv = jnp.concatenate(parts, axis=1)
    else:
        whole = [jnp.concatenate([kept, sent]) for sent, kept in zip(grads[::2], grads[1::2])]
        both = lax.psum_scatter(jnp.concatenate(whole, axis=1), "lat", scatter_dimension=0, tiled=True)
        grad_out, grad_qkv = both[:, :width], both[:, width:]

    output, lower_out, grad_in, lower_grad = call(
        finish_kernel,
        "finish",
        (
            shape(*inputs.shape),
            shape(half_rows, lon_cells, width),
            shape(*inputs.shape),
            shape(half_rows, lon_cells, width),
        ),
        (),
        (grad_cells, qkv_full, normed, inputs, cotangent, places),
        (pltpu.VMEM((cells, width), jnp.bfloat16),),
        flops=2 * cells * width * (3 * width + 2 * lon_cells * WIN_R),
    )

    def completed(result, lower):
        lower = passed_along(lower, "lat", 1)
        top = result[:half_rows].astype(jnp.float32) + lower.astype(jnp.float32)
        return result.at[:half_rows].set(top.astype(jnp.bfloat16))

    return (completed(output, lower_out), completed(grad_in, lower_grad), grad_qkv, grad_out)


def solution(mesh):
    in_specs = (
        P(("grp", "lat"), None, None),
        P(("grp", "lat"), None, None),
        P(("grp", "lat"), None),
        P("lat", None),
        P("lat", None),
        P(),
    )
    out_specs = (
        P(("grp", "lat"), None, None),
        P(("grp", "lat"), None, None),
        P(("grp", "lat"), None),
        P(("grp", "lat"), None),
    )
    return jax.shard_map(
        per_device, mesh=mesh, in_specs=in_specs, out_specs=out_specs, check_vma=False
    )
```

```python
import math

import jax
import jax.numpy as jnp
import numpy as np
from jax import lax
from jax.experimental import pallas as pl
from jax.experimental.pallas import tpu as pltpu
from jax.sharding import PartitionSpec as P

HEADS = 8
WIN_R = 6
WIN_C = 12
EPS = 1e-05
HIDDEN = -1e30
GROUP = 4
VMEM_BYTES = 40 * 1024 * 1024

NN = (((1,), (0,)), ((), ()))
NT = (((1,), (1,)), ((), ()))
TN = (((0,), (0,)), ((), ()))


def mxu(left, right, dims=NN):
    return lax.dot_general(left, right, dims, preferred_element_type=jnp.float32)


def passed_along(value, axis, steps):
    count = lax.axis_size(axis)
    first, last = (max(0, -steps), min(count, count - steps))
    return lax.ppermute(value, axis, [(source, source + steps) for source in range(first, last)])


def padded_rows():
    return -(-WIN_R * WIN_C // 16) * 16


def to_windows(field):
    lat_cells, lon_cells = field.shape
    field = field.reshape(lat_cells // WIN_R, WIN_R, lon_cells // WIN_C, WIN_C)
    field = field.transpose(0, 2, 1, 3).reshape(-1, WIN_R * WIN_C)
    return jnp.pad(field, ((0, 0), (0, padded_rows() - WIN_R * WIN_C)))


def window_places(lon_cells):
    win = padded_rows()
    places = np.zeros((WIN_R, lon_cells // WIN_C, win, lon_cells), np.float32)
    for row in range(WIN_R):
        for window in range(lon_cells // WIN_C):
            for column in range(WIN_C):
                source = (window * WIN_C + column + WIN_C // 2) % lon_cells
                places[row, window, row * WIN_C + column, source] = 1
    return places.reshape(WIN_R, -1, lon_cells)


def masked_heads(value, head_dim):
    head = lax.broadcasted_iota(jnp.int32, value.shape, 1) // head_dim
    zero = jnp.zeros_like(value)
    count = value.shape[1] // head_dim
    return jnp.concatenate([jnp.where(head == at, value, zero) for at in range(count)], axis=0)


def own_heads(stacked, head_dim):
    count = stacked.shape[1] // head_dim
    rows = stacked.shape[0] // count
    head = lax.broadcasted_iota(jnp.int32, (rows, stacked.shape[1]), 1) // head_dim
    result = stacked[:rows]
    for at in range(1, count):
        result = jnp.where(head == at, stacked[at * rows : (at + 1) * rows], result)
    return result


def turned_heads(stacked, count):
    rows = stacked.shape[0] // count
    return jnp.concatenate(
        [stacked[at * rows : (at + 1) * rows].T for at in range(count)], axis=0
    )


def prepare_kernel(
    to_slot_ref, inputs_ref, upper_in_ref, cot_ref, upper_cot_ref, places_ref,
    tokens_ref, cot_tokens_ref, turned_ref,
):
    half = upper_in_ref.shape[0]
    lat_cells = inputs_ref.shape[0]
    cells = places_ref.shape[1]
    blocks = to_slot_ref.shape[0]
    for band in range(lat_cells // WIN_R):
        rows = slice(band * cells, (band + 1) * cells)
        for own_ref, upper_ref, result_ref in (
            (inputs_ref, upper_in_ref, tokens_ref),
            (cot_ref, upper_cot_ref, cot_tokens_ref),
        ):
            total = None
            for row in range(WIN_R):
                source = band * WIN_R + row + half
                field = own_ref[source] if source < lat_cells else upper_ref[source - lat_cells]
                term = mxu(places_ref[row], field)
                total = term if total is None else total + term
            result_ref[rows, :] = total.astype(jnp.bfloat16)
    depth = tokens_ref.shape[1] // blocks
    turned = tokens_ref[...].T
    for block in range(blocks):
        rows = pl.ds(pl.multiple_of(to_slot_ref[block] * depth, depth), depth)
        turned_ref[rows, :] = turned[block * depth : (block + 1) * depth, :]


def finish_kernel(
    cells_ref, w_qkv_ref, normed_ref, inputs_ref, cot_ref, places_ref,
    output_ref, lower_out_ref, grad_in_ref, lower_grad_ref, shift_ref,
):
    lat_cells = inputs_ref.shape[0]
    half = lower_out_ref.shape[0]
    count = places_ref.shape[1]
    shift_ref[...] = mxu(cells_ref[...], w_qkv_ref[...], NT).astype(jnp.bfloat16)
    for value_ref, base_ref, result_ref, lower_ref in (
        (normed_ref, inputs_ref, output_ref, lower_out_ref),
        (shift_ref, cot_ref, grad_in_ref, lower_grad_ref),
    ):
        result_ref[:half] = base_ref[:half]
        for band in range(lat_cells // WIN_R):
            value = value_ref[band * count : (band + 1) * count, :]
            for row in range(WIN_R):
                back = mxu(places_ref[row], value, TN)
                target = band * WIN_R + row + half
                if target < lat_cells:
                    base = base_ref[target].astype(jnp.float32)
                    result_ref[target] = (base + back).astype(jnp.bfloat16)
                else:
                    lower_ref[target - lat_cells] = back.astype(jnp.bfloat16)


def block_kernel(into_ref, to_slot_ref, gain_ref, x_hbm, turned_hbm, cot_hbm, bias_hbm, *rest):
    shard_refs, rest = rest[: into_ref.shape[0]], rest[into_ref.shape[0] :]
    normed_hbm, cells_hbm, w_qkv_hbm, *grad_hbms = rest[:11]
    x_ref, turned_ref, cot_ref, bias_ref, normed_ref, cells_ref, weights_ref, grads_ref = rest[11:19]
    qkv_ref, probs_ref, mixed_ref, grad_proj_ref, grad_mix_ref = rest[19:24]
    weight_sems, in_sems, out_sems = rest[24:]
    windows, win = bias_ref.shape[:2]
    width = x_ref.shape[1]
    head_dim = width // HEADS
    group = GROUP * head_dim
    scale = head_dim ** (-0.5)
    factor = scale * math.log2(math.e)

    blocks = into_ref.shape[0]
    depth = width // blocks
    weight_copies = []
    for at, shard in enumerate(shard_refs):
        rows = pl.ds(pl.multiple_of(into_ref[at] * depth, depth), depth)
        weight_copies.append((shard, weights_ref.at[rows, :]))
    weight_copies = [
        pltpu.make_async_copy(source, target, weight_sems.at[at])
        for at, (source, target) in enumerate(weight_copies)
    ]
    pairs = ((x_hbm, x_ref), (bias_hbm, bias_ref), (cot_hbm, cot_ref), (turned_hbm, turned_ref))
    x_copy, bias_copy, cot_copy, turned_copy = [
        pltpu.make_async_copy(source, target, in_sems.at[at])
        for at, (source, target) in enumerate(pairs)
    ]
    w_qkv_ref, w_out_ref = weights_ref.at[:, : 3 * width], weights_ref.at[:, 3 * width :]
    results = ((w_qkv_ref, w_qkv_hbm), (normed_ref, normed_hbm), (cells_ref, cells_hbm))
    results += tuple((grads_ref.at[at], grad_hbms[at]) for at in range(8))
    w_copy, normed_copy, cells_copy, *grad_copies = [
        pltpu.make_async_copy(source, target, out_sems.at[at])
        for at, (source, target) in enumerate(results)
    ]
    for copy in (*weight_copies, x_copy, bias_copy, cot_copy, turned_copy):
        copy.start()
    for copy in (*weight_copies, x_copy):
        copy.wait()
    w_copy.start()

    for part in range(3):
        columns = slice(part * width, (part + 1) * width)
        qkv_ref[:, columns] = mxu(x_ref[...], w_qkv_ref[:, columns]).astype(jnp.bfloat16)

    def attend(window, carry):
        rows = pl.ds(pl.multiple_of(window * win, 16), win)
        bias = bias_ref[window]
        for at in range(HEADS // GROUP):
            columns = slice(at * group, (at + 1) * group)
            queries = qkv_ref[rows, columns]
            keys = qkv_ref[rows, width + at * group : width + (at + 1) * group]
            values = qkv_ref[rows, 2 * width + at * group : 2 * width + (at + 1) * group]
            scores = mxu(masked_heads(keys, head_dim), queries, NT)
            scores = scores.reshape(GROUP, win, win) * factor + bias
            lifted = jnp.exp2(scores - jnp.max(scores, axis=1, keepdims=True))
            total = jnp.sum(lifted, axis=1, keepdims=True)
            probs = (lifted * (1.0 / total)).astype(jnp.bfloat16)
            probs = probs.reshape(GROUP * win, win)
            probs_ref[window, at] = probs
            mixed = own_heads(mxu(turned_heads(probs, GROUP), values), head_dim)
            mixed_ref[rows, columns] = mixed.astype(jnp.bfloat16)
        return carry

    bias_copy.wait()
    lax.fori_loop(0, windows, attend, 0)

    cot_copy.wait()
    gain = gain_ref[...]

    def normalise(window, carry):
        rows = pl.ds(pl.multiple_of(window * win, 16), win)
        projected = mxu(mixed_ref[rows, :], w_out_ref[...])
        center = projected - jnp.mean(projected, axis=-1, keepdims=True)
        inverse = lax.rsqrt(jnp.mean(center * center, axis=-1, keepdims=True) + EPS)
        normal = center * inverse
        normed_ref[rows, :] = (normal * gain).astype(jnp.bfloat16)
        scaled = cot_ref[rows, :].astype(jnp.float32) * gain
        grad_proj = (
            scaled
            - jnp.mean(scaled, axis=-1, keepdims=True)
            - normal * jnp.mean(scaled * normal, axis=-1, keepdims=True)
        ) * inverse
        grad_proj_ref[rows, :] = grad_proj.astype(jnp.bfloat16)
        return carry

    lax.fori_loop(0, windows, normalise, 0)
    normed_copy.start()
    sent_ref, kept_ref = grads_ref.at[0], grads_ref.at[1]
    half = width // 2
    grad_out = mxu(mixed_ref[...], grad_proj_ref[...], TN)
    for block in range(blocks):
        slot = to_slot_ref[block]
        value = grad_out[block * depth : (block + 1) * depth, :]
        rows = pl.ds(pl.multiple_of(lax.rem(slot, blocks // 2) * depth, depth), depth)

        @pl.when(slot < blocks // 2)
        def _():
            kept_ref[rows, :] = value

        @pl.when(slot >= blocks // 2)
        def _():
            sent_ref[rows, :] = value

    grad_copies[0].start()
    grad_copies[1].start()
    grad_mix_ref[...] = mxu(grad_proj_ref[...], w_out_ref[...], NT).astype(jnp.bfloat16)

    def attend_back(window, carry):
        rows = pl.ds(pl.multiple_of(window * win, 16), win)
        for at in range(HEADS // GROUP):
            columns = slice(at * group, (at + 1) * group)
            key_columns = slice(width + at * group, width + (at + 1) * group)
            value_columns = slice(2 * width + at * group, 2 * width + (at + 1) * group)
            mix = grad_mix_ref[rows, columns]
            probs = probs_ref[window, at]
            float_probs = probs.astype(jnp.float32)
            grad_probs = mxu(masked_heads(qkv_ref[rows, value_columns], head_dim), mix, NT)
            product = (float_probs * grad_probs).reshape(GROUP, win, win)
            center = jnp.sum(product, axis=1, keepdims=True)
            grad_scores = scale * (product - float_probs.reshape(GROUP, win, win) * center)
            grad_scores = grad_scores.astype(jnp.bfloat16).reshape(GROUP * win, win)
            grad_values = own_heads(mxu(probs, mix), head_dim)
            grad_keys = own_heads(mxu(grad_scores, qkv_ref[rows, columns]), head_dim)
            turned = turned_heads(grad_scores, GROUP)
            grad_queries = own_heads(mxu(turned, qkv_ref[rows, key_columns]), head_dim)
            cells_ref[rows, columns] = grad_queries.astype(jnp.bfloat16)
            cells_ref[rows, key_columns] = grad_keys.astype(jnp.bfloat16)
            cells_ref[rows, value_columns] = grad_values.astype(jnp.bfloat16)
        return carry

    lax.fori_loop(0, windows, attend_back, 0)

    cells_copy.start()
    turned_copy.wait()
    for part in range(3):
        columns = slice(part * width, (part + 1) * width)
        for at, rows in enumerate((slice(half, width), slice(0, half))):
            grads_ref[2 + 2 * part + at] = mxu(turned_ref[rows, :], cells_ref[:, columns])
            grad_copies[2 + 2 * part + at].start()
    for copy in (w_copy, normed_copy, cells_copy, *grad_copies):
        copy.wait()


def exchanged(value, distance):
    count = lax.axis_size("lat")
    return lax.ppermute(value, "lat", [(i, i ^ distance) for i in range(count)])


def moved(value, grp_turn, distance):
    count = lax.axis_size("lat")
    groups = lax.axis_size("grp")
    pairs = []
    for grp in range(groups):
        for i in range(count):
            pairs.append((grp * count + i, (grp ^ grp_turn) * count + (i ^ distance[grp])))
    return lax.ppermute(value, ("grp", "lat"), pairs)


def gathered(block, prepare, bias):
    here = lax.axis_index("grp") == 0
    far = moved(block, 0, (8, 12))
    near = moved(block, 0, (4, 4))
    prepared = prepare(near)
    far, bias = lax.optimization_barrier((far, bias))
    far_other = moved(far, 1, (0, 0))
    side = moved(jnp.where(here, block, far), 0, (2, 2))
    near_side = moved(jnp.where(here, near, far_other), 0, (2, 2))
    side, *prepared = lax.optimization_barrier((side, *prepared))
    side_other = moved(side, 1, (0, 0))
    near_side_other = moved(near_side, 1, (0, 0))
    shards = [block, near, far, far_other, side, near_side, side_other, near_side_other]
    low = jnp.array([0, 4, 8, 12, 2, 6, 14, 10], jnp.int32)
    high = jnp.array([0, 4, 12, 8, 14, 10, 2, 6], jnp.int32)
    order = jnp.where(here, low, high)
    shards += [exchanged(shard, 1) for shard in shards]
    return tuple(shards), jnp.concatenate([order, order + 1]), prepared, bias


def reversed_bits(value, count):
    result = 0
    bit = 1
    while bit < count:
        result = 2 * result + (value & 1)
        value = value >> 1
        bit *= 2
    return result


def summed(sent, kept, distances):
    for at, distance in enumerate(distances):
        if at > 0:
            half = kept.shape[0] // 2
            kept, sent = kept[:half], kept[half:]
        kept = kept + exchanged(sent, distance)
    return kept


def call(kernel, name, outs, tables, operands, scratch=(), far=(), flops=0):
    size = sum(math.prod(o.shape) * o.dtype.itemsize for o in (*outs, *operands, *far))
    vmem = pl.BlockSpec(memory_space=pltpu.VMEM)
    hbm = pl.BlockSpec(memory_space=pl.ANY)
    return pl.pallas_call(
        kernel,
        out_shape=outs,
        in_specs=[pl.BlockSpec(memory_space=pltpu.SMEM)] * len(tables)
        + [vmem] * len(operands)
        + [hbm] * len(far),
        out_specs=[hbm if far else vmem] * len(outs),
        scratch_shapes=list(scratch),
        compiler_params=pltpu.CompilerParams(vmem_limit_bytes=VMEM_BYTES),
        cost_estimate=pl.CostEstimate(flops=flops, bytes_accessed=size, transcendentals=0),
        name=name,
    )(*tables, *operands, *far)


def per_device(inputs, cotangent, idents, w_qkv, w_out, gain):
    lat_cells, lon_cells, width = inputs.shape
    half_rows = WIN_R // 2
    win = padded_rows()
    windows = (lat_cells // WIN_R) * (lon_cells // WIN_C)
    cells = windows * win
    places = jnp.asarray(window_places(lon_cells), jnp.bfloat16)

    def shape(*dims, dtype=jnp.bfloat16):
        return jax.ShapeDtypeStruct(dims, dtype)

    count = lax.axis_size("lat")
    me = lax.axis_index("lat")
    direct = count == 16 and lax.axis_size("grp") == 2 and width % (16 * count) == 0
    if direct:
        blocks = jnp.arange(count, dtype=jnp.int32)
        to_slot = reversed_bits(blocks ^ me, count)
    else:
        to_slot = jnp.arange(16, dtype=jnp.int32)

    def prepare(first=None):
        upper_in = passed_along(inputs[:half_rows], "lat", -1)
        upper_cot = cotangent[:half_rows]
        if first is not None:
            _, upper_cot = lax.optimization_barrier((first, upper_cot))
        upper_cot = passed_along(upper_cot, "lat", -1)
        return call(
            prepare_kernel,
            "prepare",
            (shape(cells, width), shape(cells, width), shape(width, cells)),
            (to_slot,),
            (inputs, upper_in, cotangent, upper_cot, places),
            flops=4 * cells * width * lon_cells * WIN_R,
        )

    weights = jnp.concatenate([w_qkv, w_out], axis=1)
    labels = to_windows(idents + 1)
    bias = jnp.where(labels[:, :, None] == labels[:, None, :], 0.0, HIDDEN).astype(jnp.float32)
    if direct:
        shards, order, (tokens, cot, turned), bias = gathered(weights, prepare, bias)
        into = order ^ me
    else:
        weights = lax.all_gather(weights, "lat", axis=0, tiled=True)
        shards = tuple(weights.reshape(16, width // 16, 4 * width))
        into = to_slot
        tokens, cot, turned = prepare()

    normed, grad_cells, qkv_full, *grads = call(
        block_kernel,
        "block",
        (
            shape(cells, width),
            shape(cells, 3 * width),
            shape(width, 3 * width),
            *[shape(width // 2, width, dtype=jnp.float32)] * 8,
        ),
        (into, to_slot),
        (gain[None],),
        (
            pltpu.VMEM((cells, width), jnp.bfloat16),
            pltpu.VMEM((width, cells), jnp.bfloat16),
            pltpu.VMEM((cells, width), jnp.bfloat16),
            pltpu.VMEM((windows, win, win), jnp.float32),
            pltpu.VMEM((cells, width), jnp.bfloat16),
            pltpu.VMEM((cells, 3 * width), jnp.bfloat16),
            pltpu.VMEM((width, 4 * width), jnp.bfloat16),
            pltpu.VMEM((8, width // 2, width), jnp.float32),
            pltpu.VMEM((cells, 3 * width), jnp.bfloat16),
            pltpu.VMEM((windows, HEADS // GROUP, GROUP * win, win), jnp.bfloat16),
            pltpu.VMEM((cells, width), jnp.bfloat16),
            pltpu.VMEM((cells, width), jnp.bfloat16),
            pltpu.VMEM((cells, width), jnp.bfloat16),
            pltpu.SemaphoreType.DMA((len(shards),)),
            pltpu.SemaphoreType.DMA((4,)),
            pltpu.SemaphoreType.DMA((11,)),
        ),
        far=(tokens, turned, cot, bias, *shards),
        flops=2 * cells * width * width * 10,
    )
    if direct:
        distances = [2**bit for bit in range(count.bit_length() - 1)]
        sums = [summed(sent, kept, distances[:2]) for sent, kept in zip(grads[::2], grads[1::2])]
        sums[0], normed, grad_cells = lax.optimization_barrier((sums[0], normed, grad_cells))
        half = sums[0].shape[0] // 2
        grad_out, *parts = [summed(kept[half:], kept[:half], distances[2:]) for kept in sums]
        grad_qkv = jnp.concatenate(parts, axis=1)
    else:
        whole = [jnp.concatenate([kept, sent]) for sent, kept in zip(grads[::2], grads[1::2])]
        both = lax.psum_scatter(jnp.concatenate(whole, axis=1), "lat", scatter_dimension=0, tiled=True)
        grad_out, grad_qkv = both[:, :width], both[:, width:]

    output, lower_out, grad_in, lower_grad = call(
        finish_kernel,
        "finish",
        (
            shape(*inputs.shape),
            shape(half_rows, lon_cells, width),
            shape(*inputs.shape),
            shape(half_rows, lon_cells, width),
        ),
        (),
        (grad_cells, qkv_full, normed, inputs, cotangent, places),
        (pltpu.VMEM((cells, width), jnp.bfloat16),),
        flops=2 * cells * width * (3 * width + 2 * lon_cells * WIN_R),
    )

    def completed(result, lower):
        lower = passed_along(lower, "lat", 1)
        top = result[:half_rows].astype(jnp.float32) + lower.astype(jnp.float32)
        return result.at[:half_rows].set(top.astype(jnp.bfloat16))

    return (completed(output, lower_out), completed(grad_in, lower_grad), grad_qkv, grad_out)


def solution(mesh):
    in_specs = (
        P(("grp", "lat"), None, None),
        P(("grp", "lat"), None, None),
        P(("grp", "lat"), None),
        P("lat", None),
        P("lat", None),
        P(),
    )
    out_specs = (
        P(("grp", "lat"), None, None),
        P(("grp", "lat"), None, None),
        P(("grp", "lat"), None),
        P(("grp", "lat"), None),
    )
    return jax.shard_map(
        per_device, mesh=mesh, in_specs=in_specs, out_specs=out_specs, check_vma=False
    )
```

```python
import math

import jax
import jax.numpy as jnp
import numpy as np
from jax import lax
from jax.experimental import pallas as pl
from jax.experimental.pallas import tpu as pltpu
from jax.sharding import PartitionSpec as P

HEADS = 8
WIN_R = 6
WIN_C = 12
EPS = 1e-05
HIDDEN = -1e30
GROUP = 2
VMEM_BYTES = 40 * 1024 * 1024

NN = (((1,), (0,)), ((), ()))
NT = (((1,), (1,)), ((), ()))
TN = (((0,), (0,)), ((), ()))


def mxu(left, right, dims=NN):
    return lax.dot_general(left, right, dims, preferred_element_type=jnp.float32)


def passed_along(value, axis, steps):
    count = lax.axis_size(axis)
    first, last = (max(0, -steps), min(count, count - steps))
    return lax.ppermute(value, axis, [(source, source + steps) for source in range(first, last)])


def padded_rows():
    return -(-WIN_R * WIN_C // 16) * 16


def to_windows(field):
    lat_cells, lon_cells = field.shape
    field = field.reshape(lat_cells // WIN_R, WIN_R, lon_cells // WIN_C, WIN_C)
    field = field.transpose(0, 2, 1, 3).reshape(-1, WIN_R * WIN_C)
    return jnp.pad(field, ((0, 0), (0, padded_rows() - WIN_R * WIN_C)))


def window_places(lon_cells):
    win = padded_rows()
    places = np.zeros((WIN_R, lon_cells // WIN_C, win, lon_cells), np.float32)
    for row in range(WIN_R):
        for window in range(lon_cells // WIN_C):
            for column in range(WIN_C):
                source = (window * WIN_C + column + WIN_C // 2) % lon_cells
                places[row, window, row * WIN_C + column, source] = 1
    return places.reshape(WIN_R, -1, lon_cells)


def masked_heads(value, head_dim):
    head = lax.broadcasted_iota(jnp.int32, value.shape, 1) // head_dim
    zero = jnp.zeros_like(value)
    count = value.shape[1] // head_dim
    return jnp.concatenate([jnp.where(head == at, value, zero) for at in range(count)], axis=0)


def own_heads(stacked, head_dim):
    count = stacked.shape[1] // head_dim
    rows = stacked.shape[0] // count
    head = lax.broadcasted_iota(jnp.int32, (rows, stacked.shape[1]), 1) // head_dim
    result = stacked[:rows]
    for at in range(1, count):
        result = jnp.where(head == at, stacked[at * rows : (at + 1) * rows], result)
    return result


def turned_heads(stacked, count):
    rows = stacked.shape[0] // count
    return jnp.concatenate(
        [stacked[at * rows : (at + 1) * rows].T for at in range(count)], axis=0
    )


def prepare_kernel(
    to_slot_ref, inputs_ref, upper_in_ref, cot_ref, upper_cot_ref, places_ref,
    tokens_ref, cot_tokens_ref, turned_ref,
):
    half = upper_in_ref.shape[0]
    lat_cells = inputs_ref.shape[0]
    cells = places_ref.shape[1]
    blocks = to_slot_ref.shape[0]
    for band in range(lat_cells // WIN_R):
        rows = slice(band * cells, (band + 1) * cells)
        for own_ref, upper_ref, result_ref in (
            (inputs_ref, upper_in_ref, tokens_ref),
            (cot_ref, upper_cot_ref, cot_tokens_ref),
        ):
            total = None
            for row in range(WIN_R):
                source = band * WIN_R + row + half
                field = own_ref[source] if source < lat_cells else upper_ref[source - lat_cells]
                term = mxu(places_ref[row], field)
                total = term if total is None else total + term
            result_ref[rows, :] = total.astype(jnp.bfloat16)
    depth = tokens_ref.shape[1] // blocks
    turned = tokens_ref[...].T
    for block in range(blocks):
        rows = pl.ds(pl.multiple_of(to_slot_ref[block] * depth, depth), depth)
        turned_ref[rows, :] = turned[block * depth : (block + 1) * depth, :]


def finish_kernel(
    cells_ref, w_qkv_ref, normed_ref, inputs_ref, cot_ref, places_ref,
    output_ref, lower_out_ref, grad_in_ref, lower_grad_ref, shift_ref,
):
    lat_cells = inputs_ref.shape[0]
    half = lower_out_ref.shape[0]
    count = places_ref.shape[1]
    shift_ref[...] = mxu(cells_ref[...], w_qkv_ref[...], NT).astype(jnp.bfloat16)
    for value_ref, base_ref, result_ref, lower_ref in (
        (normed_ref, inputs_ref, output_ref, lower_out_ref),
        (shift_ref, cot_ref, grad_in_ref, lower_grad_ref),
    ):
        result_ref[:half] = base_ref[:half]
        for band in range(lat_cells // WIN_R):
            value = value_ref[band * count : (band + 1) * count, :]
            for row in range(WIN_R):
                back = mxu(places_ref[row], value, TN)
                target = band * WIN_R + row + half
                if target < lat_cells:
                    base = base_ref[target].astype(jnp.float32)
                    result_ref[target] = (base + back).astype(jnp.bfloat16)
                else:
                    lower_ref[target - lat_cells] = back.astype(jnp.bfloat16)


def block_kernel(into_ref, to_slot_ref, gain_ref, x_hbm, turned_hbm, cot_hbm, bias_hbm, *rest):
    shard_refs, rest = rest[: into_ref.shape[0]], rest[into_ref.shape[0] :]
    normed_hbm, cells_hbm, w_qkv_hbm, *grad_hbms = rest[:11]
    x_ref, turned_ref, cot_ref, bias_ref, normed_ref, cells_ref, weights_ref, grads_ref = rest[11:19]
    qkv_ref, probs_ref, mixed_ref, grad_proj_ref, grad_mix_ref = rest[19:24]
    weight_sems, in_sems, out_sems = rest[24:]
    windows, win = bias_ref.shape[:2]
    width = x_ref.shape[1]
    head_dim = width // HEADS
    group = GROUP * head_dim
    scale = head_dim ** (-0.5)
    factor = scale * math.log2(math.e)

    blocks = into_ref.shape[0]
    depth = width // blocks
    weight_copies = []
    for at, shard in enumerate(shard_refs):
        rows = pl.ds(pl.multiple_of(into_ref[at] * depth, depth), depth)
        weight_copies.append((shard, weights_ref.at[rows, :]))
    weight_copies = [
        pltpu.make_async_copy(source, target, weight_sems.at[at])
        for at, (source, target) in enumerate(weight_copies)
    ]
    pairs = ((x_hbm, x_ref), (bias_hbm, bias_ref), (cot_hbm, cot_ref), (turned_hbm, turned_ref))
    x_copy, bias_copy, cot_copy, turned_copy = [
        pltpu.make_async_copy(source, target, in_sems.at[at])
        for at, (source, target) in enumerate(pairs)
    ]
    w_qkv_ref, w_out_ref = weights_ref.at[:, : 3 * width], weights_ref.at[:, 3 * width :]
    results = ((w_qkv_ref, w_qkv_hbm), (normed_ref, normed_hbm), (cells_ref, cells_hbm))
    results += tuple((grads_ref.at[at], grad_hbms[at]) for at in range(8))
    w_copy, normed_copy, cells_copy, *grad_copies = [
        pltpu.make_async_copy(source, target, out_sems.at[at])
        for at, (source, target) in enumerate(results)
    ]
    for copy in (*weight_copies, x_copy, bias_copy, cot_copy, turned_copy):
        copy.start()
    for copy in (*weight_copies, x_copy):
        copy.wait()
    w_copy.start()

    for part in range(3):
        columns = slice(part * width, (part + 1) * width)
        qkv_ref[:, columns] = mxu(x_ref[...], w_qkv_ref[:, columns]).astype(jnp.bfloat16)

    def attend(window, carry):
        rows = pl.ds(pl.multiple_of(window * win, 16), win)
        bias = bias_ref[window]
        for at in range(HEADS // GROUP):
            columns = slice(at * group, (at + 1) * group)
            queries = qkv_ref[rows, columns]
            keys = qkv_ref[rows, width + at * group : width + (at + 1) * group]
            values = qkv_ref[rows, 2 * width + at * group : 2 * width + (at + 1) * group]
            scores = mxu(masked_heads(keys, head_dim), queries, NT)
            scores = scores.reshape(GROUP, win, win) * factor + bias
            lifted = jnp.exp2(scores - jnp.max(scores, axis=1, keepdims=True))
            total = jnp.sum(lifted, axis=1, keepdims=True)
            probs = (lifted * (1.0 / total)).astype(jnp.bfloat16)
            probs = probs.reshape(GROUP * win, win)
            probs_ref[window, at] = probs
            mixed = own_heads(mxu(turned_heads(probs, GROUP), values), head_dim)
            mixed_ref[rows, columns] = mixed.astype(jnp.bfloat16)
        return carry

    bias_copy.wait()
    lax.fori_loop(0, windows, attend, 0)

    cot_copy.wait()
    gain = gain_ref[...]

    def normalise(window, carry):
        rows = pl.ds(pl.multiple_of(window * win, 16), win)
        projected = mxu(mixed_ref[rows, :], w_out_ref[...])
        center = projected - jnp.mean(projected, axis=-1, keepdims=True)
        inverse = lax.rsqrt(jnp.mean(center * center, axis=-1, keepdims=True) + EPS)
        normal = center * inverse
        normed_ref[rows, :] = (normal * gain).astype(jnp.bfloat16)
        scaled = cot_ref[rows, :].astype(jnp.float32) * gain
        grad_proj = (
            scaled
            - jnp.mean(scaled, axis=-1, keepdims=True)
            - normal * jnp.mean(scaled * normal, axis=-1, keepdims=True)
        ) * inverse
        grad_proj_ref[rows, :] = grad_proj.astype(jnp.bfloat16)
        return carry

    lax.fori_loop(0, windows, normalise, 0)
    normed_copy.start()
    sent_ref, kept_ref = grads_ref.at[0], grads_ref.at[1]
    half = width // 2
    grad_out = mxu(mixed_ref[...], grad_proj_ref[...], TN)
    for block in range(blocks):
        slot = to_slot_ref[block]
        value = grad_out[block * depth : (block + 1) * depth, :]
        rows = pl.ds(pl.multiple_of(lax.rem(slot, blocks // 2) * depth, depth), depth)

        @pl.when(slot < blocks // 2)
        def _():
            kept_ref[rows, :] = value

        @pl.when(slot >= blocks // 2)
        def _():
            sent_ref[rows, :] = value

    grad_copies[0].start()
    grad_copies[1].start()
    grad_mix_ref[...] = mxu(grad_proj_ref[...], w_out_ref[...], NT).astype(jnp.bfloat16)

    def attend_back(window, carry):
        rows = pl.ds(pl.multiple_of(window * win, 16), win)
        for at in range(HEADS // GROUP):
            columns = slice(at * group, (at + 1) * group)
            key_columns = slice(width + at * group, width + (at + 1) * group)
            value_columns = slice(2 * width + at * group, 2 * width + (at + 1) * group)
            mix = grad_mix_ref[rows, columns]
            probs = probs_ref[window, at]
            float_probs = probs.astype(jnp.float32)
            grad_probs = mxu(masked_heads(qkv_ref[rows, value_columns], head_dim), mix, NT)
            product = (float_probs * grad_probs).reshape(GROUP, win, win)
            center = jnp.sum(product, axis=1, keepdims=True)
            grad_scores = scale * (product - float_probs.reshape(GROUP, win, win) * center)
            grad_scores = grad_scores.astype(jnp.bfloat16).reshape(GROUP * win, win)
            grad_values = own_heads(mxu(probs, mix), head_dim)
            grad_keys = own_heads(mxu(grad_scores, qkv_ref[rows, columns]), head_dim)
            turned = turned_heads(grad_scores, GROUP)
            grad_queries = own_heads(mxu(turned, qkv_ref[rows, key_columns]), head_dim)
            cells_ref[rows, columns] = grad_queries.astype(jnp.bfloat16)
            cells_ref[rows, key_columns] = grad_keys.astype(jnp.bfloat16)
            cells_ref[rows, value_columns] = grad_values.astype(jnp.bfloat16)
        return carry

    lax.fori_loop(0, windows, attend_back, 0)

    cells_copy.start()
    turned_copy.wait()
    for part in range(3):
        columns = slice(part * width, (part + 1) * width)
        for at, rows in enumerate((slice(half, width), slice(0, half))):
            grads_ref[2 + 2 * part + at] = mxu(turned_ref[rows, :], cells_ref[:, columns])
            grad_copies[2 + 2 * part + at].start()
    for copy in (w_copy, normed_copy, cells_copy, *grad_copies):
        copy.wait()


def exchanged(value, distance):
    count = lax.axis_size("lat")
    return lax.ppermute(value, "lat", [(i, i ^ distance) for i in range(count)])


def moved(value, grp_turn, distance):
    count = lax.axis_size("lat")
    groups = lax.axis_size("grp")
    pairs = []
    for grp in range(groups):
        for i in range(count):
            pairs.append((grp * count + i, (grp ^ grp_turn) * count + (i ^ distance[grp])))
    return lax.ppermute(value, ("grp", "lat"), pairs)


def gathered(block, halos, prepare, bias):
    here = lax.axis_index("grp") == 0
    far = moved(block, 0, (8, 12))
    near = moved(block, 0, (4, 4))
    halos = [passed_along(halo, "lat", -1) for halo in halos]
    far, bias, *halos = lax.optimization_barrier((far, bias, *halos))
    far_other = moved(far, 1, (0, 0))
    prepared = prepare(*halos)
    side = moved(jnp.where(here, block, far), 0, (2, 2))
    near_side = moved(jnp.where(here, near, far_other), 0, (2, 2))
    side, *prepared = lax.optimization_barrier((side, *prepared))
    side_other = moved(side, 1, (0, 0))
    near_side_other = moved(near_side, 1, (0, 0))
    shards = [block, near, far, far_other, side, near_side, side_other, near_side_other]
    low = jnp.array([0, 4, 8, 12, 2, 6, 14, 10], jnp.int32)
    high = jnp.array([0, 4, 12, 8, 14, 10, 2, 6], jnp.int32)
    order = jnp.where(here, low, high)
    shards += [exchanged(shard, 1) for shard in shards]
    return tuple(shards), jnp.concatenate([order, order + 1]), prepared, bias


def reversed_bits(value, count):
    result = 0
    bit = 1
    while bit < count:
        result = 2 * result + (value & 1)
        value = value >> 1
        bit *= 2
    return result


def summed(sent, kept, distances):
    for at, distance in enumerate(distances):
        if at > 0:
            half = kept.shape[0] // 2
            kept, sent = kept[:half], kept[half:]
        kept = kept + exchanged(sent, distance)
    return kept


def call(kernel, name, outs, tables, operands, scratch=(), far=(), flops=0):
    size = sum(math.prod(o.shape) * o.dtype.itemsize for o in (*outs, *operands, *far))
    vmem = pl.BlockSpec(memory_space=pltpu.VMEM)
    hbm = pl.BlockSpec(memory_space=pl.ANY)
    return pl.pallas_call(
        kernel,
        out_shape=outs,
        in_specs=[pl.BlockSpec(memory_space=pltpu.SMEM)] * len(tables)
        + [vmem] * len(operands)
        + [hbm] * len(far),
        out_specs=[hbm if far else vmem] * len(outs),
        scratch_shapes=list(scratch),
        compiler_params=pltpu.CompilerParams(vmem_limit_bytes=VMEM_BYTES),
        cost_estimate=pl.CostEstimate(flops=flops, bytes_accessed=size, transcendentals=0),
        name=name,
    )(*tables, *operands, *far)


def per_device(inputs, cotangent, idents, w_qkv, w_out, gain):
    lat_cells, lon_cells, width = inputs.shape
    half_rows = WIN_R // 2
    win = padded_rows()
    windows = (lat_cells // WIN_R) * (lon_cells // WIN_C)
    cells = windows * win
    places = jnp.asarray(window_places(lon_cells), jnp.bfloat16)

    def shape(*dims, dtype=jnp.bfloat16):
        return jax.ShapeDtypeStruct(dims, dtype)

    count = lax.axis_size("lat")
    me = lax.axis_index("lat")
    direct = count == 16 and lax.axis_size("grp") == 2 and width % (16 * count) == 0
    if direct:
        blocks = jnp.arange(count, dtype=jnp.int32)
        to_slot = reversed_bits(blocks ^ me, count)
    else:
        to_slot = jnp.arange(16, dtype=jnp.int32)

    def prepare(upper_in, upper_cot):
        return call(
            prepare_kernel,
            "prepare",
            (shape(cells, width), shape(cells, width), shape(width, cells)),
            (to_slot,),
            (inputs, upper_in, cotangent, upper_cot, places),
            flops=4 * cells * width * lon_cells * WIN_R,
        )

    weights = jnp.concatenate([w_qkv, w_out], axis=1)
    halos = (inputs[:half_rows], cotangent[:half_rows])
    labels = to_windows(idents + 1)
    bias = jnp.where(labels[:, :, None] == labels[:, None, :], 0.0, HIDDEN).astype(jnp.float32)
    if direct:
        shards, order, (tokens, cot, turned), bias = gathered(weights, halos, prepare, bias)
        into = order ^ me
    else:
        weights = lax.all_gather(weights, "lat", axis=0, tiled=True)
        shards = tuple(weights.reshape(16, width // 16, 4 * width))
        into = to_slot
        tokens, cot, turned = prepare(*[passed_along(halo, "lat", -1) for halo in halos])

    normed, grad_cells, qkv_full, *grads = call(
        block_kernel,
        "block",
        (
            shape(cells, width),
            shape(cells, 3 * width),
            shape(width, 3 * width),
            *[shape(width // 2, width, dtype=jnp.float32)] * 8,
        ),
        (into, to_slot),
        (gain[None],),
        (
            pltpu.VMEM((cells, width), jnp.bfloat16),
            pltpu.VMEM((width, cells), jnp.bfloat16),
            pltpu.VMEM((cells, width), jnp.bfloat16),
            pltpu.VMEM((windows, win, win), jnp.float32),
            pltpu.VMEM((cells, width), jnp.bfloat16),
            pltpu.VMEM((cells, 3 * width), jnp.bfloat16),
            pltpu.VMEM((width, 4 * width), jnp.bfloat16),
            pltpu.VMEM((8, width // 2, width), jnp.float32),
            pltpu.VMEM((cells, 3 * width), jnp.bfloat16),
            pltpu.VMEM((windows, HEADS // GROUP, GROUP * win, win), jnp.bfloat16),
            pltpu.VMEM((cells, width), jnp.bfloat16),
            pltpu.VMEM((cells, width), jnp.bfloat16),
            pltpu.VMEM((cells, width), jnp.bfloat16),
            pltpu.SemaphoreType.DMA((len(shards),)),
            pltpu.SemaphoreType.DMA((4,)),
            pltpu.SemaphoreType.DMA((11,)),
        ),
        far=(tokens, turned, cot, bias, *shards),
        flops=2 * cells * width * width * 10,
    )
    if direct:
        distances = [2**bit for bit in range(count.bit_length() - 1)]
        sums = [summed(sent, kept, distances[:2]) for sent, kept in zip(grads[::2], grads[1::2])]
        sums[0], normed, grad_cells = lax.optimization_barrier((sums[0], normed, grad_cells))
        half = sums[0].shape[0] // 2
        grad_out, *parts = [summed(kept[half:], kept[:half], distances[2:]) for kept in sums]
        grad_qkv = jnp.concatenate(parts, axis=1)
    else:
        whole = [jnp.concatenate([kept, sent]) for sent, kept in zip(grads[::2], grads[1::2])]
        both = lax.psum_scatter(jnp.concatenate(whole, axis=1), "lat", scatter_dimension=0, tiled=True)
        grad_out, grad_qkv = both[:, :width], both[:, width:]

    output, lower_out, grad_in, lower_grad = call(
        finish_kernel,
        "finish",
        (
            shape(*inputs.shape),
            shape(half_rows, lon_cells, width),
            shape(*inputs.shape),
            shape(half_rows, lon_cells, width),
        ),
        (),
        (grad_cells, qkv_full, normed, inputs, cotangent, places),
        (pltpu.VMEM((cells, width), jnp.bfloat16),),
        flops=2 * cells * width * (3 * width + 2 * lon_cells * WIN_R),
    )

    def completed(result, lower):
        lower = passed_along(lower, "lat", 1)
        top = result[:half_rows].astype(jnp.float32) + lower.astype(jnp.float32)
        return result.at[:half_rows].set(top.astype(jnp.bfloat16))

    return (completed(output, lower_out), completed(grad_in, lower_grad), grad_qkv, grad_out)


def solution(mesh):
    in_specs = (
        P(("grp", "lat"), None, None),
        P(("grp", "lat"), None, None),
        P(("grp", "lat"), None),
        P("lat", None),
        P("lat", None),
        P(),
    )
    out_specs = (
        P(("grp", "lat"), None, None),
        P(("grp", "lat"), None, None),
        P(("grp", "lat"), None),
        P(("grp", "lat"), None),
    )
    return jax.shard_map(
        per_device, mesh=mesh, in_specs=in_specs, out_specs=out_specs, check_vma=False
    )
```

```python
import math

import jax
import jax.numpy as jnp
import numpy as np
from jax import lax
from jax.experimental import pallas as pl
from jax.experimental.pallas import tpu as pltpu
from jax.sharding import PartitionSpec as P

HEADS = 8
WIN_R = 6
WIN_C = 12
EPS = 1e-05
HIDDEN = -1e30
GROUP = 2

NN = (((1,), (0,)), ((), ()))
NT = (((1,), (1,)), ((), ()))
TN = (((0,), (0,)), ((), ()))


def mxu(left, right, dims=NN):
    return lax.dot_general(left, right, dims, preferred_element_type=jnp.float32)


def passed_along(value, axis, steps):
    count = lax.axis_size(axis)
    first, last = (max(0, -steps), min(count, count - steps))
    return lax.ppermute(value, axis, [(source, source + steps) for source in range(first, last)])


def padded_rows():
    return -(-WIN_R * WIN_C // 16) * 16


def to_windows(field):
    lat_cells, lon_cells = field.shape
    field = field.reshape(lat_cells // WIN_R, WIN_R, lon_cells // WIN_C, WIN_C)
    field = field.transpose(0, 2, 1, 3).reshape(-1, WIN_R * WIN_C)
    return jnp.pad(field, ((0, 0), (0, padded_rows() - WIN_R * WIN_C)))


def window_places(lon_cells):
    win = padded_rows()
    places = np.zeros((WIN_R, lon_cells // WIN_C, win, lon_cells), np.float32)
    for row in range(WIN_R):
        for window in range(lon_cells // WIN_C):
            for column in range(WIN_C):
                source = (window * WIN_C + column + WIN_C // 2) % lon_cells
                places[row, window, row * WIN_C + column, source] = 1
    return places.reshape(WIN_R, -1, lon_cells)


def masked_heads(value, head_dim):
    head = lax.broadcasted_iota(jnp.int32, value.shape, 1) // head_dim
    zero = jnp.zeros_like(value)
    count = value.shape[1] // head_dim
    return jnp.concatenate([jnp.where(head == at, value, zero) for at in range(count)], axis=0)


def own_heads(stacked, head_dim):
    count = stacked.shape[1] // head_dim
    rows = stacked.shape[0] // count
    head = lax.broadcasted_iota(jnp.int32, (rows, stacked.shape[1]), 1) // head_dim
    result = stacked[:rows]
    for at in range(1, count):
        result = jnp.where(head == at, stacked[at * rows : (at + 1) * rows], result)
    return result


def turned_heads(stacked, count):
    rows = stacked.shape[0] // count
    return jnp.concatenate(
        [stacked[at * rows : (at + 1) * rows].T for at in range(count)], axis=0
    )


def prepare_kernel(
    to_slot_ref, inputs_ref, cot_ref, halo_ref, places_ref, tokens_ref, cot_tokens_ref, turned_ref
):
    half = halo_ref.shape[0] // 2
    lat_cells = inputs_ref.shape[0]
    cells = places_ref.shape[1]
    blocks = to_slot_ref.shape[0]
    for band in range(lat_cells // WIN_R):
        rows = slice(band * cells, (band + 1) * cells)
        for at, (own_ref, result_ref) in enumerate(
            ((inputs_ref, tokens_ref), (cot_ref, cot_tokens_ref))
        ):
            total = None
            for row in range(WIN_R):
                source = band * WIN_R + row + half
                beyond = at * half + source - lat_cells
                field = own_ref[source] if source < lat_cells else halo_ref[beyond]
                term = mxu(places_ref[row], field)
                total = term if total is None else total + term
            result_ref[rows, :] = total.astype(jnp.bfloat16)
    depth = tokens_ref.shape[1] // blocks
    turned = tokens_ref[...].T
    for block in range(blocks):
        rows = pl.ds(pl.multiple_of(to_slot_ref[block] * depth, depth), depth)
        turned_ref[rows, :] = turned[block * depth : (block + 1) * depth, :]


def finish_kernel(
    cells_ref, w_qkv_ref, normed_ref, inputs_ref, cot_ref, places_ref,
    output_ref, lower_out_ref, grad_in_ref, lower_grad_ref, shift_ref,
):
    lat_cells = inputs_ref.shape[0]
    half = lower_out_ref.shape[0]
    count = places_ref.shape[1]
    shift_ref[...] = mxu(cells_ref[...], w_qkv_ref[...], NT).astype(jnp.bfloat16)
    for value_ref, base_ref, result_ref, lower_ref in (
        (normed_ref, inputs_ref, output_ref, lower_out_ref),
        (shift_ref, cot_ref, grad_in_ref, lower_grad_ref),
    ):
        result_ref[:half] = base_ref[:half]
        for band in range(lat_cells // WIN_R):
            value = value_ref[band * count : (band + 1) * count, :]
            for row in range(WIN_R):
                back = mxu(places_ref[row], value, TN)
                target = band * WIN_R + row + half
                if target < lat_cells:
                    base = base_ref[target].astype(jnp.float32)
                    result_ref[target] = (base + back).astype(jnp.bfloat16)
                else:
                    lower_ref[target - lat_cells] = back.astype(jnp.bfloat16)


def block_kernel(into_ref, to_slot_ref, x_ref, turned_ref, cot_ref, bias_ref, gain_ref, *rest):
    shard_refs, rest = rest[: into_ref.shape[0]], rest[into_ref.shape[0] :]
    normed_ref, cells_ref, w_qkv_ref, *grad_refs = rest[:11]
    w_out_ref, qkv_ref, probs_ref, mixed_ref, grad_proj_ref, grad_mix_ref = rest[11:]
    windows, win = bias_ref.shape[:2]
    width = x_ref.shape[1]
    head_dim = width // HEADS
    group = GROUP * head_dim
    scale = head_dim ** (-0.5)
    factor = scale * math.log2(math.e)

    blocks = into_ref.shape[0]
    depth = width // blocks
    for at, shard_ref in enumerate(shard_refs):
        rows = pl.ds(pl.multiple_of(into_ref[at] * depth, depth), depth)
        w_qkv_ref[rows, :] = shard_ref[:, : 3 * width]
        w_out_ref[rows, :] = shard_ref[:, 3 * width :]

    for part in range(3):
        columns = slice(part * width, (part + 1) * width)
        qkv_ref[:, columns] = mxu(x_ref[...], w_qkv_ref[:, columns]).astype(jnp.bfloat16)

    def attend(window, carry):
        rows = pl.ds(pl.multiple_of(window * win, 16), win)
        bias = bias_ref[window]
        for at in range(HEADS // GROUP):
            columns = slice(at * group, (at + 1) * group)
            queries = qkv_ref[rows, columns]
            keys = qkv_ref[rows, width + at * group : width + (at + 1) * group]
            values = qkv_ref[rows, 2 * width + at * group : 2 * width + (at + 1) * group]
            scores = mxu(masked_heads(keys, head_dim), queries, NT)
            scores = scores.reshape(GROUP, win, win) * factor + bias
            lifted = jnp.exp2(scores - jnp.max(scores, axis=1, keepdims=True))
            total = jnp.sum(lifted, axis=1, keepdims=True)
            probs = (lifted * (1.0 / total)).astype(jnp.bfloat16)
            probs = probs.reshape(GROUP * win, win)
            probs_ref[window, at] = probs
            mixed = own_heads(mxu(turned_heads(probs, GROUP), values), head_dim)
            mixed_ref[rows, columns] = mixed.astype(jnp.bfloat16)
        return carry

    lax.fori_loop(0, windows, attend, 0)

    gain = gain_ref[...]

    def normalise(window, carry):
        rows = pl.ds(pl.multiple_of(window * win, 16), win)
        projected = mxu(mixed_ref[rows, :], w_out_ref[...])
        center = projected - jnp.mean(projected, axis=-1, keepdims=True)
        inverse = lax.rsqrt(jnp.mean(center * center, axis=-1, keepdims=True) + EPS)
        normal = center * inverse
        normed_ref[rows, :] = (normal * gain).astype(jnp.bfloat16)
        scaled = cot_ref[rows, :].astype(jnp.float32) * gain
        grad_proj = (
            scaled
            - jnp.mean(scaled, axis=-1, keepdims=True)
            - normal * jnp.mean(scaled * normal, axis=-1, keepdims=True)
        ) * inverse
        grad_proj_ref[rows, :] = grad_proj.astype(jnp.bfloat16)
        return carry

    lax.fori_loop(0, windows, normalise, 0)
    sent_ref, kept_ref = grad_refs[:2]
    half = kept_ref.shape[0]
    grad_out = mxu(mixed_ref[...], grad_proj_ref[...], TN)
    for block in range(blocks):
        slot = to_slot_ref[block]
        value = grad_out[block * depth : (block + 1) * depth, :]
        rows = pl.ds(pl.multiple_of(lax.rem(slot, blocks // 2) * depth, depth), depth)

        @pl.when(slot < blocks // 2)
        def _():
            kept_ref[rows, :] = value

        @pl.when(slot >= blocks // 2)
        def _():
            sent_ref[rows, :] = value

    grad_mix_ref[...] = mxu(grad_proj_ref[...], w_out_ref[...], NT).astype(jnp.bfloat16)

    def attend_back(window, carry):
        rows = pl.ds(pl.multiple_of(window * win, 16), win)
        for at in range(HEADS // GROUP):
            columns = slice(at * group, (at + 1) * group)
            key_columns = slice(width + at * group, width + (at + 1) * group)
            value_columns = slice(2 * width + at * group, 2 * width + (at + 1) * group)
            mix = grad_mix_ref[rows, columns]
            probs = probs_ref[window, at]
            float_probs = probs.astype(jnp.float32)
            grad_probs = mxu(masked_heads(qkv_ref[rows, value_columns], head_dim), mix, NT)
            product = (float_probs * grad_probs).reshape(GROUP, win, win)
            center = jnp.sum(product, axis=1, keepdims=True)
            grad_scores = scale * (product - float_probs.reshape(GROUP, win, win) * center)
            grad_scores = grad_scores.astype(jnp.bfloat16).reshape(GROUP * win, win)
            grad_values = own_heads(mxu(probs, mix), head_dim)
            grad_keys = own_heads(mxu(grad_scores, qkv_ref[rows, columns]), head_dim)
            turned = turned_heads(grad_scores, GROUP)
            grad_queries = own_heads(mxu(turned, qkv_ref[rows, key_columns]), head_dim)
            cells_ref[rows, columns] = grad_queries.astype(jnp.bfloat16)
            cells_ref[rows, key_columns] = grad_keys.astype(jnp.bfloat16)
            cells_ref[rows, value_columns] = grad_values.astype(jnp.bfloat16)
        return carry

    lax.fori_loop(0, windows, attend_back, 0)

    for part in range(3):
        columns = slice(part * width, (part + 1) * width)
        sent_ref, kept_ref = grad_refs[2 + 2 * part : 4 + 2 * part]
        sent_ref[...] = mxu(turned_ref[half:, :], cells_ref[:, columns])
        kept_ref[...] = mxu(turned_ref[:half, :], cells_ref[:, columns])


def exchanged(value, distance):
    count = lax.axis_size("lat")
    return lax.ppermute(value, "lat", [(i, i ^ distance) for i in range(count)])


def moved(value, grp_turn, distance):
    count = lax.axis_size("lat")
    groups = lax.axis_size("grp")
    pairs = []
    for grp in range(groups):
        for i in range(count):
            pairs.append((grp * count + i, (grp ^ grp_turn) * count + (i ^ distance[grp])))
    return lax.ppermute(value, ("grp", "lat"), pairs)


def gathered(block, halo, prepare, bias):
    here = lax.axis_index("grp") == 0
    far = moved(block, 0, (8, 12))
    far_side = moved(block, 0, (10, 14))
    halo = passed_along(halo, "lat", -1)
    near = moved(block, 0, (4, 6))
    side = exchanged(block, 2)
    near, bias = lax.optimization_barrier((near, bias))
    near_other, far_other = moved(near, 1, (0, 0)), moved(far, 1, (0, 0))
    far_side, halo = lax.optimization_barrier((far_side, halo))
    far_side_other = moved(far_side, 1, (0, 0))
    far_other, *prepared = lax.optimization_barrier((far_other, *prepare(halo)))
    shards = [block, side, near, near_other, far, far_other, far_side, far_side_other]
    low = jnp.array([0, 2, 4, 6, 8, 12, 10, 14], jnp.int32)
    high = jnp.array([0, 2, 6, 4, 12, 8, 14, 10], jnp.int32)
    order = jnp.where(here, low, high)
    shards += [exchanged(shard, 1) for shard in shards]
    return tuple(shards), jnp.concatenate([order, order + 1]), prepared, bias


def reversed_bits(value, count):
    result = 0
    bit = 1
    while bit < count:
        result = 2 * result + (value & 1)
        value = value >> 1
        bit *= 2
    return result


def summed(sent, kept, distances):
    for at, distance in enumerate(distances):
        if at > 0:
            half = kept.shape[0] // 2
            kept, sent = kept[:half], kept[half:]
        kept = kept + exchanged(sent, distance)
    return kept


def call(kernel, name, outs, tables, operands, scratch=(), flops=0, vmem=40):
    size = sum(math.prod(o.shape) * o.dtype.itemsize for o in (*outs, *operands))
    return pl.pallas_call(
        kernel,
        out_shape=outs,
        in_specs=[pl.BlockSpec(memory_space=pltpu.SMEM)] * len(tables)
        + [pl.BlockSpec(memory_space=pltpu.VMEM)] * len(operands),
        out_specs=[pl.BlockSpec(memory_space=pltpu.VMEM)] * len(outs),
        scratch_shapes=list(scratch),
        compiler_params=pltpu.CompilerParams(vmem_limit_bytes=vmem * 1024 * 1024),
        cost_estimate=pl.CostEstimate(flops=flops, bytes_accessed=size, transcendentals=0),
        name=name,
    )(*tables, *operands)


def per_device(inputs, cotangent, idents, w_qkv, w_out, gain):
    lat_cells, lon_cells, width = inputs.shape
    half_rows = WIN_R // 2
    win = padded_rows()
    windows = (lat_cells // WIN_R) * (lon_cells // WIN_C)
    cells = windows * win
    places = jnp.asarray(window_places(lon_cells), jnp.bfloat16)

    def shape(*dims, dtype=jnp.bfloat16):
        return jax.ShapeDtypeStruct(dims, dtype)

    count = lax.axis_size("lat")
    me = lax.axis_index("lat")
    direct = count == 16 and lax.axis_size("grp") == 2 and width % (16 * count) == 0
    if direct:
        blocks = jnp.arange(count, dtype=jnp.int32)
        to_slot = reversed_bits(blocks ^ me, count)
    else:
        to_slot = jnp.arange(16, dtype=jnp.int32)

    def prepare(halo):
        return call(
            prepare_kernel,
            "prepare",
            (shape(cells, width), shape(cells, width), shape(width, cells)),
            (to_slot,),
            (inputs, cotangent, halo, places),
            flops=4 * cells * width * lon_cells * WIN_R,
            vmem=24,
        )

    weights = jnp.concatenate([w_qkv, w_out], axis=1)
    halo = jnp.concatenate([inputs[:half_rows], cotangent[:half_rows]])
    labels = to_windows(idents + 1)
    bias = jnp.where(labels[:, :, None] == labels[:, None, :], 0.0, HIDDEN).astype(jnp.float32)
    if direct:
        shards, order, (tokens, cot, turned), bias = gathered(weights, halo, prepare, bias)
        into = order ^ me
    else:
        weights = lax.all_gather(weights, "lat", axis=0, tiled=True)
        shards = tuple(weights.reshape(16, width // 16, 4 * width))
        into = to_slot
        tokens, cot, turned = prepare(passed_along(halo, "lat", -1))

    normed, grad_cells, qkv_full, *grads = call(
        block_kernel,
        "block",
        (
            shape(cells, width),
            shape(cells, 3 * width),
            shape(width, 3 * width),
            *[shape(width // 2, width, dtype=jnp.float32)] * 8,
        ),
        (into, to_slot),
        (tokens, turned, cot, bias, gain[None], *shards),
        (
            pltpu.VMEM((width, width), jnp.bfloat16),
            pltpu.VMEM((cells, 3 * width), jnp.bfloat16),
            pltpu.VMEM((windows, HEADS // GROUP, GROUP * win, win), jnp.bfloat16),
            pltpu.VMEM((cells, width), jnp.bfloat16),
            pltpu.VMEM((cells, width), jnp.bfloat16),
            pltpu.VMEM((cells, width), jnp.bfloat16),
        ),
        flops=2 * cells * width * width * 10,
    )
    if direct:
        distances = [2**bit for bit in range(count.bit_length() - 1)]
        sums = [summed(sent, kept, distances[:2]) for sent, kept in zip(grads[::2], grads[1::2])]
        sums[0], normed, grad_cells = lax.optimization_barrier((sums[0], normed, grad_cells))
        half = sums[0].shape[0] // 2
        grad_out, *parts = [summed(kept[half:], kept[:half], distances[2:]) for kept in sums]
        grad_qkv = jnp.concatenate(parts, axis=1)
    else:
        whole = [jnp.concatenate([kept, sent]) for sent, kept in zip(grads[::2], grads[1::2])]
        both = lax.psum_scatter(jnp.concatenate(whole, axis=1), "lat", scatter_dimension=0, tiled=True)
        grad_out, grad_qkv = both[:, :width], both[:, width:]

    output, lower_out, grad_in, lower_grad = call(
        finish_kernel,
        "finish",
        (
            shape(*inputs.shape),
            shape(half_rows, lon_cells, width),
            shape(*inputs.shape),
            shape(half_rows, lon_cells, width),
        ),
        (),
        (grad_cells, qkv_full, normed, inputs, cotangent, places),
        (pltpu.VMEM((cells, width), jnp.bfloat16),),
        flops=2 * cells * width * (3 * width + 2 * lon_cells * WIN_R),
        vmem=24,
    )

    def completed(result, lower):
        lower = passed_along(lower, "lat", 1)
        top = result[:half_rows].astype(jnp.float32) + lower.astype(jnp.float32)
        return result.at[:half_rows].set(top.astype(jnp.bfloat16))

    return (completed(output, lower_out), completed(grad_in, lower_grad), grad_qkv, grad_out)


def solution(mesh):
    in_specs = (
        P(("grp", "lat"), None, None),
        P(("grp", "lat"), None, None),
        P(("grp", "lat"), None),
        P("lat", None),
        P("lat", None),
        P(),
    )
    out_specs = (
        P(("grp", "lat"), None, None),
        P(("grp", "lat"), None, None),
        P(("grp", "lat"), None),
        P(("grp", "lat"), None),
    )
    return jax.shard_map(
        per_device, mesh=mesh, in_specs=in_specs, out_specs=out_specs, check_vma=False
    )
```

```python
import math

import jax
import jax.numpy as jnp
import numpy as np
from jax import lax
from jax.experimental import pallas as pl
from jax.experimental.pallas import tpu as pltpu
from jax.sharding import PartitionSpec as P

HEADS = 8
WIN_R = 6
WIN_C = 12
EPS = 1e-05
HIDDEN = -1e30
GROUP = 2

NN = (((1,), (0,)), ((), ()))
NT = (((1,), (1,)), ((), ()))
TN = (((0,), (0,)), ((), ()))


def mxu(left, right, dims=NN):
    return lax.dot_general(left, right, dims, preferred_element_type=jnp.float32)


def passed_along(value, axis, steps):
    count = lax.axis_size(axis)
    first, last = (max(0, -steps), min(count, count - steps))
    return lax.ppermute(value, axis, [(source, source + steps) for source in range(first, last)])


def padded_rows():
    return -(-WIN_R * WIN_C // 16) * 16


def to_windows(field):
    lat_cells, lon_cells = field.shape
    field = field.reshape(lat_cells // WIN_R, WIN_R, lon_cells // WIN_C, WIN_C)
    field = field.transpose(0, 2, 1, 3).reshape(-1, WIN_R * WIN_C)
    return jnp.pad(field, ((0, 0), (0, padded_rows() - WIN_R * WIN_C)))


def window_places(lon_cells):
    win = padded_rows()
    places = np.zeros((WIN_R, lon_cells // WIN_C, win, lon_cells), np.float32)
    for row in range(WIN_R):
        for window in range(lon_cells // WIN_C):
            for column in range(WIN_C):
                source = (window * WIN_C + column + WIN_C // 2) % lon_cells
                places[row, window, row * WIN_C + column, source] = 1
    return places.reshape(WIN_R, -1, lon_cells)


def masked_heads(value, head_dim):
    head = lax.broadcasted_iota(jnp.int32, value.shape, 1) // head_dim
    zero = jnp.zeros_like(value)
    count = value.shape[1] // head_dim
    return jnp.concatenate([jnp.where(head == at, value, zero) for at in range(count)], axis=0)


def own_heads(stacked, head_dim):
    count = stacked.shape[1] // head_dim
    rows = stacked.shape[0] // count
    head = lax.broadcasted_iota(jnp.int32, (rows, stacked.shape[1]), 1) // head_dim
    result = stacked[:rows]
    for at in range(1, count):
        result = jnp.where(head == at, stacked[at * rows : (at + 1) * rows], result)
    return result


def turned_heads(stacked, count):
    rows = stacked.shape[0] // count
    return jnp.concatenate(
        [stacked[at * rows : (at + 1) * rows].T for at in range(count)], axis=0
    )


def prepare_kernel(
    to_slot_ref, inputs_ref, cot_ref, halo_ref, places_ref, tokens_ref, cot_tokens_ref, turned_ref
):
    half = halo_ref.shape[0] // 2
    lat_cells = inputs_ref.shape[0]
    cells = places_ref.shape[1]
    blocks = to_slot_ref.shape[0]
    for band in range(lat_cells // WIN_R):
        rows = slice(band * cells, (band + 1) * cells)
        for at, (own_ref, result_ref) in enumerate(
            ((inputs_ref, tokens_ref), (cot_ref, cot_tokens_ref))
        ):
            total = None
            for row in range(WIN_R):
                source = band * WIN_R + row + half
                beyond = at * half + source - lat_cells
                field = own_ref[source] if source < lat_cells else halo_ref[beyond]
                term = mxu(places_ref[row], field)
                total = term if total is None else total + term
            result_ref[rows, :] = total.astype(jnp.bfloat16)
    depth = tokens_ref.shape[1] // blocks
    turned = tokens_ref[...].T
    for block in range(blocks):
        rows = pl.ds(pl.multiple_of(to_slot_ref[block] * depth, depth), depth)
        turned_ref[rows, :] = turned[block * depth : (block + 1) * depth, :]


def finish_kernel(
    cells_ref, w_qkv_ref, normed_ref, inputs_ref, cot_ref, places_ref,
    output_ref, lower_out_ref, grad_in_ref, lower_grad_ref, shift_ref,
):
    lat_cells = inputs_ref.shape[0]
    half = lower_out_ref.shape[0]
    count = places_ref.shape[1]
    shift_ref[...] = mxu(cells_ref[...], w_qkv_ref[...], NT).astype(jnp.bfloat16)
    for value_ref, base_ref, result_ref, lower_ref in (
        (normed_ref, inputs_ref, output_ref, lower_out_ref),
        (shift_ref, cot_ref, grad_in_ref, lower_grad_ref),
    ):
        result_ref[:half] = base_ref[:half]
        for band in range(lat_cells // WIN_R):
            value = value_ref[band * count : (band + 1) * count, :]
            for row in range(WIN_R):
                back = mxu(places_ref[row], value, TN)
                target = band * WIN_R + row + half
                if target < lat_cells:
                    base = base_ref[target].astype(jnp.float32)
                    result_ref[target] = (base + back).astype(jnp.bfloat16)
                else:
                    lower_ref[target - lat_cells] = back.astype(jnp.bfloat16)


def block_kernel(into_ref, to_slot_ref, x_ref, turned_ref, cot_ref, bias_ref, gain_ref, *rest):
    shard_refs, rest = rest[: into_ref.shape[0]], rest[into_ref.shape[0] :]
    normed_ref, cells_ref, w_qkv_ref, *grad_refs = rest[:11]
    w_out_ref, qkv_ref, probs_ref, mixed_ref, grad_proj_ref, grad_mix_ref = rest[11:]
    windows, win = bias_ref.shape[:2]
    width = x_ref.shape[1]
    head_dim = width // HEADS
    group = GROUP * head_dim
    scale = head_dim ** (-0.5)
    factor = scale * math.log2(math.e)

    blocks = into_ref.shape[0]
    depth = width // blocks
    for at, shard_ref in enumerate(shard_refs):
        rows = pl.ds(pl.multiple_of(into_ref[at] * depth, depth), depth)
        w_qkv_ref[rows, :] = shard_ref[:, : 3 * width]
        w_out_ref[rows, :] = shard_ref[:, 3 * width :]

    for part in range(3):
        columns = slice(part * width, (part + 1) * width)
        qkv_ref[:, columns] = mxu(x_ref[...], w_qkv_ref[:, columns]).astype(jnp.bfloat16)

    def attend(window, carry):
        rows = pl.ds(pl.multiple_of(window * win, 16), win)
        bias = bias_ref[window]
        for at in range(HEADS // GROUP):
            columns = slice(at * group, (at + 1) * group)
            queries = qkv_ref[rows, columns]
            keys = qkv_ref[rows, width + at * group : width + (at + 1) * group]
            values = qkv_ref[rows, 2 * width + at * group : 2 * width + (at + 1) * group]
            scores = mxu(masked_heads(keys, head_dim), queries, NT)
            scores = scores.reshape(GROUP, win, win) * factor + bias
            lifted = jnp.exp2(scores - jnp.max(scores, axis=1, keepdims=True))
            total = jnp.sum(lifted, axis=1, keepdims=True)
            probs = (lifted * (1.0 / total)).astype(jnp.bfloat16)
            probs = probs.reshape(GROUP * win, win)
            probs_ref[window, at] = probs
            mixed = own_heads(mxu(turned_heads(probs, GROUP), values), head_dim)
            mixed_ref[rows, columns] = mixed.astype(jnp.bfloat16)
        return carry

    lax.fori_loop(0, windows, attend, 0)

    gain = gain_ref[...]

    def normalise(window, carry):
        rows = pl.ds(pl.multiple_of(window * win, 16), win)
        projected = mxu(mixed_ref[rows, :], w_out_ref[...])
        center = projected - jnp.mean(projected, axis=-1, keepdims=True)
        inverse = lax.rsqrt(jnp.mean(center * center, axis=-1, keepdims=True) + EPS)
        normal = center * inverse
        normed_ref[rows, :] = (normal * gain).astype(jnp.bfloat16)
        scaled = cot_ref[rows, :].astype(jnp.float32) * gain
        grad_proj = (
            scaled
            - jnp.mean(scaled, axis=-1, keepdims=True)
            - normal * jnp.mean(scaled * normal, axis=-1, keepdims=True)
        ) * inverse
        grad_proj_ref[rows, :] = grad_proj.astype(jnp.bfloat16)
        return carry

    lax.fori_loop(0, windows, normalise, 0)
    sent_ref, kept_ref = grad_refs[:2]
    half = kept_ref.shape[0]
    grad_out = mxu(mixed_ref[...], grad_proj_ref[...], TN)
    for block in range(blocks):
        slot = to_slot_ref[block]
        value = grad_out[block * depth : (block + 1) * depth, :]
        rows = pl.ds(pl.multiple_of(lax.rem(slot, blocks // 2) * depth, depth), depth)

        @pl.when(slot < blocks // 2)
        def _():
            kept_ref[rows, :] = value

        @pl.when(slot >= blocks // 2)
        def _():
            sent_ref[rows, :] = value

    grad_mix_ref[...] = mxu(grad_proj_ref[...], w_out_ref[...], NT).astype(jnp.bfloat16)

    def attend_back(window, carry):
        rows = pl.ds(pl.multiple_of(window * win, 16), win)
        for at in range(HEADS // GROUP):
            columns = slice(at * group, (at + 1) * group)
            key_columns = slice(width + at * group, width + (at + 1) * group)
            value_columns = slice(2 * width + at * group, 2 * width + (at + 1) * group)
            mix = grad_mix_ref[rows, columns]
            probs = probs_ref[window, at]
            float_probs = probs.astype(jnp.float32)
            grad_probs = mxu(masked_heads(qkv_ref[rows, value_columns], head_dim), mix, NT)
            product = (float_probs * grad_probs).reshape(GROUP, win, win)
            center = jnp.sum(product, axis=1, keepdims=True)
            grad_scores = scale * (product - float_probs.reshape(GROUP, win, win) * center)
            grad_scores = grad_scores.astype(jnp.bfloat16).reshape(GROUP * win, win)
            grad_values = own_heads(mxu(probs, mix), head_dim)
            grad_keys = own_heads(mxu(grad_scores, qkv_ref[rows, columns]), head_dim)
            turned = turned_heads(grad_scores, GROUP)
            grad_queries = own_heads(mxu(turned, qkv_ref[rows, key_columns]), head_dim)
            cells_ref[rows, columns] = grad_queries.astype(jnp.bfloat16)
            cells_ref[rows, key_columns] = grad_keys.astype(jnp.bfloat16)
            cells_ref[rows, value_columns] = grad_values.astype(jnp.bfloat16)
        return carry

    lax.fori_loop(0, windows, attend_back, 0)

    for part in range(3):
        columns = slice(part * width, (part + 1) * width)
        sent_ref, kept_ref = grad_refs[2 + 2 * part : 4 + 2 * part]
        sent_ref[...] = mxu(turned_ref[half:, :], cells_ref[:, columns])
        kept_ref[...] = mxu(turned_ref[:half, :], cells_ref[:, columns])


def exchanged(value, distance):
    count = lax.axis_size("lat")
    return lax.ppermute(value, "lat", [(i, i ^ distance) for i in range(count)])


def moved(value, grp_turn, distance):
    count = lax.axis_size("lat")
    groups = lax.axis_size("grp")
    pairs = []
    for grp in range(groups):
        for i in range(count):
            pairs.append((grp * count + i, (grp ^ grp_turn) * count + (i ^ distance[grp])))
    return lax.ppermute(value, ("grp", "lat"), pairs)


def gathered(block, halo, prepare, bias):
    here = lax.axis_index("grp") == 0
    far = moved(block, 0, (8, 12))
    halo = passed_along(halo, "lat", -1)
    near = moved(block, 0, (4, 6))
    side = exchanged(block, 2)
    near, bias = lax.optimization_barrier((near, bias))
    far_side, far_other = exchanged(far, 2), moved(far, 1, (0, 0))
    near_other = moved(near, 1, (0, 0))
    far_side_other = moved(far_side, 1, (0, 0))
    far_other, *prepared = lax.optimization_barrier((far_other, *prepare(halo)))
    shards = [block, side, near, near_other, far, far_other, far_side, far_side_other]
    low = jnp.array([0, 2, 4, 6, 8, 12, 10, 14], jnp.int32)
    high = jnp.array([0, 2, 6, 4, 12, 8, 14, 10], jnp.int32)
    order = jnp.where(here, low, high)
    shards += [exchanged(shard, 1) for shard in shards]
    return tuple(shards), jnp.concatenate([order, order + 1]), prepared, bias


def reversed_bits(value, count):
    result = 0
    bit = 1
    while bit < count:
        result = 2 * result + (value & 1)
        value = value >> 1
        bit *= 2
    return result


def summed(sent, kept, distances):
    for at, distance in enumerate(distances):
        if at > 0:
            half = kept.shape[0] // 2
            kept, sent = kept[:half], kept[half:]
        kept = kept + exchanged(sent, distance)
    return kept


def call(kernel, name, outs, tables, operands, scratch=(), flops=0, vmem=40):
    size = sum(math.prod(o.shape) * o.dtype.itemsize for o in (*outs, *operands))
    return pl.pallas_call(
        kernel,
        out_shape=outs,
        in_specs=[pl.BlockSpec(memory_space=pltpu.SMEM)] * len(tables)
        + [pl.BlockSpec(memory_space=pltpu.VMEM)] * len(operands),
        out_specs=[pl.BlockSpec(memory_space=pltpu.VMEM)] * len(outs),
        scratch_shapes=list(scratch),
        compiler_params=pltpu.CompilerParams(vmem_limit_bytes=vmem * 1024 * 1024),
        cost_estimate=pl.CostEstimate(flops=flops, bytes_accessed=size, transcendentals=0),
        name=name,
    )(*tables, *operands)


def per_device(inputs, cotangent, idents, w_qkv, w_out, gain):
    lat_cells, lon_cells, width = inputs.shape
    half_rows = WIN_R // 2
    win = padded_rows()
    windows = (lat_cells // WIN_R) * (lon_cells // WIN_C)
    cells = windows * win
    places = jnp.asarray(window_places(lon_cells), jnp.bfloat16)

    def shape(*dims, dtype=jnp.bfloat16):
        return jax.ShapeDtypeStruct(dims, dtype)

    count = lax.axis_size("lat")
    me = lax.axis_index("lat")
    direct = count == 16 and lax.axis_size("grp") == 2 and width % (16 * count) == 0
    if direct:
        blocks = jnp.arange(count, dtype=jnp.int32)
        to_slot = reversed_bits(blocks ^ me, count)
    else:
        to_slot = jnp.arange(16, dtype=jnp.int32)

    def prepare(halo):
        return call(
            prepare_kernel,
            "prepare",
            (shape(cells, width), shape(cells, width), shape(width, cells)),
            (to_slot,),
            (inputs, cotangent, halo, places),
            flops=4 * cells * width * lon_cells * WIN_R,
            vmem=24,
        )

    weights = jnp.concatenate([w_qkv, w_out], axis=1)
    halo = jnp.concatenate([inputs[:half_rows], cotangent[:half_rows]])
    labels = to_windows(idents + 1)
    bias = jnp.where(labels[:, :, None] == labels[:, None, :], 0.0, HIDDEN).astype(jnp.float32)
    if direct:
        shards, order, (tokens, cot, turned), bias = gathered(weights, halo, prepare, bias)
        into = order ^ me
    else:
        weights = lax.all_gather(weights, "lat", axis=0, tiled=True)
        shards = tuple(weights.reshape(16, width // 16, 4 * width))
        into = to_slot
        tokens, cot, turned = prepare(passed_along(halo, "lat", -1))

    normed, grad_cells, qkv_full, *grads = call(
        block_kernel,
        "block",
        (
            shape(cells, width),
            shape(cells, 3 * width),
            shape(width, 3 * width),
            *[shape(width // 2, width, dtype=jnp.float32)] * 8,
        ),
        (into, to_slot),
        (tokens, turned, cot, bias, gain[None], *shards),
        (
            pltpu.VMEM((width, width), jnp.bfloat16),
            pltpu.VMEM((cells, 3 * width), jnp.bfloat16),
            pltpu.VMEM((windows, HEADS // GROUP, GROUP * win, win), jnp.bfloat16),
            pltpu.VMEM((cells, width), jnp.bfloat16),
            pltpu.VMEM((cells, width), jnp.bfloat16),
            pltpu.VMEM((cells, width), jnp.bfloat16),
        ),
        flops=2 * cells * width * width * 10,
    )
    if direct:
        distances = [2**bit for bit in range(count.bit_length() - 1)]
        sums = [summed(sent, kept, distances[:2]) for sent, kept in zip(grads[::2], grads[1::2])]
        sums[0], normed, grad_cells = lax.optimization_barrier((sums[0], normed, grad_cells))
        half = sums[0].shape[0] // 2
        grad_out, *parts = [summed(kept[half:], kept[:half], distances[2:]) for kept in sums]
        grad_qkv = jnp.concatenate(parts, axis=1)
    else:
        whole = [jnp.concatenate([kept, sent]) for sent, kept in zip(grads[::2], grads[1::2])]
        both = lax.psum_scatter(jnp.concatenate(whole, axis=1), "lat", scatter_dimension=0, tiled=True)
        grad_out, grad_qkv = both[:, :width], both[:, width:]

    output, lower_out, grad_in, lower_grad = call(
        finish_kernel,
        "finish",
        (
            shape(*inputs.shape),
            shape(half_rows, lon_cells, width),
            shape(*inputs.shape),
            shape(half_rows, lon_cells, width),
        ),
        (),
        (grad_cells, qkv_full, normed, inputs, cotangent, places),
        (pltpu.VMEM((cells, width), jnp.bfloat16),),
        flops=2 * cells * width * (3 * width + 2 * lon_cells * WIN_R),
        vmem=24,
    )

    def completed(result, lower):
        lower = passed_along(lower, "lat", 1)
        top = result[:half_rows].astype(jnp.float32) + lower.astype(jnp.float32)
        return result.at[:half_rows].set(top.astype(jnp.bfloat16))

    return (completed(output, lower_out), completed(grad_in, lower_grad), grad_qkv, grad_out)


def solution(mesh):
    in_specs = (
        P(("grp", "lat"), None, None),
        P(("grp", "lat"), None, None),
        P(("grp", "lat"), None),
        P("lat", None),
        P("lat", None),
        P(),
    )
    out_specs = (
        P(("grp", "lat"), None, None),
        P(("grp", "lat"), None, None),
        P(("grp", "lat"), None),
        P(("grp", "lat"), None),
    )
    return jax.shard_map(
        per_device, mesh=mesh, in_specs=in_specs, out_specs=out_specs, check_vma=False
    )
```

```python
import math

import jax
import jax.numpy as jnp
import numpy as np
from jax import lax
from jax.experimental import pallas as pl
from jax.experimental.pallas import tpu as pltpu
from jax.sharding import PartitionSpec as P

HEADS = 8
WIN_R = 6
WIN_C = 12
EPS = 1e-05
HIDDEN = -1e30
STEPS = 32000.0
GRAD_PLACES = (3, 2, 1)
GROUP = 2

NN = (((1,), (0,)), ((), ()))
NT = (((1,), (1,)), ((), ()))
TN = (((0,), (0,)), ((), ()))


def mxu(left, right, dims=NN):
    return lax.dot_general(left, right, dims, preferred_element_type=jnp.float32)


def passed_along(value, axis, steps):
    count = lax.axis_size(axis)
    first, last = (max(0, -steps), min(count, count - steps))
    return lax.ppermute(value, axis, [(source, source + steps) for source in range(first, last)])


def padded_rows():
    return -(-WIN_R * WIN_C // 16) * 16


def to_windows(field):
    lat_cells, lon_cells = field.shape
    field = field.reshape(lat_cells // WIN_R, WIN_R, lon_cells // WIN_C, WIN_C)
    field = field.transpose(0, 2, 1, 3).reshape(-1, WIN_R * WIN_C)
    return jnp.pad(field, ((0, 0), (0, padded_rows() - WIN_R * WIN_C)))


def window_places(lon_cells):
    win = padded_rows()
    places = np.zeros((WIN_R, lon_cells // WIN_C, win, lon_cells), np.float32)
    for row in range(WIN_R):
        for window in range(lon_cells // WIN_C):
            for column in range(WIN_C):
                source = (window * WIN_C + column + WIN_C // 2) % lon_cells
                places[row, window, row * WIN_C + column, source] = 1
    return places.reshape(WIN_R, -1, lon_cells)


def masked_heads(value, head_dim):
    head = lax.broadcasted_iota(jnp.int32, value.shape, 1) // head_dim
    zero = jnp.zeros_like(value)
    count = value.shape[1] // head_dim
    return jnp.concatenate([jnp.where(head == at, value, zero) for at in range(count)], axis=0)


def own_heads(stacked, head_dim):
    count = stacked.shape[1] // head_dim
    rows = stacked.shape[0] // count
    head = lax.broadcasted_iota(jnp.int32, (rows, stacked.shape[1]), 1) // head_dim
    result = stacked[:rows]
    for at in range(1, count):
        result = jnp.where(head == at, stacked[at * rows : (at + 1) * rows], result)
    return result


def turned_heads(stacked, count):
    rows = stacked.shape[0] // count
    return jnp.concatenate(
        [stacked[at * rows : (at + 1) * rows].T for at in range(count)], axis=0
    )


def prepare_kernel(
    to_slot_ref, inputs_ref, cot_ref, halo_ref, places_ref, tokens_ref, cot_tokens_ref, turned_ref
):
    half = halo_ref.shape[0] // 2
    lat_cells = inputs_ref.shape[0]
    cells = places_ref.shape[1]
    blocks = to_slot_ref.shape[0]
    for band in range(lat_cells // WIN_R):
        rows = slice(band * cells, (band + 1) * cells)
        for at, (own_ref, result_ref) in enumerate(
            ((inputs_ref, tokens_ref), (cot_ref, cot_tokens_ref))
        ):
            total = None
            for row in range(WIN_R):
                source = band * WIN_R + row + half
                beyond = at * half + source - lat_cells
                field = own_ref[source] if source < lat_cells else halo_ref[beyond]
                term = mxu(places_ref[row], field)
                total = term if total is None else total + term
            result_ref[rows, :] = total.astype(jnp.bfloat16)
    depth = tokens_ref.shape[1] // blocks
    turned = tokens_ref[...].T
    for block in range(blocks):
        rows = pl.ds(pl.multiple_of(to_slot_ref[block] * depth, depth), depth)
        turned_ref[rows, :] = turned[block * depth : (block + 1) * depth, :]


def finish_kernel(
    cells_ref, w_qkv_ref, normed_ref, inputs_ref, cot_ref, places_ref,
    output_ref, grad_in_ref, lower_ref, shift_ref,
):
    lat_cells = inputs_ref.shape[0]
    half = lower_ref.shape[0] // 2
    count = places_ref.shape[1]
    shift_ref[...] = mxu(cells_ref[...], w_qkv_ref[...], NT).astype(jnp.bfloat16)
    for at, (value_ref, base_ref, result_ref) in enumerate(
        ((normed_ref, inputs_ref, output_ref), (shift_ref, cot_ref, grad_in_ref))
    ):
        result_ref[:half] = base_ref[:half]
        for band in range(lat_cells // WIN_R):
            value = value_ref[band * count : (band + 1) * count, :]
            for row in range(WIN_R):
                back = mxu(places_ref[row], value, TN)
                target = band * WIN_R + row + half
                if target < lat_cells:
                    base = base_ref[target].astype(jnp.float32)
                    result_ref[target] = (base + back).astype(jnp.bfloat16)
                else:
                    lower_ref[at * half + target - lat_cells] = back.astype(jnp.bfloat16)


def block_kernel(into_ref, to_slot_ref, x_ref, turned_ref, cot_ref, bias_ref, gain_ref, *rest):
    shard_refs, rest = rest[: into_ref.shape[0]], rest[into_ref.shape[0] :]
    normed_ref, cells_ref, w_qkv_ref, *grad_refs = rest[:7]
    w_out_ref, qkv_ref, probs_ref, mixed_ref, grad_proj_ref, grad_mix_ref = rest[7:]
    windows, win = bias_ref.shape[:2]
    width = x_ref.shape[1]
    head_dim = width // HEADS
    group = GROUP * head_dim
    scale = head_dim ** (-0.5)
    factor = scale * math.log2(math.e)

    blocks = into_ref.shape[0]
    depth = width // blocks
    for at, shard_ref in enumerate(shard_refs):
        rows = pl.ds(pl.multiple_of(into_ref[at] * depth, depth), depth)
        w_qkv_ref[rows, :] = shard_ref[:, : 3 * width]
        w_out_ref[rows, :] = shard_ref[:, 3 * width :]

    for part in range(3):
        columns = slice(part * width, (part + 1) * width)
        qkv_ref[:, columns] = mxu(x_ref[...], w_qkv_ref[:, columns]).astype(jnp.bfloat16)

    def attend(window, carry):
        rows = pl.ds(pl.multiple_of(window * win, 16), win)
        bias = bias_ref[window]
        for at in range(HEADS // GROUP):
            columns = slice(at * group, (at + 1) * group)
            queries = qkv_ref[rows, columns]
            keys = qkv_ref[rows, width + at * group : width + (at + 1) * group]
            values = qkv_ref[rows, 2 * width + at * group : 2 * width + (at + 1) * group]
            scores = mxu(masked_heads(keys, head_dim), queries, NT)
            scores = scores.reshape(GROUP, win, win) * factor + bias
            lifted = jnp.exp2(scores - jnp.max(scores, axis=1, keepdims=True))
            total = jnp.sum(lifted, axis=1, keepdims=True)
            probs = (lifted * (1.0 / total)).astype(jnp.bfloat16)
            probs = probs.reshape(GROUP * win, win)
            probs_ref[window, at] = probs
            mixed = own_heads(mxu(turned_heads(probs, GROUP), values), head_dim)
            mixed_ref[rows, columns] = mixed.astype(jnp.bfloat16)
        return carry

    lax.fori_loop(0, windows, attend, 0)

    gain = gain_ref[...]

    def normalise(window, carry):
        rows = pl.ds(pl.multiple_of(window * win, 16), win)
        projected = mxu(mixed_ref[rows, :], w_out_ref[...])
        center = projected - jnp.mean(projected, axis=-1, keepdims=True)
        inverse = lax.rsqrt(jnp.mean(center * center, axis=-1, keepdims=True) + EPS)
        normal = center * inverse
        normed_ref[rows, :] = (normal * gain).astype(jnp.bfloat16)
        scaled = cot_ref[rows, :].astype(jnp.float32) * gain
        grad_proj = (
            scaled
            - jnp.mean(scaled, axis=-1, keepdims=True)
            - normal * jnp.mean(scaled * normal, axis=-1, keepdims=True)
        ) * inverse
        grad_proj_ref[rows, :] = grad_proj.astype(jnp.bfloat16)
        return carry

    lax.fori_loop(0, windows, normalise, 0)
    half = width // 2
    sent_refs, kept_refs = grad_refs[::2], grad_refs[1::2]
    grad_out = mxu(mixed_ref[...], grad_proj_ref[...], TN)
    for block in range(blocks):
        slot = to_slot_ref[block]
        value = grad_out[block * depth : (block + 1) * depth, :]
        rows = pl.ds(pl.multiple_of(lax.rem(slot, blocks // 2) * depth, depth), depth)

        @pl.when(slot < blocks // 2)
        def _():
            kept_refs[0][rows, :width] = value

        @pl.when(slot >= blocks // 2)
        def _():
            sent_refs[0][rows, :width] = value

    grad_mix_ref[...] = mxu(grad_proj_ref[...], w_out_ref[...], NT).astype(jnp.bfloat16)

    def attend_back(window, carry):
        rows = pl.ds(pl.multiple_of(window * win, 16), win)
        for at in range(HEADS // GROUP):
            columns = slice(at * group, (at + 1) * group)
            key_columns = slice(width + at * group, width + (at + 1) * group)
            value_columns = slice(2 * width + at * group, 2 * width + (at + 1) * group)
            mix = grad_mix_ref[rows, columns]
            probs = probs_ref[window, at]
            float_probs = probs.astype(jnp.float32)
            grad_probs = mxu(masked_heads(qkv_ref[rows, value_columns], head_dim), mix, NT)
            product = (float_probs * grad_probs).reshape(GROUP, win, win)
            center = jnp.sum(product, axis=1, keepdims=True)
            grad_scores = scale * (product - float_probs.reshape(GROUP, win, win) * center)
            grad_scores = grad_scores.astype(jnp.bfloat16).reshape(GROUP * win, win)
            grad_values = own_heads(mxu(probs, mix), head_dim)
            grad_keys = own_heads(mxu(grad_scores, qkv_ref[rows, columns]), head_dim)
            turned = turned_heads(grad_scores, GROUP)
            grad_queries = own_heads(mxu(turned, qkv_ref[rows, key_columns]), head_dim)
            cells_ref[rows, columns] = grad_queries.astype(jnp.bfloat16)
            cells_ref[rows, key_columns] = grad_keys.astype(jnp.bfloat16)
            cells_ref[rows, value_columns] = grad_values.astype(jnp.bfloat16)
        return carry

    lax.fori_loop(0, windows, attend_back, 0)

    for part, place in enumerate(GRAD_PLACES):
        columns = slice(part * width, (part + 1) * width)
        target = slice(place % 2 * width, (place % 2 + 1) * width)
        sent_refs[place // 2][:, target] = mxu(turned_ref[half:, :], cells_ref[:, columns])
        kept_refs[place // 2][:, target] = mxu(turned_ref[:half, :], cells_ref[:, columns])


def coded(value):
    top = jnp.max(jnp.abs(value), axis=1, keepdims=True)
    exponent = jnp.ceil(jnp.log2(jnp.maximum(top, 1e-30)))
    codes = jnp.round(value * (jnp.exp2(-exponent) * STEPS)).astype(jnp.int32)
    exponents = jnp.broadcast_to(exponent, (value.shape[0], 128)).astype(jnp.int32)
    return codes.astype(jnp.int16), exponents.astype(jnp.int16)


def decoded(codes, exponents):
    exponent = exponents.astype(jnp.int32).astype(jnp.float32)[:, :1]
    return codes.astype(jnp.int32).astype(jnp.float32) * (jnp.exp2(exponent) * (1 / STEPS))


def fold_kernel(arrived_ref, kept_ref, *out_refs):
    columns = kept_ref.shape[1]
    rows = out_refs[0].shape[0]

    def total(part):
        arrived = arrived_ref[part, :columns]
        if arrived_ref.shape[1] > columns:
            arrived = decoded(arrived, arrived_ref[part, columns:])
        return kept_ref[part, :] + arrived

    out_refs[0][...] = total(slice(0, rows))
    if len(out_refs) > 1:
        codes, exponents = coded(total(slice(rows, 2 * rows)))
        out_refs[1][:, :columns] = codes
        out_refs[1][:, columns:] = exponents


def exchanged(value, distance):
    count = lax.axis_size("lat")
    return lax.ppermute(value, "lat", [(i, i ^ distance) for i in range(count)])


def moved(value, grp_turn, distance):
    count = lax.axis_size("lat")
    groups = lax.axis_size("grp")
    pairs = []
    for grp in range(groups):
        for i in range(count):
            pairs.append((grp * count + i, (grp ^ grp_turn) * count + (i ^ distance[grp])))
    return lax.ppermute(value, ("grp", "lat"), pairs)


def gathered(block, halo, prepare, bias):
    here = lax.axis_index("grp") == 0
    far = moved(block, 0, (8, 12))
    near = moved(block, 0, (4, 6))
    side = exchanged(block, 2)
    side, halo = lax.optimization_barrier((side, halo))
    halo = passed_along(halo, "lat", -1)
    near, bias = lax.optimization_barrier((near, bias))
    far_side, far_other = exchanged(far, 2), moved(far, 1, (0, 0))
    near_other = moved(near, 1, (0, 0))
    far_side_other = moved(far_side, 1, (0, 0))
    far_other, *prepared = lax.optimization_barrier((far_other, *prepare(halo)))
    shards = [block, side, near, near_other, far, far_other, far_side, far_side_other]
    low = jnp.array([0, 2, 4, 6, 8, 12, 10, 14], jnp.int32)
    high = jnp.array([0, 2, 6, 4, 12, 8, 14, 10], jnp.int32)
    order = jnp.where(here, low, high)
    shards += [exchanged(shard, 1) for shard in shards]
    return tuple(shards), jnp.concatenate([order, order + 1]), prepared, bias


def reversed_bits(value, count):
    result = 0
    bit = 1
    while bit < count:
        result = 2 * result + (value & 1)
        value = value >> 1
        bit *= 2
    return result


def fold(arrived, kept, last=False):
    rows, columns = kept.shape
    if last:
        outs = (jax.ShapeDtypeStruct((rows, columns), jnp.float32),)
    else:
        outs = (
            jax.ShapeDtypeStruct((rows // 2, columns), jnp.float32),
            jax.ShapeDtypeStruct((rows // 2, columns + 128), jnp.int16),
        )
    return call(fold_kernel, "fold", outs, (), (arrived, kept), flops=8 * rows * columns, vmem=16)


def call(kernel, name, outs, tables, operands, scratch=(), flops=0, vmem=40):
    size = sum(math.prod(o.shape) * o.dtype.itemsize for o in (*outs, *operands))
    return pl.pallas_call(
        kernel,
        out_shape=outs,
        in_specs=[pl.BlockSpec(memory_space=pltpu.SMEM)] * len(tables)
        + [pl.BlockSpec(memory_space=pltpu.VMEM)] * len(operands),
        out_specs=[pl.BlockSpec(memory_space=pltpu.VMEM)] * len(outs),
        scratch_shapes=list(scratch),
        compiler_params=pltpu.CompilerParams(vmem_limit_bytes=vmem * 1024 * 1024),
        cost_estimate=pl.CostEstimate(flops=flops, bytes_accessed=size, transcendentals=0),
        name=name,
    )(*tables, *operands)


def per_device(inputs, cotangent, idents, w_qkv, w_out, gain):
    lat_cells, lon_cells, width = inputs.shape
    half_rows = WIN_R // 2
    win = padded_rows()
    windows = (lat_cells // WIN_R) * (lon_cells // WIN_C)
    cells = windows * win
    places = jnp.asarray(window_places(lon_cells), jnp.bfloat16)

    def shape(*dims, dtype=jnp.bfloat16):
        return jax.ShapeDtypeStruct(dims, dtype)

    count = lax.axis_size("lat")
    me = lax.axis_index("lat")
    direct = count == 16 and lax.axis_size("grp") == 2 and width % (16 * count) == 0
    if direct:
        blocks = jnp.arange(count, dtype=jnp.int32)
        to_slot = reversed_bits(blocks ^ me, count)
    else:
        to_slot = jnp.arange(16, dtype=jnp.int32)

    def prepare(halo):
        return call(
            prepare_kernel,
            "prepare",
            (shape(cells, width), shape(cells, width), shape(width, cells)),
            (to_slot,),
            (inputs, cotangent, halo, places),
            flops=4 * cells * width * lon_cells * WIN_R,
            vmem=24,
        )

    weights = jnp.concatenate([w_qkv, w_out], axis=1)
    halo = jnp.concatenate([inputs[:half_rows], cotangent[:half_rows]])
    labels = to_windows(idents + 1)
    bias = jnp.where(labels[:, :, None] == labels[:, None, :], 0.0, HIDDEN).astype(jnp.float32)
    if direct:
        shards, order, (tokens, cot, turned), bias = gathered(weights, halo, prepare, bias)
        into = order ^ me
    else:
        weights = lax.all_gather(weights, "lat", axis=0, tiled=True)
        shards = tuple(weights.reshape(16, width // 16, 4 * width))
        into = to_slot
        tokens, cot, turned = prepare(passed_along(halo, "lat", -1))

    normed, grad_cells, qkv_full, *grads = call(
        block_kernel,
        "block",
        (
            shape(cells, width),
            shape(cells, 3 * width),
            shape(width, 3 * width),
            *[shape(width // 2, 2 * width, dtype=jnp.float32)] * 4,
        ),
        (into, to_slot),
        (tokens, turned, cot, bias, gain[None], *shards),
        (
            pltpu.VMEM((width, width), jnp.bfloat16),
            pltpu.VMEM((cells, 3 * width), jnp.bfloat16),
            pltpu.VMEM((windows, HEADS // GROUP, GROUP * win, win), jnp.bfloat16),
            pltpu.VMEM((cells, width), jnp.bfloat16),
            pltpu.VMEM((cells, width), jnp.bfloat16),
            pltpu.VMEM((cells, width), jnp.bfloat16),
        ),
        flops=2 * cells * width * width * 10,
    )
    if direct:
        pairs = [(exchanged(sent, 1), kept) for sent, kept in zip(grads[::2], grads[1::2])]
        pairs = [fold(arrived, kept) for arrived, kept in pairs]
        pairs = [(exchanged(sent, 2), kept) for kept, sent in pairs]
        first, normed, grad_cells = lax.optimization_barrier((pairs[0][0], normed, grad_cells))
        pairs[0] = (first, pairs[0][1])
        pairs = [fold(arrived, kept) for arrived, kept in pairs]
        finish_after = pairs[1][0]
        for distance in (4, 8):
            pairs = [(exchanged(sent, distance), kept) for kept, sent in pairs]
            pairs = [fold(arrived, kept, distance == 8) for arrived, kept in pairs]
            pairs = [pair if distance < 8 else pair[0] for pair in pairs]
        quarters = [pairs[at // 2][:, at % 2 * width : (at % 2 + 1) * width] for at in range(4)]
        grad_out = quarters[0]
        grad_qkv = jnp.concatenate([quarters[place] for place in GRAD_PLACES], axis=1)
    else:
        whole = [jnp.concatenate([kept, sent]) for sent, kept in zip(grads[::2], grads[1::2])]
        both = lax.psum_scatter(jnp.concatenate(whole, axis=1), "lat", scatter_dimension=0, tiled=True)
        quarters = jnp.split(both, 4, axis=1)
        grad_out = quarters[0]
        grad_qkv = jnp.concatenate([quarters[place] for place in GRAD_PLACES], axis=1)
        finish_after = None

    output, grad_in, lower = call(
        finish_kernel,
        "finish",
        (shape(*inputs.shape), shape(*inputs.shape), shape(2 * half_rows, lon_cells, width)),
        (),
        (grad_cells, qkv_full, normed, inputs, cotangent, places),
        (pltpu.VMEM((cells, width), jnp.bfloat16),),
        flops=2 * cells * width * (3 * width + 2 * lon_cells * WIN_R),
        vmem=24,
    )
    if finish_after is not None:
        lower, _ = lax.optimization_barrier((lower, finish_after))
    lower = passed_along(lower, "lat", 1)

    def completed(result, lower):
        top = result[:half_rows].astype(jnp.float32) + lower.astype(jnp.float32)
        return result.at[:half_rows].set(top.astype(jnp.bfloat16))

    output = completed(output, lower[:half_rows])
    return (output, completed(grad_in, lower[half_rows:]), grad_qkv, grad_out)


def solution(mesh):
    in_specs = (
        P(("grp", "lat"), None, None),
        P(("grp", "lat"), None, None),
        P(("grp", "lat"), None),
        P("lat", None),
        P("lat", None),
        P(),
    )
    out_specs = (
        P(("grp", "lat"), None, None),
        P(("grp", "lat"), None, None),
        P(("grp", "lat"), None),
        P(("grp", "lat"), None),
    )
    return jax.shard_map(
        per_device, mesh=mesh, in_specs=in_specs, out_specs=out_specs, check_vma=False
    )
```

```python
import math

import jax
import jax.numpy as jnp
import numpy as np
from jax import lax
from jax.experimental import pallas as pl
from jax.experimental.pallas import tpu as pltpu
from jax.sharding import PartitionSpec as P

HEADS = 8
WIN_R = 6
WIN_C = 12
EPS = 1e-05
HIDDEN = -1e30
STEPS = 32000.0
GRAD_PLACES = (3, 2, 1)
GROUP = 2

NN = (((1,), (0,)), ((), ()))
NT = (((1,), (1,)), ((), ()))
TN = (((0,), (0,)), ((), ()))


def mxu(left, right, dims=NN):
    return lax.dot_general(left, right, dims, preferred_element_type=jnp.float32)


def passed_along(value, axis, steps):
    count = lax.axis_size(axis)
    first, last = (max(0, -steps), min(count, count - steps))
    return lax.ppermute(value, axis, [(source, source + steps) for source in range(first, last)])


def padded_rows():
    return -(-WIN_R * WIN_C // 16) * 16


def to_windows(field):
    lat_cells, lon_cells = field.shape
    field = field.reshape(lat_cells // WIN_R, WIN_R, lon_cells // WIN_C, WIN_C)
    field = field.transpose(0, 2, 1, 3).reshape(-1, WIN_R * WIN_C)
    return jnp.pad(field, ((0, 0), (0, padded_rows() - WIN_R * WIN_C)))


def window_places(lon_cells):
    win = padded_rows()
    places = np.zeros((WIN_R, lon_cells // WIN_C, win, lon_cells), np.float32)
    for row in range(WIN_R):
        for window in range(lon_cells // WIN_C):
            for column in range(WIN_C):
                source = (window * WIN_C + column + WIN_C // 2) % lon_cells
                places[row, window, row * WIN_C + column, source] = 1
    return places.reshape(WIN_R, -1, lon_cells)


def masked_heads(value, head_dim):
    head = lax.broadcasted_iota(jnp.int32, value.shape, 1) // head_dim
    zero = jnp.zeros_like(value)
    count = value.shape[1] // head_dim
    return jnp.concatenate([jnp.where(head == at, value, zero) for at in range(count)], axis=0)


def own_heads(stacked, head_dim):
    count = stacked.shape[1] // head_dim
    rows = stacked.shape[0] // count
    head = lax.broadcasted_iota(jnp.int32, (rows, stacked.shape[1]), 1) // head_dim
    result = stacked[:rows]
    for at in range(1, count):
        result = jnp.where(head == at, stacked[at * rows : (at + 1) * rows], result)
    return result


def turned_heads(stacked, count):
    rows = stacked.shape[0] // count
    return jnp.concatenate(
        [stacked[at * rows : (at + 1) * rows].T for at in range(count)], axis=0
    )


def prepare_kernel(
    to_slot_ref, inputs_ref, cot_ref, halo_ref, places_ref, tokens_ref, cot_tokens_ref, turned_ref
):
    half = halo_ref.shape[0] // 2
    lat_cells = inputs_ref.shape[0]
    cells = places_ref.shape[1]
    blocks = to_slot_ref.shape[0]
    for band in range(lat_cells // WIN_R):
        rows = slice(band * cells, (band + 1) * cells)
        for at, (own_ref, result_ref) in enumerate(
            ((inputs_ref, tokens_ref), (cot_ref, cot_tokens_ref))
        ):
            total = None
            for row in range(WIN_R):
                source = band * WIN_R + row + half
                beyond = at * half + source - lat_cells
                field = own_ref[source] if source < lat_cells else halo_ref[beyond]
                term = mxu(places_ref[row], field)
                total = term if total is None else total + term
            result_ref[rows, :] = total.astype(jnp.bfloat16)
    depth = tokens_ref.shape[1] // blocks
    turned = tokens_ref[...].T
    for block in range(blocks):
        rows = pl.ds(pl.multiple_of(to_slot_ref[block] * depth, depth), depth)
        turned_ref[rows, :] = turned[block * depth : (block + 1) * depth, :]


def finish_kernel(
    cells_ref, w_qkv_ref, normed_ref, inputs_ref, cot_ref, places_ref,
    output_ref, grad_in_ref, lower_ref, shift_ref,
):
    lat_cells = inputs_ref.shape[0]
    half = lower_ref.shape[0] // 2
    count = places_ref.shape[1]
    shift_ref[...] = mxu(cells_ref[...], w_qkv_ref[...], NT).astype(jnp.bfloat16)
    for at, (value_ref, base_ref, result_ref) in enumerate(
        ((normed_ref, inputs_ref, output_ref), (shift_ref, cot_ref, grad_in_ref))
    ):
        result_ref[:half] = base_ref[:half]
        for band in range(lat_cells // WIN_R):
            value = value_ref[band * count : (band + 1) * count, :]
            for row in range(WIN_R):
                back = mxu(places_ref[row], value, TN)
                target = band * WIN_R + row + half
                if target < lat_cells:
                    base = base_ref[target].astype(jnp.float32)
                    result_ref[target] = (base + back).astype(jnp.bfloat16)
                else:
                    lower_ref[at * half + target - lat_cells] = back.astype(jnp.bfloat16)


def block_kernel(into_ref, to_slot_ref, x_ref, turned_ref, cot_ref, bias_ref, gain_ref, *rest):
    shard_refs, rest = rest[: into_ref.shape[0]], rest[into_ref.shape[0] :]
    normed_ref, cells_ref, w_qkv_ref, *grad_refs = rest[:7]
    w_out_ref, qkv_ref, probs_ref, mixed_ref, grad_proj_ref, grad_mix_ref = rest[7:]
    windows, win = bias_ref.shape[:2]
    width = x_ref.shape[1]
    head_dim = width // HEADS
    group = GROUP * head_dim
    scale = head_dim ** (-0.5)
    factor = scale * math.log2(math.e)

    blocks = into_ref.shape[0]
    depth = width // blocks
    for at, shard_ref in enumerate(shard_refs):
        rows = pl.ds(pl.multiple_of(into_ref[at] * depth, depth), depth)
        w_qkv_ref[rows, :] = shard_ref[:, : 3 * width]
        w_out_ref[rows, :] = shard_ref[:, 3 * width :]

    for part in range(3):
        columns = slice(part * width, (part + 1) * width)
        qkv_ref[:, columns] = mxu(x_ref[...], w_qkv_ref[:, columns]).astype(jnp.bfloat16)

    def attend(window, carry):
        rows = pl.ds(pl.multiple_of(window * win, 16), win)
        bias = bias_ref[window]
        for at in range(HEADS // GROUP):
            columns = slice(at * group, (at + 1) * group)
            queries = qkv_ref[rows, columns]
            keys = qkv_ref[rows, width + at * group : width + (at + 1) * group]
            values = qkv_ref[rows, 2 * width + at * group : 2 * width + (at + 1) * group]
            scores = mxu(masked_heads(keys, head_dim), queries, NT)
            scores = scores.reshape(GROUP, win, win) * factor + bias
            lifted = jnp.exp2(scores - jnp.max(scores, axis=1, keepdims=True))
            total = jnp.sum(lifted, axis=1, keepdims=True)
            probs = (lifted * (1.0 / total)).astype(jnp.bfloat16)
            probs = probs.reshape(GROUP * win, win)
            probs_ref[window, at] = probs
            mixed = own_heads(mxu(turned_heads(probs, GROUP), values), head_dim)
            mixed_ref[rows, columns] = mixed.astype(jnp.bfloat16)
        return carry

    lax.fori_loop(0, windows, attend, 0)

    gain = gain_ref[...]

    def normalise(window, carry):
        rows = pl.ds(pl.multiple_of(window * win, 16), win)
        projected = mxu(mixed_ref[rows, :], w_out_ref[...])
        center = projected - jnp.mean(projected, axis=-1, keepdims=True)
        inverse = lax.rsqrt(jnp.mean(center * center, axis=-1, keepdims=True) + EPS)
        normal = center * inverse
        normed_ref[rows, :] = (normal * gain).astype(jnp.bfloat16)
        scaled = cot_ref[rows, :].astype(jnp.float32) * gain
        grad_proj = (
            scaled
            - jnp.mean(scaled, axis=-1, keepdims=True)
            - normal * jnp.mean(scaled * normal, axis=-1, keepdims=True)
        ) * inverse
        grad_proj_ref[rows, :] = grad_proj.astype(jnp.bfloat16)
        return carry

    lax.fori_loop(0, windows, normalise, 0)
    half = width // 2
    sent_refs, kept_refs = grad_refs[::2], grad_refs[1::2]
    grad_out = mxu(mixed_ref[...], grad_proj_ref[...], TN)
    for block in range(blocks):
        slot = to_slot_ref[block]
        value = grad_out[block * depth : (block + 1) * depth, :]
        rows = pl.ds(pl.multiple_of(lax.rem(slot, blocks // 2) * depth, depth), depth)

        @pl.when(slot < blocks // 2)
        def _():
            kept_refs[0][rows, :width] = value

        @pl.when(slot >= blocks // 2)
        def _():
            sent_refs[0][rows, :width] = value

    grad_mix_ref[...] = mxu(grad_proj_ref[...], w_out_ref[...], NT).astype(jnp.bfloat16)

    def attend_back(window, carry):
        rows = pl.ds(pl.multiple_of(window * win, 16), win)
        for at in range(HEADS // GROUP):
            columns = slice(at * group, (at + 1) * group)
            key_columns = slice(width + at * group, width + (at + 1) * group)
            value_columns = slice(2 * width + at * group, 2 * width + (at + 1) * group)
            mix = grad_mix_ref[rows, columns]
            probs = probs_ref[window, at]
            float_probs = probs.astype(jnp.float32)
            grad_probs = mxu(masked_heads(qkv_ref[rows, value_columns], head_dim), mix, NT)
            product = (float_probs * grad_probs).reshape(GROUP, win, win)
            center = jnp.sum(product, axis=1, keepdims=True)
            grad_scores = scale * (product - float_probs.reshape(GROUP, win, win) * center)
            grad_scores = grad_scores.astype(jnp.bfloat16).reshape(GROUP * win, win)
            grad_values = own_heads(mxu(probs, mix), head_dim)
            grad_keys = own_heads(mxu(grad_scores, qkv_ref[rows, columns]), head_dim)
            turned = turned_heads(grad_scores, GROUP)
            grad_queries = own_heads(mxu(turned, qkv_ref[rows, key_columns]), head_dim)
            cells_ref[rows, columns] = grad_queries.astype(jnp.bfloat16)
            cells_ref[rows, key_columns] = grad_keys.astype(jnp.bfloat16)
            cells_ref[rows, value_columns] = grad_values.astype(jnp.bfloat16)
        return carry

    lax.fori_loop(0, windows, attend_back, 0)

    for part, place in enumerate(GRAD_PLACES):
        columns = slice(part * width, (part + 1) * width)
        target = slice(place % 2 * width, (place % 2 + 1) * width)
        sent_refs[place // 2][:, target] = mxu(turned_ref[half:, :], cells_ref[:, columns])
        kept_refs[place // 2][:, target] = mxu(turned_ref[:half, :], cells_ref[:, columns])


def coded(value):
    top = jnp.max(jnp.abs(value), axis=1, keepdims=True)
    exponent = jnp.ceil(jnp.log2(jnp.maximum(top, 1e-30)))
    codes = jnp.round(value * (jnp.exp2(-exponent) * STEPS)).astype(jnp.int32)
    exponents = jnp.broadcast_to(exponent, (value.shape[0], 128)).astype(jnp.int32)
    return codes.astype(jnp.int16), exponents.astype(jnp.int16)


def decoded(codes, exponents):
    exponent = exponents.astype(jnp.int32).astype(jnp.float32)[:, :1]
    return codes.astype(jnp.int32).astype(jnp.float32) * (jnp.exp2(exponent) * (1 / STEPS))


def fold_kernel(arrived_ref, kept_ref, *out_refs):
    columns = kept_ref.shape[1]
    rows = out_refs[0].shape[0]

    def total(part):
        arrived = arrived_ref[part, :columns]
        if arrived_ref.shape[1] > columns:
            arrived = decoded(arrived, arrived_ref[part, columns:])
        return kept_ref[part, :] + arrived

    out_refs[0][...] = total(slice(0, rows))
    if len(out_refs) > 1:
        codes, exponents = coded(total(slice(rows, 2 * rows)))
        out_refs[1][:, :columns] = codes
        out_refs[1][:, columns:] = exponents


def exchanged(value, distance):
    count = lax.axis_size("lat")
    return lax.ppermute(value, "lat", [(i, i ^ distance) for i in range(count)])


def moved(value, grp_turn, distance):
    count = lax.axis_size("lat")
    groups = lax.axis_size("grp")
    pairs = []
    for grp in range(groups):
        for i in range(count):
            pairs.append((grp * count + i, (grp ^ grp_turn) * count + (i ^ distance[grp])))
    return lax.ppermute(value, ("grp", "lat"), pairs)


def gathered(block, halo, prepare, bias):
    here = lax.axis_index("grp") == 0
    far = moved(block, 0, (8, 12))
    near = moved(block, 0, (4, 6))
    side = exchanged(block, 2)
    far, near, side, bias, halo = lax.optimization_barrier((far, near, side, bias, halo))
    halo = passed_along(halo, "lat", -1)
    far_side, far_other = exchanged(far, 2), moved(far, 1, (0, 0))
    near_other = moved(near, 1, (0, 0))
    far_side_other = moved(far_side, 1, (0, 0))
    far_other, *prepared = lax.optimization_barrier((far_other, *prepare(halo)))
    shards = [block, side, near, near_other, far, far_other, far_side, far_side_other]
    low = jnp.array([0, 2, 4, 6, 8, 12, 10, 14], jnp.int32)
    high = jnp.array([0, 2, 6, 4, 12, 8, 14, 10], jnp.int32)
    order = jnp.where(here, low, high)
    shards += [exchanged(shard, 1) for shard in shards]
    return tuple(shards), jnp.concatenate([order, order + 1]), prepared, bias


def reversed_bits(value, count):
    result = 0
    bit = 1
    while bit < count:
        result = 2 * result + (value & 1)
        value = value >> 1
        bit *= 2
    return result


def fold(arrived, kept, last=False):
    rows, columns = kept.shape
    if last:
        outs = (jax.ShapeDtypeStruct((rows, columns), jnp.float32),)
    else:
        outs = (
            jax.ShapeDtypeStruct((rows // 2, columns), jnp.float32),
            jax.ShapeDtypeStruct((rows // 2, columns + 128), jnp.int16),
        )
    return call(fold_kernel, "fold", outs, (), (arrived, kept), flops=8 * rows * columns, vmem=16)


def call(kernel, name, outs, tables, operands, scratch=(), flops=0, vmem=40):
    size = sum(math.prod(o.shape) * o.dtype.itemsize for o in (*outs, *operands))
    return pl.pallas_call(
        kernel,
        out_shape=outs,
        in_specs=[pl.BlockSpec(memory_space=pltpu.SMEM)] * len(tables)
        + [pl.BlockSpec(memory_space=pltpu.VMEM)] * len(operands),
        out_specs=[pl.BlockSpec(memory_space=pltpu.VMEM)] * len(outs),
        scratch_shapes=list(scratch),
        compiler_params=pltpu.CompilerParams(vmem_limit_bytes=vmem * 1024 * 1024),
        cost_estimate=pl.CostEstimate(flops=flops, bytes_accessed=size, transcendentals=0),
        name=name,
    )(*tables, *operands)


def per_device(inputs, cotangent, idents, w_qkv, w_out, gain):
    lat_cells, lon_cells, width = inputs.shape
    half_rows = WIN_R // 2
    win = padded_rows()
    windows = (lat_cells // WIN_R) * (lon_cells // WIN_C)
    cells = windows * win
    places = jnp.asarray(window_places(lon_cells), jnp.bfloat16)

    def shape(*dims, dtype=jnp.bfloat16):
        return jax.ShapeDtypeStruct(dims, dtype)

    count = lax.axis_size("lat")
    me = lax.axis_index("lat")
    direct = count == 16 and lax.axis_size("grp") == 2 and width % (16 * count) == 0
    if direct:
        blocks = jnp.arange(count, dtype=jnp.int32)
        to_slot = reversed_bits(blocks ^ me, count)
    else:
        to_slot = jnp.arange(16, dtype=jnp.int32)

    def prepare(halo):
        return call(
            prepare_kernel,
            "prepare",
            (shape(cells, width), shape(cells, width), shape(width, cells)),
            (to_slot,),
            (inputs, cotangent, halo, places),
            flops=4 * cells * width * lon_cells * WIN_R,
            vmem=24,
        )

    weights = jnp.concatenate([w_qkv, w_out], axis=1)
    halo = jnp.concatenate([inputs[:half_rows], cotangent[:half_rows]])
    labels = to_windows(idents + 1)
    bias = jnp.where(labels[:, :, None] == labels[:, None, :], 0.0, HIDDEN).astype(jnp.float32)
    if direct:
        shards, order, (tokens, cot, turned), bias = gathered(weights, halo, prepare, bias)
        into = order ^ me
    else:
        weights = lax.all_gather(weights, "lat", axis=0, tiled=True)
        shards = tuple(weights.reshape(16, width // 16, 4 * width))
        into = to_slot
        tokens, cot, turned = prepare(passed_along(halo, "lat", -1))

    normed, grad_cells, qkv_full, *grads = call(
        block_kernel,
        "block",
        (
            shape(cells, width),
            shape(cells, 3 * width),
            shape(width, 3 * width),
            *[shape(width // 2, 2 * width, dtype=jnp.float32)] * 4,
        ),
        (into, to_slot),
        (tokens, turned, cot, bias, gain[None], *shards),
        (
            pltpu.VMEM((width, width), jnp.bfloat16),
            pltpu.VMEM((cells, 3 * width), jnp.bfloat16),
            pltpu.VMEM((windows, HEADS // GROUP, GROUP * win, win), jnp.bfloat16),
            pltpu.VMEM((cells, width), jnp.bfloat16),
            pltpu.VMEM((cells, width), jnp.bfloat16),
            pltpu.VMEM((cells, width), jnp.bfloat16),
        ),
        flops=2 * cells * width * width * 10,
    )
    def finish(normed, grad_cells):
        return call(
            finish_kernel,
            "finish",
            (shape(*inputs.shape), shape(*inputs.shape), shape(2 * half_rows, lon_cells, width)),
            (),
            (grad_cells, qkv_full, normed, inputs, cotangent, places),
            (pltpu.VMEM((cells, width), jnp.bfloat16),),
            flops=2 * cells * width * (3 * width + 2 * lon_cells * WIN_R),
            vmem=24,
        )

    if direct:
        pairs = [(exchanged(sent, 1), kept) for sent, kept in zip(grads[::2], grads[1::2])]
        pairs = [fold(arrived, kept) for arrived, kept in pairs]
        kept, sent = pairs[1]
        sent, normed, grad_cells = lax.optimization_barrier((sent, normed, grad_cells))
        pairs[1] = (kept, sent)
        pairs = [(exchanged(sent, 2), kept) for kept, sent in pairs]
        output, grad_in, lower = finish(normed, grad_cells)
        arrived, kept = pairs[0]
        arrived, lower = lax.optimization_barrier((arrived, lower))
        pairs[0] = (arrived, kept)
        pairs = [fold(arrived, kept) for arrived, kept in pairs]
        lower, _ = lax.optimization_barrier((lower, pairs[1][0]))
        for distance in (4, 8):
            pairs = [(exchanged(sent, distance), kept) for kept, sent in pairs]
            pairs = [fold(arrived, kept, distance == 8) for arrived, kept in pairs]
            pairs = [pair if distance < 8 else pair[0] for pair in pairs]
        quarters = [pairs[at // 2][:, at % 2 * width : (at % 2 + 1) * width] for at in range(4)]
        grad_out = quarters[0]
        grad_qkv = jnp.concatenate([quarters[place] for place in GRAD_PLACES], axis=1)
    else:
        whole = [jnp.concatenate([kept, sent]) for sent, kept in zip(grads[::2], grads[1::2])]
        both = lax.psum_scatter(jnp.concatenate(whole, axis=1), "lat", scatter_dimension=0, tiled=True)
        quarters = jnp.split(both, 4, axis=1)
        grad_out = quarters[0]
        grad_qkv = jnp.concatenate([quarters[place] for place in GRAD_PLACES], axis=1)
        output, grad_in, lower = finish(normed, grad_cells)

    lower = passed_along(lower, "lat", 1)

    def completed(result, lower):
        top = result[:half_rows].astype(jnp.float32) + lower.astype(jnp.float32)
        return result.at[:half_rows].set(top.astype(jnp.bfloat16))

    output = completed(output, lower[:half_rows])
    return (output, completed(grad_in, lower[half_rows:]), grad_qkv, grad_out)


def solution(mesh):
    in_specs = (
        P(("grp", "lat"), None, None),
        P(("grp", "lat"), None, None),
        P(("grp", "lat"), None),
        P("lat", None),
        P("lat", None),
        P(),
    )
    out_specs = (
        P(("grp", "lat"), None, None),
        P(("grp", "lat"), None, None),
        P(("grp", "lat"), None),
        P(("grp", "lat"), None),
    )
    return jax.shard_map(
        per_device, mesh=mesh, in_specs=in_specs, out_specs=out_specs, check_vma=False
    )
```

```python
import math

import jax
import jax.numpy as jnp
import numpy as np
from jax import lax
from jax.experimental import pallas as pl
from jax.experimental.pallas import tpu as pltpu
from jax.sharding import PartitionSpec as P

HEADS = 8
WIN_R = 6
WIN_C = 12
EPS = 1e-05
HIDDEN = -1e30
STEPS = 32000.0
GRAD_PLACES = (3, 2, 1)
GROUP = 2

NN = (((1,), (0,)), ((), ()))
NT = (((1,), (1,)), ((), ()))
TN = (((0,), (0,)), ((), ()))


def mxu(left, right, dims=NN):
    return lax.dot_general(left, right, dims, preferred_element_type=jnp.float32)


def passed_along(value, axis, steps):
    count = lax.axis_size(axis)
    first, last = (max(0, -steps), min(count, count - steps))
    return lax.ppermute(value, axis, [(source, source + steps) for source in range(first, last)])


def padded_rows():
    return -(-WIN_R * WIN_C // 16) * 16


def to_windows(field):
    lat_cells, lon_cells = field.shape
    field = field.reshape(lat_cells // WIN_R, WIN_R, lon_cells // WIN_C, WIN_C)
    field = field.transpose(0, 2, 1, 3).reshape(-1, WIN_R * WIN_C)
    return jnp.pad(field, ((0, 0), (0, padded_rows() - WIN_R * WIN_C)))


def window_places(lon_cells):
    win = padded_rows()
    places = np.zeros((WIN_R, lon_cells // WIN_C, win, lon_cells), np.float32)
    for row in range(WIN_R):
        for window in range(lon_cells // WIN_C):
            for column in range(WIN_C):
                source = (window * WIN_C + column + WIN_C // 2) % lon_cells
                places[row, window, row * WIN_C + column, source] = 1
    return places.reshape(WIN_R, -1, lon_cells)


def masked_heads(value, head_dim):
    head = lax.broadcasted_iota(jnp.int32, value.shape, 1) // head_dim
    zero = jnp.zeros_like(value)
    count = value.shape[1] // head_dim
    return jnp.concatenate([jnp.where(head == at, value, zero) for at in range(count)], axis=0)


def own_heads(stacked, head_dim):
    count = stacked.shape[1] // head_dim
    rows = stacked.shape[0] // count
    head = lax.broadcasted_iota(jnp.int32, (rows, stacked.shape[1]), 1) // head_dim
    result = stacked[:rows]
    for at in range(1, count):
        result = jnp.where(head == at, stacked[at * rows : (at + 1) * rows], result)
    return result


def turned_heads(stacked, count):
    rows = stacked.shape[0] // count
    return jnp.concatenate(
        [stacked[at * rows : (at + 1) * rows].T for at in range(count)], axis=0
    )


def shift_kernel(own_ref, halo_ref, places_ref, result_ref):
    half = halo_ref.shape[0]
    lat_cells = own_ref.shape[0]
    cells = places_ref.shape[1]
    for band in range(lat_cells // WIN_R):
        total = None
        for row in range(WIN_R):
            source = band * WIN_R + row + half
            field = own_ref[source] if source < lat_cells else halo_ref[source - lat_cells]
            term = mxu(places_ref[row], field)
            total = term if total is None else total + term
        result_ref[band * cells : (band + 1) * cells, :] = total.astype(jnp.bfloat16)


def prepare_kernel(to_slot_ref, inputs_ref, halo_ref, places_ref, tokens_ref, turned_ref):
    shift_kernel(inputs_ref, halo_ref, places_ref, tokens_ref)
    blocks = to_slot_ref.shape[0]
    depth = tokens_ref.shape[1] // blocks
    turned = tokens_ref[...].T
    for block in range(blocks):
        rows = pl.ds(pl.multiple_of(to_slot_ref[block] * depth, depth), depth)
        turned_ref[rows, :] = turned[block * depth : (block + 1) * depth, :]


def finish_kernel(
    cells_ref, w_qkv_ref, normed_ref, inputs_ref, cot_ref, places_ref,
    output_ref, grad_in_ref, lower_ref, shift_ref,
):
    lat_cells = inputs_ref.shape[0]
    half = lower_ref.shape[0] // 2
    count = places_ref.shape[1]
    shift_ref[...] = mxu(cells_ref[...], w_qkv_ref[...], NT).astype(jnp.bfloat16)
    for at, (value_ref, base_ref, result_ref) in enumerate(
        ((normed_ref, inputs_ref, output_ref), (shift_ref, cot_ref, grad_in_ref))
    ):
        result_ref[:half] = base_ref[:half]
        for band in range(lat_cells // WIN_R):
            value = value_ref[band * count : (band + 1) * count, :]
            for row in range(WIN_R):
                back = mxu(places_ref[row], value, TN)
                target = band * WIN_R + row + half
                if target < lat_cells:
                    base = base_ref[target].astype(jnp.float32)
                    result_ref[target] = (base + back).astype(jnp.bfloat16)
                else:
                    lower_ref[at * half + target - lat_cells] = back.astype(jnp.bfloat16)


def forward_kernel(into_ref, x_ref, bias_ref, *rest):
    shard_refs, rest = rest[: into_ref.shape[0]], rest[into_ref.shape[0] :]
    w_qkv_ref, w_out_ref, qkv_ref, probs_ref, mixed_ref = rest
    windows, win = bias_ref.shape[:2]
    width = x_ref.shape[1]
    head_dim = width // HEADS
    group = GROUP * head_dim
    factor = head_dim ** (-0.5) * math.log2(math.e)

    blocks = into_ref.shape[0]
    depth = width // blocks
    for at, shard_ref in enumerate(shard_refs):
        rows = pl.ds(pl.multiple_of(into_ref[at] * depth, depth), depth)
        w_qkv_ref[rows, :] = shard_ref[:, : 3 * width]
        w_out_ref[rows, :] = shard_ref[:, 3 * width :]

    for part in range(3):
        columns = slice(part * width, (part + 1) * width)
        qkv_ref[:, columns] = mxu(x_ref[...], w_qkv_ref[:, columns]).astype(jnp.bfloat16)

    def attend(window, carry):
        rows = pl.ds(pl.multiple_of(window * win, 16), win)
        bias = bias_ref[window]
        for at in range(HEADS // GROUP):
            columns = slice(at * group, (at + 1) * group)
            queries = qkv_ref[rows, columns]
            keys = qkv_ref[rows, width + at * group : width + (at + 1) * group]
            values = qkv_ref[rows, 2 * width + at * group : 2 * width + (at + 1) * group]
            scores = mxu(masked_heads(keys, head_dim), queries, NT)
            scores = scores.reshape(GROUP, win, win) * factor + bias
            lifted = jnp.exp2(scores - jnp.max(scores, axis=1, keepdims=True))
            total = jnp.sum(lifted, axis=1, keepdims=True)
            probs = (lifted * (1.0 / total)).astype(jnp.bfloat16)
            probs = probs.reshape(GROUP * win, win)
            probs_ref[window, at] = probs
            mixed = own_heads(mxu(turned_heads(probs, GROUP), values), head_dim)
            mixed_ref[rows, columns] = mixed.astype(jnp.bfloat16)
        return carry

    lax.fori_loop(0, windows, attend, 0)


def backward_kernel(
    to_slot_ref, qkv_ref, probs_ref, mixed_ref, w_out_ref, turned_ref, cot_ref, gain_ref,
    normed_ref, cells_ref, *rest,
):
    grad_refs, (grad_proj_ref, grad_mix_ref) = rest[:4], rest[4:]
    windows, win = probs_ref.shape[0], probs_ref.shape[-1]
    width = cot_ref.shape[1]
    head_dim = width // HEADS
    group = GROUP * head_dim
    scale = head_dim ** (-0.5)
    blocks = to_slot_ref.shape[0]
    depth = width // blocks
    gain = gain_ref[...]

    def normalise(window, carry):
        rows = pl.ds(pl.multiple_of(window * win, 16), win)
        projected = mxu(mixed_ref[rows, :], w_out_ref[...])
        center = projected - jnp.mean(projected, axis=-1, keepdims=True)
        inverse = lax.rsqrt(jnp.mean(center * center, axis=-1, keepdims=True) + EPS)
        normal = center * inverse
        normed_ref[rows, :] = (normal * gain).astype(jnp.bfloat16)
        scaled = cot_ref[rows, :].astype(jnp.float32) * gain
        grad_proj = (
            scaled
            - jnp.mean(scaled, axis=-1, keepdims=True)
            - normal * jnp.mean(scaled * normal, axis=-1, keepdims=True)
        ) * inverse
        grad_proj_ref[rows, :] = grad_proj.astype(jnp.bfloat16)
        return carry

    lax.fori_loop(0, windows, normalise, 0)
    half = width // 2
    sent_refs, kept_refs = grad_refs[::2], grad_refs[1::2]
    grad_out = mxu(mixed_ref[...], grad_proj_ref[...], TN)
    for block in range(blocks):
        slot = to_slot_ref[block]
        value = grad_out[block * depth : (block + 1) * depth, :]
        rows = pl.ds(pl.multiple_of(lax.rem(slot, blocks // 2) * depth, depth), depth)

        @pl.when(slot < blocks // 2)
        def _():
            kept_refs[0][rows, :width] = value

        @pl.when(slot >= blocks // 2)
        def _():
            sent_refs[0][rows, :width] = value

    grad_mix_ref[...] = mxu(grad_proj_ref[...], w_out_ref[...], NT).astype(jnp.bfloat16)

    def attend_back(window, carry):
        rows = pl.ds(pl.multiple_of(window * win, 16), win)
        for at in range(HEADS // GROUP):
            columns = slice(at * group, (at + 1) * group)
            key_columns = slice(width + at * group, width + (at + 1) * group)
            value_columns = slice(2 * width + at * group, 2 * width + (at + 1) * group)
            mix = grad_mix_ref[rows, columns]
            probs = probs_ref[window, at]
            float_probs = probs.astype(jnp.float32)
            grad_probs = mxu(masked_heads(qkv_ref[rows, value_columns], head_dim), mix, NT)
            product = (float_probs * grad_probs).reshape(GROUP, win, win)
            center = jnp.sum(product, axis=1, keepdims=True)
            grad_scores = scale * (product - float_probs.reshape(GROUP, win, win) * center)
            grad_scores = grad_scores.astype(jnp.bfloat16).reshape(GROUP * win, win)
            grad_values = own_heads(mxu(probs, mix), head_dim)
            grad_keys = own_heads(mxu(grad_scores, qkv_ref[rows, columns]), head_dim)
            turned = turned_heads(grad_scores, GROUP)
            grad_queries = own_heads(mxu(turned, qkv_ref[rows, key_columns]), head_dim)
            cells_ref[rows, columns] = grad_queries.astype(jnp.bfloat16)
            cells_ref[rows, key_columns] = grad_keys.astype(jnp.bfloat16)
            cells_ref[rows, value_columns] = grad_values.astype(jnp.bfloat16)
        return carry

    lax.fori_loop(0, windows, attend_back, 0)

    for part, place in enumerate(GRAD_PLACES):
        columns = slice(part * width, (part + 1) * width)
        target = slice(place % 2 * width, (place % 2 + 1) * width)
        sent_refs[place // 2][:, target] = mxu(turned_ref[half:, :], cells_ref[:, columns])
        kept_refs[place // 2][:, target] = mxu(turned_ref[:half, :], cells_ref[:, columns])


def coded(value):
    top = jnp.max(jnp.abs(value), axis=1, keepdims=True)
    exponent = jnp.ceil(jnp.log2(jnp.maximum(top, 1e-30)))
    codes = jnp.round(value * (jnp.exp2(-exponent) * STEPS)).astype(jnp.int32)
    exponents = jnp.broadcast_to(exponent, (value.shape[0], 128)).astype(jnp.int32)
    return codes.astype(jnp.int16), exponents.astype(jnp.int16)


def decoded(codes, exponents):
    exponent = exponents.astype(jnp.int32).astype(jnp.float32)[:, :1]
    return codes.astype(jnp.int32).astype(jnp.float32) * (jnp.exp2(exponent) * (1 / STEPS))


def fold_kernel(arrived_ref, kept_ref, *out_refs):
    columns = kept_ref.shape[1]
    rows = out_refs[0].shape[0]

    def total(part):
        arrived = arrived_ref[part, :columns]
        if arrived_ref.shape[1] > columns:
            arrived = decoded(arrived, arrived_ref[part, columns:])
        return kept_ref[part, :] + arrived

    out_refs[0][...] = total(slice(0, rows))
    if len(out_refs) > 1:
        codes, exponents = coded(total(slice(rows, 2 * rows)))
        out_refs[1][:, :columns] = codes
        out_refs[1][:, columns:] = exponents


def exchanged(value, distance):
    count = lax.axis_size("lat")
    return lax.ppermute(value, "lat", [(i, i ^ distance) for i in range(count)])


def moved(value, grp_turn, distance):
    count = lax.axis_size("lat")
    groups = lax.axis_size("grp")
    pairs = []
    for grp in range(groups):
        for i in range(count):
            pairs.append((grp * count + i, (grp ^ grp_turn) * count + (i ^ distance[grp])))
    return lax.ppermute(value, ("grp", "lat"), pairs)


def gathered(block, upper_in, cot_edge, prepare, bias):
    here = lax.axis_index("grp") == 0
    far = moved(block, 0, (8, 12))
    upper_in = passed_along(upper_in, "lat", -1)
    near = moved(block, 0, (4, 6))
    side = exchanged(block, 2)
    far, near, side, bias, upper_in = lax.optimization_barrier((far, near, side, bias, upper_in))
    far_side, far_other = exchanged(far, 2), moved(far, 1, (0, 0))
    near_other = moved(near, 1, (0, 0))
    far_side_other = moved(far_side, 1, (0, 0))
    far_other, cot_edge, *prepared = lax.optimization_barrier(
        (far_other, cot_edge, *prepare(upper_in))
    )
    upper_cot = passed_along(cot_edge, "lat", -1)
    shards = [block, side, near, near_other, far, far_other, far_side, far_side_other]
    low = jnp.array([0, 2, 4, 6, 8, 12, 10, 14], jnp.int32)
    high = jnp.array([0, 2, 6, 4, 12, 8, 14, 10], jnp.int32)
    order = jnp.where(here, low, high)
    shards += [exchanged(shard, 1) for shard in shards]
    return tuple(shards), jnp.concatenate([order, order + 1]), prepared, upper_cot, bias


def reversed_bits(value, count):
    result = 0
    bit = 1
    while bit < count:
        result = 2 * result + (value & 1)
        value = value >> 1
        bit *= 2
    return result


def fold(arrived, kept, last=False):
    rows, columns = kept.shape
    if last:
        outs = (jax.ShapeDtypeStruct((rows, columns), jnp.float32),)
    else:
        outs = (
            jax.ShapeDtypeStruct((rows // 2, columns), jnp.float32),
            jax.ShapeDtypeStruct((rows // 2, columns + 128), jnp.int16),
        )
    return call(fold_kernel, "fold", outs, (), (arrived, kept), flops=8 * rows * columns, vmem=16)


def call(kernel, name, outs, tables, operands, scratch=(), flops=0, vmem=40):
    size = sum(math.prod(o.shape) * o.dtype.itemsize for o in (*outs, *operands))
    return pl.pallas_call(
        kernel,
        out_shape=outs,
        in_specs=[pl.BlockSpec(memory_space=pltpu.SMEM)] * len(tables)
        + [pl.BlockSpec(memory_space=pltpu.VMEM)] * len(operands),
        out_specs=[pl.BlockSpec(memory_space=pltpu.VMEM)] * len(outs),
        scratch_shapes=list(scratch),
        compiler_params=pltpu.CompilerParams(vmem_limit_bytes=vmem * 1024 * 1024),
        cost_estimate=pl.CostEstimate(flops=flops, bytes_accessed=size, transcendentals=0),
        name=name,
    )(*tables, *operands)


def per_device(inputs, cotangent, idents, w_qkv, w_out, gain):
    lat_cells, lon_cells, width = inputs.shape
    half_rows = WIN_R // 2
    win = padded_rows()
    windows = (lat_cells // WIN_R) * (lon_cells // WIN_C)
    cells = windows * win
    places = jnp.asarray(window_places(lon_cells), jnp.bfloat16)

    def shape(*dims, dtype=jnp.bfloat16):
        return jax.ShapeDtypeStruct(dims, dtype)

    count = lax.axis_size("lat")
    me = lax.axis_index("lat")
    direct = count == 16 and lax.axis_size("grp") == 2 and width % (16 * count) == 0
    if direct:
        blocks = jnp.arange(count, dtype=jnp.int32)
        to_slot = reversed_bits(blocks ^ me, count)
    else:
        to_slot = jnp.arange(16, dtype=jnp.int32)

    def prepare(upper_in):
        return call(
            prepare_kernel,
            "prepare",
            (shape(cells, width), shape(width, cells)),
            (to_slot,),
            (inputs, upper_in, places),
            flops=2 * cells * width * lon_cells * WIN_R,
            vmem=16,
        )

    weights = jnp.concatenate([w_qkv, w_out], axis=1)
    in_edge, cot_edge = inputs[:half_rows], cotangent[:half_rows]
    labels = to_windows(idents + 1)
    bias = jnp.where(labels[:, :, None] == labels[:, None, :], 0.0, HIDDEN).astype(jnp.float32)
    if direct:
        shards, order, (tokens, turned), upper_cot, bias = gathered(
            weights, in_edge, cot_edge, prepare, bias
        )
        into = order ^ me
    else:
        weights = lax.all_gather(weights, "lat", axis=0, tiled=True)
        shards = tuple(weights.reshape(16, width // 16, 4 * width))
        into = to_slot
        tokens, turned = prepare(passed_along(in_edge, "lat", -1))
        upper_cot = passed_along(cot_edge, "lat", -1)

    qkv_full, out_full, qkv, probs, mixed = call(
        forward_kernel,
        "forward",
        (
            shape(width, 3 * width),
            shape(width, width),
            shape(cells, 3 * width),
            shape(windows, HEADS // GROUP, GROUP * win, win),
            shape(cells, width),
        ),
        (into,),
        (tokens, bias, *shards),
        flops=2 * cells * width * width * 4,
        vmem=20,
    )
    (cot,) = call(
        shift_kernel,
        "shift",
        (shape(cells, width),),
        (),
        (cotangent, upper_cot, places),
        flops=2 * cells * width * lon_cells * WIN_R,
        vmem=16,
    )
    normed, grad_cells, *grads = call(
        backward_kernel,
        "backward",
        (
            shape(cells, width),
            shape(cells, 3 * width),
            *[shape(width // 2, 2 * width, dtype=jnp.float32)] * 4,
        ),
        (to_slot,),
        (qkv, probs, mixed, out_full, turned, cot, gain[None]),
        (pltpu.VMEM((cells, width), jnp.bfloat16), pltpu.VMEM((cells, width), jnp.bfloat16)),
        flops=2 * cells * width * width * 6,
        vmem=30,
    )

    def finish(normed, grad_cells):
        return call(
            finish_kernel,
            "finish",
            (shape(*inputs.shape), shape(*inputs.shape), shape(2 * half_rows, lon_cells, width)),
            (),
            (grad_cells, qkv_full, normed, inputs, cotangent, places),
            (pltpu.VMEM((cells, width), jnp.bfloat16),),
            flops=2 * cells * width * (3 * width + 2 * lon_cells * WIN_R),
            vmem=24,
        )

    if direct:
        pairs = [(exchanged(sent, 1), kept) for sent, kept in zip(grads[::2], grads[1::2])]
        pairs = [fold(arrived, kept) for arrived, kept in pairs]
        kept, sent = pairs[1]
        sent, normed, grad_cells = lax.optimization_barrier((sent, normed, grad_cells))
        pairs[1] = (kept, sent)
        pairs = [(exchanged(sent, 2), kept) for kept, sent in pairs]
        output, grad_in, lower = finish(normed, grad_cells)
        arrived, kept = pairs[0]
        arrived, lower = lax.optimization_barrier((arrived, lower))
        pairs[0] = (arrived, kept)
        pairs = [fold(arrived, kept) for arrived, kept in pairs]
        lower, _ = lax.optimization_barrier((lower, pairs[1][0]))
        lower = passed_along(lower, "lat", 1)
        for distance in (4, 8):
            pairs = [(exchanged(sent, distance), kept) for kept, sent in pairs]
            if distance == 8:
                arrived, kept = pairs[0]
                arrived, lower = lax.optimization_barrier((arrived, lower))
                pairs[0] = (arrived, kept)
            pairs = [fold(arrived, kept, distance == 8) for arrived, kept in pairs]
            pairs = [pair if distance < 8 else pair[0] for pair in pairs]
        quarters = [pairs[at // 2][:, at % 2 * width : (at % 2 + 1) * width] for at in range(4)]
        grad_out = quarters[0]
        grad_qkv = jnp.concatenate([quarters[place] for place in GRAD_PLACES], axis=1)
    else:
        whole = [jnp.concatenate([kept, sent]) for sent, kept in zip(grads[::2], grads[1::2])]
        both = lax.psum_scatter(jnp.concatenate(whole, axis=1), "lat", scatter_dimension=0, tiled=True)
        quarters = jnp.split(both, 4, axis=1)
        grad_out = quarters[0]
        grad_qkv = jnp.concatenate([quarters[place] for place in GRAD_PLACES], axis=1)
        output, grad_in, lower = finish(normed, grad_cells)
        lower = passed_along(lower, "lat", 1)

    def completed(result, lower):
        top = result[:half_rows].astype(jnp.float32) + lower.astype(jnp.float32)
        return result.at[:half_rows].set(top.astype(jnp.bfloat16))

    output = completed(output, lower[:half_rows])
    return (output, completed(grad_in, lower[half_rows:]), grad_qkv, grad_out)


def solution(mesh):
    in_specs = (
        P(("grp", "lat"), None, None),
        P(("grp", "lat"), None, None),
        P(("grp", "lat"), None),
        P("lat", None),
        P("lat", None),
        P(),
    )
    out_specs = (
        P(("grp", "lat"), None, None),
        P(("grp", "lat"), None, None),
        P(("grp", "lat"), None),
        P(("grp", "lat"), None),
    )
    return jax.shard_map(
        per_device, mesh=mesh, in_specs=in_specs, out_specs=out_specs, check_vma=False
    )
```

```python
import math

import jax
import jax.numpy as jnp
import numpy as np
from jax import lax
from jax.experimental import pallas as pl
from jax.experimental.pallas import tpu as pltpu
from jax.sharding import PartitionSpec as P

HEADS = 8
WIN_R = 6
WIN_C = 12
EPS = 1e-05
HIDDEN = -1e30
STEPS = 32000.0
GRAD_PLACES = (3, 2, 1)
GROUP = 2

NN = (((1,), (0,)), ((), ()))
NT = (((1,), (1,)), ((), ()))
TN = (((0,), (0,)), ((), ()))


def mxu(left, right, dims=NN):
    return lax.dot_general(left, right, dims, preferred_element_type=jnp.float32)


def passed_along(value, axis, steps):
    count = lax.axis_size(axis)
    first, last = (max(0, -steps), min(count, count - steps))
    return lax.ppermute(value, axis, [(source, source + steps) for source in range(first, last)])


def padded_rows():
    return -(-WIN_R * WIN_C // 16) * 16


def to_windows(field):
    lat_cells, lon_cells = field.shape
    field = field.reshape(lat_cells // WIN_R, WIN_R, lon_cells // WIN_C, WIN_C)
    field = field.transpose(0, 2, 1, 3).reshape(-1, WIN_R * WIN_C)
    return jnp.pad(field, ((0, 0), (0, padded_rows() - WIN_R * WIN_C)))


def window_places(lon_cells):
    win = padded_rows()
    places = np.zeros((WIN_R, lon_cells // WIN_C, win, lon_cells), np.float32)
    for row in range(WIN_R):
        for window in range(lon_cells // WIN_C):
            for column in range(WIN_C):
                source = (window * WIN_C + column + WIN_C // 2) % lon_cells
                places[row, window, row * WIN_C + column, source] = 1
    return places.reshape(WIN_R, -1, lon_cells)


def masked_heads(value, head_dim):
    head = lax.broadcasted_iota(jnp.int32, value.shape, 1) // head_dim
    zero = jnp.zeros_like(value)
    count = value.shape[1] // head_dim
    return jnp.concatenate([jnp.where(head == at, value, zero) for at in range(count)], axis=0)


def own_heads(stacked, head_dim):
    count = stacked.shape[1] // head_dim
    rows = stacked.shape[0] // count
    head = lax.broadcasted_iota(jnp.int32, (rows, stacked.shape[1]), 1) // head_dim
    result = stacked[:rows]
    for at in range(1, count):
        result = jnp.where(head == at, stacked[at * rows : (at + 1) * rows], result)
    return result


def turned_heads(stacked, count):
    rows = stacked.shape[0] // count
    return jnp.concatenate(
        [stacked[at * rows : (at + 1) * rows].T for at in range(count)], axis=0
    )


def shift_kernel(own_ref, halo_ref, places_ref, result_ref):
    half = halo_ref.shape[0]
    lat_cells = own_ref.shape[0]
    cells = places_ref.shape[1]
    for band in range(lat_cells // WIN_R):
        total = None
        for row in range(WIN_R):
            source = band * WIN_R + row + half
            field = own_ref[source] if source < lat_cells else halo_ref[source - lat_cells]
            term = mxu(places_ref[row], field)
            total = term if total is None else total + term
        result_ref[band * cells : (band + 1) * cells, :] = total.astype(jnp.bfloat16)


def prepare_kernel(to_slot_ref, inputs_ref, halo_ref, places_ref, tokens_ref, turned_ref):
    shift_kernel(inputs_ref, halo_ref, places_ref, tokens_ref)
    chunks, blocks = to_slot_ref.shape
    depth = tokens_ref.shape[1] // blocks
    turned = tokens_ref[...].T
    for chunk in range(chunks):
        for block in range(blocks):
            rows = pl.ds(pl.multiple_of(to_slot_ref[chunk, block] * depth, depth), depth)
            turned_ref[chunk, rows, :] = turned[block * depth : (block + 1) * depth, :]


def finish_kernel(
    cells_ref, w_qkv_ref, normed_ref, inputs_ref, cot_ref, places_ref,
    output_ref, grad_in_ref, lower_ref, shift_ref,
):
    lat_cells = inputs_ref.shape[0]
    half = lower_ref.shape[0] // 2
    count = places_ref.shape[1]
    shift_ref[...] = mxu(cells_ref[...], w_qkv_ref[...], NT).astype(jnp.bfloat16)
    for at, (value_ref, base_ref, result_ref) in enumerate(
        ((normed_ref, inputs_ref, output_ref), (shift_ref, cot_ref, grad_in_ref))
    ):
        result_ref[:half] = base_ref[:half]
        for band in range(lat_cells // WIN_R):
            value = value_ref[band * count : (band + 1) * count, :]
            for row in range(WIN_R):
                back = mxu(places_ref[row], value, TN)
                target = band * WIN_R + row + half
                if target < lat_cells:
                    base = base_ref[target].astype(jnp.float32)
                    result_ref[target] = (base + back).astype(jnp.bfloat16)
                else:
                    lower_ref[at * half + target - lat_cells] = back.astype(jnp.bfloat16)


def forward_kernel(into_ref, x_ref, bias_ref, *rest):
    shard_refs, rest = rest[: into_ref.shape[0]], rest[into_ref.shape[0] :]
    w_qkv_ref, w_out_ref, qkv_ref, probs_ref, mixed_ref = rest
    windows, win = bias_ref.shape[:2]
    width = x_ref.shape[1]
    head_dim = width // HEADS
    group = GROUP * head_dim
    factor = head_dim ** (-0.5) * math.log2(math.e)

    blocks = into_ref.shape[0]
    depth = width // blocks
    for at, shard_ref in enumerate(shard_refs):
        rows = pl.ds(pl.multiple_of(into_ref[at] * depth, depth), depth)
        w_qkv_ref[rows, :] = shard_ref[:, : 3 * width]
        w_out_ref[rows, :] = shard_ref[:, 3 * width :]

    for part in range(3):
        columns = slice(part * width, (part + 1) * width)
        qkv_ref[:, columns] = mxu(x_ref[...], w_qkv_ref[:, columns]).astype(jnp.bfloat16)

    def attend(window, carry):
        rows = pl.ds(pl.multiple_of(window * win, 16), win)
        bias = bias_ref[window]
        for at in range(HEADS // GROUP):
            columns = slice(at * group, (at + 1) * group)
            queries = qkv_ref[rows, columns]
            keys = qkv_ref[rows, width + at * group : width + (at + 1) * group]
            values = qkv_ref[rows, 2 * width + at * group : 2 * width + (at + 1) * group]
            scores = mxu(masked_heads(keys, head_dim), queries, NT)
            scores = scores.reshape(GROUP, win, win) * factor + bias
            lifted = jnp.exp2(scores - jnp.max(scores, axis=1, keepdims=True))
            total = jnp.sum(lifted, axis=1, keepdims=True)
            probs = (lifted * (1.0 / total)).astype(jnp.bfloat16)
            probs = probs.reshape(GROUP * win, win)
            probs_ref[window, at] = probs
            mixed = own_heads(mxu(turned_heads(probs, GROUP), values), head_dim)
            mixed_ref[rows, columns] = mixed.astype(jnp.bfloat16)
        return carry

    lax.fori_loop(0, windows, attend, 0)


def backward_kernel(
    to_slot_ref, qkv_ref, probs_ref, mixed_ref, w_out_ref, turned_ref, cot_ref, gain_ref,
    normed_ref, cells_ref, *rest,
):
    grad_refs, (grad_proj_ref, grad_mix_ref) = rest[:4], rest[4:]
    windows, win = probs_ref.shape[0], probs_ref.shape[-1]
    width = cot_ref.shape[1]
    head_dim = width // HEADS
    group = GROUP * head_dim
    scale = head_dim ** (-0.5)
    blocks = to_slot_ref.shape[1]
    depth = width // blocks
    gain = gain_ref[...]

    def normalise(window, carry):
        rows = pl.ds(pl.multiple_of(window * win, 16), win)
        projected = mxu(mixed_ref[rows, :], w_out_ref[...])
        center = projected - jnp.mean(projected, axis=-1, keepdims=True)
        inverse = lax.rsqrt(jnp.mean(center * center, axis=-1, keepdims=True) + EPS)
        normal = center * inverse
        normed_ref[rows, :] = (normal * gain).astype(jnp.bfloat16)
        scaled = cot_ref[rows, :].astype(jnp.float32) * gain
        grad_proj = (
            scaled
            - jnp.mean(scaled, axis=-1, keepdims=True)
            - normal * jnp.mean(scaled * normal, axis=-1, keepdims=True)
        ) * inverse
        grad_proj_ref[rows, :] = grad_proj.astype(jnp.bfloat16)
        return carry

    lax.fori_loop(0, windows, normalise, 0)
    half = width // 2
    sent_refs, kept_refs = grad_refs[::2], grad_refs[1::2]
    grad_out = mxu(mixed_ref[...], grad_proj_ref[...], TN)
    for block in range(blocks):
        slot = to_slot_ref[0, block]
        value = grad_out[block * depth : (block + 1) * depth, :]
        rows = pl.ds(pl.multiple_of(lax.rem(slot, blocks // 2) * depth, depth), depth)

        @pl.when(slot < blocks // 2)
        def _():
            kept_refs[0][rows, :width] = value

        @pl.when(slot >= blocks // 2)
        def _():
            sent_refs[0][rows, :width] = value

    grad_mix_ref[...] = mxu(grad_proj_ref[...], w_out_ref[...], NT).astype(jnp.bfloat16)

    def attend_back(window, carry):
        rows = pl.ds(pl.multiple_of(window * win, 16), win)
        for at in range(HEADS // GROUP):
            columns = slice(at * group, (at + 1) * group)
            key_columns = slice(width + at * group, width + (at + 1) * group)
            value_columns = slice(2 * width + at * group, 2 * width + (at + 1) * group)
            mix = grad_mix_ref[rows, columns]
            probs = probs_ref[window, at]
            float_probs = probs.astype(jnp.float32)
            grad_probs = mxu(masked_heads(qkv_ref[rows, value_columns], head_dim), mix, NT)
            product = (float_probs * grad_probs).reshape(GROUP, win, win)
            center = jnp.sum(product, axis=1, keepdims=True)
            grad_scores = scale * (product - float_probs.reshape(GROUP, win, win) * center)
            grad_scores = grad_scores.astype(jnp.bfloat16).reshape(GROUP * win, win)
            grad_values = own_heads(mxu(probs, mix), head_dim)
            grad_keys = own_heads(mxu(grad_scores, qkv_ref[rows, columns]), head_dim)
            turned = turned_heads(grad_scores, GROUP)
            grad_queries = own_heads(mxu(turned, qkv_ref[rows, key_columns]), head_dim)
            cells_ref[rows, columns] = grad_queries.astype(jnp.bfloat16)
            cells_ref[rows, key_columns] = grad_keys.astype(jnp.bfloat16)
            cells_ref[rows, value_columns] = grad_values.astype(jnp.bfloat16)
        return carry

    lax.fori_loop(0, windows, attend_back, 0)

    for part, place in enumerate(GRAD_PLACES):
        columns = slice(part * width, (part + 1) * width)
        target = slice(place % 2 * width, (place % 2 + 1) * width)
        turned = turned_ref.at[place // 2]
        sent_refs[place // 2][:, target] = mxu(turned[half:, :], cells_ref[:, columns])
        kept_refs[place // 2][:, target] = mxu(turned[:half, :], cells_ref[:, columns])


def coded(value):
    top = jnp.max(jnp.abs(value), axis=1, keepdims=True)
    exponent = jnp.ceil(jnp.log2(jnp.maximum(top, 1e-30)))
    codes = jnp.round(value * (jnp.exp2(-exponent) * STEPS)).astype(jnp.int32)
    exponents = jnp.broadcast_to(exponent, (value.shape[0], 128)).astype(jnp.int32)
    return codes.astype(jnp.int16), exponents.astype(jnp.int16)


def decoded(codes, exponents):
    exponent = exponents.astype(jnp.int32).astype(jnp.float32)[:, :1]
    return codes.astype(jnp.int32).astype(jnp.float32) * (jnp.exp2(exponent) * (1 / STEPS))


def fold_kernel(arrived_ref, kept_ref, *out_refs):
    columns = kept_ref.shape[1]
    rows = out_refs[0].shape[0]

    def total(part):
        arrived = arrived_ref[part, :columns]
        if arrived_ref.shape[1] > columns:
            arrived = decoded(arrived, arrived_ref[part, columns:])
        return kept_ref[part, :] + arrived

    out_refs[0][...] = total(slice(0, rows))
    if len(out_refs) > 1:
        codes, exponents = coded(total(slice(rows, 2 * rows)))
        out_refs[1][:, :columns] = codes
        out_refs[1][:, columns:] = exponents


def exchanged(value, distance):
    count = lax.axis_size("lat")
    return lax.ppermute(value, "lat", [(i, i ^ distance) for i in range(count)])


def moved(value, grp_turn, distance):
    count = lax.axis_size("lat")
    groups = lax.axis_size("grp")
    pairs = []
    for grp in range(groups):
        for i in range(count):
            pairs.append((grp * count + i, (grp ^ grp_turn) * count + (i ^ distance[grp])))
    return lax.ppermute(value, ("grp", "lat"), pairs)


def gathered(block, upper_in, cot_edge, prepare, bias):
    here = lax.axis_index("grp") == 0
    far = moved(block, 0, (8, 12))
    upper_in = passed_along(upper_in, "lat", -1)
    near = moved(block, 0, (4, 6))
    side = exchanged(block, 2)
    far, near, side, bias, upper_in = lax.optimization_barrier((far, near, side, bias, upper_in))
    far_side, far_other = exchanged(far, 2), moved(far, 1, (0, 0))
    near_other = moved(near, 1, (0, 0))
    far_side_other = moved(far_side, 1, (0, 0))
    far_other, *prepared = lax.optimization_barrier((far_other, *prepare(upper_in)))
    far_side_other, cot_edge = lax.optimization_barrier((far_side_other, cot_edge))
    upper_cot = passed_along(cot_edge, "lat", -1)
    shards = [block, side, near, near_other, far, far_other, far_side, far_side_other]
    low = jnp.array([0, 2, 4, 6, 8, 12, 10, 14], jnp.int32)
    high = jnp.array([0, 2, 6, 4, 12, 8, 14, 10], jnp.int32)
    order = jnp.where(here, low, high)
    shards += [exchanged(shard, 1) for shard in shards]
    return tuple(shards), jnp.concatenate([order, order + 1]), prepared, upper_cot, bias


def slots_of(distances, steps):
    result = 0
    for step in steps:
        result = 2 * result + ((distances // step) & 1)
    return result


def fold(arrived, kept, last=False):
    rows, columns = kept.shape
    if last:
        outs = (jax.ShapeDtypeStruct((rows, columns), jnp.float32),)
    else:
        outs = (
            jax.ShapeDtypeStruct((rows // 2, columns), jnp.float32),
            jax.ShapeDtypeStruct((rows // 2, columns + 128), jnp.int16),
        )
    return call(fold_kernel, "fold", outs, (), (arrived, kept), flops=8 * rows * columns, vmem=16)


def call(kernel, name, outs, tables, operands, scratch=(), flops=0, vmem=40):
    size = sum(math.prod(o.shape) * o.dtype.itemsize for o in (*outs, *operands))
    return pl.pallas_call(
        kernel,
        out_shape=outs,
        in_specs=[pl.BlockSpec(memory_space=pltpu.SMEM)] * len(tables)
        + [pl.BlockSpec(memory_space=pltpu.VMEM)] * len(operands),
        out_specs=[pl.BlockSpec(memory_space=pltpu.VMEM)] * len(outs),
        scratch_shapes=list(scratch),
        compiler_params=pltpu.CompilerParams(vmem_limit_bytes=vmem * 1024 * 1024),
        cost_estimate=pl.CostEstimate(flops=flops, bytes_accessed=size, transcendentals=0),
        name=name,
    )(*tables, *operands)


def per_device(inputs, cotangent, idents, w_qkv, w_out, gain):
    lat_cells, lon_cells, width = inputs.shape
    half_rows = WIN_R // 2
    win = padded_rows()
    windows = (lat_cells // WIN_R) * (lon_cells // WIN_C)
    cells = windows * win
    places = jnp.asarray(window_places(lon_cells), jnp.bfloat16)

    def shape(*dims, dtype=jnp.bfloat16):
        return jax.ShapeDtypeStruct(dims, dtype)

    count = lax.axis_size("lat")
    me = lax.axis_index("lat")
    direct = count == 16 and lax.axis_size("grp") == 2 and width % (16 * count) == 0
    routes = ((1, 2, 4, 8), (1, 4, 8, 2))
    if direct:
        distances = jnp.arange(count, dtype=jnp.int32) ^ me
        to_slot = jnp.stack([slots_of(distances, route) for route in routes])
    else:
        to_slot = jnp.stack([jnp.arange(16, dtype=jnp.int32)] * 2)

    def prepare(upper_in):
        return call(
            prepare_kernel,
            "prepare",
            (shape(cells, width), shape(2, width, cells)),
            (to_slot,),
            (inputs, upper_in, places),
            flops=2 * cells * width * lon_cells * WIN_R,
            vmem=16,
        )

    weights = jnp.concatenate([w_qkv, w_out], axis=1)
    in_edge, cot_edge = inputs[:half_rows], cotangent[:half_rows]
    labels = to_windows(idents + 1)
    bias = jnp.where(labels[:, :, None] == labels[:, None, :], 0.0, HIDDEN).astype(jnp.float32)
    if direct:
        shards, order, (tokens, turned), upper_cot, bias = gathered(
            weights, in_edge, cot_edge, prepare, bias
        )
        into = order ^ me
    else:
        weights = lax.all_gather(weights, "lat", axis=0, tiled=True)
        shards = tuple(weights.reshape(16, width // 16, 4 * width))
        into = to_slot[0]
        tokens, turned = prepare(passed_along(in_edge, "lat", -1))
        upper_cot = passed_along(cot_edge, "lat", -1)

    qkv_full, out_full, qkv, probs, mixed = call(
        forward_kernel,
        "forward",
        (
            shape(width, 3 * width),
            shape(width, width),
            shape(cells, 3 * width),
            shape(windows, HEADS // GROUP, GROUP * win, win),
            shape(cells, width),
        ),
        (into,),
        (tokens, bias, *shards),
        flops=2 * cells * width * width * 4,
        vmem=20,
    )
    (cot,) = call(
        shift_kernel,
        "shift",
        (shape(cells, width),),
        (),
        (cotangent, upper_cot, places),
        flops=2 * cells * width * lon_cells * WIN_R,
        vmem=16,
    )
    normed, grad_cells, *grads = call(
        backward_kernel,
        "backward",
        (
            shape(cells, width),
            shape(cells, 3 * width),
            *[shape(width // 2, 2 * width, dtype=jnp.float32)] * 4,
        ),
        (to_slot,),
        (qkv, probs, mixed, out_full, turned, cot, gain[None]),
        (pltpu.VMEM((cells, width), jnp.bfloat16), pltpu.VMEM((cells, width), jnp.bfloat16)),
        flops=2 * cells * width * width * 6,
        vmem=30,
    )

    def finish(normed, grad_cells):
        return call(
            finish_kernel,
            "finish",
            (shape(*inputs.shape), shape(*inputs.shape), shape(2 * half_rows, lon_cells, width)),
            (),
            (grad_cells, qkv_full, normed, inputs, cotangent, places),
            (pltpu.VMEM((cells, width), jnp.bfloat16),),
            flops=2 * cells * width * (3 * width + 2 * lon_cells * WIN_R),
            vmem=24,
        )

    if direct:
        pairs = [(exchanged(sent, 1), kept) for sent, kept in zip(grads[::2], grads[1::2])]
        pairs = [fold(arrived, kept) for arrived, kept in pairs]
        kept, sent = pairs[1]
        sent, normed, grad_cells = lax.optimization_barrier((sent, normed, grad_cells))
        pairs[1] = (kept, sent)
        output, grad_in, lower = finish(normed, grad_cells)
        for step in (1, 2, 3):
            pairs = [
                (exchanged(sent, route[step]), kept) for route, (kept, sent) in zip(routes, pairs)
            ]
            if step in (1, 3):
                arrived, kept = pairs[0]
                arrived, lower = lax.optimization_barrier((arrived, lower))
                pairs[0] = (arrived, kept)
            pairs = [fold(arrived, kept, step == 3) for arrived, kept in pairs]
            if step == 1:
                lower, _ = lax.optimization_barrier((lower, pairs[0][0]))
                lower = passed_along(lower, "lat", 1)
        pairs = [total for (total,) in pairs]
        quarters = [pairs[at // 2][:, at % 2 * width : (at % 2 + 1) * width] for at in range(4)]
        grad_out = quarters[0]
        grad_qkv = jnp.concatenate([quarters[place] for place in GRAD_PLACES], axis=1)
    else:
        whole = [jnp.concatenate([kept, sent]) for sent, kept in zip(grads[::2], grads[1::2])]
        both = lax.psum_scatter(jnp.concatenate(whole, axis=1), "lat", scatter_dimension=0, tiled=True)
        quarters = jnp.split(both, 4, axis=1)
        grad_out = quarters[0]
        grad_qkv = jnp.concatenate([quarters[place] for place in GRAD_PLACES], axis=1)
        output, grad_in, lower = finish(normed, grad_cells)
        lower = passed_along(lower, "lat", 1)

    def completed(result, lower):
        top = result[:half_rows].astype(jnp.float32) + lower.astype(jnp.float32)
        return result.at[:half_rows].set(top.astype(jnp.bfloat16))

    output = completed(output, lower[:half_rows])
    return (output, completed(grad_in, lower[half_rows:]), grad_qkv, grad_out)


def solution(mesh):
    in_specs = (
        P(("grp", "lat"), None, None),
        P(("grp", "lat"), None, None),
        P(("grp", "lat"), None),
        P("lat", None),
        P("lat", None),
        P(),
    )
    out_specs = (
        P(("grp", "lat"), None, None),
        P(("grp", "lat"), None, None),
        P(("grp", "lat"), None),
        P(("grp", "lat"), None),
    )
    return jax.shard_map(
        per_device, mesh=mesh, in_specs=in_specs, out_specs=out_specs, check_vma=False
    )
```

```python
import math

import jax
import jax.numpy as jnp
import numpy as np
from jax import lax
from jax.experimental import pallas as pl
from jax.experimental.pallas import tpu as pltpu
from jax.sharding import PartitionSpec as P

HEADS = 8
WIN_R = 6
WIN_C = 12
EPS = 1e-05
HIDDEN = -1e30
STEPS = 32000.0
GRAD_PLACES = (3, 2, 1)
CHUNK = 3
GROUP = 2

NN = (((1,), (0,)), ((), ()))
NT = (((1,), (1,)), ((), ()))
TN = (((0,), (0,)), ((), ()))


def mxu(left, right, dims=NN):
    return lax.dot_general(left, right, dims, preferred_element_type=jnp.float32)


def passed_along(value, axis, steps):
    count = lax.axis_size(axis)
    first, last = (max(0, -steps), min(count, count - steps))
    return lax.ppermute(value, axis, [(source, source + steps) for source in range(first, last)])


def padded_rows():
    return -(-WIN_R * WIN_C // 16) * 16


def to_windows(field):
    lat_cells, lon_cells = field.shape
    field = field.reshape(lat_cells // WIN_R, WIN_R, lon_cells // WIN_C, WIN_C)
    field = field.transpose(0, 2, 1, 3).reshape(-1, WIN_R * WIN_C)
    return jnp.pad(field, ((0, 0), (0, padded_rows() - WIN_R * WIN_C)))


def window_places(lon_cells):
    win = padded_rows()
    places = np.zeros((WIN_R, lon_cells // WIN_C, win, lon_cells), np.float32)
    for row in range(WIN_R):
        for window in range(lon_cells // WIN_C):
            for column in range(WIN_C):
                source = (window * WIN_C + column + WIN_C // 2) % lon_cells
                places[row, window, row * WIN_C + column, source] = 1
    return places.reshape(WIN_R, -1, lon_cells)


def masked_heads(value, head_dim):
    head = lax.broadcasted_iota(jnp.int32, value.shape, 1) // head_dim
    zero = jnp.zeros_like(value)
    count = value.shape[1] // head_dim
    return jnp.concatenate([jnp.where(head == at, value, zero) for at in range(count)], axis=0)


def own_heads(stacked, head_dim):
    count = stacked.shape[1] // head_dim
    rows = stacked.shape[0] // count
    head = lax.broadcasted_iota(jnp.int32, (rows, stacked.shape[1]), 1) // head_dim
    result = stacked[:rows]
    for at in range(1, count):
        result = jnp.where(head == at, stacked[at * rows : (at + 1) * rows], result)
    return result


def turned_heads(stacked, count):
    rows = stacked.shape[0] // count
    return jnp.concatenate(
        [stacked[at * rows : (at + 1) * rows].T for at in range(count)], axis=0
    )


def shift_kernel(own_ref, halo_ref, places_ref, result_ref):
    half = halo_ref.shape[0]
    lat_cells = own_ref.shape[0]
    cells = places_ref.shape[1]
    for band in range(lat_cells // WIN_R):
        total = None
        for row in range(WIN_R):
            source = band * WIN_R + row + half
            field = own_ref[source] if source < lat_cells else halo_ref[source - lat_cells]
            term = mxu(places_ref[row], field)
            total = term if total is None else total + term
        result_ref[band * cells : (band + 1) * cells, :] = total.astype(jnp.bfloat16)


def window_loop(windows, body):
    lax.fori_loop(0, windows, body, 0, unroll=3 if windows % 3 == 0 else 1)


def prepare_kernel(to_slot_ref, inputs_ref, halo_ref, places_ref, tokens_ref, turned_ref):
    shift_kernel(inputs_ref, halo_ref, places_ref, tokens_ref)
    chunks, blocks = to_slot_ref.shape
    depth = tokens_ref.shape[1] // blocks
    turned = tokens_ref[...].T
    for chunk in range(chunks):
        for block in range(blocks):
            rows = pl.ds(pl.multiple_of(to_slot_ref[chunk, block] * depth, depth), depth)
            turned_ref[chunk, rows, :] = turned[block * depth : (block + 1) * depth, :]


def finish_kernel(
    cells_ref, w_qkv_ref, normed_ref, inputs_ref, cot_ref, places_ref,
    output_ref, grad_in_ref, lower_ref, shift_ref,
):
    lat_cells = inputs_ref.shape[0]
    half = lower_ref.shape[0]
    count = places_ref.shape[1]
    shift_ref[...] = mxu(cells_ref[...], w_qkv_ref[...], NT).astype(jnp.bfloat16)
    for at, (value_ref, base_ref, result_ref) in enumerate(
        ((normed_ref, inputs_ref, output_ref), (shift_ref, cot_ref, grad_in_ref))
    ):
        result_ref[:half] = base_ref[:half]
        for band in range(lat_cells // WIN_R):
            value = value_ref[band * count : (band + 1) * count, :]
            for row in range(WIN_R):
                target = band * WIN_R + row + half
                if at == 0 and target >= lat_cells:
                    continue
                back = mxu(places_ref[row], value, TN)
                if target < lat_cells:
                    base = base_ref[target].astype(jnp.float32)
                    result_ref[target] = (base + back).astype(jnp.bfloat16)
                else:
                    lower_ref[target - lat_cells] = back.astype(jnp.bfloat16)


def forward_kernel(into_ref, x_ref, bias_ref, *rest):
    shard_refs, rest = rest[: into_ref.shape[0]], rest[into_ref.shape[0] :]
    w_qkv_ref, w_out_ref, qkv_ref, probs_ref, mixed_ref = rest
    windows, win = bias_ref.shape[:2]
    width = x_ref.shape[1]
    head_dim = width // HEADS
    group = GROUP * head_dim
    factor = head_dim ** (-0.5) * math.log2(math.e)

    blocks = into_ref.shape[0]
    depth = width // blocks
    for at, shard_ref in enumerate(shard_refs):
        rows = pl.ds(pl.multiple_of(into_ref[at] * depth, depth), depth)
        w_qkv_ref[rows, :] = shard_ref[:, : 3 * width]
        w_out_ref[rows, :] = shard_ref[:, 3 * width :]

    for part in range(3):
        columns = slice(part * width, (part + 1) * width)
        qkv_ref[:, columns] = mxu(x_ref[...], w_qkv_ref[:, columns]).astype(jnp.bfloat16)

    def attend(window, carry):
        rows = pl.ds(pl.multiple_of(window * win, 16), win)
        bias = bias_ref[window]
        for at in range(HEADS // GROUP):
            columns = slice(at * group, (at + 1) * group)
            queries = qkv_ref[rows, columns]
            keys = qkv_ref[rows, width + at * group : width + (at + 1) * group]
            values = qkv_ref[rows, 2 * width + at * group : 2 * width + (at + 1) * group]
            scores = mxu(masked_heads(keys, head_dim), queries, NT)
            scores = scores.reshape(GROUP, win, win) * factor + bias
            lifted = jnp.exp2(scores - jnp.max(scores, axis=1, keepdims=True))
            total = jnp.sum(lifted, axis=1, keepdims=True)
            probs = (lifted * (1.0 / total)).astype(jnp.bfloat16)
            probs = probs.reshape(GROUP * win, win)
            probs_ref[window, at] = probs
            mixed = own_heads(mxu(turned_heads(probs, GROUP), values), head_dim)
            mixed_ref[rows, columns] = mixed.astype(jnp.bfloat16)
        return carry

    window_loop(windows, attend)


def norm_kernel(
    mixed_ref, w_out_ref, cot_ref, gain_ref, normed_ref, grad_proj_ref, grad_mix_ref
):
    win = padded_rows()
    windows = mixed_ref.shape[0] // win
    gain = gain_ref[...]

    def normalise(window, carry):
        rows = pl.ds(pl.multiple_of(window * win, 16), win)
        projected = mxu(mixed_ref[rows, :], w_out_ref[...])
        center = projected - jnp.mean(projected, axis=-1, keepdims=True)
        inverse = lax.rsqrt(jnp.mean(center * center, axis=-1, keepdims=True) + EPS)
        normal = center * inverse
        normed_ref[rows, :] = (normal * gain).astype(jnp.bfloat16)
        scaled = cot_ref[rows, :].astype(jnp.float32) * gain
        grad_proj = (
            scaled
            - jnp.mean(scaled, axis=-1, keepdims=True)
            - normal * jnp.mean(scaled * normal, axis=-1, keepdims=True)
        ) * inverse
        grad_proj_ref[rows, :] = grad_proj.astype(jnp.bfloat16)
        return carry

    window_loop(windows, normalise)
    grad_mix_ref[...] = mxu(grad_proj_ref[...], w_out_ref[...], NT).astype(jnp.bfloat16)


def edge_kernel(value_ref, places_ref, lower_ref):
    half = lower_ref.shape[0]
    value = value_ref[value_ref.shape[0] - places_ref.shape[1] :, :]
    for row in range(half):
        back = mxu(places_ref[WIN_R - half + row], value, TN)
        lower_ref[row] = back.astype(jnp.bfloat16)


def backward_kernel(
    to_slot_ref, qkv_ref, probs_ref, mixed_ref, grad_proj_ref, grad_mix_ref, turned_ref,
    cells_ref, *grad_refs,
):
    windows, win = probs_ref.shape[0], probs_ref.shape[-1]
    width = grad_mix_ref.shape[1]
    head_dim = width // HEADS
    group = GROUP * head_dim
    scale = head_dim ** (-0.5)
    blocks = to_slot_ref.shape[1]
    depth = width // blocks
    half = width // 2
    sent_refs, kept_refs = grad_refs[::2], grad_refs[1::2]
    grad_out = mxu(mixed_ref[...], grad_proj_ref[...], TN)
    for block in range(blocks):
        slot = to_slot_ref[0, block]
        value = grad_out[block * depth : (block + 1) * depth, :]
        rows = pl.ds(pl.multiple_of(lax.rem(slot, blocks // 2) * depth, depth), depth)

        @pl.when(slot < blocks // 2)
        def _():
            kept_refs[0][rows, :width] = value

        @pl.when(slot >= blocks // 2)
        def _():
            sent_refs[0][rows, :width] = value

    def attend_back(window, carry):
        rows = pl.ds(pl.multiple_of(window * win, 16), win)
        for at in range(HEADS // GROUP):
            columns = slice(at * group, (at + 1) * group)
            key_columns = slice(width + at * group, width + (at + 1) * group)
            value_columns = slice(2 * width + at * group, 2 * width + (at + 1) * group)
            mix = grad_mix_ref[rows, columns]
            probs = probs_ref[window, at]
            float_probs = probs.astype(jnp.float32)
            grad_probs = mxu(masked_heads(qkv_ref[rows, value_columns], head_dim), mix, NT)
            product = (float_probs * grad_probs).reshape(GROUP, win, win)
            center = jnp.sum(product, axis=1, keepdims=True)
            grad_scores = scale * (product - float_probs.reshape(GROUP, win, win) * center)
            grad_scores = grad_scores.astype(jnp.bfloat16).reshape(GROUP * win, win)
            grad_values = own_heads(mxu(probs, mix), head_dim)
            grad_keys = own_heads(mxu(grad_scores, qkv_ref[rows, columns]), head_dim)
            turned = turned_heads(grad_scores, GROUP)
            grad_queries = own_heads(mxu(turned, qkv_ref[rows, key_columns]), head_dim)
            cells_ref[rows, columns] = grad_queries.astype(jnp.bfloat16)
            cells_ref[rows, key_columns] = grad_keys.astype(jnp.bfloat16)
            cells_ref[rows, value_columns] = grad_values.astype(jnp.bfloat16)
        return carry

    window_loop(windows, attend_back)

    for part, place in enumerate(GRAD_PLACES):
        columns = slice(part * width, (part + 1) * width)
        chunk, place = divmod(place, CHUNK)
        target = slice(place * width, (place + 1) * width)
        turned = turned_ref.at[chunk]
        sent_refs[chunk][:, target] = mxu(turned[half:, :], cells_ref[:, columns])
        kept_refs[chunk][:, target] = mxu(turned[:half, :], cells_ref[:, columns])


def coded(value):
    top = jnp.max(jnp.abs(value), axis=1, keepdims=True)
    exponent = jnp.ceil(jnp.log2(jnp.maximum(top, 1e-30)))
    codes = jnp.round(value * (jnp.exp2(-exponent) * STEPS)).astype(jnp.int32)
    exponents = jnp.broadcast_to(exponent, (value.shape[0], 128)).astype(jnp.int32)
    return codes.astype(jnp.int16), exponents.astype(jnp.int16)


def decoded(codes, exponents):
    exponent = exponents.astype(jnp.int32).astype(jnp.float32)[:, :1]
    return codes.astype(jnp.int32).astype(jnp.float32) * (jnp.exp2(exponent) * (1 / STEPS))


def fold_kernel(arrived_ref, kept_ref, *out_refs):
    columns = kept_ref.shape[1]
    rows = out_refs[0].shape[0]

    def total(part):
        arrived = arrived_ref[part, :columns]
        if arrived_ref.shape[1] > columns:
            arrived = decoded(arrived, arrived_ref[part, columns:])
        return kept_ref[part, :] + arrived

    out_refs[0][...] = total(slice(0, rows))
    if len(out_refs) > 1:
        codes, exponents = coded(total(slice(rows, 2 * rows)))
        out_refs[1][:, :columns] = codes
        out_refs[1][:, columns:] = exponents


def exchanged(value, distance):
    count = lax.axis_size("lat")
    return lax.ppermute(value, "lat", [(i, i ^ distance) for i in range(count)])


def moved(value, grp_turn, distance):
    count = lax.axis_size("lat")
    groups = lax.axis_size("grp")
    pairs = []
    for grp in range(groups):
        for i in range(count):
            pairs.append((grp * count + i, (grp ^ grp_turn) * count + (i ^ distance[grp])))
    return lax.ppermute(value, ("grp", "lat"), pairs)


def gathered(block, upper_in, cot_edge, prepare, bias):
    here = lax.axis_index("grp") == 0
    far = moved(block, 0, (8, 12))
    upper_in = passed_along(upper_in, "lat", -1)
    near = moved(block, 0, (4, 6))
    side = exchanged(block, 2)
    far, near, side, bias, upper_in, cot_edge = lax.optimization_barrier(
        (far, near, side, bias, upper_in, cot_edge)
    )
    far_side, far_other = exchanged(far, 2), moved(far, 1, (0, 0))
    near_other = moved(near, 1, (0, 0))
    far_side_other = moved(far_side, 1, (0, 0))
    far_other, *prepared = lax.optimization_barrier((far_other, *prepare(upper_in)))
    upper_cot = passed_along(cot_edge, "lat", -1)
    far_side_other, upper_cot = lax.optimization_barrier((far_side_other, upper_cot))
    shards = [block, side, near, near_other, far, far_other, far_side, far_side_other]
    low = jnp.array([0, 2, 4, 6, 8, 12, 10, 14], jnp.int32)
    high = jnp.array([0, 2, 6, 4, 12, 8, 14, 10], jnp.int32)
    order = jnp.where(here, low, high)
    shards += [exchanged(shard, 1) for shard in shards]
    return tuple(shards), jnp.concatenate([order, order + 1]), prepared, upper_cot, bias


def slots_of(distances, steps):
    result = 0
    for step in steps:
        result = 2 * result + ((distances // step) & 1)
    return result


def fold(arrived, kept, last=False):
    rows, columns = kept.shape
    if last:
        outs = (jax.ShapeDtypeStruct((rows, columns), jnp.float32),)
    else:
        outs = (
            jax.ShapeDtypeStruct((rows // 2, columns), jnp.float32),
            jax.ShapeDtypeStruct((rows // 2, columns + 128), jnp.int16),
        )
    return call(fold_kernel, "fold", outs, (), (arrived, kept), flops=8 * rows * columns, vmem=16)


def call(kernel, name, outs, tables, operands, scratch=(), flops=0, vmem=40):
    size = sum(math.prod(o.shape) * o.dtype.itemsize for o in (*outs, *operands))
    return pl.pallas_call(
        kernel,
        out_shape=outs,
        in_specs=[pl.BlockSpec(memory_space=pltpu.SMEM)] * len(tables)
        + [pl.BlockSpec(memory_space=pltpu.VMEM)] * len(operands),
        out_specs=[pl.BlockSpec(memory_space=pltpu.VMEM)] * len(outs),
        scratch_shapes=list(scratch),
        compiler_params=pltpu.CompilerParams(vmem_limit_bytes=vmem * 1024 * 1024),
        cost_estimate=pl.CostEstimate(flops=flops, bytes_accessed=size, transcendentals=0),
        name=name,
    )(*tables, *operands)


def per_device(inputs, cotangent, idents, w_qkv, w_out, gain):
    lat_cells, lon_cells, width = inputs.shape
    half_rows = WIN_R // 2
    win = padded_rows()
    windows = (lat_cells // WIN_R) * (lon_cells // WIN_C)
    cells = windows * win
    places = jnp.asarray(window_places(lon_cells), jnp.bfloat16)

    def shape(*dims, dtype=jnp.bfloat16):
        return jax.ShapeDtypeStruct(dims, dtype)

    count = lax.axis_size("lat")
    me = lax.axis_index("lat")
    direct = count == 16 and lax.axis_size("grp") == 2 and width % (16 * count) == 0
    routes = ((1, 2, 4, 8), (1, 4, 8, 2))
    if direct:
        distances = jnp.arange(count, dtype=jnp.int32) ^ me
        to_slot = jnp.stack([slots_of(distances, route) for route in routes])
    else:
        to_slot = jnp.stack([jnp.arange(16, dtype=jnp.int32)] * 2)

    def prepare(upper_in):
        return call(
            prepare_kernel,
            "prepare",
            (shape(cells, width), shape(2, width, cells)),
            (to_slot,),
            (inputs, upper_in, places),
            flops=2 * cells * width * lon_cells * WIN_R,
            vmem=16,
        )

    weights = jnp.concatenate([w_qkv, w_out], axis=1)
    in_edge, cot_edge = inputs[:half_rows], cotangent[:half_rows]
    labels = to_windows(idents + 1)
    bias = jnp.where(labels[:, :, None] == labels[:, None, :], 0.0, HIDDEN).astype(jnp.float32)
    if direct:
        shards, order, (tokens, turned), upper_cot, bias = gathered(
            weights, in_edge, cot_edge, prepare, bias
        )
        into = order ^ me
    else:
        weights = lax.all_gather(weights, "lat", axis=0, tiled=True)
        shards = tuple(weights.reshape(16, width // 16, 4 * width))
        into = to_slot[0]
        tokens, turned = prepare(passed_along(in_edge, "lat", -1))
        upper_cot = passed_along(cot_edge, "lat", -1)

    qkv_full, out_full, qkv, probs, mixed = call(
        forward_kernel,
        "forward",
        (
            shape(width, 3 * width),
            shape(width, width),
            shape(cells, 3 * width),
            shape(windows, HEADS // GROUP, GROUP * win, win),
            shape(cells, width),
        ),
        (into,),
        (tokens, bias, *shards),
        flops=2 * cells * width * width * 4,
        vmem=20,
    )
    (cot,) = call(
        shift_kernel,
        "shift",
        (shape(cells, width),),
        (),
        (cotangent, upper_cot, places),
        flops=2 * cells * width * lon_cells * WIN_R,
        vmem=16,
    )
    normed, grad_proj, grad_mix = call(
        norm_kernel,
        "norm",
        (shape(cells, width),) * 3,
        (),
        (mixed, out_full, cot, gain[None]),
        flops=2 * cells * width * width * 2,
        vmem=16,
    )
    (lower_out,) = call(
        edge_kernel,
        "edge",
        (shape(half_rows, lon_cells, width),),
        (),
        (normed, places),
        flops=2 * cells * width * lon_cells * half_rows,
        vmem=16,
    )
    lower_out = passed_along(lower_out, "lat", 1)
    grad_cells, *grads = call(
        backward_kernel,
        "backward",
        (
            shape(cells, 3 * width),
            *[shape(width // 2, CHUNK * width, dtype=jnp.float32)] * 2,
            *[shape(width // 2, (4 - CHUNK) * width, dtype=jnp.float32)] * 2,
        ),
        (to_slot,),
        (qkv, probs, mixed, grad_proj, grad_mix, turned),
        flops=2 * cells * width * width * 6,
        vmem=30,
    )
    lower_out, grad_cells, *grads = lax.optimization_barrier((lower_out, grad_cells, *grads))

    def finish(normed, grad_cells):
        return call(
            finish_kernel,
            "finish",
            (shape(*inputs.shape), shape(*inputs.shape), shape(half_rows, lon_cells, width)),
            (),
            (grad_cells, qkv_full, normed, inputs, cotangent, places),
            (pltpu.VMEM((cells, width), jnp.bfloat16),),
            flops=2 * cells * width * (3 * width + 2 * lon_cells * WIN_R),
            vmem=24,
        )

    if direct:
        pairs = [(exchanged(sent, 1), kept) for sent, kept in zip(grads[::2], grads[1::2])]
        pairs = [fold(arrived, kept) for arrived, kept in pairs]
        kept, sent = pairs[1]
        sent, normed, grad_cells = lax.optimization_barrier((sent, normed, grad_cells))
        pairs[1] = (kept, sent)
        output, grad_in, lower = finish(normed, grad_cells)
        for step in (1, 2, 3):
            pairs = [
                (exchanged(sent, route[step]), kept) for route, (kept, sent) in zip(routes, pairs)
            ]
            if step in (1, 3):
                arrived, kept = pairs[0]
                arrived, lower = lax.optimization_barrier((arrived, lower))
                pairs[0] = (arrived, kept)
            pairs = [fold(arrived, kept, step == 3) for arrived, kept in pairs]
            if step == 1:
                lower, _ = lax.optimization_barrier((lower, pairs[0][0]))
                lower = passed_along(lower, "lat", 1)
        pairs = [total for (total,) in pairs]
        quarters = jnp.split(pairs[0], CHUNK, axis=1) + jnp.split(pairs[1], 4 - CHUNK, axis=1)
        grad_out = quarters[0]
        grad_qkv = jnp.concatenate([quarters[place] for place in GRAD_PLACES], axis=1)
    else:
        whole = [jnp.concatenate([kept, sent]) for sent, kept in zip(grads[::2], grads[1::2])]
        both = lax.psum_scatter(jnp.concatenate(whole, axis=1), "lat", scatter_dimension=0, tiled=True)
        quarters = jnp.split(both, 4, axis=1)
        grad_out = quarters[0]
        grad_qkv = jnp.concatenate([quarters[place] for place in GRAD_PLACES], axis=1)
        output, grad_in, lower = finish(normed, grad_cells)
        lower = passed_along(lower, "lat", 1)

    def completed(result, lower):
        top = result[:half_rows].astype(jnp.float32) + lower.astype(jnp.float32)
        return result.at[:half_rows].set(top.astype(jnp.bfloat16))

    return (completed(output, lower_out), completed(grad_in, lower), grad_qkv, grad_out)


def solution(mesh):
    in_specs = (
        P(("grp", "lat"), None, None),
        P(("grp", "lat"), None, None),
        P(("grp", "lat"), None),
        P("lat", None),
        P("lat", None),
        P(),
    )
    out_specs = (
        P(("grp", "lat"), None, None),
        P(("grp", "lat"), None, None),
        P(("grp", "lat"), None),
        P(("grp", "lat"), None),
    )
    return jax.shard_map(
        per_device, mesh=mesh, in_specs=in_specs, out_specs=out_specs, check_vma=False
    )
```

```python
import math

import jax
import jax.numpy as jnp
import numpy as np
from jax import lax
from jax.experimental import pallas as pl
from jax.experimental.pallas import tpu as pltpu
from jax.sharding import PartitionSpec as P

HEADS = 8
WIN_R = 6
WIN_C = 12
EPS = 1e-05
HIDDEN = -1e30
STEPS = 32000.0
GRAD_PLACES = (3, 2, 1)
CHUNKS = (2, 1, 1)
ROUTES = ((1, 2, 4, 8), (1, 2, 4, 8), (1, 4, 8, 2))
TABLES = tuple(dict.fromkeys(ROUTES))
UNROLL = 9
GROUP = 2

NN = (((1,), (0,)), ((), ()))
NT = (((1,), (1,)), ((), ()))
TN = (((0,), (0,)), ((), ()))


def mxu(left, right, dims=NN):
    return lax.dot_general(left, right, dims, preferred_element_type=jnp.float32)


def passed_along(value, axis, steps):
    count = lax.axis_size(axis)
    first, last = (max(0, -steps), min(count, count - steps))
    return lax.ppermute(value, axis, [(source, source + steps) for source in range(first, last)])


def padded_rows():
    return -(-WIN_R * WIN_C // 16) * 16


def to_windows(field):
    lat_cells, lon_cells = field.shape
    field = field.reshape(lat_cells // WIN_R, WIN_R, lon_cells // WIN_C, WIN_C)
    field = field.transpose(0, 2, 1, 3).reshape(-1, WIN_R * WIN_C)
    return jnp.pad(field, ((0, 0), (0, padded_rows() - WIN_R * WIN_C)))


def window_places(lon_cells):
    win = padded_rows()
    places = np.zeros((WIN_R, lon_cells // WIN_C, win, lon_cells), np.float32)
    for row in range(WIN_R):
        for window in range(lon_cells // WIN_C):
            for column in range(WIN_C):
                source = (window * WIN_C + column + WIN_C // 2) % lon_cells
                places[row, window, row * WIN_C + column, source] = 1
    return places.reshape(WIN_R, -1, lon_cells)


def masked_heads(value, head_dim):
    head = lax.broadcasted_iota(jnp.int32, value.shape, 1) // head_dim
    zero = jnp.zeros_like(value)
    count = value.shape[1] // head_dim
    return jnp.concatenate([jnp.where(head == at, value, zero) for at in range(count)], axis=0)


def own_heads(stacked, head_dim):
    count = stacked.shape[1] // head_dim
    rows = stacked.shape[0] // count
    head = lax.broadcasted_iota(jnp.int32, (rows, stacked.shape[1]), 1) // head_dim
    result = stacked[:rows]
    for at in range(1, count):
        result = jnp.where(head == at, stacked[at * rows : (at + 1) * rows], result)
    return result


def turned_heads(stacked, count):
    rows = stacked.shape[0] // count
    return jnp.concatenate(
        [stacked[at * rows : (at + 1) * rows].T for at in range(count)], axis=0
    )


def shift_kernel(own_ref, halo_ref, places_ref, result_ref):
    half = halo_ref.shape[0]
    lat_cells = own_ref.shape[0]
    cells = places_ref.shape[1]
    for band in range(lat_cells // WIN_R):
        total = None
        for row in range(WIN_R):
            source = band * WIN_R + row + half
            field = own_ref[source] if source < lat_cells else halo_ref[source - lat_cells]
            term = mxu(places_ref[row], field)
            total = term if total is None else total + term
        result_ref[band * cells : (band + 1) * cells, :] = total.astype(jnp.bfloat16)


def window_loop(windows, body):
    lax.fori_loop(0, windows, body, 0, unroll=UNROLL if windows % UNROLL == 0 else 1)


def prepare_kernel(to_slot_ref, inputs_ref, halo_ref, places_ref, tokens_ref, turned_ref):
    shift_kernel(inputs_ref, halo_ref, places_ref, tokens_ref)
    chunks, blocks = to_slot_ref.shape
    depth = tokens_ref.shape[1] // blocks
    turned = tokens_ref[...].T
    for chunk in range(chunks):
        for block in range(blocks):
            rows = pl.ds(pl.multiple_of(to_slot_ref[chunk, block] * depth, depth), depth)
            turned_ref[chunk, rows, :] = turned[block * depth : (block + 1) * depth, :]


def finish_kernel(
    cells_ref, w_qkv_ref, normed_ref, inputs_ref, cot_ref, places_ref,
    output_ref, grad_in_ref, lower_ref, shift_ref,
):
    lat_cells = inputs_ref.shape[0]
    half = lower_ref.shape[0]
    count = places_ref.shape[1]
    shift_ref[...] = mxu(cells_ref[...], w_qkv_ref[...], NT).astype(jnp.bfloat16)
    for at, (value_ref, base_ref, result_ref) in enumerate(
        ((normed_ref, inputs_ref, output_ref), (shift_ref, cot_ref, grad_in_ref))
    ):
        result_ref[:half] = base_ref[:half]
        for band in range(lat_cells // WIN_R):
            value = value_ref[band * count : (band + 1) * count, :]
            for row in range(WIN_R):
                target = band * WIN_R + row + half
                if at == 0 and target >= lat_cells:
                    continue
                back = mxu(places_ref[row], value, TN)
                if target < lat_cells:
                    base = base_ref[target].astype(jnp.float32)
                    result_ref[target] = (base + back).astype(jnp.bfloat16)
                else:
                    lower_ref[target - lat_cells] = back.astype(jnp.bfloat16)


def forward_kernel(into_ref, x_ref, bias_ref, *rest):
    shard_refs, rest = rest[: into_ref.shape[0]], rest[into_ref.shape[0] :]
    w_qkv_ref, w_out_ref, qkv_ref, probs_ref, mixed_ref = rest
    windows, win = bias_ref.shape[:2]
    width = x_ref.shape[1]
    head_dim = width // HEADS
    group = GROUP * head_dim
    factor = head_dim ** (-0.5) * math.log2(math.e)

    blocks = into_ref.shape[0]
    depth = width // blocks
    for at, shard_ref in enumerate(shard_refs):
        rows = pl.ds(pl.multiple_of(into_ref[at] * depth, depth), depth)
        w_qkv_ref[rows, :] = shard_ref[:, : 3 * width]
        w_out_ref[rows, :] = shard_ref[:, 3 * width :]

    for part in range(3):
        columns = slice(part * width, (part + 1) * width)
        qkv_ref[:, columns] = mxu(x_ref[...], w_qkv_ref[:, columns]).astype(jnp.bfloat16)

    def attend(window, carry):
        rows = pl.ds(pl.multiple_of(window * win, 16), win)
        bias = bias_ref[window]
        for at in range(HEADS // GROUP):
            columns = slice(at * group, (at + 1) * group)
            queries = qkv_ref[rows, columns]
            keys = qkv_ref[rows, width + at * group : width + (at + 1) * group]
            values = qkv_ref[rows, 2 * width + at * group : 2 * width + (at + 1) * group]
            scores = mxu(masked_heads(keys, head_dim), queries, NT)
            scores = scores.reshape(GROUP, win, win) * factor + bias
            lifted = jnp.exp2(scores - jnp.max(scores, axis=1, keepdims=True))
            total = jnp.sum(lifted, axis=1, keepdims=True)
            probs = (lifted * (1.0 / total)).astype(jnp.bfloat16)
            probs = probs.reshape(GROUP * win, win)
            probs_ref[window, at] = probs
            mixed = own_heads(mxu(turned_heads(probs, GROUP), values), head_dim)
            mixed_ref[rows, columns] = mixed.astype(jnp.bfloat16)
        return carry

    window_loop(windows, attend)


def norm_kernel(
    mixed_ref, w_out_ref, cot_ref, gain_ref, normed_ref, grad_proj_ref, grad_mix_ref
):
    win = padded_rows()
    windows = mixed_ref.shape[0] // win
    gain = gain_ref[...]

    def normalise(window, carry):
        rows = pl.ds(pl.multiple_of(window * win, 16), win)
        projected = mxu(mixed_ref[rows, :], w_out_ref[...])
        center = projected - jnp.mean(projected, axis=-1, keepdims=True)
        inverse = lax.rsqrt(jnp.mean(center * center, axis=-1, keepdims=True) + EPS)
        normal = center * inverse
        normed_ref[rows, :] = (normal * gain).astype(jnp.bfloat16)
        scaled = cot_ref[rows, :].astype(jnp.float32) * gain
        grad_proj = (
            scaled
            - jnp.mean(scaled, axis=-1, keepdims=True)
            - normal * jnp.mean(scaled * normal, axis=-1, keepdims=True)
        ) * inverse
        grad_proj_ref[rows, :] = grad_proj.astype(jnp.bfloat16)
        return carry

    window_loop(windows, normalise)
    grad_mix_ref[...] = mxu(grad_proj_ref[...], w_out_ref[...], NT).astype(jnp.bfloat16)


def edge_kernel(value_ref, places_ref, lower_ref):
    half = lower_ref.shape[0]
    value = value_ref[value_ref.shape[0] - places_ref.shape[1] :, :]
    for row in range(half):
        back = mxu(places_ref[WIN_R - half + row], value, TN)
        lower_ref[row] = back.astype(jnp.bfloat16)


def backward_kernel(
    to_slot_ref, qkv_ref, probs_ref, mixed_ref, grad_proj_ref, grad_mix_ref, turned_ref,
    cells_ref, *grad_refs,
):
    windows, win = probs_ref.shape[0], probs_ref.shape[-1]
    width = grad_mix_ref.shape[1]
    head_dim = width // HEADS
    group = GROUP * head_dim
    scale = head_dim ** (-0.5)
    blocks = to_slot_ref.shape[1]
    depth = width // blocks
    half = width // 2
    sent_refs, kept_refs = grad_refs[::2], grad_refs[1::2]
    grad_out = mxu(mixed_ref[...], grad_proj_ref[...], TN)
    for block in range(blocks):
        slot = to_slot_ref[0, block]
        value = grad_out[block * depth : (block + 1) * depth, :]
        rows = pl.ds(pl.multiple_of(lax.rem(slot, blocks // 2) * depth, depth), depth)

        @pl.when(slot < blocks // 2)
        def _():
            kept_refs[0][rows, :width] = value

        @pl.when(slot >= blocks // 2)
        def _():
            sent_refs[0][rows, :width] = value

    def attend_back(window, carry):
        rows = pl.ds(pl.multiple_of(window * win, 16), win)
        for at in range(HEADS // GROUP):
            columns = slice(at * group, (at + 1) * group)
            key_columns = slice(width + at * group, width + (at + 1) * group)
            value_columns = slice(2 * width + at * group, 2 * width + (at + 1) * group)
            mix = grad_mix_ref[rows, columns]
            probs = probs_ref[window, at]
            float_probs = probs.astype(jnp.float32)
            grad_probs = mxu(masked_heads(qkv_ref[rows, value_columns], head_dim), mix, NT)
            product = (float_probs * grad_probs).reshape(GROUP, win, win)
            center = jnp.sum(product, axis=1, keepdims=True)
            grad_scores = scale * (product - float_probs.reshape(GROUP, win, win) * center)
            grad_scores = grad_scores.astype(jnp.bfloat16).reshape(GROUP * win, win)
            grad_values = own_heads(mxu(probs, mix), head_dim)
            grad_keys = own_heads(mxu(grad_scores, qkv_ref[rows, columns]), head_dim)
            turned = turned_heads(grad_scores, GROUP)
            grad_queries = own_heads(mxu(turned, qkv_ref[rows, key_columns]), head_dim)
            cells_ref[rows, columns] = grad_queries.astype(jnp.bfloat16)
            cells_ref[rows, key_columns] = grad_keys.astype(jnp.bfloat16)
            cells_ref[rows, value_columns] = grad_values.astype(jnp.bfloat16)
        return carry

    window_loop(windows, attend_back)

    for part, place in enumerate(GRAD_PLACES):
        columns = slice(part * width, (part + 1) * width)
        chunk = sum(place >= sum(CHUNKS[: at + 1]) for at in range(len(CHUNKS)))
        place -= sum(CHUNKS[:chunk])
        target = slice(place * width, (place + 1) * width)
        turned = turned_ref.at[TABLES.index(ROUTES[chunk])]
        sent_refs[chunk][:, target] = mxu(turned[half:, :], cells_ref[:, columns])
        kept_refs[chunk][:, target] = mxu(turned[:half, :], cells_ref[:, columns])


def coded(value):
    top = jnp.max(jnp.abs(value), axis=1, keepdims=True)
    exponent = jnp.ceil(jnp.log2(jnp.maximum(top, 1e-30)))
    codes = jnp.round(value * (jnp.exp2(-exponent) * STEPS)).astype(jnp.int32)
    exponents = jnp.broadcast_to(exponent, (value.shape[0], 128)).astype(jnp.int32)
    return codes.astype(jnp.int16), exponents.astype(jnp.int16)


def decoded(codes, exponents):
    exponent = exponents.astype(jnp.int32).astype(jnp.float32)[:, :1]
    return codes.astype(jnp.int32).astype(jnp.float32) * (jnp.exp2(exponent) * (1 / STEPS))


def fold_kernel(arrived_ref, kept_ref, *out_refs):
    columns = kept_ref.shape[1]
    rows = out_refs[0].shape[0]

    def total(part):
        arrived = arrived_ref[part, :columns]
        if arrived_ref.shape[1] > columns:
            arrived = decoded(arrived, arrived_ref[part, columns:])
        return kept_ref[part, :] + arrived

    out_refs[0][...] = total(slice(0, rows))
    if len(out_refs) > 1:
        codes, exponents = coded(total(slice(rows, 2 * rows)))
        out_refs[1][:, :columns] = codes
        out_refs[1][:, columns:] = exponents


def exchanged(value, distance):
    count = lax.axis_size("lat")
    return lax.ppermute(value, "lat", [(i, i ^ distance) for i in range(count)])


def moved(value, grp_turn, distance):
    count = lax.axis_size("lat")
    groups = lax.axis_size("grp")
    pairs = []
    for grp in range(groups):
        for i in range(count):
            pairs.append((grp * count + i, (grp ^ grp_turn) * count + (i ^ distance[grp])))
    return lax.ppermute(value, ("grp", "lat"), pairs)


def gathered(block, upper_in, cot_edge, prepare, bias):
    here = lax.axis_index("grp") == 0
    far = moved(block, 0, (8, 12))
    upper_in = passed_along(upper_in, "lat", -1)
    near = moved(block, 0, (4, 6))
    side = exchanged(block, 2)
    far, near, side, bias, upper_in, cot_edge = lax.optimization_barrier(
        (far, near, side, bias, upper_in, cot_edge)
    )
    far_side, far_other = exchanged(far, 2), moved(far, 1, (0, 0))
    near_other = moved(near, 1, (0, 0))
    far_side, near_other = lax.optimization_barrier((far_side, near_other))
    far_side_other = moved(far_side, 1, (0, 0))
    upper_cot = passed_along(cot_edge, "lat", -1)
    prepared = prepare(upper_in)
    shards = [block, side, near, near_other, far, far_other, far_side]
    swapped = [exchanged(shard, 1) for shard in shards]
    far_side_other, upper_cot, rest = lax.optimization_barrier(
        (far_side_other, upper_cot, swapped + list(prepared))
    )
    swapped, prepared = rest[: len(swapped)], rest[len(swapped) :]
    shards += [far_side_other] + swapped + [exchanged(far_side_other, 1)]
    low = jnp.array([0, 2, 4, 6, 8, 12, 10, 14], jnp.int32)
    high = jnp.array([0, 2, 6, 4, 12, 8, 14, 10], jnp.int32)
    order = jnp.where(here, low, high)
    return tuple(shards), jnp.concatenate([order, order + 1]), prepared, upper_cot, bias


def slots_of(distances, steps):
    result = 0
    for step in steps:
        result = 2 * result + ((distances // step) & 1)
    return result


def fold(arrived, kept, last=False):
    rows, columns = kept.shape
    if last:
        outs = (jax.ShapeDtypeStruct((rows, columns), jnp.float32),)
    else:
        outs = (
            jax.ShapeDtypeStruct((rows // 2, columns), jnp.float32),
            jax.ShapeDtypeStruct((rows // 2, columns + 128), jnp.int16),
        )
    return call(fold_kernel, "fold", outs, (), (arrived, kept), flops=8 * rows * columns, vmem=16)


def call(kernel, name, outs, tables, operands, scratch=(), flops=0, vmem=40):
    size = sum(math.prod(o.shape) * o.dtype.itemsize for o in (*outs, *operands))
    return pl.pallas_call(
        kernel,
        out_shape=outs,
        in_specs=[pl.BlockSpec(memory_space=pltpu.SMEM)] * len(tables)
        + [pl.BlockSpec(memory_space=pltpu.VMEM)] * len(operands),
        out_specs=[pl.BlockSpec(memory_space=pltpu.VMEM)] * len(outs),
        scratch_shapes=list(scratch),
        compiler_params=pltpu.CompilerParams(vmem_limit_bytes=vmem * 1024 * 1024),
        cost_estimate=pl.CostEstimate(flops=flops, bytes_accessed=size, transcendentals=0),
        name=name,
    )(*tables, *operands)


def per_device(inputs, cotangent, idents, w_qkv, w_out, gain):
    lat_cells, lon_cells, width = inputs.shape
    half_rows = WIN_R // 2
    win = padded_rows()
    windows = (lat_cells // WIN_R) * (lon_cells // WIN_C)
    cells = windows * win
    places = jnp.asarray(window_places(lon_cells), jnp.bfloat16)

    def shape(*dims, dtype=jnp.bfloat16):
        return jax.ShapeDtypeStruct(dims, dtype)

    count = lax.axis_size("lat")
    me = lax.axis_index("lat")
    direct = count == 16 and lax.axis_size("grp") == 2 and width % (16 * count) == 0
    if direct:
        distances = jnp.arange(count, dtype=jnp.int32) ^ me
        to_slot = jnp.stack([slots_of(distances, route) for route in TABLES])
    else:
        to_slot = jnp.stack([jnp.arange(16, dtype=jnp.int32)] * len(TABLES))

    def prepare(upper_in):
        return call(
            prepare_kernel,
            "prepare",
            (shape(cells, width), shape(len(TABLES), width, cells)),
            (to_slot,),
            (inputs, upper_in, places),
            flops=2 * cells * width * lon_cells * WIN_R,
            vmem=16,
        )

    weights = jnp.pad(w_qkv, ((0, 0), (0, width))) + jnp.pad(w_out, ((0, 0), (3 * width, 0)))
    in_edge, cot_edge = inputs[:half_rows], cotangent[:half_rows]
    labels = to_windows(idents + 1)
    bias = jnp.where(labels[:, :, None] == labels[:, None, :], 0.0, HIDDEN).astype(jnp.float32)
    if direct:
        shards, order, (tokens, turned), upper_cot, bias = gathered(
            weights, in_edge, cot_edge, prepare, bias
        )
        into = order ^ me
    else:
        weights = lax.all_gather(weights, "lat", axis=0, tiled=True)
        shards = tuple(weights.reshape(16, width // 16, 4 * width))
        into = to_slot[0]
        tokens, turned = prepare(passed_along(in_edge, "lat", -1))
        upper_cot = passed_along(cot_edge, "lat", -1)

    qkv_full, out_full, qkv, probs, mixed = call(
        forward_kernel,
        "forward",
        (
            shape(width, 3 * width),
            shape(width, width),
            shape(cells, 3 * width),
            shape(windows, HEADS // GROUP, GROUP * win, win),
            shape(cells, width),
        ),
        (into,),
        (tokens, bias, *shards),
        flops=2 * cells * width * width * 4,
        vmem=20,
    )
    (cot,) = call(
        shift_kernel,
        "shift",
        (shape(cells, width),),
        (),
        (cotangent, upper_cot, places),
        flops=2 * cells * width * lon_cells * WIN_R,
        vmem=16,
    )
    normed, grad_proj, grad_mix = call(
        norm_kernel,
        "norm",
        (shape(cells, width),) * 3,
        (),
        (mixed, out_full, cot, gain[None]),
        flops=2 * cells * width * width * 2,
        vmem=16,
    )
    (lower_out,) = call(
        edge_kernel,
        "edge",
        (shape(half_rows, lon_cells, width),),
        (),
        (normed, places),
        flops=2 * cells * width * lon_cells * half_rows,
        vmem=16,
    )
    lower_out = passed_along(lower_out, "lat", 1)
    grad_cells, *grads = call(
        backward_kernel,
        "backward",
        (
            shape(cells, 3 * width),
            *[shape(width // 2, CHUNKS[at // 2] * width, dtype=jnp.float32) for at in range(2 * len(CHUNKS))],
        ),
        (to_slot,),
        (qkv, probs, mixed, grad_proj, grad_mix, turned),
        flops=2 * cells * width * width * 6,
        vmem=30,
    )
    lower_out, grad_cells, *grads = lax.optimization_barrier((lower_out, grad_cells, *grads))

    def finish(normed, grad_cells):
        return call(
            finish_kernel,
            "finish",
            (shape(*inputs.shape), shape(*inputs.shape), shape(half_rows, lon_cells, width)),
            (),
            (grad_cells, qkv_full, normed, inputs, cotangent, places),
            (pltpu.VMEM((cells, width), jnp.bfloat16),),
            flops=2 * cells * width * (3 * width + 2 * lon_cells * WIN_R),
            vmem=24,
        )

    if direct:
        pairs = [(exchanged(sent, 1), kept) for sent, kept in zip(grads[::2], grads[1::2])]
        pairs = [fold(arrived, kept) for arrived, kept in pairs]
        kept, sent = pairs[-1]
        sent, normed, grad_cells = lax.optimization_barrier((sent, normed, grad_cells))
        pairs[-1] = (kept, sent)
        output, grad_in, lower = finish(normed, grad_cells)
        for step in (1, 2, 3):
            pairs = [
                (exchanged(sent, route[step]), kept) for route, (kept, sent) in zip(ROUTES, pairs)
            ]
            if step in (1, 3):
                arrived, kept = pairs[0]
                arrived, lower = lax.optimization_barrier((arrived, lower))
                pairs[0] = (arrived, kept)
            pairs = [fold(arrived, kept, step == 3) for arrived, kept in pairs]
            if step == 1:
                lower, _ = lax.optimization_barrier((lower, pairs[0][0]))
                lower = passed_along(lower, "lat", 1)
        pairs = [total for (total,) in pairs]
        quarters = [part for total in pairs for part in jnp.split(total, total.shape[1] // width, axis=1)]
        grad_out = quarters[0]
        grad_qkv = jnp.concatenate([quarters[place] for place in GRAD_PLACES], axis=1)
    else:
        whole = [jnp.concatenate([kept, sent]) for sent, kept in zip(grads[::2], grads[1::2])]
        both = lax.psum_scatter(jnp.concatenate(whole, axis=1), "lat", scatter_dimension=0, tiled=True)
        quarters = jnp.split(both, 4, axis=1)
        grad_out = quarters[0]
        grad_qkv = jnp.concatenate([quarters[place] for place in GRAD_PLACES], axis=1)
        output, grad_in, lower = finish(normed, grad_cells)
        lower = passed_along(lower, "lat", 1)

    def completed(result, lower):
        top = result[:half_rows].astype(jnp.float32) + lower.astype(jnp.float32)
        return result.at[:half_rows].set(top.astype(jnp.bfloat16))

    return (completed(output, lower_out), completed(grad_in, lower), grad_qkv, grad_out)


def solution(mesh):
    in_specs = (
        P(("grp", "lat"), None, None),
        P(("grp", "lat"), None, None),
        P(("grp", "lat"), None),
        P("lat", None),
        P("lat", None),
        P(),
    )
    out_specs = (
        P(("grp", "lat"), None, None),
        P(("grp", "lat"), None, None),
        P(("grp", "lat"), None),
        P(("grp", "lat"), None),
    )
    return jax.shard_map(
        per_device, mesh=mesh, in_specs=in_specs, out_specs=out_specs, check_vma=False
    )
```

```python
import math

import jax
import jax.numpy as jnp
import numpy as np
from jax import lax
from jax.experimental import pallas as pl
from jax.experimental.pallas import tpu as pltpu
from jax.sharding import PartitionSpec as P

HEADS = 8
WIN_R = 6
WIN_C = 12
EPS = 1e-05
HIDDEN = -1e30
STEPS = 32000.0
GRAD_PLACES = (3, 2, 1)
CHUNKS = (2, 1, 1)
ROUTES = ((1, 2, 4, 8), (1, 2, 4, 8), (1, 4, 8, 2))
TABLES = tuple(dict.fromkeys(ROUTES))
UNROLL = 9
GROUP = 4

NN = (((1,), (0,)), ((), ()))
NT = (((1,), (1,)), ((), ()))
TN = (((0,), (0,)), ((), ()))


def mxu(left, right, dims=NN):
    return lax.dot_general(left, right, dims, preferred_element_type=jnp.float32)


def passed_along(value, axis, steps):
    count = lax.axis_size(axis)
    first, last = (max(0, -steps), min(count, count - steps))
    return lax.ppermute(value, axis, [(source, source + steps) for source in range(first, last)])


def padded_rows():
    return -(-WIN_R * WIN_C // 16) * 16


def to_windows(field):
    lat_cells, lon_cells = field.shape
    field = field.reshape(lat_cells // WIN_R, WIN_R, lon_cells // WIN_C, WIN_C)
    field = field.transpose(0, 2, 1, 3).reshape(-1, WIN_R * WIN_C)
    return jnp.pad(field, ((0, 0), (0, padded_rows() - WIN_R * WIN_C)))


def window_places(lon_cells):
    win = padded_rows()
    places = np.zeros((WIN_R, lon_cells // WIN_C, win, lon_cells), np.float32)
    for row in range(WIN_R):
        for window in range(lon_cells // WIN_C):
            for column in range(WIN_C):
                source = (window * WIN_C + column + WIN_C // 2) % lon_cells
                places[row, window, row * WIN_C + column, source] = 1
    return places.reshape(WIN_R, -1, lon_cells)


def masked_heads(value, head_dim):
    head = lax.broadcasted_iota(jnp.int32, value.shape, 1) // head_dim
    zero = jnp.zeros_like(value)
    count = value.shape[1] // head_dim
    return jnp.concatenate([jnp.where(head == at, value, zero) for at in range(count)], axis=0)


def own_heads(stacked, head_dim):
    count = stacked.shape[1] // head_dim
    rows = stacked.shape[0] // count
    head = lax.broadcasted_iota(jnp.int32, (rows, stacked.shape[1]), 1) // head_dim
    result = stacked[:rows]
    for at in range(1, count):
        result = jnp.where(head == at, stacked[at * rows : (at + 1) * rows], result)
    return result


def turned_heads(stacked, count):
    rows = stacked.shape[0] // count
    return jnp.concatenate(
        [stacked[at * rows : (at + 1) * rows].T for at in range(count)], axis=0
    )


def shift_kernel(own_ref, halo_ref, places_ref, result_ref):
    half = halo_ref.shape[0]
    lat_cells = own_ref.shape[0]
    cells = places_ref.shape[1]
    for band in range(lat_cells // WIN_R):
        total = None
        for row in range(WIN_R):
            source = band * WIN_R + row + half
            field = own_ref[source] if source < lat_cells else halo_ref[source - lat_cells]
            term = mxu(places_ref[row], field)
            total = term if total is None else total + term
        result_ref[band * cells : (band + 1) * cells, :] = total.astype(jnp.bfloat16)


def window_loop(windows, body):
    lax.fori_loop(0, windows, body, 0, unroll=UNROLL if windows % UNROLL == 0 else 1)


def prepare_kernel(to_slot_ref, inputs_ref, halo_ref, places_ref, tokens_ref, turned_ref):
    shift_kernel(inputs_ref, halo_ref, places_ref, tokens_ref)
    chunks, blocks = to_slot_ref.shape
    depth = tokens_ref.shape[1] // blocks
    turned = tokens_ref[...].T
    for chunk in range(chunks):
        for block in range(blocks):
            rows = pl.ds(pl.multiple_of(to_slot_ref[chunk, block] * depth, depth), depth)
            turned_ref[chunk, rows, :] = turned[block * depth : (block + 1) * depth, :]


def finish_kernel(
    cells_ref, w_qkv_ref, normed_ref, inputs_ref, cot_ref, places_ref,
    output_ref, grad_in_ref, lower_ref, shift_ref,
):
    lat_cells = inputs_ref.shape[0]
    half = lower_ref.shape[0]
    count = places_ref.shape[1]
    shift_ref[...] = mxu(cells_ref[...], w_qkv_ref[...], NT).astype(jnp.bfloat16)
    for at, (value_ref, base_ref, result_ref) in enumerate(
        ((normed_ref, inputs_ref, output_ref), (shift_ref, cot_ref, grad_in_ref))
    ):
        result_ref[:half] = base_ref[:half]
        for band in range(lat_cells // WIN_R):
            value = value_ref[band * count : (band + 1) * count, :]
            for row in range(WIN_R):
                target = band * WIN_R + row + half
                if at == 0 and target >= lat_cells:
                    continue
                back = mxu(places_ref[row], value, TN)
                if target < lat_cells:
                    base = base_ref[target].astype(jnp.float32)
                    result_ref[target] = (base + back).astype(jnp.bfloat16)
                else:
                    lower_ref[target - lat_cells] = back.astype(jnp.bfloat16)


def forward_kernel(into_ref, x_ref, bias_ref, *rest):
    shard_refs, rest = rest[: into_ref.shape[0]], rest[into_ref.shape[0] :]
    w_qkv_ref, w_out_ref, qkv_ref, probs_ref, mixed_ref = rest
    windows, win = bias_ref.shape[:2]
    width = x_ref.shape[1]
    head_dim = width // HEADS
    group = GROUP * head_dim
    factor = head_dim ** (-0.5) * math.log2(math.e)

    blocks = into_ref.shape[0]
    depth = width // blocks
    for at, shard_ref in enumerate(shard_refs):
        rows = pl.ds(pl.multiple_of(into_ref[at] * depth, depth), depth)
        w_qkv_ref[rows, :] = shard_ref[:, : 3 * width]
        w_out_ref[rows, :] = shard_ref[:, 3 * width :]

    for part in range(3):
        columns = slice(part * width, (part + 1) * width)
        qkv_ref[:, columns] = mxu(x_ref[...], w_qkv_ref[:, columns]).astype(jnp.bfloat16)

    def attend(window, carry):
        rows = pl.ds(pl.multiple_of(window * win, 16), win)
        bias = bias_ref[window]
        for at in range(HEADS // GROUP):
            columns = slice(at * group, (at + 1) * group)
            queries = qkv_ref[rows, columns]
            keys = qkv_ref[rows, width + at * group : width + (at + 1) * group]
            values = qkv_ref[rows, 2 * width + at * group : 2 * width + (at + 1) * group]
            scores = mxu(masked_heads(keys, head_dim), queries, NT)
            scores = scores.reshape(GROUP, win, win) * factor + bias
            lifted = jnp.exp2(scores - jnp.max(scores, axis=1, keepdims=True))
            total = jnp.sum(lifted, axis=1, keepdims=True)
            probs = (lifted * (1.0 / total)).astype(jnp.bfloat16)
            probs = probs.reshape(GROUP * win, win)
            probs_ref[window, at] = probs
            mixed = own_heads(mxu(turned_heads(probs, GROUP), values), head_dim)
            mixed_ref[rows, columns] = mixed.astype(jnp.bfloat16)
        return carry

    window_loop(windows, attend)


def norm_kernel(
    mixed_ref, w_out_ref, cot_ref, gain_ref, normed_ref, grad_proj_ref, grad_mix_ref
):
    win = padded_rows()
    windows = mixed_ref.shape[0] // win
    gain = gain_ref[...]

    def normalise(window, carry):
        rows = pl.ds(pl.multiple_of(window * win, 16), win)
        projected = mxu(mixed_ref[rows, :], w_out_ref[...])
        center = projected - jnp.mean(projected, axis=-1, keepdims=True)
        inverse = lax.rsqrt(jnp.mean(center * center, axis=-1, keepdims=True) + EPS)
        normal = center * inverse
        normed_ref[rows, :] = (normal * gain).astype(jnp.bfloat16)
        scaled = cot_ref[rows, :].astype(jnp.float32) * gain
        grad_proj = (
            scaled
            - jnp.mean(scaled, axis=-1, keepdims=True)
            - normal * jnp.mean(scaled * normal, axis=-1, keepdims=True)
        ) * inverse
        grad_proj_ref[rows, :] = grad_proj.astype(jnp.bfloat16)
        return carry

    window_loop(windows, normalise)
    grad_mix_ref[...] = mxu(grad_proj_ref[...], w_out_ref[...], NT).astype(jnp.bfloat16)


def edge_kernel(value_ref, places_ref, lower_ref):
    half = lower_ref.shape[0]
    value = value_ref[value_ref.shape[0] - places_ref.shape[1] :, :]
    for row in range(half):
        back = mxu(places_ref[WIN_R - half + row], value, TN)
        lower_ref[row] = back.astype(jnp.bfloat16)


def backward_kernel(
    to_slot_ref, qkv_ref, probs_ref, mixed_ref, grad_proj_ref, grad_mix_ref, turned_ref,
    cells_ref, *grad_refs,
):
    windows, win = probs_ref.shape[0], probs_ref.shape[-1]
    width = grad_mix_ref.shape[1]
    head_dim = width // HEADS
    group = GROUP * head_dim
    scale = head_dim ** (-0.5)
    blocks = to_slot_ref.shape[1]
    depth = width // blocks
    half = width // 2
    sent_refs, kept_refs = grad_refs[::2], grad_refs[1::2]
    grad_out = mxu(mixed_ref[...], grad_proj_ref[...], TN)
    for block in range(blocks):
        slot = to_slot_ref[0, block]
        value = grad_out[block * depth : (block + 1) * depth, :]
        rows = pl.ds(pl.multiple_of(lax.rem(slot, blocks // 2) * depth, depth), depth)

        @pl.when(slot < blocks // 2)
        def _():
            kept_refs[0][rows, :width] = value

        @pl.when(slot >= blocks // 2)
        def _():
            sent_refs[0][rows, :width] = value

    def attend_back(window, carry):
        rows = pl.ds(pl.multiple_of(window * win, 16), win)
        for at in range(HEADS // GROUP):
            columns = slice(at * group, (at + 1) * group)
            key_columns = slice(width + at * group, width + (at + 1) * group)
            value_columns = slice(2 * width + at * group, 2 * width + (at + 1) * group)
            mix = grad_mix_ref[rows, columns]
            probs = probs_ref[window, at]
            float_probs = probs.astype(jnp.float32)
            grad_probs = mxu(masked_heads(qkv_ref[rows, value_columns], head_dim), mix, NT)
            product = (float_probs * grad_probs).reshape(GROUP, win, win)
            center = jnp.sum(product, axis=1, keepdims=True)
            grad_scores = scale * (product - float_probs.reshape(GROUP, win, win) * center)
            grad_scores = grad_scores.astype(jnp.bfloat16).reshape(GROUP * win, win)
            grad_values = own_heads(mxu(probs, mix), head_dim)
            grad_keys = own_heads(mxu(grad_scores, qkv_ref[rows, columns]), head_dim)
            turned = turned_heads(grad_scores, GROUP)
            grad_queries = own_heads(mxu(turned, qkv_ref[rows, key_columns]), head_dim)
            cells_ref[rows, columns] = grad_queries.astype(jnp.bfloat16)
            cells_ref[rows, key_columns] = grad_keys.astype(jnp.bfloat16)
            cells_ref[rows, value_columns] = grad_values.astype(jnp.bfloat16)
        return carry

    window_loop(windows, attend_back)

    for part, place in enumerate(GRAD_PLACES):
        columns = slice(part * width, (part + 1) * width)
        chunk = sum(place >= sum(CHUNKS[: at + 1]) for at in range(len(CHUNKS)))
        place -= sum(CHUNKS[:chunk])
        target = slice(place * width, (place + 1) * width)
        turned = turned_ref.at[TABLES.index(ROUTES[chunk])]
        sent_refs[chunk][:, target] = mxu(turned[half:, :], cells_ref[:, columns])
        kept_refs[chunk][:, target] = mxu(turned[:half, :], cells_ref[:, columns])


def coded(value):
    top = jnp.max(jnp.abs(value), axis=1, keepdims=True)
    exponent = jnp.ceil(jnp.log2(jnp.maximum(top, 1e-30)))
    codes = jnp.round(value * (jnp.exp2(-exponent) * STEPS)).astype(jnp.int32)
    exponents = jnp.broadcast_to(exponent, (value.shape[0], 128)).astype(jnp.int32)
    return codes.astype(jnp.int16), exponents.astype(jnp.int16)


def decoded(codes, exponents):
    exponent = exponents.astype(jnp.int32).astype(jnp.float32)[:, :1]
    return codes.astype(jnp.int32).astype(jnp.float32) * (jnp.exp2(exponent) * (1 / STEPS))


def fold_kernel(arrived_ref, kept_ref, *out_refs):
    columns = kept_ref.shape[1]
    rows = out_refs[0].shape[0]

    def total(part):
        arrived = arrived_ref[part, :columns]
        if arrived_ref.shape[1] > columns:
            arrived = decoded(arrived, arrived_ref[part, columns:])
        return kept_ref[part, :] + arrived

    out_refs[0][...] = total(slice(0, rows))
    if len(out_refs) > 1:
        codes, exponents = coded(total(slice(rows, 2 * rows)))
        out_refs[1][:, :columns] = codes
        out_refs[1][:, columns:] = exponents


def exchanged(value, distance):
    count = lax.axis_size("lat")
    return lax.ppermute(value, "lat", [(i, i ^ distance) for i in range(count)])


def moved(value, grp_turn, distance):
    count = lax.axis_size("lat")
    groups = lax.axis_size("grp")
    pairs = []
    for grp in range(groups):
        for i in range(count):
            pairs.append((grp * count + i, (grp ^ grp_turn) * count + (i ^ distance[grp])))
    return lax.ppermute(value, ("grp", "lat"), pairs)


def gathered(block, in_edge, cot_edge, prepare, bias):
    here = lax.axis_index("grp") == 0
    far = moved(block, 0, (8, 12))
    near = moved(block, 0, (4, 6))
    side = exchanged(block, 2)
    far, near, side, bias, in_edge, cot_edge = lax.optimization_barrier(
        (far, near, side, bias, in_edge, cot_edge)
    )
    far_side, far_other = exchanged(far, 2), moved(far, 1, (0, 0))
    near_other = moved(near, 1, (0, 0))
    far_side, near_other = lax.optimization_barrier((far_side, near_other))
    far_side_other = moved(far_side, 1, (0, 0))
    far_other, in_edge = lax.optimization_barrier((far_other, in_edge))
    upper_in = passed_along(in_edge, "lat", -1)
    upper_in, cot_edge = lax.optimization_barrier((upper_in, cot_edge))
    upper_cot = passed_along(cot_edge, "lat", -1)
    prepared = prepare(upper_in)
    shards = [block, side, near, near_other, far, far_other, far_side]
    swapped = [exchanged(shard, 1) for shard in shards]
    far_side_other, rest = lax.optimization_barrier((far_side_other, swapped + list(prepared)))
    swapped, prepared = rest[: len(swapped)], rest[len(swapped) :]
    shards += [far_side_other] + swapped + [exchanged(far_side_other, 1)]
    low = jnp.array([0, 2, 4, 6, 8, 12, 10, 14], jnp.int32)
    high = jnp.array([0, 2, 6, 4, 12, 8, 14, 10], jnp.int32)
    order = jnp.where(here, low, high)
    return tuple(shards), jnp.concatenate([order, order + 1]), prepared, upper_cot, bias


def slots_of(distances, steps):
    result = 0
    for step in steps:
        result = 2 * result + ((distances // step) & 1)
    return result


def fold(arrived, kept, last=False):
    rows, columns = kept.shape
    if last:
        outs = (jax.ShapeDtypeStruct((rows, columns), jnp.float32),)
    else:
        outs = (
            jax.ShapeDtypeStruct((rows // 2, columns), jnp.float32),
            jax.ShapeDtypeStruct((rows // 2, columns + 128), jnp.int16),
        )
    return call(fold_kernel, "fold", outs, (), (arrived, kept), flops=8 * rows * columns, vmem=16)


def call(kernel, name, outs, tables, operands, scratch=(), flops=0, vmem=40):
    size = sum(math.prod(o.shape) * o.dtype.itemsize for o in (*outs, *operands))
    return pl.pallas_call(
        kernel,
        out_shape=outs,
        in_specs=[pl.BlockSpec(memory_space=pltpu.SMEM)] * len(tables)
        + [pl.BlockSpec(memory_space=pltpu.VMEM)] * len(operands),
        out_specs=[pl.BlockSpec(memory_space=pltpu.VMEM)] * len(outs),
        scratch_shapes=list(scratch),
        compiler_params=pltpu.CompilerParams(vmem_limit_bytes=vmem * 1024 * 1024),
        cost_estimate=pl.CostEstimate(flops=flops, bytes_accessed=size, transcendentals=0),
        name=name,
    )(*tables, *operands)


def per_device(inputs, cotangent, idents, w_qkv, w_out, gain):
    lat_cells, lon_cells, width = inputs.shape
    half_rows = WIN_R // 2
    win = padded_rows()
    windows = (lat_cells // WIN_R) * (lon_cells // WIN_C)
    cells = windows * win
    places = jnp.asarray(window_places(lon_cells), jnp.bfloat16)

    def shape(*dims, dtype=jnp.bfloat16):
        return jax.ShapeDtypeStruct(dims, dtype)

    count = lax.axis_size("lat")
    me = lax.axis_index("lat")
    direct = count == 16 and lax.axis_size("grp") == 2 and width % (16 * count) == 0
    if direct:
        distances = jnp.arange(count, dtype=jnp.int32) ^ me
        to_slot = jnp.stack([slots_of(distances, route) for route in TABLES])
    else:
        to_slot = jnp.stack([jnp.arange(16, dtype=jnp.int32)] * len(TABLES))

    def prepare(upper_in):
        return call(
            prepare_kernel,
            "prepare",
            (shape(cells, width), shape(len(TABLES), width, cells)),
            (to_slot,),
            (inputs, upper_in, places),
            flops=2 * cells * width * lon_cells * WIN_R,
            vmem=16,
        )

    weights = jnp.pad(w_qkv, ((0, 0), (0, width))) + jnp.pad(w_out, ((0, 0), (3 * width, 0)))
    in_edge, cot_edge = inputs[:half_rows], cotangent[:half_rows]
    labels = to_windows(idents + 1)
    bias = jnp.where(labels[:, :, None] == labels[:, None, :], 0.0, HIDDEN).astype(jnp.float32)
    if direct:
        shards, order, (tokens, turned), upper_cot, bias = gathered(
            weights, in_edge, cot_edge, prepare, bias
        )
        into = order ^ me
    else:
        weights = lax.all_gather(weights, "lat", axis=0, tiled=True)
        shards = tuple(weights.reshape(16, width // 16, 4 * width))
        into = to_slot[0]
        tokens, turned = prepare(passed_along(in_edge, "lat", -1))
        upper_cot = passed_along(cot_edge, "lat", -1)

    qkv_full, out_full, qkv, probs, mixed = call(
        forward_kernel,
        "forward",
        (
            shape(width, 3 * width),
            shape(width, width),
            shape(cells, 3 * width),
            shape(windows, HEADS // GROUP, GROUP * win, win),
            shape(cells, width),
        ),
        (into,),
        (tokens, bias, *shards),
        flops=2 * cells * width * width * 4,
        vmem=20,
    )
    (cot,) = call(
        shift_kernel,
        "shift",
        (shape(cells, width),),
        (),
        (cotangent, upper_cot, places),
        flops=2 * cells * width * lon_cells * WIN_R,
        vmem=16,
    )
    normed, grad_proj, grad_mix = call(
        norm_kernel,
        "norm",
        (shape(cells, width),) * 3,
        (),
        (mixed, out_full, cot, gain[None]),
        flops=2 * cells * width * width * 2,
        vmem=16,
    )
    (lower_out,) = call(
        edge_kernel,
        "edge",
        (shape(half_rows, lon_cells, width),),
        (),
        (normed, places),
        flops=2 * cells * width * lon_cells * half_rows,
        vmem=16,
    )
    lower_out = passed_along(lower_out, "lat", 1)
    grad_cells, *grads = call(
        backward_kernel,
        "backward",
        (
            shape(cells, 3 * width),
            *[shape(width // 2, CHUNKS[at // 2] * width, dtype=jnp.float32) for at in range(2 * len(CHUNKS))],
        ),
        (to_slot,),
        (qkv, probs, mixed, grad_proj, grad_mix, turned),
        flops=2 * cells * width * width * 6,
        vmem=30,
    )
    lower_out, grad_cells, *grads = lax.optimization_barrier((lower_out, grad_cells, *grads))

    def finish(normed, grad_cells):
        return call(
            finish_kernel,
            "finish",
            (shape(*inputs.shape), shape(*inputs.shape), shape(half_rows, lon_cells, width)),
            (),
            (grad_cells, qkv_full, normed, inputs, cotangent, places),
            (pltpu.VMEM((cells, width), jnp.bfloat16),),
            flops=2 * cells * width * (3 * width + 2 * lon_cells * WIN_R),
            vmem=24,
        )

    if direct:
        pairs = [(exchanged(sent, 1), kept) for sent, kept in zip(grads[::2], grads[1::2])]
        pairs = [fold(arrived, kept) for arrived, kept in pairs]
        kept, sent = pairs[-1]
        sent, normed, grad_cells = lax.optimization_barrier((sent, normed, grad_cells))
        pairs[-1] = (kept, sent)
        output, grad_in, lower = finish(normed, grad_cells)
        for step in (1, 2, 3):
            pairs = [
                (exchanged(sent, route[step]), kept) for route, (kept, sent) in zip(ROUTES, pairs)
            ]
            if step in (1, 2):
                arrived, kept = pairs[0]
                arrived, lower = lax.optimization_barrier((arrived, lower))
                pairs[0] = (arrived, kept)
            pairs = [fold(arrived, kept, step == 3) for arrived, kept in pairs]
            if step == 1:
                lower = passed_along(lower, "lat", 1)
        pairs = [total for (total,) in pairs]
        quarters = [part for total in pairs for part in jnp.split(total, total.shape[1] // width, axis=1)]
        grad_out = quarters[0]
        grad_qkv = jnp.concatenate([quarters[place] for place in GRAD_PLACES], axis=1)
    else:
        whole = [jnp.concatenate([kept, sent]) for sent, kept in zip(grads[::2], grads[1::2])]
        both = lax.psum_scatter(jnp.concatenate(whole, axis=1), "lat", scatter_dimension=0, tiled=True)
        quarters = jnp.split(both, 4, axis=1)
        grad_out = quarters[0]
        grad_qkv = jnp.concatenate([quarters[place] for place in GRAD_PLACES], axis=1)
        output, grad_in, lower = finish(normed, grad_cells)
        lower = passed_along(lower, "lat", 1)

    def completed(result, lower):
        top = result[:half_rows].astype(jnp.float32) + lower.astype(jnp.float32)
        return result.at[:half_rows].set(top.astype(jnp.bfloat16))

    return (completed(output, lower_out), completed(grad_in, lower), grad_qkv, grad_out)


def solution(mesh):
    in_specs = (
        P(("grp", "lat"), None, None),
        P(("grp", "lat"), None, None),
        P(("grp", "lat"), None),
        P("lat", None),
        P("lat", None),
        P(),
    )
    out_specs = (
        P(("grp", "lat"), None, None),
        P(("grp", "lat"), None, None),
        P(("grp", "lat"), None),
        P(("grp", "lat"), None),
    )
    return jax.shard_map(
        per_device, mesh=mesh, in_specs=in_specs, out_specs=out_specs, check_vma=False
    )
```

```python
import math

import jax
import jax.numpy as jnp
import numpy as np
from jax import lax
from jax.experimental import pallas as pl
from jax.experimental.pallas import tpu as pltpu
from jax.sharding import PartitionSpec as P

HEADS = 8
WIN_R = 6
WIN_C = 12
EPS = 1e-05
HIDDEN = -1e30
STEPS = 32000.0
GRAD_PLACES = (3, 2, 1)
CHUNKS = (2, 1, 1)
ROUTES = ((1, 2, 4, 8), (1, 2, 4, 8), (1, 4, 8, 2))
TABLES = tuple(dict.fromkeys(ROUTES))
UNROLL = 9
GROUP = 4

NN = (((1,), (0,)), ((), ()))
NT = (((1,), (1,)), ((), ()))
TN = (((0,), (0,)), ((), ()))


def mxu(left, right, dims=NN):
    return lax.dot_general(left, right, dims, preferred_element_type=jnp.float32)


def passed_along(value, axis, steps):
    count = lax.axis_size(axis)
    first, last = (max(0, -steps), min(count, count - steps))
    return lax.ppermute(value, axis, [(source, source + steps) for source in range(first, last)])


def padded_rows():
    return -(-WIN_R * WIN_C // 16) * 16


def to_windows(field):
    lat_cells, lon_cells = field.shape
    field = field.reshape(lat_cells // WIN_R, WIN_R, lon_cells // WIN_C, WIN_C)
    field = field.transpose(0, 2, 1, 3).reshape(-1, WIN_R * WIN_C)
    return jnp.pad(field, ((0, 0), (0, padded_rows() - WIN_R * WIN_C)))


def window_places(lon_cells):
    win = padded_rows()
    places = np.zeros((WIN_R, lon_cells // WIN_C, win, lon_cells), np.float32)
    for row in range(WIN_R):
        for window in range(lon_cells // WIN_C):
            for column in range(WIN_C):
                source = (window * WIN_C + column + WIN_C // 2) % lon_cells
                places[row, window, row * WIN_C + column, source] = 1
    return places.reshape(WIN_R, -1, lon_cells)


def masked_heads(value, head_dim):
    head = lax.broadcasted_iota(jnp.int32, value.shape, 1) // head_dim
    zero = jnp.zeros_like(value)
    count = value.shape[1] // head_dim
    return jnp.concatenate([jnp.where(head == at, value, zero) for at in range(count)], axis=0)


def own_heads(stacked, head_dim):
    count = stacked.shape[1] // head_dim
    rows = stacked.shape[0] // count
    head = lax.broadcasted_iota(jnp.int32, (rows, stacked.shape[1]), 1) // head_dim
    result = stacked[:rows]
    for at in range(1, count):
        result = jnp.where(head == at, stacked[at * rows : (at + 1) * rows], result)
    return result


def turned_heads(stacked, count):
    rows = stacked.shape[0] // count
    return jnp.concatenate(
        [stacked[at * rows : (at + 1) * rows].T for at in range(count)], axis=0
    )


def shift_kernel(own_ref, halo_ref, places_ref, result_ref):
    half = halo_ref.shape[0]
    lat_cells = own_ref.shape[0]
    cells = places_ref.shape[1]
    for band in range(lat_cells // WIN_R):
        total = None
        for row in range(WIN_R):
            source = band * WIN_R + row + half
            field = own_ref[source] if source < lat_cells else halo_ref[source - lat_cells]
            term = mxu(places_ref[row], field)
            total = term if total is None else total + term
        result_ref[band * cells : (band + 1) * cells, :] = total.astype(jnp.bfloat16)


def window_loop(windows, body):
    lax.fori_loop(0, windows, body, 0, unroll=UNROLL if windows % UNROLL == 0 else 1)


def prepare_kernel(to_slot_ref, inputs_ref, halo_ref, places_ref, tokens_ref, turned_ref):
    shift_kernel(inputs_ref, halo_ref, places_ref, tokens_ref)
    chunks, blocks = to_slot_ref.shape
    depth = tokens_ref.shape[1] // blocks
    turned = tokens_ref[...].T
    for chunk in range(chunks):
        for block in range(blocks):
            rows = pl.ds(pl.multiple_of(to_slot_ref[chunk, block] * depth, depth), depth)
            turned_ref[chunk, rows, :] = turned[block * depth : (block + 1) * depth, :]


def finish_kernel(
    cells_ref, w_qkv_ref, normed_ref, inputs_ref, cot_ref, places_ref,
    output_ref, grad_in_ref, lower_ref, shift_ref,
):
    lat_cells = inputs_ref.shape[0]
    half = lower_ref.shape[0]
    count = places_ref.shape[1]
    shift_ref[...] = mxu(cells_ref[...], w_qkv_ref[...], NT).astype(jnp.bfloat16)
    for at, (value_ref, base_ref, result_ref) in enumerate(
        ((normed_ref, inputs_ref, output_ref), (shift_ref, cot_ref, grad_in_ref))
    ):
        result_ref[:half] = base_ref[:half]
        for band in range(lat_cells // WIN_R):
            value = value_ref[band * count : (band + 1) * count, :]
            for row in range(WIN_R):
                target = band * WIN_R + row + half
                if at == 0 and target >= lat_cells:
                    continue
                back = mxu(places_ref[row], value, TN)
                if target < lat_cells:
                    base = base_ref[target].astype(jnp.float32)
                    result_ref[target] = (base + back).astype(jnp.bfloat16)
                else:
                    lower_ref[target - lat_cells] = back.astype(jnp.bfloat16)


def forward_kernel(into_ref, x_ref, bias_ref, *rest):
    shard_refs, rest = rest[: into_ref.shape[0]], rest[into_ref.shape[0] :]
    w_qkv_ref, w_out_ref, qkv_ref, probs_ref, mixed_ref = rest
    windows, win = bias_ref.shape[:2]
    width = x_ref.shape[1]
    head_dim = width // HEADS
    group = GROUP * head_dim
    factor = head_dim ** (-0.5) * math.log2(math.e)

    blocks = into_ref.shape[0]
    depth = width // blocks
    for at, shard_ref in enumerate(shard_refs):
        rows = pl.ds(pl.multiple_of(into_ref[at] * depth, depth), depth)
        w_qkv_ref[rows, :] = shard_ref[:, : 3 * width]
        w_out_ref[rows, :] = shard_ref[:, 3 * width :]

    for part in range(3):
        columns = slice(part * width, (part + 1) * width)
        qkv_ref[:, columns] = mxu(x_ref[...], w_qkv_ref[:, columns]).astype(jnp.bfloat16)

    def attend(window, carry):
        rows = pl.ds(pl.multiple_of(window * win, 16), win)
        bias = bias_ref[window]
        for at in range(HEADS // GROUP):
            columns = slice(at * group, (at + 1) * group)
            queries = qkv_ref[rows, columns]
            keys = qkv_ref[rows, width + at * group : width + (at + 1) * group]
            values = qkv_ref[rows, 2 * width + at * group : 2 * width + (at + 1) * group]
            scores = mxu(masked_heads(keys, head_dim), queries, NT)
            scores = scores.reshape(GROUP, win, win) * factor + bias
            lifted = jnp.exp2(scores - jnp.max(scores, axis=1, keepdims=True))
            total = jnp.sum(lifted, axis=1, keepdims=True)
            probs = (lifted * (1.0 / total)).astype(jnp.bfloat16)
            probs = probs.reshape(GROUP * win, win)
            probs_ref[window, at] = probs
            mixed = own_heads(mxu(turned_heads(probs, GROUP), values), head_dim)
            mixed_ref[rows, columns] = mixed.astype(jnp.bfloat16)
        return carry

    window_loop(windows, attend)


def norm_kernel(
    mixed_ref, w_out_ref, cot_ref, gain_ref, normed_ref, grad_proj_ref, grad_mix_ref
):
    win = padded_rows()
    windows = mixed_ref.shape[0] // win
    gain = gain_ref[...]

    def normalise(window, carry):
        rows = pl.ds(pl.multiple_of(window * win, 16), win)
        projected = mxu(mixed_ref[rows, :], w_out_ref[...])
        center = projected - jnp.mean(projected, axis=-1, keepdims=True)
        inverse = lax.rsqrt(jnp.mean(center * center, axis=-1, keepdims=True) + EPS)
        normal = center * inverse
        normed_ref[rows, :] = (normal * gain).astype(jnp.bfloat16)
        scaled = cot_ref[rows, :].astype(jnp.float32) * gain
        grad_proj = (
            scaled
            - jnp.mean(scaled, axis=-1, keepdims=True)
            - normal * jnp.mean(scaled * normal, axis=-1, keepdims=True)
        ) * inverse
        grad_proj_ref[rows, :] = grad_proj.astype(jnp.bfloat16)
        return carry

    window_loop(windows, normalise)
    grad_mix_ref[...] = mxu(grad_proj_ref[...], w_out_ref[...], NT).astype(jnp.bfloat16)


def edge_kernel(value_ref, places_ref, lower_ref):
    half = lower_ref.shape[0]
    value = value_ref[value_ref.shape[0] - places_ref.shape[1] :, :]
    for row in range(half):
        back = mxu(places_ref[WIN_R - half + row], value, TN)
        lower_ref[row] = back.astype(jnp.bfloat16)


def backward_kernel(
    to_slot_ref, qkv_ref, probs_ref, mixed_ref, grad_proj_ref, grad_mix_ref, turned_ref,
    cells_ref, *grad_refs,
):
    windows, win = probs_ref.shape[0], probs_ref.shape[-1]
    width = grad_mix_ref.shape[1]
    head_dim = width // HEADS
    group = GROUP * head_dim
    scale = head_dim ** (-0.5)
    blocks = to_slot_ref.shape[1]
    depth = width // blocks
    half = width // 2
    sent_refs, kept_refs = grad_refs[::2], grad_refs[1::2]
    grad_out = mxu(mixed_ref[...], grad_proj_ref[...], TN)
    for block in range(blocks):
        slot = to_slot_ref[0, block]
        value = grad_out[block * depth : (block + 1) * depth, :]
        rows = pl.ds(pl.multiple_of(lax.rem(slot, blocks // 2) * depth, depth), depth)

        @pl.when(slot < blocks // 2)
        def _():
            kept_refs[0][rows, :width] = value

        @pl.when(slot >= blocks // 2)
        def _():
            sent_refs[0][rows, :width] = value

    def attend_back(window, carry):
        rows = pl.ds(pl.multiple_of(window * win, 16), win)
        for at in range(HEADS // GROUP):
            columns = slice(at * group, (at + 1) * group)
            key_columns = slice(width + at * group, width + (at + 1) * group)
            value_columns = slice(2 * width + at * group, 2 * width + (at + 1) * group)
            mix = grad_mix_ref[rows, columns]
            probs = probs_ref[window, at]
            float_probs = probs.astype(jnp.float32)
            grad_probs = mxu(masked_heads(qkv_ref[rows, value_columns], head_dim), mix, NT)
            product = (float_probs * grad_probs).reshape(GROUP, win, win)
            center = jnp.sum(product, axis=1, keepdims=True)
            grad_scores = scale * (product - float_probs.reshape(GROUP, win, win) * center)
            grad_scores = grad_scores.astype(jnp.bfloat16).reshape(GROUP * win, win)
            grad_values = own_heads(mxu(probs, mix), head_dim)
            grad_keys = own_heads(mxu(grad_scores, qkv_ref[rows, columns]), head_dim)
            turned = turned_heads(grad_scores, GROUP)
            grad_queries = own_heads(mxu(turned, qkv_ref[rows, key_columns]), head_dim)
            cells_ref[rows, columns] = grad_queries.astype(jnp.bfloat16)
            cells_ref[rows, key_columns] = grad_keys.astype(jnp.bfloat16)
            cells_ref[rows, value_columns] = grad_values.astype(jnp.bfloat16)
        return carry

    window_loop(windows, attend_back)

    for part, place in enumerate(GRAD_PLACES):
        columns = slice(part * width, (part + 1) * width)
        chunk = sum(place >= sum(CHUNKS[: at + 1]) for at in range(len(CHUNKS)))
        place -= sum(CHUNKS[:chunk])
        target = slice(place * width, (place + 1) * width)
        turned = turned_ref.at[TABLES.index(ROUTES[chunk])]
        sent_refs[chunk][:, target] = mxu(turned[half:, :], cells_ref[:, columns])
        kept_refs[chunk][:, target] = mxu(turned[:half, :], cells_ref[:, columns])


def coded(value):
    top = jnp.max(jnp.abs(value), axis=1, keepdims=True)
    exponent = jnp.ceil(jnp.log2(jnp.maximum(top, 1e-30)))
    codes = jnp.round(value * (jnp.exp2(-exponent) * STEPS)).astype(jnp.int32)
    exponents = jnp.broadcast_to(exponent, (value.shape[0], 128)).astype(jnp.int32)
    return codes.astype(jnp.int16), exponents.astype(jnp.int16)


def decoded(codes, exponents):
    exponent = exponents.astype(jnp.int32).astype(jnp.float32)[:, :1]
    return codes.astype(jnp.int32).astype(jnp.float32) * (jnp.exp2(exponent) * (1 / STEPS))


def fold_kernel(arrived_ref, kept_ref, *out_refs):
    columns = kept_ref.shape[1]
    rows = out_refs[0].shape[0]

    def total(part):
        arrived = arrived_ref[part, :columns]
        if arrived_ref.shape[1] > columns:
            arrived = decoded(arrived, arrived_ref[part, columns:])
        return kept_ref[part, :] + arrived

    out_refs[0][...] = total(slice(0, rows))
    if len(out_refs) > 1:
        codes, exponents = coded(total(slice(rows, 2 * rows)))
        out_refs[1][:, :columns] = codes
        out_refs[1][:, columns:] = exponents


def exchanged(value, distance):
    count = lax.axis_size("lat")
    return lax.ppermute(value, "lat", [(i, i ^ distance) for i in range(count)])


def moved(value, grp_turn, distance):
    count = lax.axis_size("lat")
    groups = lax.axis_size("grp")
    pairs = []
    for grp in range(groups):
        for i in range(count):
            pairs.append((grp * count + i, (grp ^ grp_turn) * count + (i ^ distance[grp])))
    return lax.ppermute(value, ("grp", "lat"), pairs)


def gathered(block, in_edge, cot_edge, prepare, bias):
    here = lax.axis_index("grp") == 0
    far = moved(block, 0, (8, 12))
    near = moved(block, 0, (4, 6))
    side = exchanged(block, 2)
    far, near, side, bias, in_edge, cot_edge = lax.optimization_barrier(
        (far, near, side, bias, in_edge, cot_edge)
    )
    far_side, far_other = exchanged(far, 2), moved(far, 1, (0, 0))
    near_other = moved(near, 1, (0, 0))
    far_side, near_other, in_edge = lax.optimization_barrier((far_side, near_other, in_edge))
    far_side_other = moved(far_side, 1, (0, 0))
    upper_in = passed_along(in_edge, "lat", -1)
    upper_in, cot_edge = lax.optimization_barrier((upper_in, cot_edge))
    upper_cot = passed_along(cot_edge, "lat", -1)
    prepared = prepare(upper_in)
    shards = [block, side, near, near_other, far, far_other, far_side]
    swapped = [exchanged(shard, 1) for shard in shards]
    far_side_other, rest = lax.optimization_barrier((far_side_other, swapped + list(prepared)))
    swapped, prepared = rest[: len(swapped)], rest[len(swapped) :]
    shards += [far_side_other] + swapped + [exchanged(far_side_other, 1)]
    low = jnp.array([0, 2, 4, 6, 8, 12, 10, 14], jnp.int32)
    high = jnp.array([0, 2, 6, 4, 12, 8, 14, 10], jnp.int32)
    order = jnp.where(here, low, high)
    return tuple(shards), jnp.concatenate([order, order + 1]), prepared, upper_cot, bias


def slots_of(distances, steps):
    result = 0
    for step in steps:
        result = 2 * result + ((distances // step) & 1)
    return result


def fold(arrived, kept, last=False):
    rows, columns = kept.shape
    if last:
        outs = (jax.ShapeDtypeStruct((rows, columns), jnp.float32),)
    else:
        outs = (
            jax.ShapeDtypeStruct((rows // 2, columns), jnp.float32),
            jax.ShapeDtypeStruct((rows // 2, columns + 128), jnp.int16),
        )
    return call(fold_kernel, "fold", outs, (), (arrived, kept), flops=8 * rows * columns, vmem=16)


def call(kernel, name, outs, tables, operands, scratch=(), flops=0, vmem=40):
    size = sum(math.prod(o.shape) * o.dtype.itemsize for o in (*outs, *operands))
    return pl.pallas_call(
        kernel,
        out_shape=outs,
        in_specs=[pl.BlockSpec(memory_space=pltpu.SMEM)] * len(tables)
        + [pl.BlockSpec(memory_space=pltpu.VMEM)] * len(operands),
        out_specs=[pl.BlockSpec(memory_space=pltpu.VMEM)] * len(outs),
        scratch_shapes=list(scratch),
        compiler_params=pltpu.CompilerParams(vmem_limit_bytes=vmem * 1024 * 1024),
        cost_estimate=pl.CostEstimate(flops=flops, bytes_accessed=size, transcendentals=0),
        name=name,
    )(*tables, *operands)


def per_device(inputs, cotangent, idents, w_qkv, w_out, gain):
    lat_cells, lon_cells, width = inputs.shape
    half_rows = WIN_R // 2
    win = padded_rows()
    windows = (lat_cells // WIN_R) * (lon_cells // WIN_C)
    cells = windows * win
    places = jnp.asarray(window_places(lon_cells), jnp.bfloat16)

    def shape(*dims, dtype=jnp.bfloat16):
        return jax.ShapeDtypeStruct(dims, dtype)

    count = lax.axis_size("lat")
    me = lax.axis_index("lat")
    direct = count == 16 and lax.axis_size("grp") == 2 and width % (16 * count) == 0
    if direct:
        distances = jnp.arange(count, dtype=jnp.int32) ^ me
        to_slot = jnp.stack([slots_of(distances, route) for route in TABLES])
    else:
        to_slot = jnp.stack([jnp.arange(16, dtype=jnp.int32)] * len(TABLES))

    def prepare(upper_in):
        return call(
            prepare_kernel,
            "prepare",
            (shape(cells, width), shape(len(TABLES), width, cells)),
            (to_slot,),
            (inputs, upper_in, places),
            flops=2 * cells * width * lon_cells * WIN_R,
            vmem=16,
        )

    weights = jnp.pad(w_qkv, ((0, 0), (0, width))) + jnp.pad(w_out, ((0, 0), (3 * width, 0)))
    in_edge, cot_edge = inputs[:half_rows], cotangent[:half_rows]
    labels = to_windows(idents + 1)
    bias = jnp.where(labels[:, :, None] == labels[:, None, :], 0.0, HIDDEN).astype(jnp.float32)
    if direct:
        shards, order, (tokens, turned), upper_cot, bias = gathered(
            weights, in_edge, cot_edge, prepare, bias
        )
        into = order ^ me
    else:
        weights = lax.all_gather(weights, "lat", axis=0, tiled=True)
        shards = tuple(weights.reshape(16, width // 16, 4 * width))
        into = to_slot[0]
        tokens, turned = prepare(passed_along(in_edge, "lat", -1))
        upper_cot = passed_along(cot_edge, "lat", -1)

    qkv_full, out_full, qkv, probs, mixed = call(
        forward_kernel,
        "forward",
        (
            shape(width, 3 * width),
            shape(width, width),
            shape(cells, 3 * width),
            shape(windows, HEADS // GROUP, GROUP * win, win),
            shape(cells, width),
        ),
        (into,),
        (tokens, bias, *shards),
        flops=2 * cells * width * width * 4,
        vmem=20,
    )
    (cot,) = call(
        shift_kernel,
        "shift",
        (shape(cells, width),),
        (),
        (cotangent, upper_cot, places),
        flops=2 * cells * width * lon_cells * WIN_R,
        vmem=16,
    )
    normed, grad_proj, grad_mix = call(
        norm_kernel,
        "norm",
        (shape(cells, width),) * 3,
        (),
        (mixed, out_full, cot, gain[None]),
        flops=2 * cells * width * width * 2,
        vmem=16,
    )
    (lower_out,) = call(
        edge_kernel,
        "edge",
        (shape(half_rows, lon_cells, width),),
        (),
        (normed, places),
        flops=2 * cells * width * lon_cells * half_rows,
        vmem=16,
    )
    lower_out = passed_along(lower_out, "lat", 1)
    grad_cells, *grads = call(
        backward_kernel,
        "backward",
        (
            shape(cells, 3 * width),
            *[shape(width // 2, CHUNKS[at // 2] * width, dtype=jnp.float32) for at in range(2 * len(CHUNKS))],
        ),
        (to_slot,),
        (qkv, probs, mixed, grad_proj, grad_mix, turned),
        flops=2 * cells * width * width * 6,
        vmem=30,
    )
    lower_out, grad_cells, *grads = lax.optimization_barrier((lower_out, grad_cells, *grads))

    def finish(normed, grad_cells):
        return call(
            finish_kernel,
            "finish",
            (shape(*inputs.shape), shape(*inputs.shape), shape(half_rows, lon_cells, width)),
            (),
            (grad_cells, qkv_full, normed, inputs, cotangent, places),
            (pltpu.VMEM((cells, width), jnp.bfloat16),),
            flops=2 * cells * width * (3 * width + 2 * lon_cells * WIN_R),
            vmem=24,
        )

    if direct:
        pairs = [(exchanged(sent, 1), kept) for sent, kept in zip(grads[::2], grads[1::2])]
        pairs = [fold(arrived, kept) for arrived, kept in pairs]
        kept, sent = pairs[-1]
        sent, normed, grad_cells = lax.optimization_barrier((sent, normed, grad_cells))
        pairs[-1] = (kept, sent)
        output, grad_in, lower = finish(normed, grad_cells)
        for step in (1, 2, 3):
            pairs = [
                (exchanged(sent, route[step]), kept) for route, (kept, sent) in zip(ROUTES, pairs)
            ]
            if step != 2:
                at = 0 if step == 1 else -1
                arrived, kept = pairs[at]
                arrived, lower = lax.optimization_barrier((arrived, lower))
                pairs[at] = (arrived, kept)
            pairs = [fold(arrived, kept, step == 3) for arrived, kept in pairs]
            if step == 2:
                lower, _ = lax.optimization_barrier((lower, pairs[0][0]))
                lower = passed_along(lower, "lat", 1)
        pairs = [total for (total,) in pairs]
        quarters = [part for total in pairs for part in jnp.split(total, total.shape[1] // width, axis=1)]
        grad_out = quarters[0]
        grad_qkv = jnp.concatenate([quarters[place] for place in GRAD_PLACES], axis=1)
    else:
        whole = [jnp.concatenate([kept, sent]) for sent, kept in zip(grads[::2], grads[1::2])]
        both = lax.psum_scatter(jnp.concatenate(whole, axis=1), "lat", scatter_dimension=0, tiled=True)
        quarters = jnp.split(both, 4, axis=1)
        grad_out = quarters[0]
        grad_qkv = jnp.concatenate([quarters[place] for place in GRAD_PLACES], axis=1)
        output, grad_in, lower = finish(normed, grad_cells)
        lower = passed_along(lower, "lat", 1)

    def completed(result, lower):
        top = result[:half_rows].astype(jnp.float32) + lower.astype(jnp.float32)
        return result.at[:half_rows].set(top.astype(jnp.bfloat16))

    return (completed(output, lower_out), completed(grad_in, lower), grad_qkv, grad_out)


def solution(mesh):
    in_specs = (
        P(("grp", "lat"), None, None),
        P(("grp", "lat"), None, None),
        P(("grp", "lat"), None),
        P("lat", None),
        P("lat", None),
        P(),
    )
    out_specs = (
        P(("grp", "lat"), None, None),
        P(("grp", "lat"), None, None),
        P(("grp", "lat"), None),
        P(("grp", "lat"), None),
    )
    return jax.shard_map(
        per_device, mesh=mesh, in_specs=in_specs, out_specs=out_specs, check_vma=False
    )
```

```python
import math

import jax
import jax.numpy as jnp
import numpy as np
from jax import lax
from jax.experimental import pallas as pl
from jax.experimental.pallas import tpu as pltpu
from jax.sharding import PartitionSpec as P

HEADS = 8
WIN_R = 6
WIN_C = 12
EPS = 1e-05
HIDDEN = -1e30
STEPS = 32000.0
GRAD_PLACES = (3, 2, 1)
CHUNKS = (2, 1, 1)
ROUTES = ((1, 2, 4, 8), (1, 2, 4, 8), (1, 4, 8, 2))
TURNS = (0, 1, 2, 2, 0, 1, 2, 0, 1, 2, 0, 1)
FINISH_AFTER, HALO_AFTER, HALO_DUE = 2, 6, 10
TABLES = tuple(dict.fromkeys(ROUTES))
UNROLL = 9
GROUP = 4

NN = (((1,), (0,)), ((), ()))
NT = (((1,), (1,)), ((), ()))
TN = (((0,), (0,)), ((), ()))


def mxu(left, right, dims=NN):
    return lax.dot_general(left, right, dims, preferred_element_type=jnp.float32)


def passed_along(value, axis, steps):
    count = lax.axis_size(axis)
    first, last = (max(0, -steps), min(count, count - steps))
    return lax.ppermute(value, axis, [(source, source + steps) for source in range(first, last)])


def padded_rows():
    return -(-WIN_R * WIN_C // 16) * 16


def to_windows(field):
    lat_cells, lon_cells = field.shape
    field = field.reshape(lat_cells // WIN_R, WIN_R, lon_cells // WIN_C, WIN_C)
    field = field.transpose(0, 2, 1, 3).reshape(-1, WIN_R * WIN_C)
    return jnp.pad(field, ((0, 0), (0, padded_rows() - WIN_R * WIN_C)))


def window_places(lon_cells):
    win = padded_rows()
    places = np.zeros((WIN_R, lon_cells // WIN_C, win, lon_cells), np.float32)
    for row in range(WIN_R):
        for window in range(lon_cells // WIN_C):
            for column in range(WIN_C):
                source = (window * WIN_C + column + WIN_C // 2) % lon_cells
                places[row, window, row * WIN_C + column, source] = 1
    return places.reshape(WIN_R, -1, lon_cells)


def masked_heads(value, head_dim):
    head = lax.broadcasted_iota(jnp.int32, value.shape, 1) // head_dim
    zero = jnp.zeros_like(value)
    count = value.shape[1] // head_dim
    return jnp.concatenate([jnp.where(head == at, value, zero) for at in range(count)], axis=0)


def own_heads(stacked, head_dim):
    count = stacked.shape[1] // head_dim
    rows = stacked.shape[0] // count
    head = lax.broadcasted_iota(jnp.int32, (rows, stacked.shape[1]), 1) // head_dim
    result = stacked[:rows]
    for at in range(1, count):
        result = jnp.where(head == at, stacked[at * rows : (at + 1) * rows], result)
    return result


def turned_heads(stacked, count):
    rows = stacked.shape[0] // count
    return jnp.concatenate(
        [stacked[at * rows : (at + 1) * rows].T for at in range(count)], axis=0
    )


def shift_kernel(own_ref, halo_ref, places_ref, result_ref):
    half = halo_ref.shape[0]
    lat_cells = own_ref.shape[0]
    cells = places_ref.shape[1]
    for band in range(lat_cells // WIN_R):
        total = None
        for row in range(WIN_R):
            source = band * WIN_R + row + half
            field = own_ref[source] if source < lat_cells else halo_ref[source - lat_cells]
            term = mxu(places_ref[row], field)
            total = term if total is None else total + term
        result_ref[band * cells : (band + 1) * cells, :] = total.astype(jnp.bfloat16)


def window_loop(windows, body):
    lax.fori_loop(0, windows, body, 0, unroll=UNROLL if windows % UNROLL == 0 else 1)


def prepare_kernel(
    to_slot_ref, inputs_ref, cot_ref, halo_ref, places_ref, tokens_ref, turned_ref, cot_tokens_ref
):
    half = halo_ref.shape[0] // 2
    shift_kernel(inputs_ref, halo_ref.at[:half], places_ref, tokens_ref)
    shift_kernel(cot_ref, halo_ref.at[half:], places_ref, cot_tokens_ref)
    chunks, blocks = to_slot_ref.shape
    depth = tokens_ref.shape[1] // blocks
    turned = tokens_ref[...].T
    for chunk in range(chunks):
        for block in range(blocks):
            rows = pl.ds(pl.multiple_of(to_slot_ref[chunk, block] * depth, depth), depth)
            turned_ref[chunk, rows, :] = turned[block * depth : (block + 1) * depth, :]


def finish_kernel(
    cells_ref, w_qkv_ref, normed_ref, inputs_ref, cot_ref, places_ref,
    output_ref, grad_in_ref, lower_ref, shift_ref,
):
    lat_cells = inputs_ref.shape[0]
    half = lower_ref.shape[0]
    count = places_ref.shape[1]
    shift_ref[...] = mxu(cells_ref[...], w_qkv_ref[...], NT).astype(jnp.bfloat16)
    for at, (value_ref, base_ref, result_ref) in enumerate(
        ((normed_ref, inputs_ref, output_ref), (shift_ref, cot_ref, grad_in_ref))
    ):
        result_ref[:half] = base_ref[:half]
        for band in range(lat_cells // WIN_R):
            value = value_ref[band * count : (band + 1) * count, :]
            for row in range(WIN_R):
                target = band * WIN_R + row + half
                if at == 0 and target >= lat_cells:
                    continue
                back = mxu(places_ref[row], value, TN)
                if target < lat_cells:
                    base = base_ref[target].astype(jnp.float32)
                    result_ref[target] = (base + back).astype(jnp.bfloat16)
                else:
                    lower_ref[target - lat_cells] = back.astype(jnp.bfloat16)


def forward_kernel(into_ref, x_ref, bias_ref, *rest):
    shard_refs, rest = rest[: into_ref.shape[0]], rest[into_ref.shape[0] :]
    w_qkv_ref, w_out_ref, qkv_ref, probs_ref, mixed_ref = rest
    windows, win = bias_ref.shape[:2]
    width = x_ref.shape[1]
    head_dim = width // HEADS
    group = GROUP * head_dim
    factor = head_dim ** (-0.5) * math.log2(math.e)

    blocks = into_ref.shape[0]
    depth = width // blocks
    for at, shard_ref in enumerate(shard_refs):
        rows = pl.ds(pl.multiple_of(into_ref[at] * depth, depth), depth)
        w_qkv_ref[rows, :] = shard_ref[:, : 3 * width]
        w_out_ref[rows, :] = shard_ref[:, 3 * width :]

    for part in range(3):
        columns = slice(part * width, (part + 1) * width)
        qkv_ref[:, columns] = mxu(x_ref[...], w_qkv_ref[:, columns]).astype(jnp.bfloat16)

    def attend(window, carry):
        rows = pl.ds(pl.multiple_of(window * win, 16), win)
        bias = bias_ref[window]
        for at in range(HEADS // GROUP):
            columns = slice(at * group, (at + 1) * group)
            queries = qkv_ref[rows, columns]
            keys = qkv_ref[rows, width + at * group : width + (at + 1) * group]
            values = qkv_ref[rows, 2 * width + at * group : 2 * width + (at + 1) * group]
            scores = mxu(masked_heads(keys, head_dim), queries, NT)
            scores = scores.reshape(GROUP, win, win) * factor + bias
            lifted = jnp.exp2(scores - jnp.max(scores, axis=1, keepdims=True))
            total = jnp.sum(lifted, axis=1, keepdims=True)
            probs = (lifted * (1.0 / total)).astype(jnp.bfloat16)
            probs = probs.reshape(GROUP * win, win)
            probs_ref[window, at] = probs
            mixed = own_heads(mxu(turned_heads(probs, GROUP), values), head_dim)
            mixed_ref[rows, columns] = mixed.astype(jnp.bfloat16)
        return carry

    window_loop(windows, attend)


def norm_kernel(
    mixed_ref, w_out_ref, cot_ref, gain_ref, normed_ref, grad_proj_ref, grad_mix_ref
):
    win = padded_rows()
    windows = mixed_ref.shape[0] // win
    gain = gain_ref[...]

    def normalise(window, carry):
        rows = pl.ds(pl.multiple_of(window * win, 16), win)
        projected = mxu(mixed_ref[rows, :], w_out_ref[...])
        center = projected - jnp.mean(projected, axis=-1, keepdims=True)
        inverse = lax.rsqrt(jnp.mean(center * center, axis=-1, keepdims=True) + EPS)
        normal = center * inverse
        normed_ref[rows, :] = (normal * gain).astype(jnp.bfloat16)
        scaled = cot_ref[rows, :].astype(jnp.float32) * gain
        grad_proj = (
            scaled
            - jnp.mean(scaled, axis=-1, keepdims=True)
            - normal * jnp.mean(scaled * normal, axis=-1, keepdims=True)
        ) * inverse
        grad_proj_ref[rows, :] = grad_proj.astype(jnp.bfloat16)
        return carry

    window_loop(windows, normalise)
    grad_mix_ref[...] = mxu(grad_proj_ref[...], w_out_ref[...], NT).astype(jnp.bfloat16)


def edge_kernel(value_ref, places_ref, lower_ref):
    half = lower_ref.shape[0]
    value = value_ref[value_ref.shape[0] - places_ref.shape[1] :, :]
    for row in range(half):
        back = mxu(places_ref[WIN_R - half + row], value, TN)
        lower_ref[row] = back.astype(jnp.bfloat16)


def backward_kernel(
    to_slot_ref, qkv_ref, probs_ref, mixed_ref, grad_proj_ref, grad_mix_ref, turned_ref,
    cells_ref, *grad_refs,
):
    windows, win = probs_ref.shape[0], probs_ref.shape[-1]
    width = grad_mix_ref.shape[1]
    head_dim = width // HEADS
    group = GROUP * head_dim
    scale = head_dim ** (-0.5)
    blocks = to_slot_ref.shape[1]
    depth = width // blocks
    half = width // 2
    sent_refs, kept_refs = grad_refs[::2], grad_refs[1::2]
    grad_out = mxu(mixed_ref[...], grad_proj_ref[...], TN)
    for block in range(blocks):
        slot = to_slot_ref[0, block]
        value = grad_out[block * depth : (block + 1) * depth, :]
        rows = pl.ds(pl.multiple_of(lax.rem(slot, blocks // 2) * depth, depth), depth)

        @pl.when(slot < blocks // 2)
        def _():
            kept_refs[0][rows, :width] = value

        @pl.when(slot >= blocks // 2)
        def _():
            sent_refs[0][rows, :width] = value

    def attend_back(window, carry):
        rows = pl.ds(pl.multiple_of(window * win, 16), win)
        for at in range(HEADS // GROUP):
            columns = slice(at * group, (at + 1) * group)
            key_columns = slice(width + at * group, width + (at + 1) * group)
            value_columns = slice(2 * width + at * group, 2 * width + (at + 1) * group)
            mix = grad_mix_ref[rows, columns]
            probs = probs_ref[window, at]
            float_probs = probs.astype(jnp.float32)
            grad_probs = mxu(masked_heads(qkv_ref[rows, value_columns], head_dim), mix, NT)
            product = (float_probs * grad_probs).reshape(GROUP, win, win)
            center = jnp.sum(product, axis=1, keepdims=True)
            grad_scores = scale * (product - float_probs.reshape(GROUP, win, win) * center)
            grad_scores = grad_scores.astype(jnp.bfloat16).reshape(GROUP * win, win)
            grad_values = own_heads(mxu(probs, mix), head_dim)
            grad_keys = own_heads(mxu(grad_scores, qkv_ref[rows, columns]), head_dim)
            turned = turned_heads(grad_scores, GROUP)
            grad_queries = own_heads(mxu(turned, qkv_ref[rows, key_columns]), head_dim)
            cells_ref[rows, columns] = grad_queries.astype(jnp.bfloat16)
            cells_ref[rows, key_columns] = grad_keys.astype(jnp.bfloat16)
            cells_ref[rows, value_columns] = grad_values.astype(jnp.bfloat16)
        return carry

    window_loop(windows, attend_back)

    for part, place in enumerate(GRAD_PLACES):
        columns = slice(part * width, (part + 1) * width)
        chunk = sum(place >= sum(CHUNKS[: at + 1]) for at in range(len(CHUNKS)))
        place -= sum(CHUNKS[:chunk])
        target = slice(place * width, (place + 1) * width)
        turned = turned_ref.at[TABLES.index(ROUTES[chunk])]
        sent_refs[chunk][:, target] = mxu(turned[half:, :], cells_ref[:, columns])
        kept_refs[chunk][:, target] = mxu(turned[:half, :], cells_ref[:, columns])


def coded(value):
    top = jnp.max(jnp.abs(value), axis=1, keepdims=True)
    exponent = jnp.ceil(jnp.log2(jnp.maximum(top, 1e-30)))
    codes = jnp.round(value * (jnp.exp2(-exponent) * STEPS)).astype(jnp.int32)
    exponents = jnp.broadcast_to(exponent, (value.shape[0], 128)).astype(jnp.int32)
    return codes.astype(jnp.int16), exponents.astype(jnp.int16)


def decoded(codes, exponents):
    exponent = exponents.astype(jnp.int32).astype(jnp.float32)[:, :1]
    return codes.astype(jnp.int32).astype(jnp.float32) * (jnp.exp2(exponent) * (1 / STEPS))


def fold_kernel(arrived_ref, kept_ref, *out_refs):
    columns = kept_ref.shape[1]
    rows = out_refs[0].shape[0]

    def total(part):
        arrived = arrived_ref[part, :columns]
        if arrived_ref.shape[1] > columns:
            arrived = decoded(arrived, arrived_ref[part, columns:])
        return kept_ref[part, :] + arrived

    out_refs[0][...] = total(slice(0, rows))
    if len(out_refs) > 1:
        codes, exponents = coded(total(slice(rows, 2 * rows)))
        out_refs[1][:, :columns] = codes
        out_refs[1][:, columns:] = exponents


def exchanged(value, distance):
    count = lax.axis_size("lat")
    return lax.ppermute(value, "lat", [(i, i ^ distance) for i in range(count)])


def moved(value, grp_turn, distance):
    count = lax.axis_size("lat")
    groups = lax.axis_size("grp")
    pairs = []
    for grp in range(groups):
        for i in range(count):
            pairs.append((grp * count + i, (grp ^ grp_turn) * count + (i ^ distance[grp])))
    return lax.ppermute(value, ("grp", "lat"), pairs)


def gathered(block, halo, prepare, bias):
    here = lax.axis_index("grp") == 0
    far = moved(block, 0, (8, 12))
    near = moved(block, 0, (4, 6))
    side = exchanged(block, 2)
    halo = passed_along(halo, "lat", -1)
    far, near, side, bias, halo = lax.optimization_barrier((far, near, side, bias, halo))
    far_side, far_other = exchanged(far, 2), moved(far, 1, (0, 0))
    near_other = moved(near, 1, (0, 0))
    far_side, near_other, *prepared = lax.optimization_barrier(
        (far_side, near_other, *prepare(halo))
    )
    far_side_other = moved(far_side, 1, (0, 0))
    shards = [block, side, near, near_other, far, far_other, far_side]
    swapped = [exchanged(shard, 1) for shard in shards]
    far_side_other, swapped = lax.optimization_barrier((far_side_other, swapped))
    shards += [far_side_other] + swapped + [exchanged(far_side_other, 1)]
    low = jnp.array([0, 2, 4, 6, 8, 12, 10, 14], jnp.int32)
    high = jnp.array([0, 2, 6, 4, 12, 8, 14, 10], jnp.int32)
    order = jnp.where(here, low, high)
    return tuple(shards), jnp.concatenate([order, order + 1]), prepared, bias


def slots_of(distances, steps):
    result = 0
    for step in steps:
        result = 2 * result + ((distances // step) & 1)
    return result


def fold(arrived, kept, last=False):
    rows, columns = kept.shape
    if last:
        outs = (jax.ShapeDtypeStruct((rows, columns), jnp.float32),)
    else:
        outs = (
            jax.ShapeDtypeStruct((rows // 2, columns), jnp.float32),
            jax.ShapeDtypeStruct((rows // 2, columns + 128), jnp.int16),
        )
    return call(fold_kernel, "fold", outs, (), (arrived, kept), flops=8 * rows * columns, vmem=16)


def call(kernel, name, outs, tables, operands, scratch=(), flops=0, vmem=40):
    size = sum(math.prod(o.shape) * o.dtype.itemsize for o in (*outs, *operands))
    return pl.pallas_call(
        kernel,
        out_shape=outs,
        in_specs=[pl.BlockSpec(memory_space=pltpu.SMEM)] * len(tables)
        + [pl.BlockSpec(memory_space=pltpu.VMEM)] * len(operands),
        out_specs=[pl.BlockSpec(memory_space=pltpu.VMEM)] * len(outs),
        scratch_shapes=list(scratch),
        compiler_params=pltpu.CompilerParams(vmem_limit_bytes=vmem * 1024 * 1024),
        cost_estimate=pl.CostEstimate(flops=flops, bytes_accessed=size, transcendentals=0),
        name=name,
    )(*tables, *operands)


def per_device(inputs, cotangent, idents, w_qkv, w_out, gain):
    lat_cells, lon_cells, width = inputs.shape
    half_rows = WIN_R // 2
    win = padded_rows()
    windows = (lat_cells // WIN_R) * (lon_cells // WIN_C)
    cells = windows * win
    places = jnp.asarray(window_places(lon_cells), jnp.bfloat16)

    def shape(*dims, dtype=jnp.bfloat16):
        return jax.ShapeDtypeStruct(dims, dtype)

    count = lax.axis_size("lat")
    me = lax.axis_index("lat")
    direct = count == 16 and lax.axis_size("grp") == 2 and width % (16 * count) == 0
    if direct:
        distances = jnp.arange(count, dtype=jnp.int32) ^ me
        to_slot = jnp.stack([slots_of(distances, route) for route in TABLES])
    else:
        to_slot = jnp.stack([jnp.arange(16, dtype=jnp.int32)] * len(TABLES))

    def prepare(halo):
        return call(
            prepare_kernel,
            "prepare",
            (shape(cells, width), shape(len(TABLES), width, cells), shape(cells, width)),
            (to_slot,),
            (inputs, cotangent, halo, places),
            flops=4 * cells * width * lon_cells * WIN_R,
            vmem=20,
        )

    weights = jnp.pad(w_qkv, ((0, 0), (0, width))) + jnp.pad(w_out, ((0, 0), (3 * width, 0)))
    halo = jnp.concatenate([inputs[:half_rows], cotangent[:half_rows]])
    labels = to_windows(idents + 1)
    bias = jnp.where(labels[:, :, None] == labels[:, None, :], 0.0, HIDDEN).astype(jnp.float32)
    if direct:
        shards, order, (tokens, turned, cot), bias = gathered(weights, halo, prepare, bias)
        into = order ^ me
    else:
        weights = lax.all_gather(weights, "lat", axis=0, tiled=True)
        shards = tuple(weights.reshape(16, width // 16, 4 * width))
        into = to_slot[0]
        tokens, turned, cot = prepare(passed_along(halo, "lat", -1))

    qkv_full, out_full, qkv, probs, mixed = call(
        forward_kernel,
        "forward",
        (
            shape(width, 3 * width),
            shape(width, width),
            shape(cells, 3 * width),
            shape(windows, HEADS // GROUP, GROUP * win, win),
            shape(cells, width),
        ),
        (into,),
        (tokens, bias, *shards),
        flops=2 * cells * width * width * 4,
        vmem=20,
    )
    normed, grad_proj, grad_mix = call(
        norm_kernel,
        "norm",
        (shape(cells, width),) * 3,
        (),
        (mixed, out_full, cot, gain[None]),
        flops=2 * cells * width * width * 2,
        vmem=16,
    )
    (lower_out,) = call(
        edge_kernel,
        "edge",
        (shape(half_rows, lon_cells, width),),
        (),
        (normed, places),
        flops=2 * cells * width * lon_cells * half_rows,
        vmem=16,
    )
    lower_out = passed_along(lower_out, "lat", 1)
    grad_cells, *grads = call(
        backward_kernel,
        "backward",
        (
            shape(cells, 3 * width),
            *[shape(width // 2, CHUNKS[at // 2] * width, dtype=jnp.float32) for at in range(2 * len(CHUNKS))],
        ),
        (to_slot,),
        (qkv, probs, mixed, grad_proj, grad_mix, turned),
        flops=2 * cells * width * width * 6,
        vmem=30,
    )
    lower_out, grad_cells, *grads = lax.optimization_barrier((lower_out, grad_cells, *grads))

    def finish(normed, grad_cells):
        return call(
            finish_kernel,
            "finish",
            (shape(*inputs.shape), shape(*inputs.shape), shape(half_rows, lon_cells, width)),
            (),
            (grad_cells, qkv_full, normed, inputs, cotangent, places),
            (pltpu.VMEM((cells, width), jnp.bfloat16),),
            flops=2 * cells * width * (3 * width + 2 * lon_cells * WIN_R),
            vmem=24,
        )

    if direct:
        sent, kept, steps = list(grads[::2]), list(grads[1::2]), [0] * len(CHUNKS)
        arrived = [exchanged(value, 1) for value in sent]
        done = kept[0]
        for turn, at in enumerate(TURNS):
            step = steps[at]
            arrived[at], done = lax.optimization_barrier((arrived[at], done))
            if turn == HALO_DUE:
                arrived[at], lower = lax.optimization_barrier((arrived[at], lower))
            if step == 3:
                (kept[at],) = fold(arrived[at], kept[at], True)
            else:
                kept[at], sent[at] = fold(arrived[at], kept[at])
                arrived[at] = exchanged(sent[at], ROUTES[at][step + 1])
            steps[at] += 1
            done = kept[at]
            if turn == FINISH_AFTER:
                done, normed, grad_cells = lax.optimization_barrier((done, normed, grad_cells))
                output, grad_in, lower = finish(normed, grad_cells)
                done, lower = lax.optimization_barrier((done, lower))
            if turn == HALO_AFTER:
                done, lower = lax.optimization_barrier((done, lower))
                lower = passed_along(lower, "lat", 1)
        pairs = kept
        quarters = [part for total in pairs for part in jnp.split(total, total.shape[1] // width, axis=1)]
        grad_out = quarters[0]
        grad_qkv = jnp.concatenate([quarters[place] for place in GRAD_PLACES], axis=1)
    else:
        whole = [jnp.concatenate([kept, sent]) for sent, kept in zip(grads[::2], grads[1::2])]
        both = lax.psum_scatter(jnp.concatenate(whole, axis=1), "lat", scatter_dimension=0, tiled=True)
        quarters = jnp.split(both, 4, axis=1)
        grad_out = quarters[0]
        grad_qkv = jnp.concatenate([quarters[place] for place in GRAD_PLACES], axis=1)
        output, grad_in, lower = finish(normed, grad_cells)
        lower = passed_along(lower, "lat", 1)

    def completed(result, lower):
        top = result[:half_rows].astype(jnp.float32) + lower.astype(jnp.float32)
        return result.at[:half_rows].set(top.astype(jnp.bfloat16))

    return (completed(output, lower_out), completed(grad_in, lower), grad_qkv, grad_out)


def solution(mesh):
    in_specs = (
        P(("grp", "lat"), None, None),
        P(("grp", "lat"), None, None),
        P(("grp", "lat"), None),
        P("lat", None),
        P("lat", None),
        P(),
    )
    out_specs = (
        P(("grp", "lat"), None, None),
        P(("grp", "lat"), None, None),
        P(("grp", "lat"), None),
        P(("grp", "lat"), None),
    )
    return jax.shard_map(
        per_device, mesh=mesh, in_specs=in_specs, out_specs=out_specs, check_vma=False
    )
```

```python
import math

import jax
import jax.numpy as jnp
import numpy as np
from jax import lax
from jax.experimental import pallas as pl
from jax.experimental.pallas import tpu as pltpu
from jax.sharding import PartitionSpec as P

HEADS = 8
WIN_R = 6
WIN_C = 12
EPS = 1e-05
HIDDEN = -1e30
STEPS = 32000.0
GRAD_PLACES = (3, 2, 1)
CHUNKS = (2, 1, 1)
ROUTES = ((1, 2, 4, 8), (1, 2, 4, 8), (1, 4, 8, 2))
TABLES = tuple(dict.fromkeys(ROUTES))
UNROLL = 9
GROUP = 4

NN = (((1,), (0,)), ((), ()))
NT = (((1,), (1,)), ((), ()))
TN = (((0,), (0,)), ((), ()))


def mxu(left, right, dims=NN):
    return lax.dot_general(left, right, dims, preferred_element_type=jnp.float32)


def passed_along(value, axis, steps):
    count = lax.axis_size(axis)
    first, last = (max(0, -steps), min(count, count - steps))
    return lax.ppermute(value, axis, [(source, source + steps) for source in range(first, last)])


def padded_rows():
    return -(-WIN_R * WIN_C // 16) * 16


def to_windows(field):
    lat_cells, lon_cells = field.shape
    field = field.reshape(lat_cells // WIN_R, WIN_R, lon_cells // WIN_C, WIN_C)
    field = field.transpose(0, 2, 1, 3).reshape(-1, WIN_R * WIN_C)
    return jnp.pad(field, ((0, 0), (0, padded_rows() - WIN_R * WIN_C)))


def window_places(lon_cells):
    win = padded_rows()
    places = np.zeros((WIN_R, lon_cells // WIN_C, win, lon_cells), np.float32)
    for row in range(WIN_R):
        for window in range(lon_cells // WIN_C):
            for column in range(WIN_C):
                source = (window * WIN_C + column + WIN_C // 2) % lon_cells
                places[row, window, row * WIN_C + column, source] = 1
    return places.reshape(WIN_R, -1, lon_cells)


def masked_heads(value, head_dim):
    head = lax.broadcasted_iota(jnp.int32, value.shape, 1) // head_dim
    zero = jnp.zeros_like(value)
    count = value.shape[1] // head_dim
    return jnp.concatenate([jnp.where(head == at, value, zero) for at in range(count)], axis=0)


def own_heads(stacked, head_dim):
    count = stacked.shape[1] // head_dim
    rows = stacked.shape[0] // count
    head = lax.broadcasted_iota(jnp.int32, (rows, stacked.shape[1]), 1) // head_dim
    result = stacked[:rows]
    for at in range(1, count):
        result = jnp.where(head == at, stacked[at * rows : (at + 1) * rows], result)
    return result


def turned_heads(stacked, count):
    rows = stacked.shape[0] // count
    return jnp.concatenate(
        [stacked[at * rows : (at + 1) * rows].T for at in range(count)], axis=0
    )


def shift_kernel(own_ref, halo_ref, places_ref, result_ref):
    half = halo_ref.shape[0]
    lat_cells = own_ref.shape[0]
    cells = places_ref.shape[1]
    for band in range(lat_cells // WIN_R):
        total = None
        for row in range(WIN_R):
            source = band * WIN_R + row + half
            field = own_ref[source] if source < lat_cells else halo_ref[source - lat_cells]
            term = mxu(places_ref[row], field)
            total = term if total is None else total + term
        result_ref[band * cells : (band + 1) * cells, :] = total.astype(jnp.bfloat16)


def window_loop(windows, body):
    lax.fori_loop(0, windows, body, 0, unroll=UNROLL if windows % UNROLL == 0 else 1)


def prepare_kernel(to_slot_ref, inputs_ref, halo_ref, places_ref, tokens_ref, turned_ref):
    shift_kernel(inputs_ref, halo_ref, places_ref, tokens_ref)
    chunks, blocks = to_slot_ref.shape
    depth = tokens_ref.shape[1] // blocks
    turned = tokens_ref[...].T
    for chunk in range(chunks):
        for block in range(blocks):
            rows = pl.ds(pl.multiple_of(to_slot_ref[chunk, block] * depth, depth), depth)
            turned_ref[chunk, rows, :] = turned[block * depth : (block + 1) * depth, :]


def finish_kernel(
    cells_ref, w_qkv_ref, normed_ref, inputs_ref, cot_ref, places_ref,
    output_ref, grad_in_ref, lower_ref, shift_ref,
):
    lat_cells = inputs_ref.shape[0]
    half = lower_ref.shape[0]
    count = places_ref.shape[1]
    shift_ref[...] = mxu(cells_ref[...], w_qkv_ref[...], NT).astype(jnp.bfloat16)
    for at, (value_ref, base_ref, result_ref) in enumerate(
        ((normed_ref, inputs_ref, output_ref), (shift_ref, cot_ref, grad_in_ref))
    ):
        result_ref[:half] = base_ref[:half]
        for band in range(lat_cells // WIN_R):
            value = value_ref[band * count : (band + 1) * count, :]
            for row in range(WIN_R):
                target = band * WIN_R + row + half
                if at == 0 and target >= lat_cells:
                    continue
                back = mxu(places_ref[row], value, TN)
                if target < lat_cells:
                    base = base_ref[target].astype(jnp.float32)
                    result_ref[target] = (base + back).astype(jnp.bfloat16)
                else:
                    lower_ref[target - lat_cells] = back.astype(jnp.bfloat16)


def forward_kernel(into_ref, x_ref, bias_ref, *rest):
    shard_refs, rest = rest[: into_ref.shape[0]], rest[into_ref.shape[0] :]
    w_qkv_ref, w_out_ref, qkv_ref, probs_ref, mixed_ref = rest
    windows, win = bias_ref.shape[:2]
    width = x_ref.shape[1]
    head_dim = width // HEADS
    group = GROUP * head_dim
    factor = head_dim ** (-0.5) * math.log2(math.e)

    blocks = into_ref.shape[0]
    depth = width // blocks
    for at, shard_ref in enumerate(shard_refs):
        rows = pl.ds(pl.multiple_of(into_ref[at] * depth, depth), depth)
        w_qkv_ref[rows, :] = shard_ref[:, : 3 * width]
        w_out_ref[rows, :] = shard_ref[:, 3 * width :]

    for part in range(3):
        columns = slice(part * width, (part + 1) * width)
        qkv_ref[:, columns] = mxu(x_ref[...], w_qkv_ref[:, columns]).astype(jnp.bfloat16)

    def attend(window, carry):
        rows = pl.ds(pl.multiple_of(window * win, 16), win)
        bias = bias_ref[window]
        for at in range(HEADS // GROUP):
            columns = slice(at * group, (at + 1) * group)
            queries = qkv_ref[rows, columns]
            keys = qkv_ref[rows, width + at * group : width + (at + 1) * group]
            values = qkv_ref[rows, 2 * width + at * group : 2 * width + (at + 1) * group]
            scores = mxu(masked_heads(keys, head_dim), queries, NT)
            scores = scores.reshape(GROUP, win, win) * factor + bias
            lifted = jnp.exp2(scores - jnp.max(scores, axis=1, keepdims=True))
            total = jnp.sum(lifted, axis=1, keepdims=True)
            probs = (lifted * (1.0 / total)).astype(jnp.bfloat16)
            probs = probs.reshape(GROUP * win, win)
            probs_ref[window, at] = probs
            mixed = own_heads(mxu(turned_heads(probs, GROUP), values), head_dim)
            mixed_ref[rows, columns] = mixed.astype(jnp.bfloat16)
        return carry

    window_loop(windows, attend)


def norm_kernel(
    mixed_ref, w_out_ref, cot_ref, gain_ref, normed_ref, grad_proj_ref, grad_mix_ref
):
    win = padded_rows()
    windows = mixed_ref.shape[0] // win
    gain = gain_ref[...]

    def normalise(window, carry):
        rows = pl.ds(pl.multiple_of(window * win, 16), win)
        projected = mxu(mixed_ref[rows, :], w_out_ref[...])
        center = projected - jnp.mean(projected, axis=-1, keepdims=True)
        inverse = lax.rsqrt(jnp.mean(center * center, axis=-1, keepdims=True) + EPS)
        normal = center * inverse
        normed_ref[rows, :] = (normal * gain).astype(jnp.bfloat16)
        scaled = cot_ref[rows, :].astype(jnp.float32) * gain
        grad_proj = (
            scaled
            - jnp.mean(scaled, axis=-1, keepdims=True)
            - normal * jnp.mean(scaled * normal, axis=-1, keepdims=True)
        ) * inverse
        grad_proj_ref[rows, :] = grad_proj.astype(jnp.bfloat16)
        return carry

    window_loop(windows, normalise)
    grad_mix_ref[...] = mxu(grad_proj_ref[...], w_out_ref[...], NT).astype(jnp.bfloat16)


def edge_kernel(value_ref, places_ref, lower_ref):
    half = lower_ref.shape[0]
    value = value_ref[value_ref.shape[0] - places_ref.shape[1] :, :]
    for row in range(half):
        back = mxu(places_ref[WIN_R - half + row], value, TN)
        lower_ref[row] = back.astype(jnp.bfloat16)


def backward_kernel(
    to_slot_ref, qkv_ref, probs_ref, mixed_ref, grad_proj_ref, grad_mix_ref, turned_ref,
    cells_ref, *grad_refs,
):
    windows, win = probs_ref.shape[0], probs_ref.shape[-1]
    width = grad_mix_ref.shape[1]
    head_dim = width // HEADS
    group = GROUP * head_dim
    scale = head_dim ** (-0.5)
    blocks = to_slot_ref.shape[1]
    depth = width // blocks
    half = width // 2
    sent_refs, kept_refs = grad_refs[::2], grad_refs[1::2]
    grad_out = mxu(mixed_ref[...], grad_proj_ref[...], TN)
    for block in range(blocks):
        slot = to_slot_ref[0, block]
        value = grad_out[block * depth : (block + 1) * depth, :]
        rows = pl.ds(pl.multiple_of(lax.rem(slot, blocks // 2) * depth, depth), depth)

        @pl.when(slot < blocks // 2)
        def _():
            kept_refs[0][rows, :width] = value

        @pl.when(slot >= blocks // 2)
        def _():
            sent_refs[0][rows, :width] = value

    def attend_back(window, carry):
        rows = pl.ds(pl.multiple_of(window * win, 16), win)
        for at in range(HEADS // GROUP):
            columns = slice(at * group, (at + 1) * group)
            key_columns = slice(width + at * group, width + (at + 1) * group)
            value_columns = slice(2 * width + at * group, 2 * width + (at + 1) * group)
            mix = grad_mix_ref[rows, columns]
            probs = probs_ref[window, at]
            float_probs = probs.astype(jnp.float32)
            grad_probs = mxu(masked_heads(qkv_ref[rows, value_columns], head_dim), mix, NT)
            product = (float_probs * grad_probs).reshape(GROUP, win, win)
            center = jnp.sum(product, axis=1, keepdims=True)
            grad_scores = scale * (product - float_probs.reshape(GROUP, win, win) * center)
            grad_scores = grad_scores.astype(jnp.bfloat16).reshape(GROUP * win, win)
            grad_values = own_heads(mxu(probs, mix), head_dim)
            grad_keys = own_heads(mxu(grad_scores, qkv_ref[rows, columns]), head_dim)
            turned = turned_heads(grad_scores, GROUP)
            grad_queries = own_heads(mxu(turned, qkv_ref[rows, key_columns]), head_dim)
            cells_ref[rows, columns] = grad_queries.astype(jnp.bfloat16)
            cells_ref[rows, key_columns] = grad_keys.astype(jnp.bfloat16)
            cells_ref[rows, value_columns] = grad_values.astype(jnp.bfloat16)
        return carry

    window_loop(windows, attend_back)

    for part, place in enumerate(GRAD_PLACES):
        columns = slice(part * width, (part + 1) * width)
        chunk = sum(place >= sum(CHUNKS[: at + 1]) for at in range(len(CHUNKS)))
        place -= sum(CHUNKS[:chunk])
        target = slice(place * width, (place + 1) * width)
        turned = turned_ref.at[TABLES.index(ROUTES[chunk])]
        sent_refs[chunk][:, target] = mxu(turned[half:, :], cells_ref[:, columns])
        kept_refs[chunk][:, target] = mxu(turned[:half, :], cells_ref[:, columns])


def coded(value):
    top = jnp.max(jnp.abs(value), axis=1, keepdims=True)
    exponent = jnp.ceil(jnp.log2(jnp.maximum(top, 1e-30)))
    codes = jnp.round(value * (jnp.exp2(-exponent) * STEPS)).astype(jnp.int32)
    exponents = jnp.broadcast_to(exponent, (value.shape[0], 128)).astype(jnp.int32)
    return codes.astype(jnp.int16), exponents.astype(jnp.int16)


def decoded(codes, exponents):
    exponent = exponents.astype(jnp.int32).astype(jnp.float32)[:, :1]
    return codes.astype(jnp.int32).astype(jnp.float32) * (jnp.exp2(exponent) * (1 / STEPS))


def fold_kernel(arrived_ref, kept_ref, *out_refs):
    columns = kept_ref.shape[1]
    rows = out_refs[0].shape[0]

    def total(part):
        arrived = arrived_ref[part, :columns]
        if arrived_ref.shape[1] > columns:
            arrived = decoded(arrived, arrived_ref[part, columns:])
        return kept_ref[part, :] + arrived

    out_refs[0][...] = total(slice(0, rows))
    if len(out_refs) > 1:
        codes, exponents = coded(total(slice(rows, 2 * rows)))
        out_refs[1][:, :columns] = codes
        out_refs[1][:, columns:] = exponents


def exchanged(value, distance):
    count = lax.axis_size("lat")
    return lax.ppermute(value, "lat", [(i, i ^ distance) for i in range(count)])


def moved(value, grp_turn, distance):
    count = lax.axis_size("lat")
    groups = lax.axis_size("grp")
    pairs = []
    for grp in range(groups):
        for i in range(count):
            pairs.append((grp * count + i, (grp ^ grp_turn) * count + (i ^ distance[grp])))
    return lax.ppermute(value, ("grp", "lat"), pairs)


def gathered(block, upper_in, cot_edge, prepare, bias):
    here = lax.axis_index("grp") == 0
    far = moved(block, 0, (8, 12))
    upper_in = passed_along(upper_in, "lat", -1)
    near = moved(block, 0, (4, 6))
    side = exchanged(block, 2)
    far, near, side, bias, upper_in, cot_edge = lax.optimization_barrier(
        (far, near, side, bias, upper_in, cot_edge)
    )
    far_side, far_other = exchanged(far, 2), moved(far, 1, (0, 0))
    near_other = moved(near, 1, (0, 0))
    far_side, near_other = lax.optimization_barrier((far_side, near_other))
    far_side_other = moved(far_side, 1, (0, 0))
    upper_cot = passed_along(cot_edge, "lat", -1)
    prepared = prepare(upper_in)
    shards = [block, side, near, near_other, far, far_other, far_side]
    swapped = [exchanged(shard, 1) for shard in shards]
    far_side_other, upper_cot, rest = lax.optimization_barrier(
        (far_side_other, upper_cot, swapped + list(prepared))
    )
    swapped, prepared = rest[: len(swapped)], rest[len(swapped) :]
    shards += [far_side_other] + swapped + [exchanged(far_side_other, 1)]
    low = jnp.array([0, 2, 4, 6, 8, 12, 10, 14], jnp.int32)
    high = jnp.array([0, 2, 6, 4, 12, 8, 14, 10], jnp.int32)
    order = jnp.where(here, low, high)
    return tuple(shards), jnp.concatenate([order, order + 1]), prepared, upper_cot, bias


def slots_of(distances, steps):
    result = 0
    for step in steps:
        result = 2 * result + ((distances // step) & 1)
    return result


def fold(arrived, kept, last=False):
    rows, columns = kept.shape
    if last:
        outs = (jax.ShapeDtypeStruct((rows, columns), jnp.float32),)
    else:
        outs = (
            jax.ShapeDtypeStruct((rows // 2, columns), jnp.float32),
            jax.ShapeDtypeStruct((rows // 2, columns + 128), jnp.int16),
        )
    return call(fold_kernel, "fold", outs, (), (arrived, kept), vmem=16)


def call(kernel, name, outs, tables, operands, scratch=(), vmem=40):
    return pl.pallas_call(
        kernel,
        out_shape=outs,
        in_specs=[pl.BlockSpec(memory_space=pltpu.SMEM)] * len(tables)
        + [pl.BlockSpec(memory_space=pltpu.VMEM)] * len(operands),
        out_specs=[pl.BlockSpec(memory_space=pltpu.VMEM)] * len(outs),
        scratch_shapes=list(scratch),
        compiler_params=pltpu.CompilerParams(vmem_limit_bytes=vmem * 1024 * 1024),
        cost_estimate=pl.CostEstimate(flops=1, bytes_accessed=1, transcendentals=0),
        name=name,
    )(*tables, *operands)


def per_device(inputs, cotangent, idents, w_qkv, w_out, gain):
    lat_cells, lon_cells, width = inputs.shape
    half_rows = WIN_R // 2
    win = padded_rows()
    windows = (lat_cells // WIN_R) * (lon_cells // WIN_C)
    cells = windows * win
    places = jnp.asarray(window_places(lon_cells), jnp.bfloat16)

    def shape(*dims, dtype=jnp.bfloat16):
        return jax.ShapeDtypeStruct(dims, dtype)

    count = lax.axis_size("lat")
    me = lax.axis_index("lat")
    direct = count == 16 and lax.axis_size("grp") == 2 and width % (16 * count) == 0
    if direct:
        distances = jnp.arange(count, dtype=jnp.int32) ^ me
        to_slot = jnp.stack([slots_of(distances, route) for route in TABLES])
    else:
        to_slot = jnp.stack([jnp.arange(16, dtype=jnp.int32)] * len(TABLES))

    def prepare(upper_in):
        return call(
            prepare_kernel,
            "prepare",
            (shape(cells, width), shape(len(TABLES), width, cells)),
            (to_slot,),
            (inputs, upper_in, places),
            vmem=16,
        )

    weights = jnp.pad(w_qkv, ((0, 0), (0, width))) + jnp.pad(w_out, ((0, 0), (3 * width, 0)))
    in_edge, cot_edge = inputs[:half_rows], cotangent[:half_rows]
    labels = to_windows(idents + 1)
    bias = jnp.where(labels[:, :, None] == labels[:, None, :], 0.0, HIDDEN).astype(jnp.float32)
    if direct:
        shards, order, (tokens, turned), upper_cot, bias = gathered(
            weights, in_edge, cot_edge, prepare, bias
        )
        into = order ^ me
    else:
        weights = lax.all_gather(weights, "lat", axis=0, tiled=True)
        shards = tuple(weights.reshape(16, width // 16, 4 * width))
        into = to_slot[0]
        tokens, turned = prepare(passed_along(in_edge, "lat", -1))
        upper_cot = passed_along(cot_edge, "lat", -1)

    qkv_full, out_full, qkv, probs, mixed = call(
        forward_kernel,
        "forward",
        (
            shape(width, 3 * width),
            shape(width, width),
            shape(cells, 3 * width),
            shape(windows, HEADS // GROUP, GROUP * win, win),
            shape(cells, width),
        ),
        (into,),
        (tokens, bias, *shards),
        vmem=20,
    )
    (cot,) = call(
        shift_kernel,
        "shift",
        (shape(cells, width),),
        (),
        (cotangent, upper_cot, places),
        vmem=16,
    )
    normed, grad_proj, grad_mix = call(
        norm_kernel,
        "norm",
        (shape(cells, width),) * 3,
        (),
        (mixed, out_full, cot, gain[None]),
        vmem=16,
    )
    (lower_out,) = call(
        edge_kernel,
        "edge",
        (shape(half_rows, lon_cells, width),),
        (),
        (normed, places),
        vmem=16,
    )
    lower_out = passed_along(lower_out, "lat", 1)
    grad_cells, *grads = call(
        backward_kernel,
        "backward",
        (
            shape(cells, 3 * width),
            *[shape(width // 2, CHUNKS[at // 2] * width, dtype=jnp.float32) for at in range(2 * len(CHUNKS))],
        ),
        (to_slot,),
        (qkv, probs, mixed, grad_proj, grad_mix, turned),
        vmem=30,
    )
    lower_out, grad_cells, *grads = lax.optimization_barrier((lower_out, grad_cells, *grads))

    def finish(normed, grad_cells):
        return call(
            finish_kernel,
            "finish",
            (shape(*inputs.shape), shape(*inputs.shape), shape(half_rows, lon_cells, width)),
            (),
            (grad_cells, qkv_full, normed, inputs, cotangent, places),
            (pltpu.VMEM((cells, width), jnp.bfloat16),),
            vmem=24,
        )

    if direct:
        pairs = [(exchanged(sent, 1), kept) for sent, kept in zip(grads[::2], grads[1::2])]
        pairs = [fold(arrived, kept) for arrived, kept in pairs]
        kept, sent = pairs[-1]
        sent, normed, grad_cells = lax.optimization_barrier((sent, normed, grad_cells))
        pairs[-1] = (kept, sent)
        output, grad_in, lower = finish(normed, grad_cells)
        for step in (1, 2, 3):
            pairs = [
                (exchanged(sent, route[step]), kept) for route, (kept, sent) in zip(ROUTES, pairs)
            ]
            if step in (1, 3):
                arrived, kept = pairs[0]
                arrived, lower = lax.optimization_barrier((arrived, lower))
                pairs[0] = (arrived, kept)
            pairs = [fold(arrived, kept, step == 3) for arrived, kept in pairs]
            if step == 1:
                lower = passed_along(lower, "lat", 1)
        pairs = [total for (total,) in pairs]
        quarters = [part for total in pairs for part in jnp.split(total, total.shape[1] // width, axis=1)]
        grad_out = quarters[0]
        grad_qkv = jnp.concatenate([quarters[place] for place in GRAD_PLACES], axis=1)
    else:
        whole = [jnp.concatenate([kept, sent]) for sent, kept in zip(grads[::2], grads[1::2])]
        both = lax.psum_scatter(jnp.concatenate(whole, axis=1), "lat", scatter_dimension=0, tiled=True)
        quarters = jnp.split(both, 4, axis=1)
        grad_out = quarters[0]
        grad_qkv = jnp.concatenate([quarters[place] for place in GRAD_PLACES], axis=1)
        output, grad_in, lower = finish(normed, grad_cells)
        lower = passed_along(lower, "lat", 1)

    def completed(result, lower):
        top = result[:half_rows].astype(jnp.float32) + lower.astype(jnp.float32)
        return result.at[:half_rows].set(top.astype(jnp.bfloat16))

    return (completed(output, lower_out), completed(grad_in, lower), grad_qkv, grad_out)


def solution(mesh):
    in_specs = (
        P(("grp", "lat"), None, None),
        P(("grp", "lat"), None, None),
        P(("grp", "lat"), None),
        P("lat", None),
        P("lat", None),
        P(),
    )
    out_specs = (
        P(("grp", "lat"), None, None),
        P(("grp", "lat"), None, None),
        P(("grp", "lat"), None),
        P(("grp", "lat"), None),
    )
    return jax.shard_map(
        per_device, mesh=mesh, in_specs=in_specs, out_specs=out_specs, check_vma=False
    )
```

```python
import math

import jax
import jax.numpy as jnp
import numpy as np
from jax import lax
from jax.experimental import pallas as pl
from jax.experimental.pallas import tpu as pltpu
from jax.sharding import PartitionSpec as P

HEADS = 8
WIN_R = 6
WIN_C = 12
EPS = 1e-05
HIDDEN = -1e30
STEPS = 32000.0
GRAD_PLACES = (3, 2, 1)
CHUNKS = (2, 1, 1)
ROUTES = ((1, 2, 4, 8), (1, 2, 4, 8), (1, 4, 8, 2))
TABLES = tuple(dict.fromkeys(ROUTES))
UNROLL = 9
GROUP = 4

NN = (((1,), (0,)), ((), ()))
NT = (((1,), (1,)), ((), ()))
TN = (((0,), (0,)), ((), ()))


def mxu(left, right, dims=NN):
    return lax.dot_general(left, right, dims, preferred_element_type=jnp.float32)


def passed_along(value, axis, steps):
    count = lax.axis_size(axis)
    first, last = (max(0, -steps), min(count, count - steps))
    return lax.ppermute(value, axis, [(source, source + steps) for source in range(first, last)])


def padded_rows():
    return -(-WIN_R * WIN_C // 16) * 16


def to_windows(field):
    lat_cells, lon_cells = field.shape
    field = field.reshape(lat_cells // WIN_R, WIN_R, lon_cells // WIN_C, WIN_C)
    field = field.transpose(0, 2, 1, 3).reshape(-1, WIN_R * WIN_C)
    return jnp.pad(field, ((0, 0), (0, padded_rows() - WIN_R * WIN_C)))


def window_places(lon_cells):
    win = padded_rows()
    places = np.zeros((WIN_R, lon_cells // WIN_C, win, lon_cells), np.float32)
    for row in range(WIN_R):
        for window in range(lon_cells // WIN_C):
            for column in range(WIN_C):
                source = (window * WIN_C + column + WIN_C // 2) % lon_cells
                places[row, window, row * WIN_C + column, source] = 1
    return places.reshape(WIN_R, -1, lon_cells)


def masked_heads(value, head_dim):
    head = lax.broadcasted_iota(jnp.int32, value.shape, 1) // head_dim
    zero = jnp.zeros_like(value)
    count = value.shape[1] // head_dim
    return jnp.concatenate([jnp.where(head == at, value, zero) for at in range(count)], axis=0)


def own_heads(stacked, head_dim):
    count = stacked.shape[1] // head_dim
    rows = stacked.shape[0] // count
    head = lax.broadcasted_iota(jnp.int32, (rows, stacked.shape[1]), 1) // head_dim
    result = stacked[:rows]
    for at in range(1, count):
        result = jnp.where(head == at, stacked[at * rows : (at + 1) * rows], result)
    return result


def turned_heads(stacked, count):
    rows = stacked.shape[0] // count
    return jnp.concatenate(
        [stacked[at * rows : (at + 1) * rows].T for at in range(count)], axis=0
    )


def shift_kernel(own_ref, halo_ref, places_ref, result_ref):
    half = halo_ref.shape[0]
    lat_cells = own_ref.shape[0]
    cells = places_ref.shape[1]
    for band in range(lat_cells // WIN_R):
        total = None
        for row in range(WIN_R):
            source = band * WIN_R + row + half
            field = own_ref[source] if source < lat_cells else halo_ref[source - lat_cells]
            term = mxu(places_ref[row], field)
            total = term if total is None else total + term
        result_ref[band * cells : (band + 1) * cells, :] = total.astype(jnp.bfloat16)


def window_loop(windows, body):
    lax.fori_loop(0, windows, body, 0, unroll=UNROLL if windows % UNROLL == 0 else 1)


def prepare_kernel(to_slot_ref, inputs_ref, halo_ref, places_ref, tokens_ref, turned_ref):
    shift_kernel(inputs_ref, halo_ref, places_ref, tokens_ref)
    chunks, blocks = to_slot_ref.shape
    depth = tokens_ref.shape[1] // blocks
    turned = tokens_ref[...].T
    for chunk in range(chunks):
        for block in range(blocks):
            rows = pl.ds(pl.multiple_of(to_slot_ref[chunk, block] * depth, depth), depth)
            turned_ref[chunk, rows, :] = turned[block * depth : (block + 1) * depth, :]


def finish_kernel(
    normed_ref, shift_ref, inputs_ref, cot_ref, places_ref, output_ref, grad_in_ref
):
    lat_cells = inputs_ref.shape[0]
    half = WIN_R // 2
    count = places_ref.shape[1]
    for value_ref, base_ref, result_ref in (
        (normed_ref, inputs_ref, output_ref),
        (shift_ref, cot_ref, grad_in_ref),
    ):
        result_ref[:half] = base_ref[:half]
        for target in range(half, lat_cells):
            band, row = divmod(target - half, WIN_R)
            value = value_ref[band * count : (band + 1) * count, :]
            back = mxu(places_ref[row], value, TN)
            result_ref[target] = (base_ref[target].astype(jnp.float32) + back).astype(jnp.bfloat16)


def forward_kernel(into_ref, x_ref, bias_ref, *rest):
    shard_refs, rest = rest[: into_ref.shape[0]], rest[into_ref.shape[0] :]
    w_qkv_ref, w_out_ref, qkv_ref, probs_ref, mixed_ref = rest
    windows, win = bias_ref.shape[:2]
    width = x_ref.shape[1]
    head_dim = width // HEADS
    group = GROUP * head_dim
    factor = head_dim ** (-0.5) * math.log2(math.e)

    blocks = into_ref.shape[0]
    depth = width // blocks
    for at, shard_ref in enumerate(shard_refs):
        rows = pl.ds(pl.multiple_of(into_ref[at] * depth, depth), depth)
        w_qkv_ref[rows, :] = shard_ref[:, : 3 * width]
        w_out_ref[rows, :] = shard_ref[:, 3 * width :]

    for part in range(3):
        columns = slice(part * width, (part + 1) * width)
        qkv_ref[:, columns] = mxu(x_ref[...], w_qkv_ref[:, columns]).astype(jnp.bfloat16)

    def attend(window, carry):
        rows = pl.ds(pl.multiple_of(window * win, 16), win)
        bias = bias_ref[window]
        for at in range(HEADS // GROUP):
            columns = slice(at * group, (at + 1) * group)
            queries = qkv_ref[rows, columns]
            keys = qkv_ref[rows, width + at * group : width + (at + 1) * group]
            values = qkv_ref[rows, 2 * width + at * group : 2 * width + (at + 1) * group]
            scores = mxu(masked_heads(keys, head_dim), queries, NT)
            scores = scores.reshape(GROUP, win, win) * factor + bias
            lifted = jnp.exp2(scores - jnp.max(scores, axis=1, keepdims=True))
            total = jnp.sum(lifted, axis=1, keepdims=True)
            probs = (lifted * (1.0 / total)).astype(jnp.bfloat16)
            probs = probs.reshape(GROUP * win, win)
            probs_ref[window, at] = probs
            mixed = own_heads(mxu(turned_heads(probs, GROUP), values), head_dim)
            mixed_ref[rows, columns] = mixed.astype(jnp.bfloat16)
        return carry

    window_loop(windows, attend)


def norm_kernel(
    mixed_ref, w_out_ref, cot_ref, gain_ref, normed_ref, grad_proj_ref, grad_mix_ref
):
    win = padded_rows()
    windows = mixed_ref.shape[0] // win
    gain = gain_ref[...]

    def normalise(window, carry):
        rows = pl.ds(pl.multiple_of(window * win, 16), win)
        projected = mxu(mixed_ref[rows, :], w_out_ref[...])
        center = projected - jnp.mean(projected, axis=-1, keepdims=True)
        inverse = lax.rsqrt(jnp.mean(center * center, axis=-1, keepdims=True) + EPS)
        normal = center * inverse
        normed_ref[rows, :] = (normal * gain).astype(jnp.bfloat16)
        scaled = cot_ref[rows, :].astype(jnp.float32) * gain
        grad_proj = (
            scaled
            - jnp.mean(scaled, axis=-1, keepdims=True)
            - normal * jnp.mean(scaled * normal, axis=-1, keepdims=True)
        ) * inverse
        grad_proj_ref[rows, :] = grad_proj.astype(jnp.bfloat16)
        return carry

    window_loop(windows, normalise)
    grad_mix_ref[...] = mxu(grad_proj_ref[...], w_out_ref[...], NT).astype(jnp.bfloat16)


def edge_kernel(value_ref, places_ref, lower_ref):
    half = lower_ref.shape[0]
    value = value_ref[value_ref.shape[0] - places_ref.shape[1] :, :]
    for row in range(half):
        back = mxu(places_ref[WIN_R - half + row], value, TN)
        lower_ref[row] = back.astype(jnp.bfloat16)


def shift_back_kernel(cells_ref, w_qkv_ref, places_ref, shift_ref, lower_ref):
    shift_ref[...] = mxu(cells_ref[...], w_qkv_ref[...], NT).astype(jnp.bfloat16)
    edge_kernel(shift_ref, places_ref, lower_ref)


def backward_kernel(
    to_slot_ref, qkv_ref, probs_ref, mixed_ref, grad_proj_ref, grad_mix_ref, turned_ref,
    cells_ref, *grad_refs,
):
    windows, win = probs_ref.shape[0], probs_ref.shape[-1]
    width = grad_mix_ref.shape[1]
    head_dim = width // HEADS
    group = GROUP * head_dim
    scale = head_dim ** (-0.5)
    blocks = to_slot_ref.shape[1]
    depth = width // blocks
    half = width // 2
    sent_refs, kept_refs = grad_refs[::2], grad_refs[1::2]
    grad_out = mxu(mixed_ref[...], grad_proj_ref[...], TN)
    for block in range(blocks):
        slot = to_slot_ref[0, block]
        value = grad_out[block * depth : (block + 1) * depth, :]
        rows = pl.ds(pl.multiple_of(lax.rem(slot, blocks // 2) * depth, depth), depth)

        @pl.when(slot < blocks // 2)
        def _():
            kept_refs[0][rows, :width] = value

        @pl.when(slot >= blocks // 2)
        def _():
            sent_refs[0][rows, :width] = value

    def attend_back(window, carry):
        rows = pl.ds(pl.multiple_of(window * win, 16), win)
        for at in range(HEADS // GROUP):
            columns = slice(at * group, (at + 1) * group)
            key_columns = slice(width + at * group, width + (at + 1) * group)
            value_columns = slice(2 * width + at * group, 2 * width + (at + 1) * group)
            mix = grad_mix_ref[rows, columns]
            probs = probs_ref[window, at]
            float_probs = probs.astype(jnp.float32)
            grad_probs = mxu(masked_heads(qkv_ref[rows, value_columns], head_dim), mix, NT)
            product = (float_probs * grad_probs).reshape(GROUP, win, win)
            center = jnp.sum(product, axis=1, keepdims=True)
            grad_scores = scale * (product - float_probs.reshape(GROUP, win, win) * center)
            grad_scores = grad_scores.astype(jnp.bfloat16).reshape(GROUP * win, win)
            grad_values = own_heads(mxu(probs, mix), head_dim)
            grad_keys = own_heads(mxu(grad_scores, qkv_ref[rows, columns]), head_dim)
            turned = turned_heads(grad_scores, GROUP)
            grad_queries = own_heads(mxu(turned, qkv_ref[rows, key_columns]), head_dim)
            cells_ref[rows, columns] = grad_queries.astype(jnp.bfloat16)
            cells_ref[rows, key_columns] = grad_keys.astype(jnp.bfloat16)
            cells_ref[rows, value_columns] = grad_values.astype(jnp.bfloat16)
        return carry

    window_loop(windows, attend_back)

    for part, place in enumerate(GRAD_PLACES):
        columns = slice(part * width, (part + 1) * width)
        chunk = sum(place >= sum(CHUNKS[: at + 1]) for at in range(len(CHUNKS)))
        place -= sum(CHUNKS[:chunk])
        target = slice(place * width, (place + 1) * width)
        turned = turned_ref.at[TABLES.index(ROUTES[chunk])]
        sent_refs[chunk][:, target] = mxu(turned[half:, :], cells_ref[:, columns])
        kept_refs[chunk][:, target] = mxu(turned[:half, :], cells_ref[:, columns])


def coded(value):
    top = jnp.max(jnp.abs(value), axis=1, keepdims=True)
    exponent = jnp.ceil(jnp.log2(jnp.maximum(top, 1e-30)))
    codes = jnp.round(value * (jnp.exp2(-exponent) * STEPS)).astype(jnp.int32)
    exponents = jnp.broadcast_to(exponent, (value.shape[0], 128)).astype(jnp.int32)
    return codes.astype(jnp.int16), exponents.astype(jnp.int16)


def decoded(codes, exponents):
    exponent = exponents.astype(jnp.int32).astype(jnp.float32)[:, :1]
    return codes.astype(jnp.int32).astype(jnp.float32) * (jnp.exp2(exponent) * (1 / STEPS))


def fold_kernel(arrived_ref, kept_ref, *out_refs):
    columns = kept_ref.shape[1]
    rows = out_refs[0].shape[0]

    def total(part):
        arrived = arrived_ref[part, :columns]
        if arrived_ref.shape[1] > columns:
            arrived = decoded(arrived, arrived_ref[part, columns:])
        return kept_ref[part, :] + arrived

    out_refs[0][...] = total(slice(0, rows))
    if len(out_refs) > 1:
        codes, exponents = coded(total(slice(rows, 2 * rows)))
        out_refs[1][:, :columns] = codes
        out_refs[1][:, columns:] = exponents


def exchanged(value, distance):
    count = lax.axis_size("lat")
    return lax.ppermute(value, "lat", [(i, i ^ distance) for i in range(count)])


def moved(value, grp_turn, distance):
    count = lax.axis_size("lat")
    groups = lax.axis_size("grp")
    pairs = []
    for grp in range(groups):
        for i in range(count):
            pairs.append((grp * count + i, (grp ^ grp_turn) * count + (i ^ distance[grp])))
    return lax.ppermute(value, ("grp", "lat"), pairs)


def gathered(block, upper_in, cot_edge, prepare, bias):
    here = lax.axis_index("grp") == 0
    far = moved(block, 0, (8, 12))
    upper_in = passed_along(upper_in, "lat", -1)
    near = moved(block, 0, (4, 6))
    side = exchanged(block, 2)
    far, near, side, bias, upper_in, cot_edge = lax.optimization_barrier(
        (far, near, side, bias, upper_in, cot_edge)
    )
    far_side, far_other = exchanged(far, 2), moved(far, 1, (0, 0))
    near_other = moved(near, 1, (0, 0))
    far_side, near_other = lax.optimization_barrier((far_side, near_other))
    far_side_other = moved(far_side, 1, (0, 0))
    upper_cot = passed_along(cot_edge, "lat", -1)
    far_other, upper_cot = lax.optimization_barrier((far_other, upper_cot))
    prepared = prepare(upper_in)
    shards = [block, side, near, near_other, far, far_other, far_side]
    swapped = [exchanged(shard, 1) for shard in shards]
    far_side_other, rest = lax.optimization_barrier((far_side_other, swapped + list(prepared)))
    swapped, prepared = rest[: len(swapped)], rest[len(swapped) :]
    shards += [far_side_other] + swapped + [exchanged(far_side_other, 1)]
    low = jnp.array([0, 2, 4, 6, 8, 12, 10, 14], jnp.int32)
    high = jnp.array([0, 2, 6, 4, 12, 8, 14, 10], jnp.int32)
    order = jnp.where(here, low, high)
    return tuple(shards), jnp.concatenate([order, order + 1]), prepared, upper_cot, bias


def slots_of(distances, steps):
    result = 0
    for step in steps:
        result = 2 * result + ((distances // step) & 1)
    return result


def fold(arrived, kept, last=False):
    rows, columns = kept.shape
    if last:
        outs = (jax.ShapeDtypeStruct((rows, columns), jnp.float32),)
    else:
        outs = (
            jax.ShapeDtypeStruct((rows // 2, columns), jnp.float32),
            jax.ShapeDtypeStruct((rows // 2, columns + 128), jnp.int16),
        )
    return call(fold_kernel, "fold", outs, (), (arrived, kept), flops=8 * rows * columns, vmem=16)


def call(kernel, name, outs, tables, operands, scratch=(), flops=0, vmem=40):
    size = sum(math.prod(o.shape) * o.dtype.itemsize for o in (*outs, *operands))
    return pl.pallas_call(
        kernel,
        out_shape=outs,
        in_specs=[pl.BlockSpec(memory_space=pltpu.SMEM)] * len(tables)
        + [pl.BlockSpec(memory_space=pltpu.VMEM)] * len(operands),
        out_specs=[pl.BlockSpec(memory_space=pltpu.VMEM)] * len(outs),
        scratch_shapes=list(scratch),
        compiler_params=pltpu.CompilerParams(vmem_limit_bytes=vmem * 1024 * 1024),
        cost_estimate=pl.CostEstimate(flops=flops, bytes_accessed=size, transcendentals=0),
        name=name,
    )(*tables, *operands)


def per_device(inputs, cotangent, idents, w_qkv, w_out, gain):
    lat_cells, lon_cells, width = inputs.shape
    half_rows = WIN_R // 2
    win = padded_rows()
    windows = (lat_cells // WIN_R) * (lon_cells // WIN_C)
    cells = windows * win
    places = jnp.asarray(window_places(lon_cells), jnp.bfloat16)

    def shape(*dims, dtype=jnp.bfloat16):
        return jax.ShapeDtypeStruct(dims, dtype)

    count = lax.axis_size("lat")
    me = lax.axis_index("lat")
    direct = count == 16 and lax.axis_size("grp") == 2 and width % (16 * count) == 0
    if direct:
        distances = jnp.arange(count, dtype=jnp.int32) ^ me
        to_slot = jnp.stack([slots_of(distances, route) for route in TABLES])
    else:
        to_slot = jnp.stack([jnp.arange(16, dtype=jnp.int32)] * len(TABLES))

    def prepare(upper_in):
        return call(
            prepare_kernel,
            "prepare",
            (shape(cells, width), shape(len(TABLES), width, cells)),
            (to_slot,),
            (inputs, upper_in, places),
            flops=2 * cells * width * lon_cells * WIN_R,
            vmem=16,
        )

    weights = jnp.pad(w_qkv, ((0, 0), (0, width))) + jnp.pad(w_out, ((0, 0), (3 * width, 0)))
    in_edge, cot_edge = inputs[:half_rows], cotangent[:half_rows]
    labels = to_windows(idents + 1)
    bias = jnp.where(labels[:, :, None] == labels[:, None, :], 0.0, HIDDEN).astype(jnp.float32)
    if direct:
        shards, order, (tokens, turned), upper_cot, bias = gathered(
            weights, in_edge, cot_edge, prepare, bias
        )
        into = order ^ me
    else:
        weights = lax.all_gather(weights, "lat", axis=0, tiled=True)
        shards = tuple(weights.reshape(16, width // 16, 4 * width))
        into = to_slot[0]
        tokens, turned = prepare(passed_along(in_edge, "lat", -1))
        upper_cot = passed_along(cot_edge, "lat", -1)

    qkv_full, out_full, qkv, probs, mixed = call(
        forward_kernel,
        "forward",
        (
            shape(width, 3 * width),
            shape(width, width),
            shape(cells, 3 * width),
            shape(windows, HEADS // GROUP, GROUP * win, win),
            shape(cells, width),
        ),
        (into,),
        (tokens, bias, *shards),
        flops=2 * cells * width * width * 4,
        vmem=20,
    )
    (cot,) = call(
        shift_kernel,
        "shift",
        (shape(cells, width),),
        (),
        (cotangent, upper_cot, places),
        flops=2 * cells * width * lon_cells * WIN_R,
        vmem=16,
    )
    normed, grad_proj, grad_mix = call(
        norm_kernel,
        "norm",
        (shape(cells, width),) * 3,
        (),
        (mixed, out_full, cot, gain[None]),
        flops=2 * cells * width * width * 2,
        vmem=16,
    )
    (lower_out,) = call(
        edge_kernel,
        "edge",
        (shape(half_rows, lon_cells, width),),
        (),
        (normed, places),
        flops=2 * cells * width * lon_cells * half_rows,
        vmem=16,
    )
    lower_out = passed_along(lower_out, "lat", 1)
    grad_cells, *grads = call(
        backward_kernel,
        "backward",
        (
            shape(cells, 3 * width),
            *[shape(width // 2, CHUNKS[at // 2] * width, dtype=jnp.float32) for at in range(2 * len(CHUNKS))],
        ),
        (to_slot,),
        (qkv, probs, mixed, grad_proj, grad_mix, turned),
        flops=2 * cells * width * width * 6,
        vmem=30,
    )
    lower_out, grad_cells, *grads = lax.optimization_barrier((lower_out, grad_cells, *grads))

    grad_shift, lower = call(
        shift_back_kernel,
        "shift_back",
        (shape(cells, width), shape(half_rows, lon_cells, width)),
        (),
        (grad_cells, qkv_full, places),
        flops=2 * cells * width * (3 * width + lon_cells * half_rows),
        vmem=16,
    )
    lower = passed_along(lower, "lat", 1)
    output, grad_in = call(
        finish_kernel,
        "finish",
        (shape(*inputs.shape), shape(*inputs.shape)),
        (),
        (normed, grad_shift, inputs, cotangent, places),
        flops=4 * cells * width * lon_cells * half_rows,
        vmem=16,
    )

    if direct:
        pairs = [(exchanged(sent, 1), kept) for sent, kept in zip(grads[::2], grads[1::2])]
        pairs = [fold(arrived, kept) for arrived, kept in pairs]
        for step in (1, 2, 3):
            pairs = [
                (exchanged(sent, route[step]), kept) for route, (kept, sent) in zip(ROUTES, pairs)
            ]
            arrived, kept = pairs[0]
            if step == 1:
                arrived, lower = lax.optimization_barrier((arrived, lower))
            if step == 2:
                arrived, output, grad_in = lax.optimization_barrier((arrived, output, grad_in))
            pairs[0] = (arrived, kept)
            pairs = [fold(arrived, kept, step == 3) for arrived, kept in pairs]
        pairs = [total for (total,) in pairs]
        quarters = [part for total in pairs for part in jnp.split(total, total.shape[1] // width, axis=1)]
        grad_out = quarters[0]
        grad_qkv = jnp.concatenate([quarters[place] for place in GRAD_PLACES], axis=1)
    else:
        whole = [jnp.concatenate([kept, sent]) for sent, kept in zip(grads[::2], grads[1::2])]
        both = lax.psum_scatter(jnp.concatenate(whole, axis=1), "lat", scatter_dimension=0, tiled=True)
        quarters = jnp.split(both, 4, axis=1)
        grad_out = quarters[0]
        grad_qkv = jnp.concatenate([quarters[place] for place in GRAD_PLACES], axis=1)

    def completed(result, lower):
        top = result[:half_rows].astype(jnp.float32) + lower.astype(jnp.float32)
        return result.at[:half_rows].set(top.astype(jnp.bfloat16))

    return (completed(output, lower_out), completed(grad_in, lower), grad_qkv, grad_out)


def solution(mesh):
    in_specs = (
        P(("grp", "lat"), None, None),
        P(("grp", "lat"), None, None),
        P(("grp", "lat"), None),
        P("lat", None),
        P("lat", None),
        P(),
    )
    out_specs = (
        P(("grp", "lat"), None, None),
        P(("grp", "lat"), None, None),
        P(("grp", "lat"), None),
        P(("grp", "lat"), None),
    )
    return jax.shard_map(
        per_device, mesh=mesh, in_specs=in_specs, out_specs=out_specs, check_vma=False
    )
```

```python
import math

import jax
import jax.numpy as jnp
import numpy as np
from jax import lax
from jax.experimental import pallas as pl
from jax.experimental.pallas import tpu as pltpu
from jax.sharding import PartitionSpec as P

HEADS = 8
WIN_R = 6
WIN_C = 12
EPS = 1e-05
HIDDEN = -1e30
STEPS = 32000.0
GRAD_PLACES = (3, 2, 1)
CHUNKS = (2, 1, 1)
ROUTES = ((1, 2, 4, 8), (1, 2, 4, 8), (1, 4, 8, 2))
TABLES = tuple(dict.fromkeys(ROUTES))
UNROLL = 9
GROUP = 4

NN = (((1,), (0,)), ((), ()))
NT = (((1,), (1,)), ((), ()))
TN = (((0,), (0,)), ((), ()))


def mxu(left, right, dims=NN):
    return lax.dot_general(left, right, dims, preferred_element_type=jnp.float32)


def passed_along(value, axis, steps):
    count = lax.axis_size(axis)
    first, last = (max(0, -steps), min(count, count - steps))
    return lax.ppermute(value, axis, [(source, source + steps) for source in range(first, last)])


def padded_rows():
    return -(-WIN_R * WIN_C // 16) * 16


def to_windows(field):
    lat_cells, lon_cells = field.shape
    field = field.reshape(lat_cells // WIN_R, WIN_R, lon_cells // WIN_C, WIN_C)
    field = field.transpose(0, 2, 1, 3).reshape(-1, WIN_R * WIN_C)
    return jnp.pad(field, ((0, 0), (0, padded_rows() - WIN_R * WIN_C)))


def window_places(lon_cells):
    win = padded_rows()
    places = np.zeros((WIN_R, lon_cells // WIN_C, win, lon_cells), np.float32)
    for row in range(WIN_R):
        for window in range(lon_cells // WIN_C):
            for column in range(WIN_C):
                source = (window * WIN_C + column + WIN_C // 2) % lon_cells
                places[row, window, row * WIN_C + column, source] = 1
    return places.reshape(WIN_R, -1, lon_cells)


def masked_heads(value, head_dim):
    head = lax.broadcasted_iota(jnp.int32, value.shape, 1) // head_dim
    zero = jnp.zeros_like(value)
    count = value.shape[1] // head_dim
    return jnp.concatenate([jnp.where(head == at, value, zero) for at in range(count)], axis=0)


def own_heads(stacked, head_dim):
    count = stacked.shape[1] // head_dim
    rows = stacked.shape[0] // count
    head = lax.broadcasted_iota(jnp.int32, (rows, stacked.shape[1]), 1) // head_dim
    result = stacked[:rows]
    for at in range(1, count):
        result = jnp.where(head == at, stacked[at * rows : (at + 1) * rows], result)
    return result


def turned_heads(stacked, count):
    rows = stacked.shape[0] // count
    return jnp.concatenate(
        [stacked[at * rows : (at + 1) * rows].T for at in range(count)], axis=0
    )


def shift_kernel(own_ref, halo_ref, places_ref, result_ref):
    half = halo_ref.shape[0]
    lat_cells = own_ref.shape[0]
    cells = places_ref.shape[1]
    for band in range(lat_cells // WIN_R):
        total = None
        for row in range(WIN_R):
            source = band * WIN_R + row + half
            field = own_ref[source] if source < lat_cells else halo_ref[source - lat_cells]
            term = mxu(places_ref[row], field)
            total = term if total is None else total + term
        result_ref[band * cells : (band + 1) * cells, :] = total.astype(jnp.bfloat16)


def window_loop(windows, body):
    lax.fori_loop(0, windows, body, 0, unroll=UNROLL if windows % UNROLL == 0 else 1)


def prepare_kernel(to_slot_ref, inputs_ref, halo_ref, places_ref, tokens_ref, turned_ref):
    shift_kernel(inputs_ref, halo_ref, places_ref, tokens_ref)
    chunks, blocks = to_slot_ref.shape
    depth = tokens_ref.shape[1] // blocks
    turned = tokens_ref[...].T
    for chunk in range(chunks):
        for block in range(blocks):
            rows = pl.ds(pl.multiple_of(to_slot_ref[chunk, block] * depth, depth), depth)
            turned_ref[chunk, rows, :] = turned[block * depth : (block + 1) * depth, :]


def finish_kernel(
    cells_ref, w_qkv_ref, normed_ref, inputs_ref, cot_ref, places_ref,
    output_ref, grad_in_ref, lower_ref, shift_ref,
):
    lat_cells = inputs_ref.shape[0]
    half = lower_ref.shape[0]
    count = places_ref.shape[1]
    shift_ref[...] = mxu(cells_ref[...], w_qkv_ref[...], NT).astype(jnp.bfloat16)
    for at, (value_ref, base_ref, result_ref) in enumerate(
        ((normed_ref, inputs_ref, output_ref), (shift_ref, cot_ref, grad_in_ref))
    ):
        result_ref[:half] = base_ref[:half]
        for band in range(lat_cells // WIN_R):
            value = value_ref[band * count : (band + 1) * count, :]
            for row in range(WIN_R):
                target = band * WIN_R + row + half
                if at == 0 and target >= lat_cells:
                    continue
                back = mxu(places_ref[row], value, TN)
                if target < lat_cells:
                    base = base_ref[target].astype(jnp.float32)
                    result_ref[target] = (base + back).astype(jnp.bfloat16)
                else:
                    lower_ref[target - lat_cells] = back.astype(jnp.bfloat16)


def forward_kernel(into_ref, x_ref, bias_ref, *rest):
    shard_refs, rest = rest[: into_ref.shape[0]], rest[into_ref.shape[0] :]
    w_qkv_ref, w_out_ref, qkv_ref, probs_ref, mixed_ref = rest
    windows, win = bias_ref.shape[:2]
    width = x_ref.shape[1]
    head_dim = width // HEADS
    group = GROUP * head_dim
    factor = head_dim ** (-0.5) * math.log2(math.e)

    blocks = into_ref.shape[0]
    depth = width // blocks
    for at, shard_ref in enumerate(shard_refs):
        rows = pl.ds(pl.multiple_of(into_ref[at] * depth, depth), depth)
        w_qkv_ref[rows, :] = shard_ref[:, : 3 * width]
        w_out_ref[rows, :] = shard_ref[:, 3 * width :]

    for part in range(3):
        columns = slice(part * width, (part + 1) * width)
        qkv_ref[:, columns] = mxu(x_ref[...], w_qkv_ref[:, columns]).astype(jnp.bfloat16)

    def attend(window, carry):
        rows = pl.ds(pl.multiple_of(window * win, 16), win)
        bias = bias_ref[window]
        for at in range(HEADS // GROUP):
            columns = slice(at * group, (at + 1) * group)
            queries = qkv_ref[rows, columns]
            keys = qkv_ref[rows, width + at * group : width + (at + 1) * group]
            values = qkv_ref[rows, 2 * width + at * group : 2 * width + (at + 1) * group]
            scores = mxu(masked_heads(keys, head_dim), queries, NT)
            scores = scores.reshape(GROUP, win, win) * factor + bias
            lifted = jnp.exp2(scores - jnp.max(scores, axis=1, keepdims=True))
            total = jnp.sum(lifted, axis=1, keepdims=True)
            probs = (lifted * (1.0 / total)).astype(jnp.bfloat16)
            probs = probs.reshape(GROUP * win, win)
            probs_ref[window, at] = probs
            mixed = own_heads(mxu(turned_heads(probs, GROUP), values), head_dim)
            mixed_ref[rows, columns] = mixed.astype(jnp.bfloat16)
        return carry

    window_loop(windows, attend)


def norm_kernel(
    mixed_ref, w_out_ref, cot_ref, gain_ref, normed_ref, grad_proj_ref, grad_mix_ref
):
    win = padded_rows()
    windows = mixed_ref.shape[0] // win
    gain = gain_ref[...]

    def normalise(window, carry):
        rows = pl.ds(pl.multiple_of(window * win, 16), win)
        projected = mxu(mixed_ref[rows, :], w_out_ref[...])
        center = projected - jnp.mean(projected, axis=-1, keepdims=True)
        inverse = lax.rsqrt(jnp.mean(center * center, axis=-1, keepdims=True) + EPS)
        normal = center * inverse
        normed_ref[rows, :] = (normal * gain).astype(jnp.bfloat16)
        scaled = cot_ref[rows, :].astype(jnp.float32) * gain
        grad_proj = (
            scaled
            - jnp.mean(scaled, axis=-1, keepdims=True)
            - normal * jnp.mean(scaled * normal, axis=-1, keepdims=True)
        ) * inverse
        grad_proj_ref[rows, :] = grad_proj.astype(jnp.bfloat16)
        return carry

    window_loop(windows, normalise)
    grad_mix_ref[...] = mxu(grad_proj_ref[...], w_out_ref[...], NT).astype(jnp.bfloat16)


def edge_kernel(value_ref, places_ref, lower_ref):
    half = lower_ref.shape[0]
    value = value_ref[value_ref.shape[0] - places_ref.shape[1] :, :]
    for row in range(half):
        back = mxu(places_ref[WIN_R - half + row], value, TN)
        lower_ref[row] = back.astype(jnp.bfloat16)


def backward_kernel(
    to_slot_ref, qkv_ref, probs_ref, mixed_ref, grad_proj_ref, grad_mix_ref, turned_ref,
    cells_ref, *grad_refs,
):
    windows, win = probs_ref.shape[0], probs_ref.shape[-1]
    width = grad_mix_ref.shape[1]
    head_dim = width // HEADS
    group = GROUP * head_dim
    scale = head_dim ** (-0.5)
    blocks = to_slot_ref.shape[1]
    depth = width // blocks
    half = width // 2
    sent_refs, kept_refs = grad_refs[::2], grad_refs[1::2]
    grad_out = mxu(mixed_ref[...], grad_proj_ref[...], TN)
    for block in range(blocks):
        slot = to_slot_ref[0, block]
        value = grad_out[block * depth : (block + 1) * depth, :]
        rows = pl.ds(pl.multiple_of(lax.rem(slot, blocks // 2) * depth, depth), depth)

        @pl.when(slot < blocks // 2)
        def _():
            kept_refs[0][rows, :width] = value

        @pl.when(slot >= blocks // 2)
        def _():
            sent_refs[0][rows, :width] = value

    def attend_back(window, carry):
        rows = pl.ds(pl.multiple_of(window * win, 16), win)
        for at in range(HEADS // GROUP):
            columns = slice(at * group, (at + 1) * group)
            key_columns = slice(width + at * group, width + (at + 1) * group)
            value_columns = slice(2 * width + at * group, 2 * width + (at + 1) * group)
            mix = grad_mix_ref[rows, columns]
            probs = probs_ref[window, at]
            float_probs = probs.astype(jnp.float32)
            grad_probs = mxu(masked_heads(qkv_ref[rows, value_columns], head_dim), mix, NT)
            product = (float_probs * grad_probs).reshape(GROUP, win, win)
            center = jnp.sum(product, axis=1, keepdims=True)
            grad_scores = scale * (product - float_probs.reshape(GROUP, win, win) * center)
            grad_scores = grad_scores.astype(jnp.bfloat16).reshape(GROUP * win, win)
            grad_values = own_heads(mxu(probs, mix), head_dim)
            grad_keys = own_heads(mxu(grad_scores, qkv_ref[rows, columns]), head_dim)
            turned = turned_heads(grad_scores, GROUP)
            grad_queries = own_heads(mxu(turned, qkv_ref[rows, key_columns]), head_dim)
            cells_ref[rows, columns] = grad_queries.astype(jnp.bfloat16)
            cells_ref[rows, key_columns] = grad_keys.astype(jnp.bfloat16)
            cells_ref[rows, value_columns] = grad_values.astype(jnp.bfloat16)
        return carry

    window_loop(windows, attend_back)

    for part, place in enumerate(GRAD_PLACES):
        columns = slice(part * width, (part + 1) * width)
        chunk = sum(place >= sum(CHUNKS[: at + 1]) for at in range(len(CHUNKS)))
        place -= sum(CHUNKS[:chunk])
        target = slice(place * width, (place + 1) * width)
        turned = turned_ref.at[TABLES.index(ROUTES[chunk])]
        sent_refs[chunk][:, target] = mxu(turned[half:, :], cells_ref[:, columns])
        kept_refs[chunk][:, target] = mxu(turned[:half, :], cells_ref[:, columns])


def coded(value):
    top = jnp.max(jnp.abs(value), axis=1, keepdims=True)
    exponent = jnp.ceil(jnp.log2(jnp.maximum(top, 1e-30)))
    codes = jnp.round(value * (jnp.exp2(-exponent) * STEPS)).astype(jnp.int32)
    exponents = jnp.broadcast_to(exponent, (value.shape[0], 128)).astype(jnp.int32)
    return codes.astype(jnp.int16), exponents.astype(jnp.int16)


def decoded(codes, exponents):
    exponent = exponents.astype(jnp.int32).astype(jnp.float32)[:, :1]
    return codes.astype(jnp.int32).astype(jnp.float32) * (jnp.exp2(exponent) * (1 / STEPS))


def fold_kernel(arrived_ref, kept_ref, *out_refs):
    columns = kept_ref.shape[1]
    rows = out_refs[0].shape[0]

    def total(part):
        arrived = arrived_ref[part, :columns]
        if arrived_ref.shape[1] > columns:
            arrived = decoded(arrived, arrived_ref[part, columns:])
        return kept_ref[part, :] + arrived

    out_refs[0][...] = total(slice(0, rows))
    if len(out_refs) > 1:
        codes, exponents = coded(total(slice(rows, 2 * rows)))
        out_refs[1][:, :columns] = codes
        out_refs[1][:, columns:] = exponents


def exchanged(value, distance):
    count = lax.axis_size("lat")
    return lax.ppermute(value, "lat", [(i, i ^ distance) for i in range(count)])


def moved(value, grp_turn, distance):
    count = lax.axis_size("lat")
    groups = lax.axis_size("grp")
    pairs = []
    for grp in range(groups):
        for i in range(count):
            pairs.append((grp * count + i, (grp ^ grp_turn) * count + (i ^ distance[grp])))
    return lax.ppermute(value, ("grp", "lat"), pairs)


def gathered(block, upper_in, cot_edge, prepare, bias):
    here = lax.axis_index("grp") == 0
    far = moved(block, 0, (8, 12))
    upper_in = passed_along(upper_in, "lat", -1)
    near = moved(block, 0, (4, 6))
    side = exchanged(block, 2)
    upper_cot = passed_along(cot_edge, "lat", -1)
    far, near, side, bias, upper_in, upper_cot = lax.optimization_barrier(
        (far, near, side, bias, upper_in, upper_cot)
    )
    far_side, far_other = exchanged(far, 2), moved(far, 1, (0, 0))
    near_other = moved(near, 1, (0, 0))
    far_side, near_other = lax.optimization_barrier((far_side, near_other))
    far_side_other = moved(far_side, 1, (0, 0))
    prepared = prepare(upper_in)
    shards = [block, side, near, near_other, far, far_other, far_side]
    swapped = [exchanged(shard, 1) for shard in shards]
    far_side_other, rest = lax.optimization_barrier((far_side_other, swapped + list(prepared)))
    swapped, prepared = rest[: len(swapped)], rest[len(swapped) :]
    shards += [far_side_other] + swapped + [exchanged(far_side_other, 1)]
    low = jnp.array([0, 2, 4, 6, 8, 12, 10, 14], jnp.int32)
    high = jnp.array([0, 2, 6, 4, 12, 8, 14, 10], jnp.int32)
    order = jnp.where(here, low, high)
    return tuple(shards), jnp.concatenate([order, order + 1]), prepared, upper_cot, bias


def slots_of(distances, steps):
    result = 0
    for step in steps:
        result = 2 * result + ((distances // step) & 1)
    return result


def fold(arrived, kept, last=False):
    rows, columns = kept.shape
    if last:
        outs = (jax.ShapeDtypeStruct((rows, columns), jnp.float32),)
    else:
        outs = (
            jax.ShapeDtypeStruct((rows // 2, columns), jnp.float32),
            jax.ShapeDtypeStruct((rows // 2, columns + 128), jnp.int16),
        )
    return call(fold_kernel, "fold", outs, (), (arrived, kept), flops=8 * rows * columns, vmem=16)


def call(kernel, name, outs, tables, operands, scratch=(), flops=0, vmem=40):
    size = sum(math.prod(o.shape) * o.dtype.itemsize for o in (*outs, *operands))
    return pl.pallas_call(
        kernel,
        out_shape=outs,
        in_specs=[pl.BlockSpec(memory_space=pltpu.SMEM)] * len(tables)
        + [pl.BlockSpec(memory_space=pltpu.VMEM)] * len(operands),
        out_specs=[pl.BlockSpec(memory_space=pltpu.VMEM)] * len(outs),
        scratch_shapes=list(scratch),
        compiler_params=pltpu.CompilerParams(vmem_limit_bytes=vmem * 1024 * 1024),
        cost_estimate=pl.CostEstimate(flops=flops, bytes_accessed=size, transcendentals=0),
        name=name,
    )(*tables, *operands)


def per_device(inputs, cotangent, idents, w_qkv, w_out, gain):
    lat_cells, lon_cells, width = inputs.shape
    half_rows = WIN_R // 2
    win = padded_rows()
    windows = (lat_cells // WIN_R) * (lon_cells // WIN_C)
    cells = windows * win
    places = jnp.asarray(window_places(lon_cells), jnp.bfloat16)

    def shape(*dims, dtype=jnp.bfloat16):
        return jax.ShapeDtypeStruct(dims, dtype)

    count = lax.axis_size("lat")
    me = lax.axis_index("lat")
    direct = count == 16 and lax.axis_size("grp") == 2 and width % (16 * count) == 0
    if direct:
        distances = jnp.arange(count, dtype=jnp.int32) ^ me
        to_slot = jnp.stack([slots_of(distances, route) for route in TABLES])
    else:
        to_slot = jnp.stack([jnp.arange(16, dtype=jnp.int32)] * len(TABLES))

    def prepare(upper_in):
        return call(
            prepare_kernel,
            "prepare",
            (shape(cells, width), shape(len(TABLES), width, cells)),
            (to_slot,),
            (inputs, upper_in, places),
            flops=2 * cells * width * lon_cells * WIN_R,
            vmem=16,
        )

    weights = jnp.pad(w_qkv, ((0, 0), (0, width))) + jnp.pad(w_out, ((0, 0), (3 * width, 0)))
    in_edge, cot_edge = inputs[:half_rows], cotangent[:half_rows]
    labels = to_windows(idents + 1)
    bias = jnp.where(labels[:, :, None] == labels[:, None, :], 0.0, HIDDEN).astype(jnp.float32)
    if direct:
        shards, order, (tokens, turned), upper_cot, bias = gathered(
            weights, in_edge, cot_edge, prepare, bias
        )
        into = order ^ me
    else:
        weights = lax.all_gather(weights, "lat", axis=0, tiled=True)
        shards = tuple(weights.reshape(16, width // 16, 4 * width))
        into = to_slot[0]
        tokens, turned = prepare(passed_along(in_edge, "lat", -1))
        upper_cot = passed_along(cot_edge, "lat", -1)

    qkv_full, out_full, qkv, probs, mixed = call(
        forward_kernel,
        "forward",
        (
            shape(width, 3 * width),
            shape(width, width),
            shape(cells, 3 * width),
            shape(windows, HEADS // GROUP, GROUP * win, win),
            shape(cells, width),
        ),
        (into,),
        (tokens, bias, *shards),
        flops=2 * cells * width * width * 4,
        vmem=20,
    )
    (cot,) = call(
        shift_kernel,
        "shift",
        (shape(cells, width),),
        (),
        (cotangent, upper_cot, places),
        flops=2 * cells * width * lon_cells * WIN_R,
        vmem=16,
    )
    normed, grad_proj, grad_mix = call(
        norm_kernel,
        "norm",
        (shape(cells, width),) * 3,
        (),
        (mixed, out_full, cot, gain[None]),
        flops=2 * cells * width * width * 2,
        vmem=16,
    )
    (lower_out,) = call(
        edge_kernel,
        "edge",
        (shape(half_rows, lon_cells, width),),
        (),
        (normed, places),
        flops=2 * cells * width * lon_cells * half_rows,
        vmem=16,
    )
    lower_out = passed_along(lower_out, "lat", 1)
    grad_cells, *grads = call(
        backward_kernel,
        "backward",
        (
            shape(cells, 3 * width),
            *[shape(width // 2, CHUNKS[at // 2] * width, dtype=jnp.float32) for at in range(2 * len(CHUNKS))],
        ),
        (to_slot,),
        (qkv, probs, mixed, grad_proj, grad_mix, turned),
        flops=2 * cells * width * width * 6,
        vmem=30,
    )
    lower_out, grad_cells, *grads = lax.optimization_barrier((lower_out, grad_cells, *grads))

    def finish(normed, grad_cells):
        return call(
            finish_kernel,
            "finish",
            (shape(*inputs.shape), shape(*inputs.shape), shape(half_rows, lon_cells, width)),
            (),
            (grad_cells, qkv_full, normed, inputs, cotangent, places),
            (pltpu.VMEM((cells, width), jnp.bfloat16),),
            flops=2 * cells * width * (3 * width + 2 * lon_cells * WIN_R),
            vmem=24,
        )

    if direct:
        pairs = [(exchanged(sent, 1), kept) for sent, kept in zip(grads[::2], grads[1::2])]
        pairs = [fold(arrived, kept) for arrived, kept in pairs]
        kept, sent = pairs[-1]
        sent, normed, grad_cells = lax.optimization_barrier((sent, normed, grad_cells))
        pairs[-1] = (kept, sent)
        output, grad_in, lower = finish(normed, grad_cells)
        for step in (1, 2, 3):
            pairs = [
                (exchanged(sent, route[step]), kept) for route, (kept, sent) in zip(ROUTES, pairs)
            ]
            if step in (1, 3):
                arrived, kept = pairs[0]
                arrived, lower = lax.optimization_barrier((arrived, lower))
                pairs[0] = (arrived, kept)
            pairs = [fold(arrived, kept, step == 3) for arrived, kept in pairs]
            if step == 1:
                lower, _ = lax.optimization_barrier((lower, pairs[0][0]))
                lower = passed_along(lower, "lat", 1)
        pairs = [total for (total,) in pairs]
        quarters = [part for total in pairs for part in jnp.split(total, total.shape[1] // width, axis=1)]
        grad_out = quarters[0]
        grad_qkv = jnp.concatenate([quarters[place] for place in GRAD_PLACES], axis=1)
    else:
        whole = [jnp.concatenate([kept, sent]) for sent, kept in zip(grads[::2], grads[1::2])]
        both = lax.psum_scatter(jnp.concatenate(whole, axis=1), "lat", scatter_dimension=0, tiled=True)
        quarters = jnp.split(both, 4, axis=1)
        grad_out = quarters[0]
        grad_qkv = jnp.concatenate([quarters[place] for place in GRAD_PLACES], axis=1)
        output, grad_in, lower = finish(normed, grad_cells)
        lower = passed_along(lower, "lat", 1)

    def completed(result, lower):
        top = result[:half_rows].astype(jnp.float32) + lower.astype(jnp.float32)
        return result.at[:half_rows].set(top.astype(jnp.bfloat16))

    return (completed(output, lower_out), completed(grad_in, lower), grad_qkv, grad_out)


def solution(mesh):
    in_specs = (
        P(("grp", "lat"), None, None),
        P(("grp", "lat"), None, None),
        P(("grp", "lat"), None),
        P("lat", None),
        P("lat", None),
        P(),
    )
    out_specs = (
        P(("grp", "lat"), None, None),
        P(("grp", "lat"), None, None),
        P(("grp", "lat"), None),
        P(("grp", "lat"), None),
    )
    return jax.shard_map(
        per_device, mesh=mesh, in_specs=in_specs, out_specs=out_specs, check_vma=False
    )
```

```python
import math

import jax
import jax.numpy as jnp
import numpy as np
from jax import lax
from jax.experimental import pallas as pl
from jax.experimental.pallas import tpu as pltpu
from jax.sharding import PartitionSpec as P

HEADS = 8
WIN_R = 6
WIN_C = 12
EPS = 1e-05
HIDDEN = -1e30
STEPS = 32000.0
GRAD_PLACES = (3, 2, 1)
CHUNKS = (2, 1, 1)
ROUTES = ((1, 2, 4, 8), (1, 2, 4, 8), (1, 4, 8, 2))
TABLES = tuple(dict.fromkeys(ROUTES))
UNROLL = 9
GROUP = 4

NN = (((1,), (0,)), ((), ()))
NT = (((1,), (1,)), ((), ()))
TN = (((0,), (0,)), ((), ()))


def mxu(left, right, dims=NN):
    return lax.dot_general(left, right, dims, preferred_element_type=jnp.float32)


def passed_along(value, axis, steps):
    count = lax.axis_size(axis)
    first, last = (max(0, -steps), min(count, count - steps))
    return lax.ppermute(value, axis, [(source, source + steps) for source in range(first, last)])


def padded_rows():
    return -(-WIN_R * WIN_C // 16) * 16


def to_windows(field):
    lat_cells, lon_cells = field.shape
    field = field.reshape(lat_cells // WIN_R, WIN_R, lon_cells // WIN_C, WIN_C)
    field = field.transpose(0, 2, 1, 3).reshape(-1, WIN_R * WIN_C)
    return jnp.pad(field, ((0, 0), (0, padded_rows() - WIN_R * WIN_C)))


def window_places(lon_cells):
    win = padded_rows()
    places = np.zeros((WIN_R, lon_cells // WIN_C, win, lon_cells), np.float32)
    for row in range(WIN_R):
        for window in range(lon_cells // WIN_C):
            for column in range(WIN_C):
                source = (window * WIN_C + column + WIN_C // 2) % lon_cells
                places[row, window, row * WIN_C + column, source] = 1
    return places.reshape(WIN_R, -1, lon_cells)


def masked_heads(value, head_dim):
    head = lax.broadcasted_iota(jnp.int32, value.shape, 1) // head_dim
    zero = jnp.zeros_like(value)
    count = value.shape[1] // head_dim
    return jnp.concatenate([jnp.where(head == at, value, zero) for at in range(count)], axis=0)


def own_heads(stacked, head_dim):
    count = stacked.shape[1] // head_dim
    rows = stacked.shape[0] // count
    head = lax.broadcasted_iota(jnp.int32, (rows, stacked.shape[1]), 1) // head_dim
    result = stacked[:rows]
    for at in range(1, count):
        result = jnp.where(head == at, stacked[at * rows : (at + 1) * rows], result)
    return result


def turned_heads(stacked, count):
    rows = stacked.shape[0] // count
    return jnp.concatenate(
        [stacked[at * rows : (at + 1) * rows].T for at in range(count)], axis=0
    )


def shift_kernel(own_ref, halo_ref, places_ref, result_ref):
    half = halo_ref.shape[0]
    lat_cells = own_ref.shape[0]
    cells = places_ref.shape[1]
    for band in range(lat_cells // WIN_R):
        total = None
        for row in range(WIN_R):
            source = band * WIN_R + row + half
            field = own_ref[source] if source < lat_cells else halo_ref[source - lat_cells]
            term = mxu(places_ref[row], field)
            total = term if total is None else total + term
        result_ref[band * cells : (band + 1) * cells, :] = total.astype(jnp.bfloat16)


def window_loop(windows, body):
    lax.fori_loop(0, windows, body, 0, unroll=UNROLL if windows % UNROLL == 0 else 1)


def prepare_kernel(to_slot_ref, inputs_ref, halo_ref, places_ref, tokens_ref, turned_ref):
    shift_kernel(inputs_ref, halo_ref, places_ref, tokens_ref)
    chunks, blocks = to_slot_ref.shape
    depth = tokens_ref.shape[1] // blocks
    turned = tokens_ref[...].T
    for chunk in range(chunks):
        for block in range(blocks):
            rows = pl.ds(pl.multiple_of(to_slot_ref[chunk, block] * depth, depth), depth)
            turned_ref[chunk, rows, :] = turned[block * depth : (block + 1) * depth, :]


def finish_kernel(
    cells_ref, w_qkv_ref, normed_ref, inputs_ref, cot_ref, places_ref,
    output_ref, grad_in_ref, lower_ref, shift_ref,
):
    lat_cells = inputs_ref.shape[0]
    half = lower_ref.shape[0]
    count = places_ref.shape[1]
    shift_ref[...] = mxu(cells_ref[...], w_qkv_ref[...], NT).astype(jnp.bfloat16)
    for at, (value_ref, base_ref, result_ref) in enumerate(
        ((normed_ref, inputs_ref, output_ref), (shift_ref, cot_ref, grad_in_ref))
    ):
        result_ref[:half] = base_ref[:half]
        for band in range(lat_cells // WIN_R):
            value = value_ref[band * count : (band + 1) * count, :]
            for row in range(WIN_R):
                target = band * WIN_R + row + half
                if at == 0 and target >= lat_cells:
                    continue
                back = mxu(places_ref[row], value, TN)
                if target < lat_cells:
                    base = base_ref[target].astype(jnp.float32)
                    result_ref[target] = (base + back).astype(jnp.bfloat16)
                else:
                    lower_ref[target - lat_cells] = back.astype(jnp.bfloat16)


def forward_kernel(into_ref, x_ref, bias_ref, *rest):
    shard_refs, rest = rest[: into_ref.shape[0]], rest[into_ref.shape[0] :]
    w_qkv_ref, w_out_ref, qkv_ref, probs_ref, mixed_ref = rest
    windows, win = bias_ref.shape[:2]
    width = x_ref.shape[1]
    head_dim = width // HEADS
    group = GROUP * head_dim
    factor = head_dim ** (-0.5) * math.log2(math.e)

    blocks = into_ref.shape[0]
    depth = width // blocks
    for at, shard_ref in enumerate(shard_refs):
        rows = pl.ds(pl.multiple_of(into_ref[at] * depth, depth), depth)
        w_qkv_ref[rows, :] = shard_ref[:, : 3 * width]
        w_out_ref[rows, :] = shard_ref[:, 3 * width :]

    for part in range(3):
        columns = slice(part * width, (part + 1) * width)
        qkv_ref[:, columns] = mxu(x_ref[...], w_qkv_ref[:, columns]).astype(jnp.bfloat16)

    def attend(window, carry):
        rows = pl.ds(pl.multiple_of(window * win, 16), win)
        bias = bias_ref[window]
        for at in range(HEADS // GROUP):
            columns = slice(at * group, (at + 1) * group)
            queries = qkv_ref[rows, columns]
            keys = qkv_ref[rows, width + at * group : width + (at + 1) * group]
            values = qkv_ref[rows, 2 * width + at * group : 2 * width + (at + 1) * group]
            scores = mxu(masked_heads(keys, head_dim), queries, NT)
            scores = scores.reshape(GROUP, win, win) * factor + bias
            lifted = jnp.exp2(scores - jnp.max(scores, axis=1, keepdims=True))
            total = jnp.sum(lifted, axis=1, keepdims=True)
            probs = (lifted * (1.0 / total)).astype(jnp.bfloat16)
            probs = probs.reshape(GROUP * win, win)
            probs_ref[window, at] = probs
            mixed = own_heads(mxu(turned_heads(probs, GROUP), values), head_dim)
            mixed_ref[rows, columns] = mixed.astype(jnp.bfloat16)
        return carry

    window_loop(windows, attend)


def norm_kernel(
    mixed_ref, w_out_ref, cot_ref, gain_ref, normed_ref, grad_proj_ref, grad_mix_ref
):
    win = padded_rows()
    windows = mixed_ref.shape[0] // win
    gain = gain_ref[...]

    def normalise(window, carry):
        rows = pl.ds(pl.multiple_of(window * win, 16), win)
        projected = mxu(mixed_ref[rows, :], w_out_ref[...])
        center = projected - jnp.mean(projected, axis=-1, keepdims=True)
        inverse = lax.rsqrt(jnp.mean(center * center, axis=-1, keepdims=True) + EPS)
        normal = center * inverse
        normed_ref[rows, :] = (normal * gain).astype(jnp.bfloat16)
        scaled = cot_ref[rows, :].astype(jnp.float32) * gain
        grad_proj = (
            scaled
            - jnp.mean(scaled, axis=-1, keepdims=True)
            - normal * jnp.mean(scaled * normal, axis=-1, keepdims=True)
        ) * inverse
        grad_proj_ref[rows, :] = grad_proj.astype(jnp.bfloat16)
        return carry

    window_loop(windows, normalise)
    grad_mix_ref[...] = mxu(grad_proj_ref[...], w_out_ref[...], NT).astype(jnp.bfloat16)


def edge_kernel(value_ref, places_ref, lower_ref):
    half = lower_ref.shape[0]
    value = value_ref[value_ref.shape[0] - places_ref.shape[1] :, :]
    for row in range(half):
        back = mxu(places_ref[WIN_R - half + row], value, TN)
        lower_ref[row] = back.astype(jnp.bfloat16)


def backward_kernel(
    to_slot_ref, qkv_ref, probs_ref, mixed_ref, grad_proj_ref, grad_mix_ref, turned_ref,
    cells_ref, *grad_refs,
):
    windows, win = probs_ref.shape[0], probs_ref.shape[-1]
    width = grad_mix_ref.shape[1]
    head_dim = width // HEADS
    group = GROUP * head_dim
    scale = head_dim ** (-0.5)
    blocks = to_slot_ref.shape[1]
    depth = width // blocks
    half = width // 2
    sent_refs, kept_refs = grad_refs[::2], grad_refs[1::2]
    grad_out = mxu(mixed_ref[...], grad_proj_ref[...], TN)
    for block in range(blocks):
        slot = to_slot_ref[0, block]
        value = grad_out[block * depth : (block + 1) * depth, :]
        rows = pl.ds(pl.multiple_of(lax.rem(slot, blocks // 2) * depth, depth), depth)

        @pl.when(slot < blocks // 2)
        def _():
            kept_refs[0][rows, :width] = value

        @pl.when(slot >= blocks // 2)
        def _():
            sent_refs[0][rows, :width] = value

    def attend_back(window, carry):
        rows = pl.ds(pl.multiple_of(window * win, 16), win)
        for at in range(HEADS // GROUP):
            columns = slice(at * group, (at + 1) * group)
            key_columns = slice(width + at * group, width + (at + 1) * group)
            value_columns = slice(2 * width + at * group, 2 * width + (at + 1) * group)
            mix = grad_mix_ref[rows, columns]
            probs = probs_ref[window, at]
            float_probs = probs.astype(jnp.float32)
            grad_probs = mxu(masked_heads(qkv_ref[rows, value_columns], head_dim), mix, NT)
            product = (float_probs * grad_probs).reshape(GROUP, win, win)
            center = jnp.sum(product, axis=1, keepdims=True)
            grad_scores = scale * (product - float_probs.reshape(GROUP, win, win) * center)
            grad_scores = grad_scores.astype(jnp.bfloat16).reshape(GROUP * win, win)
            grad_values = own_heads(mxu(probs, mix), head_dim)
            grad_keys = own_heads(mxu(grad_scores, qkv_ref[rows, columns]), head_dim)
            turned = turned_heads(grad_scores, GROUP)
            grad_queries = own_heads(mxu(turned, qkv_ref[rows, key_columns]), head_dim)
            cells_ref[rows, columns] = grad_queries.astype(jnp.bfloat16)
            cells_ref[rows, key_columns] = grad_keys.astype(jnp.bfloat16)
            cells_ref[rows, value_columns] = grad_values.astype(jnp.bfloat16)
        return carry

    window_loop(windows, attend_back)

    for part, place in enumerate(GRAD_PLACES):
        columns = slice(part * width, (part + 1) * width)
        chunk = sum(place >= sum(CHUNKS[: at + 1]) for at in range(len(CHUNKS)))
        place -= sum(CHUNKS[:chunk])
        target = slice(place * width, (place + 1) * width)
        turned = turned_ref.at[TABLES.index(ROUTES[chunk])]
        sent_refs[chunk][:, target] = mxu(turned[half:, :], cells_ref[:, columns])
        kept_refs[chunk][:, target] = mxu(turned[:half, :], cells_ref[:, columns])


def coded(value):
    top = jnp.max(jnp.abs(value), axis=1, keepdims=True)
    exponent = jnp.ceil(jnp.log2(jnp.maximum(top, 1e-30)))
    codes = jnp.round(value * (jnp.exp2(-exponent) * STEPS)).astype(jnp.int32)
    exponents = jnp.broadcast_to(exponent, (value.shape[0], 128)).astype(jnp.int32)
    return codes.astype(jnp.int16), exponents.astype(jnp.int16)


def decoded(codes, exponents):
    exponent = exponents.astype(jnp.int32).astype(jnp.float32)[:, :1]
    return codes.astype(jnp.int32).astype(jnp.float32) * (jnp.exp2(exponent) * (1 / STEPS))


def fold_kernel(arrived_ref, kept_ref, *out_refs):
    columns = kept_ref.shape[1]
    rows = out_refs[0].shape[0]

    def total(part):
        arrived = arrived_ref[part, :columns]
        if arrived_ref.shape[1] > columns:
            arrived = decoded(arrived, arrived_ref[part, columns:])
        return kept_ref[part, :] + arrived

    out_refs[0][...] = total(slice(0, rows))
    if len(out_refs) > 1:
        codes, exponents = coded(total(slice(rows, 2 * rows)))
        out_refs[1][:, :columns] = codes
        out_refs[1][:, columns:] = exponents


def exchanged(value, distance):
    count = lax.axis_size("lat")
    return lax.ppermute(value, "lat", [(i, i ^ distance) for i in range(count)])


def moved(value, grp_turn, distance):
    count = lax.axis_size("lat")
    groups = lax.axis_size("grp")
    pairs = []
    for grp in range(groups):
        for i in range(count):
            pairs.append((grp * count + i, (grp ^ grp_turn) * count + (i ^ distance[grp])))
    return lax.ppermute(value, ("grp", "lat"), pairs)


def gathered(block, upper_in, cot_edge, prepare, bias):
    here = lax.axis_index("grp") == 0
    far = moved(block, 0, (8, 12))
    upper_in = passed_along(upper_in, "lat", -1)
    near = moved(block, 0, (4, 6))
    side = exchanged(block, 2)
    far, near, side, bias, upper_in, cot_edge = lax.optimization_barrier(
        (far, near, side, bias, upper_in, cot_edge)
    )
    far_side, far_other = exchanged(far, 2), moved(far, 1, (0, 0))
    near_other = moved(near, 1, (0, 0))
    far_side, near_other = lax.optimization_barrier((far_side, near_other))
    far_side_other = moved(far_side, 1, (0, 0))
    upper_cot = passed_along(cot_edge, "lat", -1)
    prepared = prepare(upper_in)
    shards = [block, side, near, near_other, far, far_other, far_side]
    swapped = [exchanged(shard, 1) for shard in shards]
    far_side_other, upper_cot, rest = lax.optimization_barrier(
        (far_side_other, upper_cot, swapped + list(prepared))
    )
    swapped, prepared = rest[: len(swapped)], rest[len(swapped) :]
    shards += [far_side_other] + swapped + [exchanged(far_side_other, 1)]
    low = jnp.array([0, 2, 4, 6, 8, 12, 10, 14], jnp.int32)
    high = jnp.array([0, 2, 6, 4, 12, 8, 14, 10], jnp.int32)
    order = jnp.where(here, low, high)
    return tuple(shards), jnp.concatenate([order, order + 1]), prepared, upper_cot, bias


def slots_of(distances, steps):
    result = 0
    for step in steps:
        result = 2 * result + ((distances // step) & 1)
    return result


def fold(arrived, kept, last=False):
    rows, columns = kept.shape
    if last:
        outs = (jax.ShapeDtypeStruct((rows, columns), jnp.float32),)
    else:
        outs = (
            jax.ShapeDtypeStruct((rows // 2, columns), jnp.float32),
            jax.ShapeDtypeStruct((rows // 2, columns + 128), jnp.int16),
        )
    return call(fold_kernel, "fold", outs, (), (arrived, kept), flops=8 * rows * columns, vmem=16)


def call(kernel, name, outs, tables, operands, scratch=(), flops=0, vmem=40):
    size = sum(math.prod(o.shape) * o.dtype.itemsize for o in (*outs, *operands))
    return pl.pallas_call(
        kernel,
        out_shape=outs,
        in_specs=[pl.BlockSpec(memory_space=pltpu.SMEM)] * len(tables)
        + [pl.BlockSpec(memory_space=pltpu.VMEM)] * len(operands),
        out_specs=[pl.BlockSpec(memory_space=pltpu.VMEM)] * len(outs),
        scratch_shapes=list(scratch),
        compiler_params=pltpu.CompilerParams(vmem_limit_bytes=vmem * 1024 * 1024),
        cost_estimate=pl.CostEstimate(flops=flops, bytes_accessed=size, transcendentals=0),
        name=name,
    )(*tables, *operands)


def per_device(inputs, cotangent, idents, w_qkv, w_out, gain):
    lat_cells, lon_cells, width = inputs.shape
    half_rows = WIN_R // 2
    win = padded_rows()
    windows = (lat_cells // WIN_R) * (lon_cells // WIN_C)
    cells = windows * win
    places = jnp.asarray(window_places(lon_cells), jnp.bfloat16)

    def shape(*dims, dtype=jnp.bfloat16):
        return jax.ShapeDtypeStruct(dims, dtype)

    count = lax.axis_size("lat")
    me = lax.axis_index("lat")
    direct = count == 16 and lax.axis_size("grp") == 2 and width % (16 * count) == 0
    if direct:
        distances = jnp.arange(count, dtype=jnp.int32) ^ me
        to_slot = jnp.stack([slots_of(distances, route) for route in TABLES])
    else:
        to_slot = jnp.stack([jnp.arange(16, dtype=jnp.int32)] * len(TABLES))

    def prepare(upper_in):
        return call(
            prepare_kernel,
            "prepare",
            (shape(cells, width), shape(len(TABLES), width, cells)),
            (to_slot,),
            (inputs, upper_in, places),
            flops=2 * cells * width * lon_cells * WIN_R,
            vmem=16,
        )

    weights = jnp.pad(w_qkv, ((0, 0), (0, width))) + jnp.pad(w_out, ((0, 0), (3 * width, 0)))
    in_edge, cot_edge = inputs[:half_rows], cotangent[:half_rows]
    labels = to_windows(idents + 1)
    bias = jnp.where(labels[:, :, None] == labels[:, None, :], 0.0, HIDDEN).astype(jnp.float32)
    if direct:
        shards, order, (tokens, turned), upper_cot, bias = gathered(
            weights, in_edge, cot_edge, prepare, bias
        )
        into = order ^ me
    else:
        weights = lax.all_gather(weights, "lat", axis=0, tiled=True)
        shards = tuple(weights.reshape(16, width // 16, 4 * width))
        into = to_slot[0]
        tokens, turned = prepare(passed_along(in_edge, "lat", -1))
        upper_cot = passed_along(cot_edge, "lat", -1)

    qkv_full, out_full, qkv, probs, mixed = call(
        forward_kernel,
        "forward",
        (
            shape(width, 3 * width),
            shape(width, width),
            shape(cells, 3 * width),
            shape(windows, HEADS // GROUP, GROUP * win, win),
            shape(cells, width),
        ),
        (into,),
        (tokens, bias, *shards),
        flops=2 * cells * width * width * 4,
        vmem=20,
    )
    (cot,) = call(
        shift_kernel,
        "shift",
        (shape(cells, width),),
        (),
        (cotangent, upper_cot, places),
        flops=2 * cells * width * lon_cells * WIN_R,
        vmem=16,
    )
    normed, grad_proj, grad_mix = call(
        norm_kernel,
        "norm",
        (shape(cells, width),) * 3,
        (),
        (mixed, out_full, cot, gain[None]),
        flops=2 * cells * width * width * 2,
        vmem=16,
    )
    (lower_out,) = call(
        edge_kernel,
        "edge",
        (shape(half_rows, lon_cells, width),),
        (),
        (normed, places),
        flops=2 * cells * width * lon_cells * half_rows,
        vmem=16,
    )
    lower_out = passed_along(lower_out, "lat", 1)
    grad_cells, *grads = call(
        backward_kernel,
        "backward",
        (
            shape(cells, 3 * width),
            *[shape(width // 2, CHUNKS[at // 2] * width, dtype=jnp.float32) for at in range(2 * len(CHUNKS))],
        ),
        (to_slot,),
        (qkv, probs, mixed, grad_proj, grad_mix, turned),
        flops=2 * cells * width * width * 6,
        vmem=30,
    )
    lower_out, grad_cells, *grads = lax.optimization_barrier((lower_out, grad_cells, *grads))

    def finish(normed, grad_cells):
        return call(
            finish_kernel,
            "finish",
            (shape(*inputs.shape), shape(*inputs.shape), shape(half_rows, lon_cells, width)),
            (),
            (grad_cells, qkv_full, normed, inputs, cotangent, places),
            (pltpu.VMEM((cells, width), jnp.bfloat16),),
            flops=2 * cells * width * (3 * width + 2 * lon_cells * WIN_R),
            vmem=24,
        )

    if direct:
        pairs = [(exchanged(sent, 1), kept) for sent, kept in zip(grads[::2], grads[1::2])]
        pairs = [fold(arrived, kept) for arrived, kept in pairs]
        kept, sent = pairs[-1]
        sent, normed, grad_cells = lax.optimization_barrier((sent, normed, grad_cells))
        pairs[-1] = (kept, sent)
        output, grad_in, lower = finish(normed, grad_cells)
        for step in (1, 2, 3):
            pairs = [
                (exchanged(sent, route[step]), kept) for route, (kept, sent) in zip(ROUTES, pairs)
            ]
            if step in (1, 3):
                arrived, kept = pairs[0]
                arrived, lower = lax.optimization_barrier((arrived, lower))
                pairs[0] = (arrived, kept)
            folded = []
            for at, (arrived, kept) in enumerate(pairs):
                if step == 2 and at > 0:
                    first, sent = folded[0]
                    arrived, first = lax.optimization_barrier((arrived, first))
                    folded[0] = (first, sent)
                folded.append(fold(arrived, kept, step == 3))
            pairs = folded
            if step == 2:
                kept, sent = pairs[1]
                kept, lower = lax.optimization_barrier((kept, lower))
                pairs[1] = (kept, sent)
                lower = passed_along(lower, "lat", 1)
        pairs = [total for (total,) in pairs]
        quarters = [part for total in pairs for part in jnp.split(total, total.shape[1] // width, axis=1)]
        grad_out = quarters[0]
        grad_qkv = jnp.concatenate([quarters[place] for place in GRAD_PLACES], axis=1)
    else:
        whole = [jnp.concatenate([kept, sent]) for sent, kept in zip(grads[::2], grads[1::2])]
        both = lax.psum_scatter(jnp.concatenate(whole, axis=1), "lat", scatter_dimension=0, tiled=True)
        quarters = jnp.split(both, 4, axis=1)
        grad_out = quarters[0]
        grad_qkv = jnp.concatenate([quarters[place] for place in GRAD_PLACES], axis=1)
        output, grad_in, lower = finish(normed, grad_cells)
        lower = passed_along(lower, "lat", 1)

    def completed(result, lower):
        top = result[:half_rows].astype(jnp.float32) + lower.astype(jnp.float32)
        return result.at[:half_rows].set(top.astype(jnp.bfloat16))

    return (completed(output, lower_out), completed(grad_in, lower), grad_qkv, grad_out)


def solution(mesh):
    in_specs = (
        P(("grp", "lat"), None, None),
        P(("grp", "lat"), None, None),
        P(("grp", "lat"), None),
        P("lat", None),
        P("lat", None),
        P(),
    )
    out_specs = (
        P(("grp", "lat"), None, None),
        P(("grp", "lat"), None, None),
        P(("grp", "lat"), None),
        P(("grp", "lat"), None),
    )
    return jax.shard_map(
        per_device, mesh=mesh, in_specs=in_specs, out_specs=out_specs, check_vma=False
    )
```

```python
import math

import jax
import jax.numpy as jnp
import numpy as np
from jax import lax
from jax.experimental import pallas as pl
from jax.experimental.pallas import tpu as pltpu
from jax.sharding import PartitionSpec as P

HEADS = 8
WIN_R = 6
WIN_C = 12
EPS = 1e-05
HIDDEN = -1e30
STEPS = 32000.0
GRAD_PLACES = (3, 2, 1)
CHUNKS = (2, 1, 1)
ROUTES = ((1, 2, 4, 8), (1, 2, 4, 8), (1, 4, 8, 2))
TABLES = tuple(dict.fromkeys(ROUTES))
UNROLL = 9
GROUP = 4

NN = (((1,), (0,)), ((), ()))
NT = (((1,), (1,)), ((), ()))
TN = (((0,), (0,)), ((), ()))


def mxu(left, right, dims=NN):
    return lax.dot_general(left, right, dims, preferred_element_type=jnp.float32)


def passed_along(value, axis, steps):
    count = lax.axis_size(axis)
    first, last = (max(0, -steps), min(count, count - steps))
    return lax.ppermute(value, axis, [(source, source + steps) for source in range(first, last)])


def padded_rows():
    return -(-WIN_R * WIN_C // 16) * 16


def to_windows(field):
    lat_cells, lon_cells = field.shape
    field = field.reshape(lat_cells // WIN_R, WIN_R, lon_cells // WIN_C, WIN_C)
    field = field.transpose(0, 2, 1, 3).reshape(-1, WIN_R * WIN_C)
    return jnp.pad(field, ((0, 0), (0, padded_rows() - WIN_R * WIN_C)))


def window_places(lon_cells):
    win = padded_rows()
    places = np.zeros((WIN_R, lon_cells // WIN_C, win, lon_cells), np.float32)
    for row in range(WIN_R):
        for window in range(lon_cells // WIN_C):
            for column in range(WIN_C):
                source = (window * WIN_C + column + WIN_C // 2) % lon_cells
                places[row, window, row * WIN_C + column, source] = 1
    return places.reshape(WIN_R, -1, lon_cells)


def masked_heads(value, head_dim):
    head = lax.broadcasted_iota(jnp.int32, value.shape, 1) // head_dim
    zero = jnp.zeros_like(value)
    count = value.shape[1] // head_dim
    return jnp.concatenate([jnp.where(head == at, value, zero) for at in range(count)], axis=0)


def own_heads(stacked, head_dim):
    count = stacked.shape[1] // head_dim
    rows = stacked.shape[0] // count
    head = lax.broadcasted_iota(jnp.int32, (rows, stacked.shape[1]), 1) // head_dim
    result = stacked[:rows]
    for at in range(1, count):
        result = jnp.where(head == at, stacked[at * rows : (at + 1) * rows], result)
    return result


def turned_heads(stacked, count):
    rows = stacked.shape[0] // count
    return jnp.concatenate(
        [stacked[at * rows : (at + 1) * rows].T for at in range(count)], axis=0
    )


def shift_kernel(own_ref, halo_ref, places_ref, result_ref):
    half = halo_ref.shape[0]
    lat_cells = own_ref.shape[0]
    cells = places_ref.shape[1]
    for band in range(lat_cells // WIN_R):
        total = None
        for row in range(WIN_R):
            source = band * WIN_R + row + half
            field = own_ref[source] if source < lat_cells else halo_ref[source - lat_cells]
            term = mxu(places_ref[row], field)
            total = term if total is None else total + term
        result_ref[band * cells : (band + 1) * cells, :] = total.astype(jnp.bfloat16)


def window_loop(windows, body):
    lax.fori_loop(0, windows, body, 0, unroll=UNROLL if windows % UNROLL == 0 else 1)


def prepare_kernel(to_slot_ref, inputs_ref, halo_ref, places_ref, tokens_ref, turned_ref):
    shift_kernel(inputs_ref, halo_ref, places_ref, tokens_ref)
    chunks, blocks = to_slot_ref.shape
    depth = tokens_ref.shape[1] // blocks
    turned = tokens_ref[...].T
    for chunk in range(chunks):
        for block in range(blocks):
            rows = pl.ds(pl.multiple_of(to_slot_ref[chunk, block] * depth, depth), depth)
            turned_ref[chunk, rows, :] = turned[block * depth : (block + 1) * depth, :]


def finish_kernel(
    cells_ref, w_qkv_ref, normed_ref, inputs_ref, cot_ref, places_ref,
    output_ref, grad_in_ref, lower_ref, shift_ref,
):
    lat_cells = inputs_ref.shape[0]
    half = lower_ref.shape[0]
    count = places_ref.shape[1]
    shift_ref[...] = mxu(cells_ref[...], w_qkv_ref[...], NT).astype(jnp.bfloat16)
    for at, (value_ref, base_ref, result_ref) in enumerate(
        ((normed_ref, inputs_ref, output_ref), (shift_ref, cot_ref, grad_in_ref))
    ):
        result_ref[:half] = base_ref[:half]
        for band in range(lat_cells // WIN_R):
            value = value_ref[band * count : (band + 1) * count, :]
            for row in range(WIN_R):
                target = band * WIN_R + row + half
                if at == 0 and target >= lat_cells:
                    continue
                back = mxu(places_ref[row], value, TN)
                if target < lat_cells:
                    base = base_ref[target].astype(jnp.float32)
                    result_ref[target] = (base + back).astype(jnp.bfloat16)
                else:
                    lower_ref[target - lat_cells] = back.astype(jnp.bfloat16)


def forward_kernel(into_ref, x_ref, bias_ref, *rest):
    shard_refs, rest = rest[: into_ref.shape[0]], rest[into_ref.shape[0] :]
    w_qkv_ref, w_out_ref, qkv_ref, probs_ref, mixed_ref = rest
    windows, win = bias_ref.shape[:2]
    width = x_ref.shape[1]
    head_dim = width // HEADS
    group = GROUP * head_dim
    factor = head_dim ** (-0.5) * math.log2(math.e)

    blocks = into_ref.shape[0]
    depth = width // blocks
    for at, shard_ref in enumerate(shard_refs):
        rows = pl.ds(pl.multiple_of(into_ref[at] * depth, depth), depth)
        w_qkv_ref[rows, :] = shard_ref[:, : 3 * width]
        w_out_ref[rows, :] = shard_ref[:, 3 * width :]

    for part in range(3):
        columns = slice(part * width, (part + 1) * width)
        qkv_ref[:, columns] = mxu(x_ref[...], w_qkv_ref[:, columns]).astype(jnp.bfloat16)

    def attend(window, carry):
        rows = pl.ds(pl.multiple_of(window * win, 16), win)
        bias = bias_ref[window]
        for at in range(HEADS // GROUP):
            columns = slice(at * group, (at + 1) * group)
            queries = qkv_ref[rows, columns]
            keys = qkv_ref[rows, width + at * group : width + (at + 1) * group]
            values = qkv_ref[rows, 2 * width + at * group : 2 * width + (at + 1) * group]
            scores = mxu(masked_heads(keys, head_dim), queries, NT)
            scores = scores.reshape(GROUP, win, win) * factor + bias
            lifted = jnp.exp2(scores - jnp.max(scores, axis=1, keepdims=True))
            total = jnp.sum(lifted, axis=1, keepdims=True)
            probs = (lifted * (1.0 / total)).astype(jnp.bfloat16)
            probs = probs.reshape(GROUP * win, win)
            probs_ref[window, at] = probs
            mixed = own_heads(mxu(turned_heads(probs, GROUP), values), head_dim)
            mixed_ref[rows, columns] = mixed.astype(jnp.bfloat16)
        return carry

    window_loop(windows, attend)


def norm_kernel(
    mixed_ref, w_out_ref, cot_ref, gain_ref, normed_ref, grad_proj_ref, grad_mix_ref
):
    win = padded_rows()
    windows = mixed_ref.shape[0] // win
    gain = gain_ref[...]

    def normalise(window, carry):
        rows = pl.ds(pl.multiple_of(window * win, 16), win)
        projected = mxu(mixed_ref[rows, :], w_out_ref[...])
        center = projected - jnp.mean(projected, axis=-1, keepdims=True)
        inverse = lax.rsqrt(jnp.mean(center * center, axis=-1, keepdims=True) + EPS)
        normal = center * inverse
        normed_ref[rows, :] = (normal * gain).astype(jnp.bfloat16)
        scaled = cot_ref[rows, :].astype(jnp.float32) * gain
        grad_proj = (
            scaled
            - jnp.mean(scaled, axis=-1, keepdims=True)
            - normal * jnp.mean(scaled * normal, axis=-1, keepdims=True)
        ) * inverse
        grad_proj_ref[rows, :] = grad_proj.astype(jnp.bfloat16)
        return carry

    window_loop(windows, normalise)
    grad_mix_ref[...] = mxu(grad_proj_ref[...], w_out_ref[...], NT).astype(jnp.bfloat16)


def edge_kernel(value_ref, places_ref, lower_ref):
    half = lower_ref.shape[0]
    value = value_ref[value_ref.shape[0] - places_ref.shape[1] :, :]
    for row in range(half):
        back = mxu(places_ref[WIN_R - half + row], value, TN)
        lower_ref[row] = back.astype(jnp.bfloat16)


def backward_kernel(
    to_slot_ref, qkv_ref, probs_ref, mixed_ref, grad_proj_ref, grad_mix_ref, turned_ref,
    cells_ref, *grad_refs,
):
    windows, win = probs_ref.shape[0], probs_ref.shape[-1]
    width = grad_mix_ref.shape[1]
    head_dim = width // HEADS
    group = GROUP * head_dim
    scale = head_dim ** (-0.5)
    blocks = to_slot_ref.shape[1]
    depth = width // blocks
    half = width // 2
    sent_refs, kept_refs = grad_refs[::2], grad_refs[1::2]
    grad_out = mxu(mixed_ref[...], grad_proj_ref[...], TN)
    for block in range(blocks):
        slot = to_slot_ref[0, block]
        value = grad_out[block * depth : (block + 1) * depth, :]
        rows = pl.ds(pl.multiple_of(lax.rem(slot, blocks // 2) * depth, depth), depth)

        @pl.when(slot < blocks // 2)
        def _():
            kept_refs[0][rows, :width] = value

        @pl.when(slot >= blocks // 2)
        def _():
            sent_refs[0][rows, :width] = value

    def attend_back(window, carry):
        rows = pl.ds(pl.multiple_of(window * win, 16), win)
        for at in range(HEADS // GROUP):
            columns = slice(at * group, (at + 1) * group)
            key_columns = slice(width + at * group, width + (at + 1) * group)
            value_columns = slice(2 * width + at * group, 2 * width + (at + 1) * group)
            mix = grad_mix_ref[rows, columns]
            probs = probs_ref[window, at]
            float_probs = probs.astype(jnp.float32)
            grad_probs = mxu(masked_heads(qkv_ref[rows, value_columns], head_dim), mix, NT)
            product = (float_probs * grad_probs).reshape(GROUP, win, win)
            center = jnp.sum(product, axis=1, keepdims=True)
            grad_scores = scale * (product - float_probs.reshape(GROUP, win, win) * center)
            grad_scores = grad_scores.astype(jnp.bfloat16).reshape(GROUP * win, win)
            grad_values = own_heads(mxu(probs, mix), head_dim)
            grad_keys = own_heads(mxu(grad_scores, qkv_ref[rows, columns]), head_dim)
            turned = turned_heads(grad_scores, GROUP)
            grad_queries = own_heads(mxu(turned, qkv_ref[rows, key_columns]), head_dim)
            cells_ref[rows, columns] = grad_queries.astype(jnp.bfloat16)
            cells_ref[rows, key_columns] = grad_keys.astype(jnp.bfloat16)
            cells_ref[rows, value_columns] = grad_values.astype(jnp.bfloat16)
        return carry

    window_loop(windows, attend_back)

    for part, place in enumerate(GRAD_PLACES):
        columns = slice(part * width, (part + 1) * width)
        chunk = sum(place >= sum(CHUNKS[: at + 1]) for at in range(len(CHUNKS)))
        place -= sum(CHUNKS[:chunk])
        target = slice(place * width, (place + 1) * width)
        turned = turned_ref.at[TABLES.index(ROUTES[chunk])]
        sent_refs[chunk][:, target] = mxu(turned[half:, :], cells_ref[:, columns])
        kept_refs[chunk][:, target] = mxu(turned[:half, :], cells_ref[:, columns])


def coded(value):
    top = jnp.max(jnp.abs(value), axis=1, keepdims=True)
    exponent = jnp.ceil(jnp.log2(jnp.maximum(top, 1e-30)))
    codes = jnp.round(value * (jnp.exp2(-exponent) * STEPS)).astype(jnp.int32)
    exponents = jnp.broadcast_to(exponent, (value.shape[0], 128)).astype(jnp.int32)
    return codes.astype(jnp.int16), exponents.astype(jnp.int16)


def decoded(codes, exponents):
    exponent = exponents.astype(jnp.int32).astype(jnp.float32)[:, :1]
    return codes.astype(jnp.int32).astype(jnp.float32) * (jnp.exp2(exponent) * (1 / STEPS))


def added(arrived_ref, kept_ref, rows, columns):
    total = kept_ref.shape[1]
    arrived = arrived_ref[rows, columns]
    if arrived_ref.shape[1] > total:
        arrived = decoded(arrived, arrived_ref[rows, total:])
    return kept_ref[rows, columns] + arrived


def fold_kernel(arrived_ref, kept_ref, half_ref, coded_ref):
    rows, columns = half_ref.shape
    every = slice(0, columns)
    half_ref[...] = added(arrived_ref, kept_ref, slice(0, rows), every)
    codes, exponents = coded(added(arrived_ref, kept_ref, slice(rows, 2 * rows), every))
    coded_ref[:, :columns] = codes
    coded_ref[:, columns:] = exponents


def last_kernel(*refs):
    pair_refs, (grad_out_ref, grad_qkv_ref) = refs[:-2], refs[-2:]
    rows, width = grad_out_ref.shape
    every = slice(0, rows)
    quarters = []
    for at, quarter_count in enumerate(CHUNKS):
        for place in range(quarter_count):
            columns = slice(place * width, (place + 1) * width)
            quarters.append((pair_refs[2 * at], pair_refs[2 * at + 1], every, columns))
    grad_out_ref[...] = added(*quarters[0])
    for part, place in enumerate(GRAD_PLACES):
        grad_qkv_ref[:, part * width : (part + 1) * width] = added(*quarters[place])


def exchanged(value, distance):
    count = lax.axis_size("lat")
    return lax.ppermute(value, "lat", [(i, i ^ distance) for i in range(count)])


def moved(value, grp_turn, distance):
    count = lax.axis_size("lat")
    groups = lax.axis_size("grp")
    pairs = []
    for grp in range(groups):
        for i in range(count):
            pairs.append((grp * count + i, (grp ^ grp_turn) * count + (i ^ distance[grp])))
    return lax.ppermute(value, ("grp", "lat"), pairs)


def gathered(block, upper_in, cot_edge, prepare, bias):
    here = lax.axis_index("grp") == 0
    far = moved(block, 0, (8, 12))
    upper_in = passed_along(upper_in, "lat", -1)
    near = moved(block, 0, (4, 6))
    side = exchanged(block, 2)
    far, near, side, bias, upper_in, cot_edge = lax.optimization_barrier(
        (far, near, side, bias, upper_in, cot_edge)
    )
    far_side, far_other = exchanged(far, 2), moved(far, 1, (0, 0))
    near_other = moved(near, 1, (0, 0))
    far_side, near_other = lax.optimization_barrier((far_side, near_other))
    far_side_other = moved(far_side, 1, (0, 0))
    upper_cot = passed_along(cot_edge, "lat", -1)
    prepared = prepare(upper_in)
    shards = [block, side, near, near_other, far, far_other, far_side]
    swapped = [exchanged(shard, 1) for shard in shards]
    far_side_other, upper_cot, rest = lax.optimization_barrier(
        (far_side_other, upper_cot, swapped + list(prepared))
    )
    swapped, prepared = rest[: len(swapped)], rest[len(swapped) :]
    shards += [far_side_other] + swapped + [exchanged(far_side_other, 1)]
    low = jnp.array([0, 2, 4, 6, 8, 12, 10, 14], jnp.int32)
    high = jnp.array([0, 2, 6, 4, 12, 8, 14, 10], jnp.int32)
    order = jnp.where(here, low, high)
    return tuple(shards), jnp.concatenate([order, order + 1]), prepared, upper_cot, bias


def slots_of(distances, steps):
    result = 0
    for step in steps:
        result = 2 * result + ((distances // step) & 1)
    return result


def fold(arrived, kept):
    rows, columns = kept.shape
    outs = (
        jax.ShapeDtypeStruct((rows // 2, columns), jnp.float32),
        jax.ShapeDtypeStruct((rows // 2, columns + 128), jnp.int16),
    )
    return call(fold_kernel, "fold", outs, (), (arrived, kept), flops=8 * rows * columns, vmem=16)


def call(kernel, name, outs, tables, operands, scratch=(), flops=0, vmem=40):
    size = sum(math.prod(o.shape) * o.dtype.itemsize for o in (*outs, *operands))
    return pl.pallas_call(
        kernel,
        out_shape=outs,
        in_specs=[pl.BlockSpec(memory_space=pltpu.SMEM)] * len(tables)
        + [pl.BlockSpec(memory_space=pltpu.VMEM)] * len(operands),
        out_specs=[pl.BlockSpec(memory_space=pltpu.VMEM)] * len(outs),
        scratch_shapes=list(scratch),
        compiler_params=pltpu.CompilerParams(vmem_limit_bytes=vmem * 1024 * 1024),
        cost_estimate=pl.CostEstimate(flops=flops, bytes_accessed=size, transcendentals=0),
        name=name,
    )(*tables, *operands)


def per_device(inputs, cotangent, idents, w_qkv, w_out, gain):
    lat_cells, lon_cells, width = inputs.shape
    half_rows = WIN_R // 2
    win = padded_rows()
    windows = (lat_cells // WIN_R) * (lon_cells // WIN_C)
    cells = windows * win
    places = jnp.asarray(window_places(lon_cells), jnp.bfloat16)

    def shape(*dims, dtype=jnp.bfloat16):
        return jax.ShapeDtypeStruct(dims, dtype)

    count = lax.axis_size("lat")
    me = lax.axis_index("lat")
    direct = count == 16 and lax.axis_size("grp") == 2 and width % (16 * count) == 0
    if direct:
        distances = jnp.arange(count, dtype=jnp.int32) ^ me
        to_slot = jnp.stack([slots_of(distances, route) for route in TABLES])
    else:
        to_slot = jnp.stack([jnp.arange(16, dtype=jnp.int32)] * len(TABLES))

    def prepare(upper_in):
        return call(
            prepare_kernel,
            "prepare",
            (shape(cells, width), shape(len(TABLES), width, cells)),
            (to_slot,),
            (inputs, upper_in, places),
            flops=2 * cells * width * lon_cells * WIN_R,
            vmem=16,
        )

    weights = jnp.pad(w_qkv, ((0, 0), (0, width))) + jnp.pad(w_out, ((0, 0), (3 * width, 0)))
    in_edge, cot_edge = inputs[:half_rows], cotangent[:half_rows]
    labels = to_windows(idents + 1)
    bias = jnp.where(labels[:, :, None] == labels[:, None, :], 0.0, HIDDEN).astype(jnp.float32)
    if direct:
        shards, order, (tokens, turned), upper_cot, bias = gathered(
            weights, in_edge, cot_edge, prepare, bias
        )
        into = order ^ me
    else:
        weights = lax.all_gather(weights, "lat", axis=0, tiled=True)
        shards = tuple(weights.reshape(16, width // 16, 4 * width))
        into = to_slot[0]
        tokens, turned = prepare(passed_along(in_edge, "lat", -1))
        upper_cot = passed_along(cot_edge, "lat", -1)

    qkv_full, out_full, qkv, probs, mixed = call(
        forward_kernel,
        "forward",
        (
            shape(width, 3 * width),
            shape(width, width),
            shape(cells, 3 * width),
            shape(windows, HEADS // GROUP, GROUP * win, win),
            shape(cells, width),
        ),
        (into,),
        (tokens, bias, *shards),
        flops=2 * cells * width * width * 4,
        vmem=20,
    )
    (cot,) = call(
        shift_kernel,
        "shift",
        (shape(cells, width),),
        (),
        (cotangent, upper_cot, places),
        flops=2 * cells * width * lon_cells * WIN_R,
        vmem=16,
    )
    normed, grad_proj, grad_mix = call(
        norm_kernel,
        "norm",
        (shape(cells, width),) * 3,
        (),
        (mixed, out_full, cot, gain[None]),
        flops=2 * cells * width * width * 2,
        vmem=16,
    )
    (lower_out,) = call(
        edge_kernel,
        "edge",
        (shape(half_rows, lon_cells, width),),
        (),
        (normed, places),
        flops=2 * cells * width * lon_cells * half_rows,
        vmem=16,
    )
    lower_out = passed_along(lower_out, "lat", 1)
    grad_cells, *grads = call(
        backward_kernel,
        "backward",
        (
            shape(cells, 3 * width),
            *[shape(width // 2, CHUNKS[at // 2] * width, dtype=jnp.float32) for at in range(2 * len(CHUNKS))],
        ),
        (to_slot,),
        (qkv, probs, mixed, grad_proj, grad_mix, turned),
        flops=2 * cells * width * width * 6,
        vmem=30,
    )
    lower_out, grad_cells, *grads = lax.optimization_barrier((lower_out, grad_cells, *grads))

    def finish(normed, grad_cells):
        return call(
            finish_kernel,
            "finish",
            (shape(*inputs.shape), shape(*inputs.shape), shape(half_rows, lon_cells, width)),
            (),
            (grad_cells, qkv_full, normed, inputs, cotangent, places),
            (pltpu.VMEM((cells, width), jnp.bfloat16),),
            flops=2 * cells * width * (3 * width + 2 * lon_cells * WIN_R),
            vmem=24,
        )

    if direct:
        pairs = [(exchanged(sent, 1), kept) for sent, kept in zip(grads[::2], grads[1::2])]
        pairs = [fold(arrived, kept) for arrived, kept in pairs]
        kept, sent = pairs[-1]
        sent, normed, grad_cells = lax.optimization_barrier((sent, normed, grad_cells))
        pairs[-1] = (kept, sent)
        output, grad_in, lower = finish(normed, grad_cells)
        for step in (1, 2, 3):
            pairs = [
                (exchanged(sent, route[step]), kept) for route, (kept, sent) in zip(ROUTES, pairs)
            ]
            if step in (1, 3):
                arrived, kept = pairs[0]
                arrived, lower = lax.optimization_barrier((arrived, lower))
                pairs[0] = (arrived, kept)
            if step == 3:
                break
            pairs = [fold(arrived, kept) for arrived, kept in pairs]
            if step == 1:
                lower, _ = lax.optimization_barrier((lower, pairs[0][0]))
                lower = passed_along(lower, "lat", 1)
        grad_out, grad_qkv = call(
            last_kernel,
            "last",
            (
                shape(width // count, width, dtype=jnp.float32),
                shape(width // count, 3 * width, dtype=jnp.float32),
            ),
            (),
            [value for pair in pairs for value in pair],
            flops=8 * width * width,
            vmem=16,
        )
    else:
        whole = [jnp.concatenate([kept, sent]) for sent, kept in zip(grads[::2], grads[1::2])]
        both = lax.psum_scatter(jnp.concatenate(whole, axis=1), "lat", scatter_dimension=0, tiled=True)
        quarters = jnp.split(both, 4, axis=1)
        grad_out = quarters[0]
        grad_qkv = jnp.concatenate([quarters[place] for place in GRAD_PLACES], axis=1)
        output, grad_in, lower = finish(normed, grad_cells)
        lower = passed_along(lower, "lat", 1)

    def completed(result, lower):
        top = result[:half_rows].astype(jnp.float32) + lower.astype(jnp.float32)
        return result.at[:half_rows].set(top.astype(jnp.bfloat16))

    return (completed(output, lower_out), completed(grad_in, lower), grad_qkv, grad_out)


def solution(mesh):
    in_specs = (
        P(("grp", "lat"), None, None),
        P(("grp", "lat"), None, None),
        P(("grp", "lat"), None),
        P("lat", None),
        P("lat", None),
        P(),
    )
    out_specs = (
        P(("grp", "lat"), None, None),
        P(("grp", "lat"), None, None),
        P(("grp", "lat"), None),
        P(("grp", "lat"), None),
    )
    return jax.shard_map(
        per_device, mesh=mesh, in_specs=in_specs, out_specs=out_specs, check_vma=False
    )
```

```python
import math

import jax
import jax.numpy as jnp
import numpy as np
from jax import lax
from jax.experimental import pallas as pl
from jax.experimental.pallas import tpu as pltpu
from jax.sharding import PartitionSpec as P

HEADS = 8
WIN_R = 6
WIN_C = 12
EPS = 1e-05
HIDDEN = -1e30
STEPS = 32000.0
GRAD_PLACES = (3, 2, 1)
CHUNKS = (2, 1, 1)
ROUTES = ((1, 2, 4, 8), (1, 2, 4, 8), (1, 4, 8, 2))
TABLES = tuple(dict.fromkeys(ROUTES))
UNROLL = 9
GROUP = 4

NN = (((1,), (0,)), ((), ()))
NT = (((1,), (1,)), ((), ()))
TN = (((0,), (0,)), ((), ()))


def mxu(left, right, dims=NN):
    return lax.dot_general(left, right, dims, preferred_element_type=jnp.float32)


def passed_along(value, axis, steps):
    count = lax.axis_size(axis)
    first, last = (max(0, -steps), min(count, count - steps))
    return lax.ppermute(value, axis, [(source, source + steps) for source in range(first, last)])


def padded_rows():
    return -(-WIN_R * WIN_C // 16) * 16


def to_windows(field):
    lat_cells, lon_cells = field.shape
    field = field.reshape(lat_cells // WIN_R, WIN_R, lon_cells // WIN_C, WIN_C)
    field = field.transpose(0, 2, 1, 3).reshape(-1, WIN_R * WIN_C)
    return jnp.pad(field, ((0, 0), (0, padded_rows() - WIN_R * WIN_C)))


def window_places(lon_cells):
    win = padded_rows()
    places = np.zeros((WIN_R, lon_cells // WIN_C, win, lon_cells), np.float32)
    for row in range(WIN_R):
        for window in range(lon_cells // WIN_C):
            for column in range(WIN_C):
                source = (window * WIN_C + column + WIN_C // 2) % lon_cells
                places[row, window, row * WIN_C + column, source] = 1
    return places.reshape(WIN_R, -1, lon_cells)


def masked_heads(value, head_dim):
    head = lax.broadcasted_iota(jnp.int32, value.shape, 1) // head_dim
    zero = jnp.zeros_like(value)
    count = value.shape[1] // head_dim
    return jnp.concatenate([jnp.where(head == at, value, zero) for at in range(count)], axis=0)


def own_heads(stacked, head_dim):
    count = stacked.shape[1] // head_dim
    rows = stacked.shape[0] // count
    head = lax.broadcasted_iota(jnp.int32, (rows, stacked.shape[1]), 1) // head_dim
    result = stacked[:rows]
    for at in range(1, count):
        result = jnp.where(head == at, stacked[at * rows : (at + 1) * rows], result)
    return result


def turned_heads(stacked, count):
    rows = stacked.shape[0] // count
    return jnp.concatenate(
        [stacked[at * rows : (at + 1) * rows].T for at in range(count)], axis=0
    )


def shift_kernel(own_ref, halo_ref, places_ref, result_ref):
    half = halo_ref.shape[0]
    lat_cells = own_ref.shape[0]
    cells = places_ref.shape[1]
    for band in range(lat_cells // WIN_R):
        total = None
        for row in range(WIN_R):
            source = band * WIN_R + row + half
            field = own_ref[source] if source < lat_cells else halo_ref[source - lat_cells]
            term = mxu(places_ref[row], field)
            total = term if total is None else total + term
        result_ref[band * cells : (band + 1) * cells, :] = total.astype(jnp.bfloat16)


def window_loop(windows, body):
    lax.fori_loop(0, windows, body, 0, unroll=UNROLL if windows % UNROLL == 0 else 1)


def prepare_kernel(to_slot_ref, inputs_ref, halo_ref, places_ref, tokens_ref, turned_ref):
    shift_kernel(inputs_ref, halo_ref, places_ref, tokens_ref)
    chunks, blocks = to_slot_ref.shape
    depth = tokens_ref.shape[1] // blocks
    turned = tokens_ref[...].T
    for chunk in range(chunks):
        for block in range(blocks):
            rows = pl.ds(pl.multiple_of(to_slot_ref[chunk, block] * depth, depth), depth)
            turned_ref[chunk, rows, :] = turned[block * depth : (block + 1) * depth, :]


def finish_kernel(
    cells_ref, w_qkv_ref, normed_ref, inputs_ref, cot_ref, places_ref,
    output_ref, grad_in_ref, lower_ref, shift_ref,
):
    lat_cells = inputs_ref.shape[0]
    half = lower_ref.shape[0]
    count = places_ref.shape[1]
    shift_ref[...] = mxu(cells_ref[...], w_qkv_ref[...], NT).astype(jnp.bfloat16)
    for at, (value_ref, base_ref, result_ref) in enumerate(
        ((normed_ref, inputs_ref, output_ref), (shift_ref, cot_ref, grad_in_ref))
    ):
        result_ref[:half] = base_ref[:half]
        for band in range(lat_cells // WIN_R):
            value = value_ref[band * count : (band + 1) * count, :]
            for row in range(WIN_R):
                target = band * WIN_R + row + half
                if at == 0 and target >= lat_cells:
                    continue
                back = mxu(places_ref[row], value, TN)
                if target < lat_cells:
                    base = base_ref[target].astype(jnp.float32)
                    result_ref[target] = (base + back).astype(jnp.bfloat16)
                else:
                    lower_ref[target - lat_cells] = back.astype(jnp.bfloat16)


def forward_kernel(into_ref, x_ref, bias_ref, *rest):
    shard_refs, rest = rest[: into_ref.shape[0]], rest[into_ref.shape[0] :]
    w_qkv_ref, w_out_ref, qkv_ref, probs_ref, mixed_ref = rest
    windows, win = bias_ref.shape[:2]
    width = x_ref.shape[1]
    head_dim = width // HEADS
    group = GROUP * head_dim
    factor = head_dim ** (-0.5) * math.log2(math.e)

    blocks = into_ref.shape[0]
    depth = width // blocks
    for at, shard_ref in enumerate(shard_refs):
        rows = pl.ds(pl.multiple_of(into_ref[at] * depth, depth), depth)
        w_qkv_ref[rows, :] = shard_ref[:, : 3 * width]
        w_out_ref[rows, :] = shard_ref[:, 3 * width :]

    for part in range(3):
        columns = slice(part * width, (part + 1) * width)
        qkv_ref[:, columns] = mxu(x_ref[...], w_qkv_ref[:, columns]).astype(jnp.bfloat16)

    def attend(window, carry):
        rows = pl.ds(pl.multiple_of(window * win, 16), win)
        bias = bias_ref[window]
        for at in range(HEADS // GROUP):
            columns = slice(at * group, (at + 1) * group)
            queries = qkv_ref[rows, columns]
            keys = qkv_ref[rows, width + at * group : width + (at + 1) * group]
            values = qkv_ref[rows, 2 * width + at * group : 2 * width + (at + 1) * group]
            scores = mxu(masked_heads(keys, head_dim), queries, NT)
            scores = scores.reshape(GROUP, win, win) * factor + bias
            lifted = jnp.exp2(scores - jnp.max(scores, axis=1, keepdims=True))
            total = jnp.sum(lifted, axis=1, keepdims=True)
            probs = (lifted * (1.0 / total)).astype(jnp.bfloat16)
            probs = probs.reshape(GROUP * win, win)
            probs_ref[window, at] = probs
            mixed = own_heads(mxu(turned_heads(probs, GROUP), values), head_dim)
            mixed_ref[rows, columns] = mixed.astype(jnp.bfloat16)
        return carry

    window_loop(windows, attend)


def norm_kernel(
    mixed_ref, w_out_ref, cot_ref, gain_ref, normed_ref, grad_proj_ref, grad_mix_ref
):
    win = padded_rows()
    windows = mixed_ref.shape[0] // win
    gain = gain_ref[...]

    def normalise(window, carry):
        rows = pl.ds(pl.multiple_of(window * win, 16), win)
        projected = mxu(mixed_ref[rows, :], w_out_ref[...])
        center = projected - jnp.mean(projected, axis=-1, keepdims=True)
        inverse = lax.rsqrt(jnp.mean(center * center, axis=-1, keepdims=True) + EPS)
        normal = center * inverse
        normed_ref[rows, :] = (normal * gain).astype(jnp.bfloat16)
        scaled = cot_ref[rows, :].astype(jnp.float32) * gain
        grad_proj = (
            scaled
            - jnp.mean(scaled, axis=-1, keepdims=True)
            - normal * jnp.mean(scaled * normal, axis=-1, keepdims=True)
        ) * inverse
        grad_proj_ref[rows, :] = grad_proj.astype(jnp.bfloat16)
        return carry

    window_loop(windows, normalise)
    grad_mix_ref[...] = mxu(grad_proj_ref[...], w_out_ref[...], NT).astype(jnp.bfloat16)


def edge_kernel(value_ref, places_ref, lower_ref):
    half = lower_ref.shape[0]
    value = value_ref[value_ref.shape[0] - places_ref.shape[1] :, :]
    for row in range(half):
        back = mxu(places_ref[WIN_R - half + row], value, TN)
        lower_ref[row] = back.astype(jnp.bfloat16)


def backward_kernel(
    to_slot_ref, qkv_ref, probs_ref, mixed_ref, grad_proj_ref, grad_mix_ref, turned_ref,
    cells_ref, *grad_refs,
):
    windows, win = probs_ref.shape[0], probs_ref.shape[-1]
    width = grad_mix_ref.shape[1]
    head_dim = width // HEADS
    group = GROUP * head_dim
    scale = head_dim ** (-0.5)
    blocks = to_slot_ref.shape[1]
    depth = width // blocks
    half = width // 2
    sent_refs, kept_refs = grad_refs[::2], grad_refs[1::2]
    grad_out = mxu(mixed_ref[...], grad_proj_ref[...], TN)
    for block in range(blocks):
        slot = to_slot_ref[0, block]
        value = grad_out[block * depth : (block + 1) * depth, :]
        rows = pl.ds(pl.multiple_of(lax.rem(slot, blocks // 2) * depth, depth), depth)

        @pl.when(slot < blocks // 2)
        def _():
            kept_refs[0][rows, :width] = value

        @pl.when(slot >= blocks // 2)
        def _():
            sent_refs[0][rows, :width] = value

    def attend_back(window, carry):
        rows = pl.ds(pl.multiple_of(window * win, 16), win)
        for at in range(HEADS // GROUP):
            columns = slice(at * group, (at + 1) * group)
            key_columns = slice(width + at * group, width + (at + 1) * group)
            value_columns = slice(2 * width + at * group, 2 * width + (at + 1) * group)
            mix = grad_mix_ref[rows, columns]
            probs = probs_ref[window, at]
            float_probs = probs.astype(jnp.float32)
            grad_probs = mxu(masked_heads(qkv_ref[rows, value_columns], head_dim), mix, NT)
            product = (float_probs * grad_probs).reshape(GROUP, win, win)
            center = jnp.sum(product, axis=1, keepdims=True)
            grad_scores = scale * (product - float_probs.reshape(GROUP, win, win) * center)
            grad_scores = grad_scores.astype(jnp.bfloat16).reshape(GROUP * win, win)
            grad_values = own_heads(mxu(probs, mix), head_dim)
            grad_keys = own_heads(mxu(grad_scores, qkv_ref[rows, columns]), head_dim)
            turned = turned_heads(grad_scores, GROUP)
            grad_queries = own_heads(mxu(turned, qkv_ref[rows, key_columns]), head_dim)
            cells_ref[rows, columns] = grad_queries.astype(jnp.bfloat16)
            cells_ref[rows, key_columns] = grad_keys.astype(jnp.bfloat16)
            cells_ref[rows, value_columns] = grad_values.astype(jnp.bfloat16)
        return carry

    window_loop(windows, attend_back)

    for part, place in enumerate(GRAD_PLACES):
        columns = slice(part * width, (part + 1) * width)
        chunk = sum(place >= sum(CHUNKS[: at + 1]) for at in range(len(CHUNKS)))
        place -= sum(CHUNKS[:chunk])
        target = slice(place * width, (place + 1) * width)
        turned = turned_ref.at[TABLES.index(ROUTES[chunk])]
        sent_refs[chunk][:, target] = mxu(turned[half:, :], cells_ref[:, columns])
        kept_refs[chunk][:, target] = mxu(turned[:half, :], cells_ref[:, columns])


def coded(value):
    top = jnp.max(jnp.abs(value), axis=1, keepdims=True)
    exponent = jnp.ceil(jnp.log2(jnp.maximum(top, 1e-30)))
    codes = jnp.round(value * (jnp.exp2(-exponent) * STEPS)).astype(jnp.int32)
    exponents = jnp.broadcast_to(exponent, (value.shape[0], 128)).astype(jnp.int32)
    return codes.astype(jnp.int16), exponents.astype(jnp.int16)


def decoded(codes, exponents):
    exponent = exponents.astype(jnp.int32).astype(jnp.float32)[:, :1]
    return codes.astype(jnp.int32).astype(jnp.float32) * (jnp.exp2(exponent) * (1 / STEPS))


def added(arrived_ref, kept_ref, rows, columns):
    total = kept_ref.shape[1]
    arrived = arrived_ref[rows, columns]
    if arrived_ref.shape[1] > total:
        arrived = decoded(arrived, arrived_ref[rows, total:])
    return kept_ref[rows, columns] + arrived


def fold_kernel(arrived_ref, kept_ref, half_ref, coded_ref):
    rows, columns = half_ref.shape
    every = slice(0, columns)
    half_ref[...] = added(arrived_ref, kept_ref, slice(0, rows), every)
    codes, exponents = coded(added(arrived_ref, kept_ref, slice(rows, 2 * rows), every))
    coded_ref[:, :columns] = codes
    coded_ref[:, columns:] = exponents


def last_kernel(*refs):
    pair_refs, (grad_out_ref, grad_qkv_ref) = refs[:-2], refs[-2:]
    rows, width = grad_out_ref.shape
    every = slice(0, rows)
    quarters = []
    for at, quarter_count in enumerate(CHUNKS):
        for place in range(quarter_count):
            columns = slice(place * width, (place + 1) * width)
            quarters.append((pair_refs[2 * at], pair_refs[2 * at + 1], every, columns))
    grad_out_ref[...] = added(*quarters[0])
    for part, place in enumerate(GRAD_PLACES):
        grad_qkv_ref[:, part * width : (part + 1) * width] = added(*quarters[place])


def exchanged(value, distance):
    count = lax.axis_size("lat")
    return lax.ppermute(value, "lat", [(i, i ^ distance) for i in range(count)])


def moved(value, grp_turn, distance):
    count = lax.axis_size("lat")
    groups = lax.axis_size("grp")
    pairs = []
    for grp in range(groups):
        for i in range(count):
            pairs.append((grp * count + i, (grp ^ grp_turn) * count + (i ^ distance[grp])))
    return lax.ppermute(value, ("grp", "lat"), pairs)


def gathered(block, upper_in, cot_edge, prepare, bias):
    here = lax.axis_index("grp") == 0
    far = moved(block, 0, (8, 12))
    upper_in = passed_along(upper_in, "lat", -1)
    near = moved(block, 0, (4, 6))
    side = exchanged(block, 2)
    far, near, side, bias, cot_edge = lax.optimization_barrier((far, near, side, bias, cot_edge))
    far_side, far_other = exchanged(far, 2), moved(far, 1, (0, 0))
    near_other = moved(near, 1, (0, 0))
    far_side, near_other, upper_in = lax.optimization_barrier((far_side, near_other, upper_in))
    far_side_other = moved(far_side, 1, (0, 0))
    upper_cot = passed_along(cot_edge, "lat", -1)
    prepared = prepare(upper_in)
    shards = [block, side, near, near_other, far, far_other, far_side]
    swapped = [exchanged(shard, 1) for shard in shards]
    far_side_other, upper_cot, rest = lax.optimization_barrier(
        (far_side_other, upper_cot, swapped + list(prepared))
    )
    swapped, prepared = rest[: len(swapped)], rest[len(swapped) :]
    shards += [far_side_other] + swapped + [exchanged(far_side_other, 1)]
    low = jnp.array([0, 2, 4, 6, 8, 12, 10, 14], jnp.int32)
    high = jnp.array([0, 2, 6, 4, 12, 8, 14, 10], jnp.int32)
    order = jnp.where(here, low, high)
    return tuple(shards), jnp.concatenate([order, order + 1]), prepared, upper_cot, bias


def slots_of(distances, steps):
    result = 0
    for step in steps:
        result = 2 * result + ((distances // step) & 1)
    return result


def fold(arrived, kept):
    rows, columns = kept.shape
    outs = (
        jax.ShapeDtypeStruct((rows // 2, columns), jnp.float32),
        jax.ShapeDtypeStruct((rows // 2, columns + 128), jnp.int16),
    )
    return call(fold_kernel, "fold", outs, (), (arrived, kept), flops=8 * rows * columns, vmem=16)


def call(kernel, name, outs, tables, operands, scratch=(), flops=0, vmem=40):
    size = sum(math.prod(o.shape) * o.dtype.itemsize for o in (*outs, *operands))
    return pl.pallas_call(
        kernel,
        out_shape=outs,
        in_specs=[pl.BlockSpec(memory_space=pltpu.SMEM)] * len(tables)
        + [pl.BlockSpec(memory_space=pltpu.VMEM)] * len(operands),
        out_specs=[pl.BlockSpec(memory_space=pltpu.VMEM)] * len(outs),
        scratch_shapes=list(scratch),
        compiler_params=pltpu.CompilerParams(vmem_limit_bytes=vmem * 1024 * 1024),
        cost_estimate=pl.CostEstimate(flops=flops, bytes_accessed=size, transcendentals=0),
        name=name,
    )(*tables, *operands)


def per_device(inputs, cotangent, idents, w_qkv, w_out, gain):
    lat_cells, lon_cells, width = inputs.shape
    half_rows = WIN_R // 2
    win = padded_rows()
    windows = (lat_cells // WIN_R) * (lon_cells // WIN_C)
    cells = windows * win
    places = jnp.asarray(window_places(lon_cells), jnp.bfloat16)

    def shape(*dims, dtype=jnp.bfloat16):
        return jax.ShapeDtypeStruct(dims, dtype)

    count = lax.axis_size("lat")
    me = lax.axis_index("lat")
    direct = count == 16 and lax.axis_size("grp") == 2 and width % (16 * count) == 0
    if direct:
        distances = jnp.arange(count, dtype=jnp.int32) ^ me
        to_slot = jnp.stack([slots_of(distances, route) for route in TABLES])
    else:
        to_slot = jnp.stack([jnp.arange(16, dtype=jnp.int32)] * len(TABLES))

    def prepare(upper_in):
        return call(
            prepare_kernel,
            "prepare",
            (shape(cells, width), shape(len(TABLES), width, cells)),
            (to_slot,),
            (inputs, upper_in, places),
            flops=2 * cells * width * lon_cells * WIN_R,
            vmem=16,
        )

    weights = jnp.pad(w_qkv, ((0, 0), (0, width))) + jnp.pad(w_out, ((0, 0), (3 * width, 0)))
    in_edge, cot_edge = inputs[:half_rows], cotangent[:half_rows]
    labels = to_windows(idents + 1)
    bias = jnp.where(labels[:, :, None] == labels[:, None, :], 0.0, HIDDEN).astype(jnp.float32)
    if direct:
        shards, order, (tokens, turned), upper_cot, bias = gathered(
            weights, in_edge, cot_edge, prepare, bias
        )
        into = order ^ me
    else:
        weights = lax.all_gather(weights, "lat", axis=0, tiled=True)
        shards = tuple(weights.reshape(16, width // 16, 4 * width))
        into = to_slot[0]
        tokens, turned = prepare(passed_along(in_edge, "lat", -1))
        upper_cot = passed_along(cot_edge, "lat", -1)

    qkv_full, out_full, qkv, probs, mixed = call(
        forward_kernel,
        "forward",
        (
            shape(width, 3 * width),
            shape(width, width),
            shape(cells, 3 * width),
            shape(windows, HEADS // GROUP, GROUP * win, win),
            shape(cells, width),
        ),
        (into,),
        (tokens, bias, *shards),
        flops=2 * cells * width * width * 4,
        vmem=20,
    )
    (cot,) = call(
        shift_kernel,
        "shift",
        (shape(cells, width),),
        (),
        (cotangent, upper_cot, places),
        flops=2 * cells * width * lon_cells * WIN_R,
        vmem=16,
    )
    normed, grad_proj, grad_mix = call(
        norm_kernel,
        "norm",
        (shape(cells, width),) * 3,
        (),
        (mixed, out_full, cot, gain[None]),
        flops=2 * cells * width * width * 2,
        vmem=16,
    )
    (lower_out,) = call(
        edge_kernel,
        "edge",
        (shape(half_rows, lon_cells, width),),
        (),
        (normed, places),
        flops=2 * cells * width * lon_cells * half_rows,
        vmem=16,
    )
    lower_out = passed_along(lower_out, "lat", 1)
    grad_cells, *grads = call(
        backward_kernel,
        "backward",
        (
            shape(cells, 3 * width),
            *[shape(width // 2, CHUNKS[at // 2] * width, dtype=jnp.float32) for at in range(2 * len(CHUNKS))],
        ),
        (to_slot,),
        (qkv, probs, mixed, grad_proj, grad_mix, turned),
        flops=2 * cells * width * width * 6,
        vmem=30,
    )
    lower_out, grad_cells, *grads = lax.optimization_barrier((lower_out, grad_cells, *grads))

    def finish(normed, grad_cells):
        return call(
            finish_kernel,
            "finish",
            (shape(*inputs.shape), shape(*inputs.shape), shape(half_rows, lon_cells, width)),
            (),
            (grad_cells, qkv_full, normed, inputs, cotangent, places),
            (pltpu.VMEM((cells, width), jnp.bfloat16),),
            flops=2 * cells * width * (3 * width + 2 * lon_cells * WIN_R),
            vmem=24,
        )

    if direct:
        pairs = [(exchanged(sent, 1), kept) for sent, kept in zip(grads[::2], grads[1::2])]
        pairs = [fold(arrived, kept) for arrived, kept in pairs]
        kept, sent = pairs[-1]
        sent, normed, grad_cells = lax.optimization_barrier((sent, normed, grad_cells))
        pairs[-1] = (kept, sent)
        output, grad_in, lower = finish(normed, grad_cells)
        for step in (1, 2, 3):
            pairs = [
                (exchanged(sent, route[step]), kept) for route, (kept, sent) in zip(ROUTES, pairs)
            ]
            if step in (1, 3):
                arrived, kept = pairs[0]
                arrived, lower = lax.optimization_barrier((arrived, lower))
                pairs[0] = (arrived, kept)
            if step == 3:
                break
            pairs = [fold(arrived, kept) for arrived, kept in pairs]
            if step == 1:
                lower, _ = lax.optimization_barrier((lower, pairs[0][0]))
                lower = passed_along(lower, "lat", 1)
        grad_out, grad_qkv = call(
            last_kernel,
            "last",
            (
                shape(width // count, width, dtype=jnp.float32),
                shape(width // count, 3 * width, dtype=jnp.float32),
            ),
            (),
            [value for pair in pairs for value in pair],
            flops=8 * width * width,
            vmem=16,
        )
    else:
        whole = [jnp.concatenate([kept, sent]) for sent, kept in zip(grads[::2], grads[1::2])]
        both = lax.psum_scatter(jnp.concatenate(whole, axis=1), "lat", scatter_dimension=0, tiled=True)
        quarters = jnp.split(both, 4, axis=1)
        grad_out = quarters[0]
        grad_qkv = jnp.concatenate([quarters[place] for place in GRAD_PLACES], axis=1)
        output, grad_in, lower = finish(normed, grad_cells)
        lower = passed_along(lower, "lat", 1)

    def completed(result, lower):
        top = result[:half_rows].astype(jnp.float32) + lower.astype(jnp.float32)
        return result.at[:half_rows].set(top.astype(jnp.bfloat16))

    return (completed(output, lower_out), completed(grad_in, lower), grad_qkv, grad_out)


def solution(mesh):
    in_specs = (
        P(("grp", "lat"), None, None),
        P(("grp", "lat"), None, None),
        P(("grp", "lat"), None),
        P("lat", None),
        P("lat", None),
        P(),
    )
    out_specs = (
        P(("grp", "lat"), None, None),
        P(("grp", "lat"), None, None),
        P(("grp", "lat"), None),
        P(("grp", "lat"), None),
    )
    return jax.shard_map(
        per_device, mesh=mesh, in_specs=in_specs, out_specs=out_specs, check_vma=False
    )
```

```python
import math

import jax
import jax.numpy as jnp
import numpy as np
from jax import lax
from jax.experimental import pallas as pl
from jax.experimental.pallas import tpu as pltpu
from jax.sharding import PartitionSpec as P

HEADS = 8
WIN_R = 6
WIN_C = 12
EPS = 1e-05
HIDDEN = -1e30
STEPS = 32000.0
GRAD_PLACES = (3, 2, 1)
CHUNKS = (2, 1, 1)
ROUTES = ((1, 2, 4, 8), (1, 2, 4, 8), (1, 4, 8, 2))
TABLES = tuple(dict.fromkeys(ROUTES))
UNROLL = 9
GROUP = 4

NN = (((1,), (0,)), ((), ()))
NT = (((1,), (1,)), ((), ()))
TN = (((0,), (0,)), ((), ()))


def mxu(left, right, dims=NN):
    return lax.dot_general(left, right, dims, preferred_element_type=jnp.float32)


def passed_along(value, axis, steps):
    count = lax.axis_size(axis)
    first, last = (max(0, -steps), min(count, count - steps))
    return lax.ppermute(value, axis, [(source, source + steps) for source in range(first, last)])


def padded_rows():
    return -(-WIN_R * WIN_C // 16) * 16


def to_windows(field):
    lat_cells, lon_cells = field.shape
    field = field.reshape(lat_cells // WIN_R, WIN_R, lon_cells // WIN_C, WIN_C)
    field = field.transpose(0, 2, 1, 3).reshape(-1, WIN_R * WIN_C)
    return jnp.pad(field, ((0, 0), (0, padded_rows() - WIN_R * WIN_C)))


def window_places(lon_cells):
    win = padded_rows()
    places = np.zeros((WIN_R, lon_cells // WIN_C, win, lon_cells), np.float32)
    for row in range(WIN_R):
        for window in range(lon_cells // WIN_C):
            for column in range(WIN_C):
                source = (window * WIN_C + column + WIN_C // 2) % lon_cells
                places[row, window, row * WIN_C + column, source] = 1
    return places.reshape(WIN_R, -1, lon_cells)


def masked_heads(value, head_dim):
    head = lax.broadcasted_iota(jnp.int32, value.shape, 1) // head_dim
    zero = jnp.zeros_like(value)
    count = value.shape[1] // head_dim
    return jnp.concatenate([jnp.where(head == at, value, zero) for at in range(count)], axis=0)


def own_heads(stacked, head_dim):
    count = stacked.shape[1] // head_dim
    rows = stacked.shape[0] // count
    head = lax.broadcasted_iota(jnp.int32, (rows, stacked.shape[1]), 1) // head_dim
    result = stacked[:rows]
    for at in range(1, count):
        result = jnp.where(head == at, stacked[at * rows : (at + 1) * rows], result)
    return result


def turned_heads(stacked, count):
    rows = stacked.shape[0] // count
    return jnp.concatenate(
        [stacked[at * rows : (at + 1) * rows].T for at in range(count)], axis=0
    )


def shift_kernel(own_ref, halo_ref, places_ref, result_ref):
    half = halo_ref.shape[0]
    lat_cells = own_ref.shape[0]
    cells = places_ref.shape[1]
    for band in range(lat_cells // WIN_R):
        total = None
        for row in range(WIN_R):
            source = band * WIN_R + row + half
            field = own_ref[source] if source < lat_cells else halo_ref[source - lat_cells]
            term = mxu(places_ref[row], field)
            total = term if total is None else total + term
        result_ref[band * cells : (band + 1) * cells, :] = total.astype(jnp.bfloat16)


def window_loop(windows, body):
    lax.fori_loop(0, windows, body, 0, unroll=UNROLL if windows % UNROLL == 0 else 1)


def prepare_kernel(to_slot_ref, inputs_ref, halo_ref, places_ref, tokens_ref, turned_ref):
    shift_kernel(inputs_ref, halo_ref, places_ref, tokens_ref)
    chunks, blocks = to_slot_ref.shape
    depth = tokens_ref.shape[1] // blocks
    turned = tokens_ref[...].T
    for chunk in range(chunks):
        for block in range(blocks):
            rows = pl.ds(pl.multiple_of(to_slot_ref[chunk, block] * depth, depth), depth)
            turned_ref[chunk, rows, :] = turned[block * depth : (block + 1) * depth, :]


def finish_kernel(
    cells_ref, w_qkv_ref, normed_ref, inputs_ref, cot_ref, places_ref,
    output_ref, grad_in_ref, lower_ref, shift_ref,
):
    lat_cells = inputs_ref.shape[0]
    half = lower_ref.shape[0]
    count = places_ref.shape[1]
    shift_ref[...] = mxu(cells_ref[...], w_qkv_ref[...], NT).astype(jnp.bfloat16)
    for at, (value_ref, base_ref, result_ref) in enumerate(
        ((normed_ref, inputs_ref, output_ref), (shift_ref, cot_ref, grad_in_ref))
    ):
        result_ref[:half] = base_ref[:half]
        for band in range(lat_cells // WIN_R):
            value = value_ref[band * count : (band + 1) * count, :]
            for row in range(WIN_R):
                target = band * WIN_R + row + half
                if at == 0 and target >= lat_cells:
                    continue
                back = mxu(places_ref[row], value, TN)
                if target < lat_cells:
                    base = base_ref[target].astype(jnp.float32)
                    result_ref[target] = (base + back).astype(jnp.bfloat16)
                else:
                    lower_ref[target - lat_cells] = back.astype(jnp.bfloat16)


def forward_kernel(into_ref, x_ref, bias_ref, *rest):
    shard_refs, rest = rest[: into_ref.shape[0]], rest[into_ref.shape[0] :]
    w_qkv_ref, w_out_ref, qkv_ref, probs_ref, mixed_ref = rest
    windows, win = bias_ref.shape[:2]
    width = x_ref.shape[1]
    head_dim = width // HEADS
    group = GROUP * head_dim
    factor = head_dim ** (-0.5) * math.log2(math.e)

    blocks = into_ref.shape[0]
    depth = width // blocks
    for at, shard_ref in enumerate(shard_refs):
        rows = pl.ds(pl.multiple_of(into_ref[at] * depth, depth), depth)
        w_qkv_ref[rows, :] = shard_ref[:, : 3 * width]
        w_out_ref[rows, :] = shard_ref[:, 3 * width :]

    for part in range(3):
        columns = slice(part * width, (part + 1) * width)
        qkv_ref[:, columns] = mxu(x_ref[...], w_qkv_ref[:, columns]).astype(jnp.bfloat16)

    def attend(window, carry):
        rows = pl.ds(pl.multiple_of(window * win, 16), win)
        bias = bias_ref[window]
        for at in range(HEADS // GROUP):
            columns = slice(at * group, (at + 1) * group)
            queries = qkv_ref[rows, columns]
            keys = qkv_ref[rows, width + at * group : width + (at + 1) * group]
            values = qkv_ref[rows, 2 * width + at * group : 2 * width + (at + 1) * group]
            scores = mxu(masked_heads(keys, head_dim), queries, NT)
            scores = scores.reshape(GROUP, win, win) * factor + bias
            lifted = jnp.exp2(scores - jnp.max(scores, axis=1, keepdims=True))
            total = jnp.sum(lifted, axis=1, keepdims=True)
            probs = (lifted * (1.0 / total)).astype(jnp.bfloat16)
            probs = probs.reshape(GROUP * win, win)
            probs_ref[window, at] = probs
            mixed = own_heads(mxu(turned_heads(probs, GROUP), values), head_dim)
            mixed_ref[rows, columns] = mixed.astype(jnp.bfloat16)
        return carry

    window_loop(windows, attend)


def norm_kernel(
    mixed_ref, w_out_ref, cot_ref, gain_ref, normed_ref, grad_proj_ref, grad_mix_ref
):
    win = padded_rows()
    windows = mixed_ref.shape[0] // win
    gain = gain_ref[...]

    def normalise(window, carry):
        rows = pl.ds(pl.multiple_of(window * win, 16), win)
        projected = mxu(mixed_ref[rows, :], w_out_ref[...])
        center = projected - jnp.mean(projected, axis=-1, keepdims=True)
        inverse = lax.rsqrt(jnp.mean(center * center, axis=-1, keepdims=True) + EPS)
        normal = center * inverse
        normed_ref[rows, :] = (normal * gain).astype(jnp.bfloat16)
        scaled = cot_ref[rows, :].astype(jnp.float32) * gain
        grad_proj = (
            scaled
            - jnp.mean(scaled, axis=-1, keepdims=True)
            - normal * jnp.mean(scaled * normal, axis=-1, keepdims=True)
        ) * inverse
        grad_proj_ref[rows, :] = grad_proj.astype(jnp.bfloat16)
        return carry

    window_loop(windows, normalise)
    grad_mix_ref[...] = mxu(grad_proj_ref[...], w_out_ref[...], NT).astype(jnp.bfloat16)


def edge_kernel(value_ref, places_ref, lower_ref):
    half = lower_ref.shape[0]
    value = value_ref[value_ref.shape[0] - places_ref.shape[1] :, :]
    for row in range(half):
        back = mxu(places_ref[WIN_R - half + row], value, TN)
        lower_ref[row] = back.astype(jnp.bfloat16)


def backward_kernel(
    to_slot_ref, qkv_ref, probs_ref, mixed_ref, grad_proj_ref, grad_mix_ref, turned_ref,
    cells_ref, *grad_refs,
):
    windows, win = probs_ref.shape[0], probs_ref.shape[-1]
    width = grad_mix_ref.shape[1]
    head_dim = width // HEADS
    group = GROUP * head_dim
    scale = head_dim ** (-0.5)
    blocks = to_slot_ref.shape[1]
    depth = width // blocks
    half = width // 2
    sent_refs, kept_refs = grad_refs[::2], grad_refs[1::2]
    grad_out = mxu(mixed_ref[...], grad_proj_ref[...], TN)
    for block in range(blocks):
        slot = to_slot_ref[0, block]
        value = grad_out[block * depth : (block + 1) * depth, :]
        rows = pl.ds(pl.multiple_of(lax.rem(slot, blocks // 2) * depth, depth), depth)

        @pl.when(slot < blocks // 2)
        def _():
            kept_refs[0][rows, :width] = value

        @pl.when(slot >= blocks // 2)
        def _():
            sent_refs[0][rows, :width] = value

    def attend_back(window, carry):
        rows = pl.ds(pl.multiple_of(window * win, 16), win)
        for at in range(HEADS // GROUP):
            columns = slice(at * group, (at + 1) * group)
            key_columns = slice(width + at * group, width + (at + 1) * group)
            value_columns = slice(2 * width + at * group, 2 * width + (at + 1) * group)
            mix = grad_mix_ref[rows, columns]
            probs = probs_ref[window, at]
            float_probs = probs.astype(jnp.float32)
            grad_probs = mxu(masked_heads(qkv_ref[rows, value_columns], head_dim), mix, NT)
            product = (float_probs * grad_probs).reshape(GROUP, win, win)
            center = jnp.sum(product, axis=1, keepdims=True)
            grad_scores = scale * (product - float_probs.reshape(GROUP, win, win) * center)
            grad_scores = grad_scores.astype(jnp.bfloat16).reshape(GROUP * win, win)
            grad_values = own_heads(mxu(probs, mix), head_dim)
            grad_keys = own_heads(mxu(grad_scores, qkv_ref[rows, columns]), head_dim)
            turned = turned_heads(grad_scores, GROUP)
            grad_queries = own_heads(mxu(turned, qkv_ref[rows, key_columns]), head_dim)
            cells_ref[rows, columns] = grad_queries.astype(jnp.bfloat16)
            cells_ref[rows, key_columns] = grad_keys.astype(jnp.bfloat16)
            cells_ref[rows, value_columns] = grad_values.astype(jnp.bfloat16)
        return carry

    window_loop(windows, attend_back)

    for part, place in enumerate(GRAD_PLACES):
        columns = slice(part * width, (part + 1) * width)
        chunk = sum(place >= sum(CHUNKS[: at + 1]) for at in range(len(CHUNKS)))
        place -= sum(CHUNKS[:chunk])
        target = slice(place * width, (place + 1) * width)
        turned = turned_ref.at[TABLES.index(ROUTES[chunk])]
        sent_refs[chunk][:, target] = mxu(turned[half:, :], cells_ref[:, columns])
        kept_refs[chunk][:, target] = mxu(turned[:half, :], cells_ref[:, columns])


def coded(value):
    top = jnp.max(jnp.abs(value), axis=1, keepdims=True)
    exponent = jnp.ceil(jnp.log2(jnp.maximum(top, 1e-30)))
    codes = jnp.round(value * (jnp.exp2(-exponent) * STEPS)).astype(jnp.int32)
    exponents = jnp.broadcast_to(exponent, (value.shape[0], 128)).astype(jnp.int32)
    return codes.astype(jnp.int16), exponents.astype(jnp.int16)


def decoded(codes, exponents):
    exponent = exponents.astype(jnp.int32).astype(jnp.float32)[:, :1]
    return codes.astype(jnp.int32).astype(jnp.float32) * (jnp.exp2(exponent) * (1 / STEPS))


def added(arrived_ref, kept_ref, rows, columns):
    total = kept_ref.shape[1]
    arrived = arrived_ref[rows, columns]
    if arrived_ref.shape[1] > total:
        arrived = decoded(arrived, arrived_ref[rows, total:])
    return kept_ref[rows, columns] + arrived


def fold_kernel(arrived_ref, kept_ref, half_ref, coded_ref):
    rows, columns = half_ref.shape
    every = slice(0, columns)
    half_ref[...] = added(arrived_ref, kept_ref, slice(0, rows), every)
    codes, exponents = coded(added(arrived_ref, kept_ref, slice(rows, 2 * rows), every))
    coded_ref[:, :columns] = codes
    coded_ref[:, columns:] = exponents


def last_kernel(*refs):
    pair_refs, (grad_out_ref, grad_qkv_ref) = refs[:-2], refs[-2:]
    rows, width = grad_out_ref.shape
    every = slice(0, rows)
    quarters = []
    for at, quarter_count in enumerate(CHUNKS):
        for place in range(quarter_count):
            columns = slice(place * width, (place + 1) * width)
            quarters.append((pair_refs[2 * at], pair_refs[2 * at + 1], every, columns))
    grad_out_ref[...] = added(*quarters[0])
    for part, place in enumerate(GRAD_PLACES):
        grad_qkv_ref[:, part * width : (part + 1) * width] = added(*quarters[place])


def exchanged(value, distance):
    count = lax.axis_size("lat")
    return lax.ppermute(value, "lat", [(i, i ^ distance) for i in range(count)])


def moved(value, grp_turn, distance):
    count = lax.axis_size("lat")
    groups = lax.axis_size("grp")
    pairs = []
    for grp in range(groups):
        for i in range(count):
            pairs.append((grp * count + i, (grp ^ grp_turn) * count + (i ^ distance[grp])))
    return lax.ppermute(value, ("grp", "lat"), pairs)


def gathered(block, upper_in, cot_edge, prepare, bias):
    here = lax.axis_index("grp") == 0
    far = moved(block, 0, (8, 12))
    upper_in = passed_along(upper_in, "lat", -1)
    near = moved(block, 0, (4, 6))
    side = exchanged(block, 2)
    far, near, side, bias, cot_edge = lax.optimization_barrier((far, near, side, bias, cot_edge))
    far_side, far_other = exchanged(far, 2), moved(far, 1, (0, 0))
    near_other = moved(near, 1, (0, 0))
    early = [exchanged(shard, 1) for shard in (block, side, near, far)]
    far_side, near_other, upper_in, early = lax.optimization_barrier(
        (far_side, near_other, upper_in, early)
    )
    far_side_other = moved(far_side, 1, (0, 0))
    upper_cot = passed_along(cot_edge, "lat", -1)
    prepared = prepare(upper_in)
    shards = [block, side, near, near_other, far, far_other, far_side]
    late = [exchanged(shard, 1) for shard in (near_other, far_other, far_side)]
    far_side_other, upper_cot, rest = lax.optimization_barrier(
        (far_side_other, upper_cot, late + list(prepared))
    )
    late, prepared = rest[: len(late)], rest[len(late) :]
    swapped = early[:3] + [late[0], early[3]] + late[1:]
    shards += [far_side_other] + swapped + [exchanged(far_side_other, 1)]
    low = jnp.array([0, 2, 4, 6, 8, 12, 10, 14], jnp.int32)
    high = jnp.array([0, 2, 6, 4, 12, 8, 14, 10], jnp.int32)
    order = jnp.where(here, low, high)
    return tuple(shards), jnp.concatenate([order, order + 1]), prepared, upper_cot, bias


def slots_of(distances, steps):
    result = 0
    for step in steps:
        result = 2 * result + ((distances // step) & 1)
    return result


def fold(arrived, kept):
    rows, columns = kept.shape
    outs = (
        jax.ShapeDtypeStruct((rows // 2, columns), jnp.float32),
        jax.ShapeDtypeStruct((rows // 2, columns + 128), jnp.int16),
    )
    return call(fold_kernel, "fold", outs, (), (arrived, kept), flops=8 * rows * columns, vmem=16)


def call(kernel, name, outs, tables, operands, scratch=(), flops=0, vmem=40):
    size = sum(math.prod(o.shape) * o.dtype.itemsize for o in (*outs, *operands))
    return pl.pallas_call(
        kernel,
        out_shape=outs,
        in_specs=[pl.BlockSpec(memory_space=pltpu.SMEM)] * len(tables)
        + [pl.BlockSpec(memory_space=pltpu.VMEM)] * len(operands),
        out_specs=[pl.BlockSpec(memory_space=pltpu.VMEM)] * len(outs),
        scratch_shapes=list(scratch),
        compiler_params=pltpu.CompilerParams(vmem_limit_bytes=vmem * 1024 * 1024),
        cost_estimate=pl.CostEstimate(flops=flops, bytes_accessed=size, transcendentals=0),
        name=name,
    )(*tables, *operands)


def per_device(inputs, cotangent, idents, w_qkv, w_out, gain):
    lat_cells, lon_cells, width = inputs.shape
    half_rows = WIN_R // 2
    win = padded_rows()
    windows = (lat_cells // WIN_R) * (lon_cells // WIN_C)
    cells = windows * win
    places = jnp.asarray(window_places(lon_cells), jnp.bfloat16)

    def shape(*dims, dtype=jnp.bfloat16):
        return jax.ShapeDtypeStruct(dims, dtype)

    count = lax.axis_size("lat")
    me = lax.axis_index("lat")
    direct = count == 16 and lax.axis_size("grp") == 2 and width % (16 * count) == 0
    if direct:
        distances = jnp.arange(count, dtype=jnp.int32) ^ me
        to_slot = jnp.stack([slots_of(distances, route) for route in TABLES])
    else:
        to_slot = jnp.stack([jnp.arange(16, dtype=jnp.int32)] * len(TABLES))

    def prepare(upper_in):
        return call(
            prepare_kernel,
            "prepare",
            (shape(cells, width), shape(len(TABLES), width, cells)),
            (to_slot,),
            (inputs, upper_in, places),
            flops=2 * cells * width * lon_cells * WIN_R,
            vmem=16,
        )

    weights = jnp.pad(w_qkv, ((0, 0), (0, width))) + jnp.pad(w_out, ((0, 0), (3 * width, 0)))
    in_edge, cot_edge = inputs[:half_rows], cotangent[:half_rows]
    labels = to_windows(idents + 1)
    bias = jnp.where(labels[:, :, None] == labels[:, None, :], 0.0, HIDDEN).astype(jnp.float32)
    if direct:
        shards, order, (tokens, turned), upper_cot, bias = gathered(
            weights, in_edge, cot_edge, prepare, bias
        )
        into = order ^ me
    else:
        weights = lax.all_gather(weights, "lat", axis=0, tiled=True)
        shards = tuple(weights.reshape(16, width // 16, 4 * width))
        into = to_slot[0]
        tokens, turned = prepare(passed_along(in_edge, "lat", -1))
        upper_cot = passed_along(cot_edge, "lat", -1)

    qkv_full, out_full, qkv, probs, mixed = call(
        forward_kernel,
        "forward",
        (
            shape(width, 3 * width),
            shape(width, width),
            shape(cells, 3 * width),
            shape(windows, HEADS // GROUP, GROUP * win, win),
            shape(cells, width),
        ),
        (into,),
        (tokens, bias, *shards),
        flops=2 * cells * width * width * 4,
        vmem=20,
    )
    (cot,) = call(
        shift_kernel,
        "shift",
        (shape(cells, width),),
        (),
        (cotangent, upper_cot, places),
        flops=2 * cells * width * lon_cells * WIN_R,
        vmem=16,
    )
    normed, grad_proj, grad_mix = call(
        norm_kernel,
        "norm",
        (shape(cells, width),) * 3,
        (),
        (mixed, out_full, cot, gain[None]),
        flops=2 * cells * width * width * 2,
        vmem=16,
    )
    (lower_out,) = call(
        edge_kernel,
        "edge",
        (shape(half_rows, lon_cells, width),),
        (),
        (normed, places),
        flops=2 * cells * width * lon_cells * half_rows,
        vmem=16,
    )
    lower_out = passed_along(lower_out, "lat", 1)
    grad_cells, *grads = call(
        backward_kernel,
        "backward",
        (
            shape(cells, 3 * width),
            *[shape(width // 2, CHUNKS[at // 2] * width, dtype=jnp.float32) for at in range(2 * len(CHUNKS))],
        ),
        (to_slot,),
        (qkv, probs, mixed, grad_proj, grad_mix, turned),
        flops=2 * cells * width * width * 6,
        vmem=30,
    )
    lower_out, grad_cells, *grads = lax.optimization_barrier((lower_out, grad_cells, *grads))

    def finish(normed, grad_cells):
        return call(
            finish_kernel,
            "finish",
            (shape(*inputs.shape), shape(*inputs.shape), shape(half_rows, lon_cells, width)),
            (),
            (grad_cells, qkv_full, normed, inputs, cotangent, places),
            (pltpu.VMEM((cells, width), jnp.bfloat16),),
            flops=2 * cells * width * (3 * width + 2 * lon_cells * WIN_R),
            vmem=24,
        )

    if direct:
        pairs = [(exchanged(sent, 1), kept) for sent, kept in zip(grads[::2], grads[1::2])]
        pairs = [fold(arrived, kept) for arrived, kept in pairs]
        kept, sent = pairs[-1]
        sent, normed, grad_cells = lax.optimization_barrier((sent, normed, grad_cells))
        pairs[-1] = (kept, sent)
        output, grad_in, lower = finish(normed, grad_cells)
        for step in (1, 2, 3):
            pairs = [
                (exchanged(sent, route[step]), kept) for route, (kept, sent) in zip(ROUTES, pairs)
            ]
            if step == 1:
                arrived, kept = pairs[-1]
                arrived, lower = lax.optimization_barrier((arrived, lower))
                kept, sent = fold(arrived, kept)
                arrived, first_kept = pairs[0]
                arrived, kept, lower = lax.optimization_barrier((arrived, kept, lower))
                pairs[0], last = (arrived, first_kept), (kept, sent)
                pairs = [fold(arrived, kept) for arrived, kept in pairs[:-1]] + [last]
                kept, sent = pairs[0]
                kept, lower = lax.optimization_barrier((kept, lower))
                pairs[0] = (kept, sent)
                lower = passed_along(lower, "lat", 1)
                continue
            if step == 3:
                arrived, kept = pairs[0]
                arrived, lower = lax.optimization_barrier((arrived, lower))
                pairs[0] = (arrived, kept)
            if step == 3:
                break
            pairs = [fold(arrived, kept) for arrived, kept in pairs]
        grad_out, grad_qkv = call(
            last_kernel,
            "last",
            (
                shape(width // count, width, dtype=jnp.float32),
                shape(width // count, 3 * width, dtype=jnp.float32),
            ),
            (),
            [value for pair in pairs for value in pair],
            flops=8 * width * width,
            vmem=16,
        )
    else:
        whole = [jnp.concatenate([kept, sent]) for sent, kept in zip(grads[::2], grads[1::2])]
        both = lax.psum_scatter(jnp.concatenate(whole, axis=1), "lat", scatter_dimension=0, tiled=True)
        quarters = jnp.split(both, 4, axis=1)
        grad_out = quarters[0]
        grad_qkv = jnp.concatenate([quarters[place] for place in GRAD_PLACES], axis=1)
        output, grad_in, lower = finish(normed, grad_cells)
        lower = passed_along(lower, "lat", 1)

    def completed(result, lower):
        top = result[:half_rows].astype(jnp.float32) + lower.astype(jnp.float32)
        return result.at[:half_rows].set(top.astype(jnp.bfloat16))

    return (completed(output, lower_out), completed(grad_in, lower), grad_qkv, grad_out)


def solution(mesh):
    in_specs = (
        P(("grp", "lat"), None, None),
        P(("grp", "lat"), None, None),
        P(("grp", "lat"), None),
        P("lat", None),
        P("lat", None),
        P(),
    )
    out_specs = (
        P(("grp", "lat"), None, None),
        P(("grp", "lat"), None, None),
        P(("grp", "lat"), None),
        P(("grp", "lat"), None),
    )
    return jax.shard_map(
        per_device, mesh=mesh, in_specs=in_specs, out_specs=out_specs, check_vma=False
    )
```

```python
import math

import jax
import jax.numpy as jnp
import numpy as np
from jax import lax
from jax.experimental import pallas as pl
from jax.experimental.pallas import tpu as pltpu
from jax.sharding import PartitionSpec as P

HEADS = 8
WIN_R = 6
WIN_C = 12
EPS = 1e-05
HIDDEN = -1e30
STEPS = 32000.0
GRAD_PLACES = (3, 2, 1)
CHUNKS = (2, 1, 1)
ROUTES = ((1, 2, 4, 8), (1, 2, 4, 8), (1, 4, 8, 2))
TABLES = tuple(dict.fromkeys(ROUTES))
UNROLL = 9
GROUP = 4

NN = (((1,), (0,)), ((), ()))
NT = (((1,), (1,)), ((), ()))
TN = (((0,), (0,)), ((), ()))


def mxu(left, right, dims=NN):
    return lax.dot_general(left, right, dims, preferred_element_type=jnp.float32)


def passed_along(value, axis, steps):
    count = lax.axis_size(axis)
    first, last = (max(0, -steps), min(count, count - steps))
    return lax.ppermute(value, axis, [(source, source + steps) for source in range(first, last)])


def padded_rows():
    return -(-WIN_R * WIN_C // 16) * 16


def to_windows(field):
    lat_cells, lon_cells = field.shape
    field = field.reshape(lat_cells // WIN_R, WIN_R, lon_cells // WIN_C, WIN_C)
    field = field.transpose(0, 2, 1, 3).reshape(-1, WIN_R * WIN_C)
    return jnp.pad(field, ((0, 0), (0, padded_rows() - WIN_R * WIN_C)))


def window_places(lon_cells):
    win = padded_rows()
    places = np.zeros((WIN_R, lon_cells // WIN_C, win, lon_cells), np.float32)
    for row in range(WIN_R):
        for window in range(lon_cells // WIN_C):
            for column in range(WIN_C):
                source = (window * WIN_C + column + WIN_C // 2) % lon_cells
                places[row, window, row * WIN_C + column, source] = 1
    return places.reshape(WIN_R, -1, lon_cells)


def masked_heads(value, head_dim):
    head = lax.broadcasted_iota(jnp.int32, value.shape, 1) // head_dim
    zero = jnp.zeros_like(value)
    count = value.shape[1] // head_dim
    return jnp.concatenate([jnp.where(head == at, value, zero) for at in range(count)], axis=0)


def own_heads(stacked, head_dim):
    count = stacked.shape[1] // head_dim
    rows = stacked.shape[0] // count
    head = lax.broadcasted_iota(jnp.int32, (rows, stacked.shape[1]), 1) // head_dim
    result = stacked[:rows]
    for at in range(1, count):
        result = jnp.where(head == at, stacked[at * rows : (at + 1) * rows], result)
    return result


def turned_heads(stacked, count):
    rows = stacked.shape[0] // count
    return jnp.concatenate(
        [stacked[at * rows : (at + 1) * rows].T for at in range(count)], axis=0
    )


def shift_kernel(own_ref, halo_ref, places_ref, result_ref):
    half = halo_ref.shape[0]
    lat_cells = own_ref.shape[0]
    cells = places_ref.shape[1]
    for band in range(lat_cells // WIN_R):
        total = None
        for row in range(WIN_R):
            source = band * WIN_R + row + half
            field = own_ref[source] if source < lat_cells else halo_ref[source - lat_cells]
            term = mxu(places_ref[row], field)
            total = term if total is None else total + term
        result_ref[band * cells : (band + 1) * cells, :] = total.astype(jnp.bfloat16)


def window_loop(windows, body):
    lax.fori_loop(0, windows, body, 0, unroll=UNROLL if windows % UNROLL == 0 else 1)


def prepare_kernel(to_slot_ref, inputs_ref, halo_ref, places_ref, tokens_ref, turned_ref):
    shift_kernel(inputs_ref, halo_ref, places_ref, tokens_ref)
    chunks, blocks = to_slot_ref.shape
    depth = tokens_ref.shape[1] // blocks
    turned = tokens_ref[...].T
    for chunk in range(chunks):
        for block in range(blocks):
            rows = pl.ds(pl.multiple_of(to_slot_ref[chunk, block] * depth, depth), depth)
            turned_ref[chunk, rows, :] = turned[block * depth : (block + 1) * depth, :]


def finish_kernel(
    cells_ref, w_qkv_ref, normed_ref, inputs_ref, cot_ref, places_ref,
    output_ref, grad_in_ref, lower_ref, shift_ref,
):
    lat_cells = inputs_ref.shape[0]
    half = lower_ref.shape[0]
    count = places_ref.shape[1]
    shift_ref[...] = mxu(cells_ref[...], w_qkv_ref[...], NT).astype(jnp.bfloat16)
    for at, (value_ref, base_ref, result_ref) in enumerate(
        ((normed_ref, inputs_ref, output_ref), (shift_ref, cot_ref, grad_in_ref))
    ):
        result_ref[:half] = base_ref[:half]
        for band in range(lat_cells // WIN_R):
            value = value_ref[band * count : (band + 1) * count, :]
            for row in range(WIN_R):
                target = band * WIN_R + row + half
                if at == 0 and target >= lat_cells:
                    continue
                back = mxu(places_ref[row], value, TN)
                if target < lat_cells:
                    base = base_ref[target].astype(jnp.float32)
                    result_ref[target] = (base + back).astype(jnp.bfloat16)
                else:
                    lower_ref[target - lat_cells] = back.astype(jnp.bfloat16)


def forward_kernel(into_ref, x_ref, bias_ref, *rest):
    shard_refs, rest = rest[: into_ref.shape[0]], rest[into_ref.shape[0] :]
    w_qkv_ref, w_out_ref, qkv_ref, probs_ref, mixed_ref = rest
    windows, win = bias_ref.shape[:2]
    width = x_ref.shape[1]
    head_dim = width // HEADS
    group = GROUP * head_dim
    factor = head_dim ** (-0.5) * math.log2(math.e)

    blocks = into_ref.shape[0]
    depth = width // blocks
    for at, shard_ref in enumerate(shard_refs):
        rows = pl.ds(pl.multiple_of(into_ref[at] * depth, depth), depth)
        w_qkv_ref[rows, :] = shard_ref[:, : 3 * width]
        w_out_ref[rows, :] = shard_ref[:, 3 * width :]

    for part in range(3):
        columns = slice(part * width, (part + 1) * width)
        qkv_ref[:, columns] = mxu(x_ref[...], w_qkv_ref[:, columns]).astype(jnp.bfloat16)

    def attend(window, carry):
        rows = pl.ds(pl.multiple_of(window * win, 16), win)
        bias = bias_ref[window]
        for at in range(HEADS // GROUP):
            columns = slice(at * group, (at + 1) * group)
            queries = qkv_ref[rows, columns]
            keys = qkv_ref[rows, width + at * group : width + (at + 1) * group]
            values = qkv_ref[rows, 2 * width + at * group : 2 * width + (at + 1) * group]
            scores = mxu(masked_heads(keys, head_dim), queries, NT)
            scores = scores.reshape(GROUP, win, win) * factor + bias
            lifted = jnp.exp2(scores - jnp.max(scores, axis=1, keepdims=True))
            total = jnp.sum(lifted, axis=1, keepdims=True)
            probs = (lifted * (1.0 / total)).astype(jnp.bfloat16)
            probs = probs.reshape(GROUP * win, win)
            probs_ref[window, at] = probs
            mixed = own_heads(mxu(turned_heads(probs, GROUP), values), head_dim)
            mixed_ref[rows, columns] = mixed.astype(jnp.bfloat16)
        return carry

    window_loop(windows, attend)


def norm_kernel(
    mixed_ref, w_out_ref, cot_ref, gain_ref, normed_ref, grad_proj_ref, grad_mix_ref
):
    win = padded_rows()
    windows = mixed_ref.shape[0] // win
    gain = gain_ref[...]

    def normalise(window, carry):
        rows = pl.ds(pl.multiple_of(window * win, 16), win)
        projected = mxu(mixed_ref[rows, :], w_out_ref[...])
        center = projected - jnp.mean(projected, axis=-1, keepdims=True)
        inverse = lax.rsqrt(jnp.mean(center * center, axis=-1, keepdims=True) + EPS)
        normal = center * inverse
        normed_ref[rows, :] = (normal * gain).astype(jnp.bfloat16)
        scaled = cot_ref[rows, :].astype(jnp.float32) * gain
        grad_proj = (
            scaled
            - jnp.mean(scaled, axis=-1, keepdims=True)
            - normal * jnp.mean(scaled * normal, axis=-1, keepdims=True)
        ) * inverse
        grad_proj_ref[rows, :] = grad_proj.astype(jnp.bfloat16)
        return carry

    window_loop(windows, normalise)
    grad_mix_ref[...] = mxu(grad_proj_ref[...], w_out_ref[...], NT).astype(jnp.bfloat16)


def edge_kernel(value_ref, places_ref, lower_ref):
    half = lower_ref.shape[0]
    value = value_ref[value_ref.shape[0] - places_ref.shape[1] :, :]
    for row in range(half):
        back = mxu(places_ref[WIN_R - half + row], value, TN)
        lower_ref[row] = back.astype(jnp.bfloat16)


def backward_kernel(
    to_slot_ref, qkv_ref, probs_ref, mixed_ref, grad_proj_ref, grad_mix_ref, turned_ref,
    cells_ref, *grad_refs,
):
    windows, win = probs_ref.shape[0], probs_ref.shape[-1]
    width = grad_mix_ref.shape[1]
    head_dim = width // HEADS
    group = GROUP * head_dim
    scale = head_dim ** (-0.5)
    blocks = to_slot_ref.shape[1]
    depth = width // blocks
    half = width // 2
    sent_refs, kept_refs = grad_refs[::2], grad_refs[1::2]
    grad_out = mxu(mixed_ref[...], grad_proj_ref[...], TN)
    for block in range(blocks):
        slot = to_slot_ref[0, block]
        value = grad_out[block * depth : (block + 1) * depth, :]
        rows = pl.ds(pl.multiple_of(lax.rem(slot, blocks // 2) * depth, depth), depth)

        @pl.when(slot < blocks // 2)
        def _():
            kept_refs[0][rows, :width] = value

        @pl.when(slot >= blocks // 2)
        def _():
            sent_refs[0][rows, :width] = value

    def attend_back(window, carry):
        rows = pl.ds(pl.multiple_of(window * win, 16), win)
        for at in range(HEADS // GROUP):
            columns = slice(at * group, (at + 1) * group)
            key_columns = slice(width + at * group, width + (at + 1) * group)
            value_columns = slice(2 * width + at * group, 2 * width + (at + 1) * group)
            mix = grad_mix_ref[rows, columns]
            probs = probs_ref[window, at]
            float_probs = probs.astype(jnp.float32)
            grad_probs = mxu(masked_heads(qkv_ref[rows, value_columns], head_dim), mix, NT)
            product = (float_probs * grad_probs).reshape(GROUP, win, win)
            center = jnp.sum(product, axis=1, keepdims=True)
            grad_scores = scale * (product - float_probs.reshape(GROUP, win, win) * center)
            grad_scores = grad_scores.astype(jnp.bfloat16).reshape(GROUP * win, win)
            grad_values = own_heads(mxu(probs, mix), head_dim)
            grad_keys = own_heads(mxu(grad_scores, qkv_ref[rows, columns]), head_dim)
            turned = turned_heads(grad_scores, GROUP)
            grad_queries = own_heads(mxu(turned, qkv_ref[rows, key_columns]), head_dim)
            cells_ref[rows, columns] = grad_queries.astype(jnp.bfloat16)
            cells_ref[rows, key_columns] = grad_keys.astype(jnp.bfloat16)
            cells_ref[rows, value_columns] = grad_values.astype(jnp.bfloat16)
        return carry

    window_loop(windows, attend_back)

    for part, place in enumerate(GRAD_PLACES):
        columns = slice(part * width, (part + 1) * width)
        chunk = sum(place >= sum(CHUNKS[: at + 1]) for at in range(len(CHUNKS)))
        place -= sum(CHUNKS[:chunk])
        target = slice(place * width, (place + 1) * width)
        turned = turned_ref.at[TABLES.index(ROUTES[chunk])]
        sent_refs[chunk][:, target] = mxu(turned[half:, :], cells_ref[:, columns])
        kept_refs[chunk][:, target] = mxu(turned[:half, :], cells_ref[:, columns])


def coded(value):
    top = jnp.max(jnp.abs(value), axis=1, keepdims=True)
    exponent = jnp.ceil(jnp.log2(jnp.maximum(top, 1e-30)))
    codes = jnp.round(value * (jnp.exp2(-exponent) * STEPS)).astype(jnp.int32)
    exponents = jnp.broadcast_to(exponent, (value.shape[0], 128)).astype(jnp.int32)
    return codes.astype(jnp.int16), exponents.astype(jnp.int16)


def decoded(codes, exponents):
    exponent = exponents.astype(jnp.int32).astype(jnp.float32)[:, :1]
    return codes.astype(jnp.int32).astype(jnp.float32) * (jnp.exp2(exponent) * (1 / STEPS))


def added(arrived_ref, kept_ref, rows, columns):
    total = kept_ref.shape[1]
    arrived = arrived_ref[rows, columns]
    if arrived_ref.shape[1] > total:
        arrived = decoded(arrived, arrived_ref[rows, total:])
    return kept_ref[rows, columns] + arrived


def fold_kernel(arrived_ref, kept_ref, half_ref, coded_ref):
    rows, columns = half_ref.shape
    every = slice(0, columns)
    half_ref[...] = added(arrived_ref, kept_ref, slice(0, rows), every)
    codes, exponents = coded(added(arrived_ref, kept_ref, slice(rows, 2 * rows), every))
    coded_ref[:, :columns] = codes
    coded_ref[:, columns:] = exponents


def last_kernel(*refs):
    pair_refs, (grad_out_ref, grad_qkv_ref) = refs[:-2], refs[-2:]
    rows, width = grad_out_ref.shape
    every = slice(0, rows)
    quarters = []
    for at, quarter_count in enumerate(CHUNKS):
        for place in range(quarter_count):
            columns = slice(place * width, (place + 1) * width)
            quarters.append((pair_refs[2 * at], pair_refs[2 * at + 1], every, columns))
    grad_out_ref[...] = added(*quarters[0])
    for part, place in enumerate(GRAD_PLACES):
        grad_qkv_ref[:, part * width : (part + 1) * width] = added(*quarters[place])


def exchanged(value, distance):
    count = lax.axis_size("lat")
    return lax.ppermute(value, "lat", [(i, i ^ distance) for i in range(count)])


def moved(value, grp_turn, distance):
    count = lax.axis_size("lat")
    groups = lax.axis_size("grp")
    pairs = []
    for grp in range(groups):
        for i in range(count):
            pairs.append((grp * count + i, (grp ^ grp_turn) * count + (i ^ distance[grp])))
    return lax.ppermute(value, ("grp", "lat"), pairs)


def gathered(block, upper_in, cot_edge, prepare, bias):
    here = lax.axis_index("grp") == 0
    far = moved(block, 0, (8, 12))
    upper_in = passed_along(upper_in, "lat", -1)
    near = moved(block, 0, (4, 6))
    side = exchanged(block, 2)
    far, near, side, bias, cot_edge = lax.optimization_barrier((far, near, side, bias, cot_edge))
    far_side, far_other = exchanged(far, 2), moved(far, 1, (0, 0))
    near_other = moved(near, 1, (0, 0))
    far_side, near_other, upper_in = lax.optimization_barrier((far_side, near_other, upper_in))
    far_side_other = moved(far_side, 1, (0, 0))
    upper_cot = passed_along(cot_edge, "lat", -1)
    prepared = prepare(upper_in)
    shards = [block, side, near, near_other, far, far_other, far_side]
    swapped = [exchanged(shard, 1) for shard in shards]
    far_side_other, rest = lax.optimization_barrier((far_side_other, swapped + list(prepared)))
    swapped, prepared = rest[: len(swapped)], rest[len(swapped) :]
    shards += [far_side_other] + swapped + [exchanged(far_side_other, 1)]
    low = jnp.array([0, 2, 4, 6, 8, 12, 10, 14], jnp.int32)
    high = jnp.array([0, 2, 6, 4, 12, 8, 14, 10], jnp.int32)
    order = jnp.where(here, low, high)
    return tuple(shards), jnp.concatenate([order, order + 1]), prepared, upper_cot, bias


def slots_of(distances, steps):
    result = 0
    for step in steps:
        result = 2 * result + ((distances // step) & 1)
    return result


def fold(arrived, kept):
    rows, columns = kept.shape
    outs = (
        jax.ShapeDtypeStruct((rows // 2, columns), jnp.float32),
        jax.ShapeDtypeStruct((rows // 2, columns + 128), jnp.int16),
    )
    return call(fold_kernel, "fold", outs, (), (arrived, kept), flops=8 * rows * columns, vmem=16)


def call(kernel, name, outs, tables, operands, scratch=(), flops=0, vmem=40):
    size = sum(math.prod(o.shape) * o.dtype.itemsize for o in (*outs, *operands))
    return pl.pallas_call(
        kernel,
        out_shape=outs,
        in_specs=[pl.BlockSpec(memory_space=pltpu.SMEM)] * len(tables)
        + [pl.BlockSpec(memory_space=pltpu.VMEM)] * len(operands),
        out_specs=[pl.BlockSpec(memory_space=pltpu.VMEM)] * len(outs),
        scratch_shapes=list(scratch),
        compiler_params=pltpu.CompilerParams(vmem_limit_bytes=vmem * 1024 * 1024),
        cost_estimate=pl.CostEstimate(flops=flops, bytes_accessed=size, transcendentals=0),
        name=name,
    )(*tables, *operands)


def per_device(inputs, cotangent, idents, w_qkv, w_out, gain):
    lat_cells, lon_cells, width = inputs.shape
    half_rows = WIN_R // 2
    win = padded_rows()
    windows = (lat_cells // WIN_R) * (lon_cells // WIN_C)
    cells = windows * win
    places = jnp.asarray(window_places(lon_cells), jnp.bfloat16)

    def shape(*dims, dtype=jnp.bfloat16):
        return jax.ShapeDtypeStruct(dims, dtype)

    count = lax.axis_size("lat")
    me = lax.axis_index("lat")
    direct = count == 16 and lax.axis_size("grp") == 2 and width % (16 * count) == 0
    if direct:
        distances = jnp.arange(count, dtype=jnp.int32) ^ me
        to_slot = jnp.stack([slots_of(distances, route) for route in TABLES])
    else:
        to_slot = jnp.stack([jnp.arange(16, dtype=jnp.int32)] * len(TABLES))

    def prepare(upper_in):
        return call(
            prepare_kernel,
            "prepare",
            (shape(cells, width), shape(len(TABLES), width, cells)),
            (to_slot,),
            (inputs, upper_in, places),
            flops=2 * cells * width * lon_cells * WIN_R,
            vmem=16,
        )

    weights = jnp.pad(w_qkv, ((0, 0), (0, width))) + jnp.pad(w_out, ((0, 0), (3 * width, 0)))
    in_edge, cot_edge = inputs[:half_rows], cotangent[:half_rows]
    labels = to_windows(idents + 1)
    bias = jnp.where(labels[:, :, None] == labels[:, None, :], 0.0, HIDDEN).astype(jnp.float32)
    if direct:
        shards, order, (tokens, turned), upper_cot, bias = gathered(
            weights, in_edge, cot_edge, prepare, bias
        )
        into = order ^ me
    else:
        weights = lax.all_gather(weights, "lat", axis=0, tiled=True)
        shards = tuple(weights.reshape(16, width // 16, 4 * width))
        into = to_slot[0]
        tokens, turned = prepare(passed_along(in_edge, "lat", -1))
        upper_cot = passed_along(cot_edge, "lat", -1)

    qkv_full, out_full, qkv, probs, mixed = call(
        forward_kernel,
        "forward",
        (
            shape(width, 3 * width),
            shape(width, width),
            shape(cells, 3 * width),
            shape(windows, HEADS // GROUP, GROUP * win, win),
            shape(cells, width),
        ),
        (into,),
        (tokens, bias, *shards),
        flops=2 * cells * width * width * 4,
        vmem=20,
    )
    (cot,) = call(
        shift_kernel,
        "shift",
        (shape(cells, width),),
        (),
        (cotangent, upper_cot, places),
        flops=2 * cells * width * lon_cells * WIN_R,
        vmem=16,
    )
    normed, grad_proj, grad_mix = call(
        norm_kernel,
        "norm",
        (shape(cells, width),) * 3,
        (),
        (mixed, out_full, cot, gain[None]),
        flops=2 * cells * width * width * 2,
        vmem=16,
    )
    (lower_out,) = call(
        edge_kernel,
        "edge",
        (shape(half_rows, lon_cells, width),),
        (),
        (normed, places),
        flops=2 * cells * width * lon_cells * half_rows,
        vmem=16,
    )
    lower_out = passed_along(lower_out, "lat", 1)
    grad_cells, *grads = call(
        backward_kernel,
        "backward",
        (
            shape(cells, 3 * width),
            *[shape(width // 2, CHUNKS[at // 2] * width, dtype=jnp.float32) for at in range(2 * len(CHUNKS))],
        ),
        (to_slot,),
        (qkv, probs, mixed, grad_proj, grad_mix, turned),
        flops=2 * cells * width * width * 6,
        vmem=30,
    )
    lower_out, grad_cells, *grads = lax.optimization_barrier((lower_out, grad_cells, *grads))

    def finish(normed, grad_cells):
        return call(
            finish_kernel,
            "finish",
            (shape(*inputs.shape), shape(*inputs.shape), shape(half_rows, lon_cells, width)),
            (),
            (grad_cells, qkv_full, normed, inputs, cotangent, places),
            (pltpu.VMEM((cells, width), jnp.bfloat16),),
            flops=2 * cells * width * (3 * width + 2 * lon_cells * WIN_R),
            vmem=24,
        )

    if direct:
        pairs = [(exchanged(sent, 1), kept) for sent, kept in zip(grads[::2], grads[1::2])]
        pairs = [fold(arrived, kept) for arrived, kept in pairs]
        kept, sent = pairs[-1]
        sent, normed, grad_cells = lax.optimization_barrier((sent, normed, grad_cells))
        pairs[-1] = (kept, sent)
        output, grad_in, lower = finish(normed, grad_cells)
        for step in (1, 2, 3):
            pairs = [
                (exchanged(sent, route[step]), kept) for route, (kept, sent) in zip(ROUTES, pairs)
            ]
            if step == 1:
                arrived, kept = pairs[-1]
                arrived, lower = lax.optimization_barrier((arrived, lower))
                kept, sent = fold(arrived, kept)
                arrived, first_kept = pairs[0]
                arrived, kept, lower = lax.optimization_barrier((arrived, kept, lower))
                pairs[0], last = (arrived, first_kept), (kept, sent)
                pairs = [fold(arrived, kept) for arrived, kept in pairs[:-1]] + [last]
                kept, sent = pairs[0]
                kept, lower = lax.optimization_barrier((kept, lower))
                pairs[0] = (kept, sent)
                lower = passed_along(lower, "lat", 1)
                continue
            if step == 3:
                arrived, kept = pairs[0]
                arrived, lower = lax.optimization_barrier((arrived, lower))
                pairs[0] = (arrived, kept)
            if step == 3:
                break
            pairs = [fold(arrived, kept) for arrived, kept in pairs]
        grad_out, grad_qkv = call(
            last_kernel,
            "last",
            (
                shape(width // count, width, dtype=jnp.float32),
                shape(width // count, 3 * width, dtype=jnp.float32),
            ),
            (),
            [value for pair in pairs for value in pair],
            flops=8 * width * width,
            vmem=16,
        )
    else:
        whole = [jnp.concatenate([kept, sent]) for sent, kept in zip(grads[::2], grads[1::2])]
        both = lax.psum_scatter(jnp.concatenate(whole, axis=1), "lat", scatter_dimension=0, tiled=True)
        quarters = jnp.split(both, 4, axis=1)
        grad_out = quarters[0]
        grad_qkv = jnp.concatenate([quarters[place] for place in GRAD_PLACES], axis=1)
        output, grad_in, lower = finish(normed, grad_cells)
        lower = passed_along(lower, "lat", 1)

    def completed(result, lower):
        top = result[:half_rows].astype(jnp.float32) + lower.astype(jnp.float32)
        return result.at[:half_rows].set(top.astype(jnp.bfloat16))

    return (completed(output, lower_out), completed(grad_in, lower), grad_qkv, grad_out)


def solution(mesh):
    in_specs = (
        P(("grp", "lat"), None, None),
        P(("grp", "lat"), None, None),
        P(("grp", "lat"), None),
        P("lat", None),
        P("lat", None),
        P(),
    )
    out_specs = (
        P(("grp", "lat"), None, None),
        P(("grp", "lat"), None, None),
        P(("grp", "lat"), None),
        P(("grp", "lat"), None),
    )
    return jax.shard_map(
        per_device, mesh=mesh, in_specs=in_specs, out_specs=out_specs, check_vma=False
    )
```

```python
import math

import jax
import jax.numpy as jnp
import numpy as np
from jax import lax
from jax.experimental import pallas as pl
from jax.experimental.pallas import tpu as pltpu
from jax.sharding import PartitionSpec as P

HEADS = 8
WIN_R = 6
WIN_C = 12
EPS = 1e-05
HIDDEN = -1e30
STEPS = 32000.0
GRAD_PLACES = (3, 2, 1)
CHUNKS = (2, 1, 1)
ROUTES = ((1, 2, 4, 8), (1, 2, 4, 8), (1, 4, 8, 2))
TABLES = tuple(dict.fromkeys(ROUTES))
UNROLL = 9
GROUP = 4

NN = (((1,), (0,)), ((), ()))
NT = (((1,), (1,)), ((), ()))
TN = (((0,), (0,)), ((), ()))


def mxu(left, right, dims=NN):
    return lax.dot_general(left, right, dims, preferred_element_type=jnp.float32)


def passed_along(value, axis, steps):
    count = lax.axis_size(axis)
    first, last = (max(0, -steps), min(count, count - steps))
    return lax.ppermute(value, axis, [(source, source + steps) for source in range(first, last)])


def padded_rows():
    return -(-WIN_R * WIN_C // 16) * 16


def to_windows(field):
    lat_cells, lon_cells = field.shape
    field = field.reshape(lat_cells // WIN_R, WIN_R, lon_cells // WIN_C, WIN_C)
    field = field.transpose(0, 2, 1, 3).reshape(-1, WIN_R * WIN_C)
    return jnp.pad(field, ((0, 0), (0, padded_rows() - WIN_R * WIN_C)))


def window_places(lon_cells):
    win = padded_rows()
    places = np.zeros((WIN_R, lon_cells // WIN_C, win, lon_cells), np.float32)
    for row in range(WIN_R):
        for window in range(lon_cells // WIN_C):
            for column in range(WIN_C):
                source = (window * WIN_C + column + WIN_C // 2) % lon_cells
                places[row, window, row * WIN_C + column, source] = 1
    return places.reshape(WIN_R, -1, lon_cells)


def masked_heads(value, head_dim):
    head = lax.broadcasted_iota(jnp.int32, value.shape, 1) // head_dim
    zero = jnp.zeros_like(value)
    count = value.shape[1] // head_dim
    return jnp.concatenate([jnp.where(head == at, value, zero) for at in range(count)], axis=0)


def own_heads(stacked, head_dim):
    count = stacked.shape[1] // head_dim
    rows = stacked.shape[0] // count
    head = lax.broadcasted_iota(jnp.int32, (rows, stacked.shape[1]), 1) // head_dim
    result = stacked[:rows]
    for at in range(1, count):
        result = jnp.where(head == at, stacked[at * rows : (at + 1) * rows], result)
    return result


def turned_heads(stacked, count):
    rows = stacked.shape[0] // count
    return jnp.concatenate(
        [stacked[at * rows : (at + 1) * rows].T for at in range(count)], axis=0
    )


def shift_kernel(own_ref, halo_ref, places_ref, result_ref):
    half = halo_ref.shape[0]
    lat_cells = own_ref.shape[0]
    cells = places_ref.shape[1]
    for band in range(lat_cells // WIN_R):
        total = None
        for row in range(WIN_R):
            source = band * WIN_R + row + half
            field = own_ref[source] if source < lat_cells else halo_ref[source - lat_cells]
            term = mxu(places_ref[row], field)
            total = term if total is None else total + term
        result_ref[band * cells : (band + 1) * cells, :] = total.astype(jnp.bfloat16)


def window_loop(windows, body):
    lax.fori_loop(0, windows, body, 0, unroll=UNROLL if windows % UNROLL == 0 else 1)


def prepare_kernel(to_slot_ref, inputs_ref, halo_ref, places_ref, tokens_ref, turned_ref):
    shift_kernel(inputs_ref, halo_ref, places_ref, tokens_ref)
    chunks, blocks = to_slot_ref.shape
    depth = tokens_ref.shape[1] // blocks
    turned = tokens_ref[...].T
    for chunk in range(chunks):
        for block in range(blocks):
            rows = pl.ds(pl.multiple_of(to_slot_ref[chunk, block] * depth, depth), depth)
            turned_ref[chunk, rows, :] = turned[block * depth : (block + 1) * depth, :]


def finish_kernel(
    cells_ref, w_qkv_ref, normed_ref, inputs_ref, cot_ref, places_ref,
    output_ref, grad_in_ref, lower_ref, shift_ref,
):
    lat_cells = inputs_ref.shape[0]
    half = lower_ref.shape[0]
    count = places_ref.shape[1]
    shift_ref[...] = mxu(cells_ref[...], w_qkv_ref[...], NT).astype(jnp.bfloat16)
    for at, (value_ref, base_ref, result_ref) in enumerate(
        ((normed_ref, inputs_ref, output_ref), (shift_ref, cot_ref, grad_in_ref))
    ):
        result_ref[:half] = base_ref[:half]
        for band in range(lat_cells // WIN_R):
            value = value_ref[band * count : (band + 1) * count, :]
            for row in range(WIN_R):
                target = band * WIN_R + row + half
                if at == 0 and target >= lat_cells:
                    continue
                back = mxu(places_ref[row], value, TN)
                if target < lat_cells:
                    base = base_ref[target].astype(jnp.float32)
                    result_ref[target] = (base + back).astype(jnp.bfloat16)
                else:
                    lower_ref[target - lat_cells] = back.astype(jnp.bfloat16)


def forward_kernel(into_ref, x_ref, bias_ref, *rest):
    shard_refs, rest = rest[: into_ref.shape[0]], rest[into_ref.shape[0] :]
    w_qkv_ref, w_out_ref, qkv_ref, probs_ref, mixed_ref = rest
    windows, win = bias_ref.shape[:2]
    width = x_ref.shape[1]
    head_dim = width // HEADS
    group = GROUP * head_dim
    factor = head_dim ** (-0.5) * math.log2(math.e)

    blocks = into_ref.shape[0]
    depth = width // blocks
    for at, shard_ref in enumerate(shard_refs):
        rows = pl.ds(pl.multiple_of(into_ref[at] * depth, depth), depth)
        w_qkv_ref[rows, :] = shard_ref[:, : 3 * width]
        w_out_ref[rows, :] = shard_ref[:, 3 * width :]

    for part in range(3):
        columns = slice(part * width, (part + 1) * width)
        qkv_ref[:, columns] = mxu(x_ref[...], w_qkv_ref[:, columns]).astype(jnp.bfloat16)

    def attend(window, carry):
        rows = pl.ds(pl.multiple_of(window * win, 16), win)
        bias = bias_ref[window]
        for at in range(HEADS // GROUP):
            columns = slice(at * group, (at + 1) * group)
            queries = qkv_ref[rows, columns]
            keys = qkv_ref[rows, width + at * group : width + (at + 1) * group]
            values = qkv_ref[rows, 2 * width + at * group : 2 * width + (at + 1) * group]
            scores = mxu(masked_heads(keys, head_dim), queries, NT)
            scores = scores.reshape(GROUP, win, win) * factor + bias
            lifted = jnp.exp2(scores - jnp.max(scores, axis=1, keepdims=True))
            total = jnp.sum(lifted, axis=1, keepdims=True)
            probs = (lifted * (1.0 / total)).astype(jnp.bfloat16)
            probs = probs.reshape(GROUP * win, win)
            probs_ref[window, at] = probs
            mixed = own_heads(mxu(turned_heads(probs, GROUP), values), head_dim)
            mixed_ref[rows, columns] = mixed.astype(jnp.bfloat16)
        return carry

    window_loop(windows, attend)


def norm_kernel(
    mixed_ref, w_out_ref, cot_ref, gain_ref, normed_ref, grad_proj_ref, grad_mix_ref
):
    win = padded_rows()
    windows = mixed_ref.shape[0] // win
    gain = gain_ref[...]

    def normalise(window, carry):
        rows = pl.ds(pl.multiple_of(window * win, 16), win)
        projected = mxu(mixed_ref[rows, :], w_out_ref[...])
        center = projected - jnp.mean(projected, axis=-1, keepdims=True)
        inverse = lax.rsqrt(jnp.mean(center * center, axis=-1, keepdims=True) + EPS)
        normal = center * inverse
        normed_ref[rows, :] = (normal * gain).astype(jnp.bfloat16)
        scaled = cot_ref[rows, :].astype(jnp.float32) * gain
        grad_proj = (
            scaled
            - jnp.mean(scaled, axis=-1, keepdims=True)
            - normal * jnp.mean(scaled * normal, axis=-1, keepdims=True)
        ) * inverse
        grad_proj_ref[rows, :] = grad_proj.astype(jnp.bfloat16)
        return carry

    window_loop(windows, normalise)
    grad_mix_ref[...] = mxu(grad_proj_ref[...], w_out_ref[...], NT).astype(jnp.bfloat16)


def edge_kernel(value_ref, places_ref, lower_ref):
    half = lower_ref.shape[0]
    value = value_ref[value_ref.shape[0] - places_ref.shape[1] :, :]
    for row in range(half):
        back = mxu(places_ref[WIN_R - half + row], value, TN)
        lower_ref[row] = back.astype(jnp.bfloat16)


def backward_kernel(
    to_slot_ref, qkv_ref, probs_ref, mixed_ref, grad_proj_ref, grad_mix_ref, turned_ref,
    cells_ref, *grad_refs,
):
    windows, win = probs_ref.shape[0], probs_ref.shape[-1]
    width = grad_mix_ref.shape[1]
    head_dim = width // HEADS
    group = GROUP * head_dim
    scale = head_dim ** (-0.5)
    blocks = to_slot_ref.shape[1]
    depth = width // blocks
    half = width // 2
    sent_refs, kept_refs = grad_refs[::2], grad_refs[1::2]
    grad_out = mxu(mixed_ref[...], grad_proj_ref[...], TN)
    for block in range(blocks):
        slot = to_slot_ref[0, block]
        value = grad_out[block * depth : (block + 1) * depth, :]
        rows = pl.ds(pl.multiple_of(lax.rem(slot, blocks // 2) * depth, depth), depth)

        @pl.when(slot < blocks // 2)
        def _():
            kept_refs[0][rows, :width] = value

        @pl.when(slot >= blocks // 2)
        def _():
            sent_refs[0][rows, :width] = value

    def attend_back(window, carry):
        rows = pl.ds(pl.multiple_of(window * win, 16), win)
        for at in range(HEADS // GROUP):
            columns = slice(at * group, (at + 1) * group)
            key_columns = slice(width + at * group, width + (at + 1) * group)
            value_columns = slice(2 * width + at * group, 2 * width + (at + 1) * group)
            mix = grad_mix_ref[rows, columns]
            probs = probs_ref[window, at]
            float_probs = probs.astype(jnp.float32)
            grad_probs = mxu(masked_heads(qkv_ref[rows, value_columns], head_dim), mix, NT)
            product = (float_probs * grad_probs).reshape(GROUP, win, win)
            center = jnp.sum(product, axis=1, keepdims=True)
            grad_scores = scale * (product - float_probs.reshape(GROUP, win, win) * center)
            grad_scores = grad_scores.astype(jnp.bfloat16).reshape(GROUP * win, win)
            grad_values = own_heads(mxu(probs, mix), head_dim)
            grad_keys = own_heads(mxu(grad_scores, qkv_ref[rows, columns]), head_dim)
            turned = turned_heads(grad_scores, GROUP)
            grad_queries = own_heads(mxu(turned, qkv_ref[rows, key_columns]), head_dim)
            cells_ref[rows, columns] = grad_queries.astype(jnp.bfloat16)
            cells_ref[rows, key_columns] = grad_keys.astype(jnp.bfloat16)
            cells_ref[rows, value_columns] = grad_values.astype(jnp.bfloat16)
        return carry

    window_loop(windows, attend_back)

    for part, place in enumerate(GRAD_PLACES):
        columns = slice(part * width, (part + 1) * width)
        chunk = sum(place >= sum(CHUNKS[: at + 1]) for at in range(len(CHUNKS)))
        place -= sum(CHUNKS[:chunk])
        target = slice(place * width, (place + 1) * width)
        turned = turned_ref.at[TABLES.index(ROUTES[chunk])]
        sent_refs[chunk][:, target] = mxu(turned[half:, :], cells_ref[:, columns])
        kept_refs[chunk][:, target] = mxu(turned[:half, :], cells_ref[:, columns])


def coded(value):
    top = jnp.max(jnp.abs(value), axis=1, keepdims=True)
    exponent = jnp.ceil(jnp.log2(jnp.maximum(top, 1e-30)))
    codes = jnp.round(value * (jnp.exp2(-exponent) * STEPS)).astype(jnp.int32)
    exponents = jnp.broadcast_to(exponent, (value.shape[0], 128)).astype(jnp.int32)
    return codes.astype(jnp.int16), exponents.astype(jnp.int16)


def decoded(codes, exponents):
    exponent = exponents.astype(jnp.int32).astype(jnp.float32)[:, :1]
    return codes.astype(jnp.int32).astype(jnp.float32) * (jnp.exp2(exponent) * (1 / STEPS))


def added(arrived_ref, kept_ref, rows, columns):
    total = kept_ref.shape[1]
    arrived = arrived_ref[rows, columns]
    if arrived_ref.shape[1] > total:
        arrived = decoded(arrived, arrived_ref[rows, total:])
    return kept_ref[rows, columns] + arrived


def fold_kernel(arrived_ref, kept_ref, half_ref, coded_ref):
    rows, columns = half_ref.shape
    every = slice(0, columns)
    half_ref[...] = added(arrived_ref, kept_ref, slice(0, rows), every)
    codes, exponents = coded(added(arrived_ref, kept_ref, slice(rows, 2 * rows), every))
    coded_ref[:, :columns] = codes
    coded_ref[:, columns:] = exponents


def last_kernel(*refs):
    pair_refs, (grad_out_ref, grad_qkv_ref) = refs[:-2], refs[-2:]
    rows, width = grad_out_ref.shape
    every = slice(0, rows)
    quarters = []
    for at, quarter_count in enumerate(CHUNKS):
        for place in range(quarter_count):
            columns = slice(place * width, (place + 1) * width)
            quarters.append((pair_refs[2 * at], pair_refs[2 * at + 1], every, columns))
    grad_out_ref[...] = added(*quarters[0])
    for part, place in enumerate(GRAD_PLACES):
        grad_qkv_ref[:, part * width : (part + 1) * width] = added(*quarters[place])


def exchanged(value, distance):
    count = lax.axis_size("lat")
    return lax.ppermute(value, "lat", [(i, i ^ distance) for i in range(count)])


def moved(value, grp_turn, distance):
    count = lax.axis_size("lat")
    groups = lax.axis_size("grp")
    pairs = []
    for grp in range(groups):
        for i in range(count):
            pairs.append((grp * count + i, (grp ^ grp_turn) * count + (i ^ distance[grp])))
    return lax.ppermute(value, ("grp", "lat"), pairs)


def gathered(block, upper_in, cot_edge, prepare, bias):
    here = lax.axis_index("grp") == 0
    far = moved(block, 0, (8, 12))
    upper_in = passed_along(upper_in, "lat", -1)
    near = moved(block, 0, (4, 6))
    side = exchanged(block, 2)
    far, near, side, bias, cot_edge = lax.optimization_barrier((far, near, side, bias, cot_edge))
    far_side, far_other = exchanged(far, 2), moved(far, 1, (0, 0))
    near_other = moved(near, 1, (0, 0))
    far_side, near_other, upper_in = lax.optimization_barrier((far_side, near_other, upper_in))
    far_side_other = moved(far_side, 1, (0, 0))
    upper_cot = passed_along(cot_edge, "lat", -1)
    prepared = prepare(upper_in)
    shards = [block, side, near, near_other, far, far_other, far_side]
    swapped = [exchanged(shard, 1) for shard in shards]
    far_side_other, upper_cot, rest = lax.optimization_barrier(
        (far_side_other, upper_cot, swapped + list(prepared))
    )
    swapped, prepared = rest[: len(swapped)], rest[len(swapped) :]
    shards += [far_side_other] + swapped + [exchanged(far_side_other, 1)]
    low = jnp.array([0, 2, 4, 6, 8, 12, 10, 14], jnp.int32)
    high = jnp.array([0, 2, 6, 4, 12, 8, 14, 10], jnp.int32)
    order = jnp.where(here, low, high)
    return tuple(shards), jnp.concatenate([order, order + 1]), prepared, upper_cot, bias


def slots_of(distances, steps):
    result = 0
    for step in steps:
        result = 2 * result + ((distances // step) & 1)
    return result


def fold(arrived, kept):
    rows, columns = kept.shape
    outs = (
        jax.ShapeDtypeStruct((rows // 2, columns), jnp.float32),
        jax.ShapeDtypeStruct((rows // 2, columns + 128), jnp.int16),
    )
    return call(fold_kernel, "fold", outs, (), (arrived, kept), flops=8 * rows * columns, vmem=16)


def call(kernel, name, outs, tables, operands, scratch=(), flops=0, vmem=40):
    size = sum(math.prod(o.shape) * o.dtype.itemsize for o in (*outs, *operands))
    return pl.pallas_call(
        kernel,
        out_shape=outs,
        in_specs=[pl.BlockSpec(memory_space=pltpu.SMEM)] * len(tables)
        + [pl.BlockSpec(memory_space=pltpu.VMEM)] * len(operands),
        out_specs=[pl.BlockSpec(memory_space=pltpu.VMEM)] * len(outs),
        scratch_shapes=list(scratch),
        compiler_params=pltpu.CompilerParams(vmem_limit_bytes=vmem * 1024 * 1024),
        cost_estimate=pl.CostEstimate(flops=flops, bytes_accessed=size, transcendentals=0),
        name=name,
    )(*tables, *operands)


def per_device(inputs, cotangent, idents, w_qkv, w_out, gain):
    lat_cells, lon_cells, width = inputs.shape
    half_rows = WIN_R // 2
    win = padded_rows()
    windows = (lat_cells // WIN_R) * (lon_cells // WIN_C)
    cells = windows * win
    places = jnp.asarray(window_places(lon_cells), jnp.bfloat16)

    def shape(*dims, dtype=jnp.bfloat16):
        return jax.ShapeDtypeStruct(dims, dtype)

    count = lax.axis_size("lat")
    me = lax.axis_index("lat")
    direct = count == 16 and lax.axis_size("grp") == 2 and width % (16 * count) == 0
    if direct:
        distances = jnp.arange(count, dtype=jnp.int32) ^ me
        to_slot = jnp.stack([slots_of(distances, route) for route in TABLES])
    else:
        to_slot = jnp.stack([jnp.arange(16, dtype=jnp.int32)] * len(TABLES))

    def prepare(upper_in):
        return call(
            prepare_kernel,
            "prepare",
            (shape(cells, width), shape(len(TABLES), width, cells)),
            (to_slot,),
            (inputs, upper_in, places),
            flops=2 * cells * width * lon_cells * WIN_R,
            vmem=16,
        )

    weights = jnp.pad(w_qkv, ((0, 0), (0, width))) + jnp.pad(w_out, ((0, 0), (3 * width, 0)))
    in_edge, cot_edge = inputs[:half_rows], cotangent[:half_rows]
    labels = to_windows(idents + 1)
    bias = jnp.where(labels[:, :, None] == labels[:, None, :], 0.0, HIDDEN).astype(jnp.float32)
    if direct:
        shards, order, (tokens, turned), upper_cot, bias = gathered(
            weights, in_edge, cot_edge, prepare, bias
        )
        into = order ^ me
    else:
        weights = lax.all_gather(weights, "lat", axis=0, tiled=True)
        shards = tuple(weights.reshape(16, width // 16, 4 * width))
        into = to_slot[0]
        tokens, turned = prepare(passed_along(in_edge, "lat", -1))
        upper_cot = passed_along(cot_edge, "lat", -1)

    qkv_full, out_full, qkv, probs, mixed = call(
        forward_kernel,
        "forward",
        (
            shape(width, 3 * width),
            shape(width, width),
            shape(cells, 3 * width),
            shape(windows, HEADS // GROUP, GROUP * win, win),
            shape(cells, width),
        ),
        (into,),
        (tokens, bias, *shards),
        flops=2 * cells * width * width * 4,
        vmem=20,
    )
    (cot,) = call(
        shift_kernel,
        "shift",
        (shape(cells, width),),
        (),
        (cotangent, upper_cot, places),
        flops=2 * cells * width * lon_cells * WIN_R,
        vmem=16,
    )
    normed, grad_proj, grad_mix = call(
        norm_kernel,
        "norm",
        (shape(cells, width),) * 3,
        (),
        (mixed, out_full, cot, gain[None]),
        flops=2 * cells * width * width * 2,
        vmem=16,
    )
    (lower_out,) = call(
        edge_kernel,
        "edge",
        (shape(half_rows, lon_cells, width),),
        (),
        (normed, places),
        flops=2 * cells * width * lon_cells * half_rows,
        vmem=16,
    )
    lower_out = passed_along(lower_out, "lat", 1)
    grad_cells, *grads = call(
        backward_kernel,
        "backward",
        (
            shape(cells, 3 * width),
            *[shape(width // 2, CHUNKS[at // 2] * width, dtype=jnp.float32) for at in range(2 * len(CHUNKS))],
        ),
        (to_slot,),
        (qkv, probs, mixed, grad_proj, grad_mix, turned),
        flops=2 * cells * width * width * 6,
        vmem=30,
    )
    lower_out, grad_cells, *grads = lax.optimization_barrier((lower_out, grad_cells, *grads))

    def finish(normed, grad_cells):
        return call(
            finish_kernel,
            "finish",
            (shape(*inputs.shape), shape(*inputs.shape), shape(half_rows, lon_cells, width)),
            (),
            (grad_cells, qkv_full, normed, inputs, cotangent, places),
            (pltpu.VMEM((cells, width), jnp.bfloat16),),
            flops=2 * cells * width * (3 * width + 2 * lon_cells * WIN_R),
            vmem=24,
        )

    if direct:
        pairs = [(exchanged(sent, 1), kept) for sent, kept in zip(grads[::2], grads[1::2])]
        pairs = [fold(arrived, kept) for arrived, kept in pairs]
        kept, sent = pairs[-1]
        sent, normed, grad_cells = lax.optimization_barrier((sent, normed, grad_cells))
        pairs[-1] = (kept, sent)
        output, grad_in, lower = finish(normed, grad_cells)
        for step in (1, 2, 3):
            pairs = [
                (exchanged(sent, route[step]), kept) for route, (kept, sent) in zip(ROUTES, pairs)
            ]
            if step == 1:
                arrived, kept = pairs[-1]
                arrived, lower = lax.optimization_barrier((arrived, lower))
                kept, sent = fold(arrived, kept)
                arrived, first_kept = pairs[0]
                arrived, kept, lower = lax.optimization_barrier((arrived, kept, lower))
                pairs[0], last = (arrived, first_kept), (kept, sent)
                pairs = [fold(arrived, kept) for arrived, kept in pairs[:-1]] + [last]
                kept, sent = pairs[0]
                kept, lower = lax.optimization_barrier((kept, lower))
                pairs[0] = (kept, sent)
                lower = passed_along(lower, "lat", 1)
                continue
            if step == 3:
                arrived, kept = pairs[0]
                arrived, lower = lax.optimization_barrier((arrived, lower))
                pairs[0] = (arrived, kept)
                break
            pairs = [fold(arrived, kept) for arrived, kept in pairs]
        grad_out, grad_qkv = call(
            last_kernel,
            "last",
            (
                shape(width // count, width, dtype=jnp.float32),
                shape(width // count, 3 * width, dtype=jnp.float32),
            ),
            (),
            [value for pair in pairs for value in pair],
            flops=8 * width * width,
            vmem=16,
        )
    else:
        whole = [jnp.concatenate([kept, sent]) for sent, kept in zip(grads[::2], grads[1::2])]
        both = lax.psum_scatter(jnp.concatenate(whole, axis=1), "lat", scatter_dimension=0, tiled=True)
        quarters = jnp.split(both, 4, axis=1)
        grad_out = quarters[0]
        grad_qkv = jnp.concatenate([quarters[place] for place in GRAD_PLACES], axis=1)
        output, grad_in, lower = finish(normed, grad_cells)
        lower = passed_along(lower, "lat", 1)

    def completed(result, lower):
        top = result[:half_rows].astype(jnp.float32) + lower.astype(jnp.float32)
        return result.at[:half_rows].set(top.astype(jnp.bfloat16))

    return (completed(output, lower_out), completed(grad_in, lower), grad_qkv, grad_out)


def solution(mesh):
    in_specs = (
        P(("grp", "lat"), None, None),
        P(("grp", "lat"), None, None),
        P(("grp", "lat"), None),
        P("lat", None),
        P("lat", None),
        P(),
    )
    out_specs = (
        P(("grp", "lat"), None, None),
        P(("grp", "lat"), None, None),
        P(("grp", "lat"), None),
        P(("grp", "lat"), None),
    )
    return jax.shard_map(
        per_device, mesh=mesh, in_specs=in_specs, out_specs=out_specs, check_vma=False
    )
```

```python
import math

import jax
import jax.numpy as jnp
import numpy as np
from jax import lax
from jax.experimental import pallas as pl
from jax.experimental.pallas import tpu as pltpu
from jax.sharding import PartitionSpec as P

HEADS = 8
WIN_R = 6
WIN_C = 12
EPS = 1e-05
HIDDEN = -1e30
STEPS = 32000.0
GRAD_PLACES = (3, 2, 1)
CHUNKS = (2, 1, 1)
ROUTES = ((1, 2, 4, 8), (1, 4, 8, 2), (1, 4, 8, 2))
TABLES = tuple(dict.fromkeys(ROUTES))
UNROLL = 9
GROUP = 4

NN = (((1,), (0,)), ((), ()))
NT = (((1,), (1,)), ((), ()))
TN = (((0,), (0,)), ((), ()))


def mxu(left, right, dims=NN):
    return lax.dot_general(left, right, dims, preferred_element_type=jnp.float32)


def passed_along(value, axis, steps):
    count = lax.axis_size(axis)
    first, last = (max(0, -steps), min(count, count - steps))
    return lax.ppermute(value, axis, [(source, source + steps) for source in range(first, last)])


def padded_rows():
    return -(-WIN_R * WIN_C // 16) * 16


def to_windows(field):
    lat_cells, lon_cells = field.shape
    field = field.reshape(lat_cells // WIN_R, WIN_R, lon_cells // WIN_C, WIN_C)
    field = field.transpose(0, 2, 1, 3).reshape(-1, WIN_R * WIN_C)
    return jnp.pad(field, ((0, 0), (0, padded_rows() - WIN_R * WIN_C)))


def window_places(lon_cells):
    win = padded_rows()
    places = np.zeros((WIN_R, lon_cells // WIN_C, win, lon_cells), np.float32)
    for row in range(WIN_R):
        for window in range(lon_cells // WIN_C):
            for column in range(WIN_C):
                source = (window * WIN_C + column + WIN_C // 2) % lon_cells
                places[row, window, row * WIN_C + column, source] = 1
    return places.reshape(WIN_R, -1, lon_cells)


def masked_heads(value, head_dim):
    head = lax.broadcasted_iota(jnp.int32, value.shape, 1) // head_dim
    zero = jnp.zeros_like(value)
    count = value.shape[1] // head_dim
    return jnp.concatenate([jnp.where(head == at, value, zero) for at in range(count)], axis=0)


def own_heads(stacked, head_dim):
    count = stacked.shape[1] // head_dim
    rows = stacked.shape[0] // count
    head = lax.broadcasted_iota(jnp.int32, (rows, stacked.shape[1]), 1) // head_dim
    result = stacked[:rows]
    for at in range(1, count):
        result = jnp.where(head == at, stacked[at * rows : (at + 1) * rows], result)
    return result


def turned_heads(stacked, count):
    rows = stacked.shape[0] // count
    return jnp.concatenate(
        [stacked[at * rows : (at + 1) * rows].T for at in range(count)], axis=0
    )


def shift_kernel(own_ref, halo_ref, places_ref, result_ref):
    half = halo_ref.shape[0]
    lat_cells = own_ref.shape[0]
    cells = places_ref.shape[1]
    for band in range(lat_cells // WIN_R):
        total = None
        for row in range(WIN_R):
            source = band * WIN_R + row + half
            field = own_ref[source] if source < lat_cells else halo_ref[source - lat_cells]
            term = mxu(places_ref[row], field)
            total = term if total is None else total + term
        result_ref[band * cells : (band + 1) * cells, :] = total.astype(jnp.bfloat16)


def window_loop(windows, body):
    lax.fori_loop(0, windows, body, 0, unroll=UNROLL if windows % UNROLL == 0 else 1)


def prepare_kernel(to_slot_ref, inputs_ref, halo_ref, places_ref, tokens_ref, turned_ref):
    shift_kernel(inputs_ref, halo_ref, places_ref, tokens_ref)
    chunks, blocks = to_slot_ref.shape
    depth = tokens_ref.shape[1] // blocks
    turned = tokens_ref[...].T
    for chunk in range(chunks):
        for block in range(blocks):
            rows = pl.ds(pl.multiple_of(to_slot_ref[chunk, block] * depth, depth), depth)
            turned_ref[chunk, rows, :] = turned[block * depth : (block + 1) * depth, :]


def finish_kernel(
    cells_ref, w_qkv_ref, normed_ref, inputs_ref, cot_ref, places_ref,
    output_ref, grad_in_ref, lower_ref, shift_ref,
):
    lat_cells = inputs_ref.shape[0]
    half = lower_ref.shape[0]
    count = places_ref.shape[1]
    shift_ref[...] = mxu(cells_ref[...], w_qkv_ref[...], NT).astype(jnp.bfloat16)
    for at, (value_ref, base_ref, result_ref) in enumerate(
        ((normed_ref, inputs_ref, output_ref), (shift_ref, cot_ref, grad_in_ref))
    ):
        result_ref[:half] = base_ref[:half]
        for band in range(lat_cells // WIN_R):
            value = value_ref[band * count : (band + 1) * count, :]
            for row in range(WIN_R):
                target = band * WIN_R + row + half
                if at == 0 and target >= lat_cells:
                    continue
                back = mxu(places_ref[row], value, TN)
                if target < lat_cells:
                    base = base_ref[target].astype(jnp.float32)
                    result_ref[target] = (base + back).astype(jnp.bfloat16)
                else:
                    lower_ref[target - lat_cells] = back.astype(jnp.bfloat16)


def forward_kernel(into_ref, x_ref, bias_ref, *rest):
    shard_refs, rest = rest[: into_ref.shape[0]], rest[into_ref.shape[0] :]
    w_qkv_ref, w_out_ref, qkv_ref, probs_ref, mixed_ref = rest
    windows, win = bias_ref.shape[:2]
    width = x_ref.shape[1]
    head_dim = width // HEADS
    group = GROUP * head_dim
    factor = head_dim ** (-0.5) * math.log2(math.e)

    blocks = into_ref.shape[0]
    depth = width // blocks
    for at, shard_ref in enumerate(shard_refs):
        rows = pl.ds(pl.multiple_of(into_ref[at] * depth, depth), depth)
        w_qkv_ref[rows, :] = shard_ref[:, : 3 * width]
        w_out_ref[rows, :] = shard_ref[:, 3 * width :]

    for part in range(3):
        columns = slice(part * width, (part + 1) * width)
        qkv_ref[:, columns] = mxu(x_ref[...], w_qkv_ref[:, columns]).astype(jnp.bfloat16)

    def attend(window, carry):
        rows = pl.ds(pl.multiple_of(window * win, 16), win)
        bias = bias_ref[window]
        for at in range(HEADS // GROUP):
            columns = slice(at * group, (at + 1) * group)
            queries = qkv_ref[rows, columns]
            keys = qkv_ref[rows, width + at * group : width + (at + 1) * group]
            values = qkv_ref[rows, 2 * width + at * group : 2 * width + (at + 1) * group]
            scores = mxu(masked_heads(keys, head_dim), queries, NT)
            scores = scores.reshape(GROUP, win, win) * factor + bias
            lifted = jnp.exp2(scores - jnp.max(scores, axis=1, keepdims=True))
            total = jnp.sum(lifted, axis=1, keepdims=True)
            probs = (lifted * (1.0 / total)).astype(jnp.bfloat16)
            probs = probs.reshape(GROUP * win, win)
            probs_ref[window, at] = probs
            mixed = own_heads(mxu(turned_heads(probs, GROUP), values), head_dim)
            mixed_ref[rows, columns] = mixed.astype(jnp.bfloat16)
        return carry

    window_loop(windows, attend)


def norm_kernel(
    mixed_ref, w_out_ref, cot_ref, gain_ref, normed_ref, grad_proj_ref, grad_mix_ref
):
    win = padded_rows()
    windows = mixed_ref.shape[0] // win
    gain = gain_ref[...]

    def normalise(window, carry):
        rows = pl.ds(pl.multiple_of(window * win, 16), win)
        projected = mxu(mixed_ref[rows, :], w_out_ref[...])
        center = projected - jnp.mean(projected, axis=-1, keepdims=True)
        inverse = lax.rsqrt(jnp.mean(center * center, axis=-1, keepdims=True) + EPS)
        normal = center * inverse
        normed_ref[rows, :] = (normal * gain).astype(jnp.bfloat16)
        scaled = cot_ref[rows, :].astype(jnp.float32) * gain
        grad_proj = (
            scaled
            - jnp.mean(scaled, axis=-1, keepdims=True)
            - normal * jnp.mean(scaled * normal, axis=-1, keepdims=True)
        ) * inverse
        grad_proj_ref[rows, :] = grad_proj.astype(jnp.bfloat16)
        return carry

    window_loop(windows, normalise)
    grad_mix_ref[...] = mxu(grad_proj_ref[...], w_out_ref[...], NT).astype(jnp.bfloat16)


def edge_kernel(value_ref, places_ref, lower_ref):
    half = lower_ref.shape[0]
    value = value_ref[value_ref.shape[0] - places_ref.shape[1] :, :]
    for row in range(half):
        back = mxu(places_ref[WIN_R - half + row], value, TN)
        lower_ref[row] = back.astype(jnp.bfloat16)


def backward_kernel(
    to_slot_ref, qkv_ref, probs_ref, mixed_ref, grad_proj_ref, grad_mix_ref, turned_ref,
    cells_ref, *grad_refs,
):
    windows, win = probs_ref.shape[0], probs_ref.shape[-1]
    width = grad_mix_ref.shape[1]
    head_dim = width // HEADS
    group = GROUP * head_dim
    scale = head_dim ** (-0.5)
    blocks = to_slot_ref.shape[1]
    depth = width // blocks
    half = width // 2
    sent_refs, kept_refs = grad_refs[::2], grad_refs[1::2]
    grad_out = mxu(mixed_ref[...], grad_proj_ref[...], TN)
    for block in range(blocks):
        slot = to_slot_ref[0, block]
        value = grad_out[block * depth : (block + 1) * depth, :]
        rows = pl.ds(pl.multiple_of(lax.rem(slot, blocks // 2) * depth, depth), depth)

        @pl.when(slot < blocks // 2)
        def _():
            kept_refs[0][rows, :width] = value

        @pl.when(slot >= blocks // 2)
        def _():
            sent_refs[0][rows, :width] = value

    def attend_back(window, carry):
        rows = pl.ds(pl.multiple_of(window * win, 16), win)
        for at in range(HEADS // GROUP):
            columns = slice(at * group, (at + 1) * group)
            key_columns = slice(width + at * group, width + (at + 1) * group)
            value_columns = slice(2 * width + at * group, 2 * width + (at + 1) * group)
            mix = grad_mix_ref[rows, columns]
            probs = probs_ref[window, at]
            float_probs = probs.astype(jnp.float32)
            grad_probs = mxu(masked_heads(qkv_ref[rows, value_columns], head_dim), mix, NT)
            product = (float_probs * grad_probs).reshape(GROUP, win, win)
            center = jnp.sum(product, axis=1, keepdims=True)
            grad_scores = scale * (product - float_probs.reshape(GROUP, win, win) * center)
            grad_scores = grad_scores.astype(jnp.bfloat16).reshape(GROUP * win, win)
            grad_values = own_heads(mxu(probs, mix), head_dim)
            grad_keys = own_heads(mxu(grad_scores, qkv_ref[rows, columns]), head_dim)
            turned = turned_heads(grad_scores, GROUP)
            grad_queries = own_heads(mxu(turned, qkv_ref[rows, key_columns]), head_dim)
            cells_ref[rows, columns] = grad_queries.astype(jnp.bfloat16)
            cells_ref[rows, key_columns] = grad_keys.astype(jnp.bfloat16)
            cells_ref[rows, value_columns] = grad_values.astype(jnp.bfloat16)
        return carry

    window_loop(windows, attend_back)

    for part, place in enumerate(GRAD_PLACES):
        columns = slice(part * width, (part + 1) * width)
        chunk = sum(place >= sum(CHUNKS[: at + 1]) for at in range(len(CHUNKS)))
        place -= sum(CHUNKS[:chunk])
        target = slice(place * width, (place + 1) * width)
        turned = turned_ref.at[TABLES.index(ROUTES[chunk])]
        sent_refs[chunk][:, target] = mxu(turned[half:, :], cells_ref[:, columns])
        kept_refs[chunk][:, target] = mxu(turned[:half, :], cells_ref[:, columns])


def coded(value):
    top = jnp.max(jnp.abs(value), axis=1, keepdims=True)
    exponent = jnp.ceil(jnp.log2(jnp.maximum(top, 1e-30)))
    codes = jnp.round(value * (jnp.exp2(-exponent) * STEPS)).astype(jnp.int32)
    exponents = jnp.broadcast_to(exponent, (value.shape[0], 128)).astype(jnp.int32)
    return codes.astype(jnp.int16), exponents.astype(jnp.int16)


def decoded(codes, exponents):
    exponent = exponents.astype(jnp.int32).astype(jnp.float32)[:, :1]
    return codes.astype(jnp.int32).astype(jnp.float32) * (jnp.exp2(exponent) * (1 / STEPS))


def added(arrived_ref, kept_ref, rows, columns):
    total = kept_ref.shape[1]
    arrived = arrived_ref[rows, columns]
    if arrived_ref.shape[1] > total:
        arrived = decoded(arrived, arrived_ref[rows, total:])
    return kept_ref[rows, columns] + arrived


def fold_kernel(arrived_ref, kept_ref, half_ref, coded_ref):
    rows, columns = half_ref.shape
    every = slice(0, columns)
    half_ref[...] = added(arrived_ref, kept_ref, slice(0, rows), every)
    codes, exponents = coded(added(arrived_ref, kept_ref, slice(rows, 2 * rows), every))
    coded_ref[:, :columns] = codes
    coded_ref[:, columns:] = exponents


def last_kernel(*refs):
    pair_refs, (grad_out_ref, grad_qkv_ref) = refs[:-2], refs[-2:]
    rows, width = grad_out_ref.shape
    every = slice(0, rows)
    quarters = []
    for at, quarter_count in enumerate(CHUNKS):
        for place in range(quarter_count):
            columns = slice(place * width, (place + 1) * width)
            quarters.append((pair_refs[2 * at], pair_refs[2 * at + 1], every, columns))
    grad_out_ref[...] = added(*quarters[0])
    for part, place in enumerate(GRAD_PLACES):
        grad_qkv_ref[:, part * width : (part + 1) * width] = added(*quarters[place])


def exchanged(value, distance):
    count = lax.axis_size("lat")
    return lax.ppermute(value, "lat", [(i, i ^ distance) for i in range(count)])


def moved(value, grp_turn, distance):
    count = lax.axis_size("lat")
    groups = lax.axis_size("grp")
    pairs = []
    for grp in range(groups):
        for i in range(count):
            pairs.append((grp * count + i, (grp ^ grp_turn) * count + (i ^ distance[grp])))
    return lax.ppermute(value, ("grp", "lat"), pairs)


def gathered(block, upper_in, cot_edge, prepare, bias):
    here = lax.axis_index("grp") == 0
    far = moved(block, 0, (8, 12))
    upper_in = passed_along(upper_in, "lat", -1)
    near = moved(block, 0, (4, 6))
    side = exchanged(block, 2)
    far, near, side, bias, cot_edge = lax.optimization_barrier((far, near, side, bias, cot_edge))
    far_side, far_other = exchanged(far, 2), moved(far, 1, (0, 0))
    near_other = moved(near, 1, (0, 0))
    far_side, near_other, upper_in = lax.optimization_barrier((far_side, near_other, upper_in))
    far_side_other = moved(far_side, 1, (0, 0))
    upper_cot = passed_along(cot_edge, "lat", -1)
    prepared = prepare(upper_in)
    shards = [block, side, near, near_other, far, far_other, far_side]
    swapped = [exchanged(shard, 1) for shard in shards]
    far_side_other, upper_cot, rest = lax.optimization_barrier(
        (far_side_other, upper_cot, swapped + list(prepared))
    )
    swapped, prepared = rest[: len(swapped)], rest[len(swapped) :]
    shards += [far_side_other] + swapped + [exchanged(far_side_other, 1)]
    low = jnp.array([0, 2, 4, 6, 8, 12, 10, 14], jnp.int32)
    high = jnp.array([0, 2, 6, 4, 12, 8, 14, 10], jnp.int32)
    order = jnp.where(here, low, high)
    return tuple(shards), jnp.concatenate([order, order + 1]), prepared, upper_cot, bias


def slots_of(distances, steps):
    result = 0
    for step in steps:
        result = 2 * result + ((distances // step) & 1)
    return result


def fold(arrived, kept):
    rows, columns = kept.shape
    outs = (
        jax.ShapeDtypeStruct((rows // 2, columns), jnp.float32),
        jax.ShapeDtypeStruct((rows // 2, columns + 128), jnp.int16),
    )
    return call(fold_kernel, "fold", outs, (), (arrived, kept), flops=8 * rows * columns, vmem=16)


def call(kernel, name, outs, tables, operands, scratch=(), flops=0, vmem=40):
    size = sum(math.prod(o.shape) * o.dtype.itemsize for o in (*outs, *operands))
    return pl.pallas_call(
        kernel,
        out_shape=outs,
        in_specs=[pl.BlockSpec(memory_space=pltpu.SMEM)] * len(tables)
        + [pl.BlockSpec(memory_space=pltpu.VMEM)] * len(operands),
        out_specs=[pl.BlockSpec(memory_space=pltpu.VMEM)] * len(outs),
        scratch_shapes=list(scratch),
        compiler_params=pltpu.CompilerParams(vmem_limit_bytes=vmem * 1024 * 1024),
        cost_estimate=pl.CostEstimate(flops=flops, bytes_accessed=size, transcendentals=0),
        name=name,
    )(*tables, *operands)


def per_device(inputs, cotangent, idents, w_qkv, w_out, gain):
    lat_cells, lon_cells, width = inputs.shape
    half_rows = WIN_R // 2
    win = padded_rows()
    windows = (lat_cells // WIN_R) * (lon_cells // WIN_C)
    cells = windows * win
    places = jnp.asarray(window_places(lon_cells), jnp.bfloat16)

    def shape(*dims, dtype=jnp.bfloat16):
        return jax.ShapeDtypeStruct(dims, dtype)

    count = lax.axis_size("lat")
    me = lax.axis_index("lat")
    direct = count == 16 and lax.axis_size("grp") == 2 and width % (16 * count) == 0
    if direct:
        distances = jnp.arange(count, dtype=jnp.int32) ^ me
        to_slot = jnp.stack([slots_of(distances, route) for route in TABLES])
    else:
        to_slot = jnp.stack([jnp.arange(16, dtype=jnp.int32)] * len(TABLES))

    def prepare(upper_in):
        return call(
            prepare_kernel,
            "prepare",
            (shape(cells, width), shape(len(TABLES), width, cells)),
            (to_slot,),
            (inputs, upper_in, places),
            flops=2 * cells * width * lon_cells * WIN_R,
            vmem=16,
        )

    weights = jnp.pad(w_qkv, ((0, 0), (0, width))) + jnp.pad(w_out, ((0, 0), (3 * width, 0)))
    in_edge, cot_edge = inputs[:half_rows], cotangent[:half_rows]
    labels = to_windows(idents + 1)
    bias = jnp.where(labels[:, :, None] == labels[:, None, :], 0.0, HIDDEN).astype(jnp.float32)
    if direct:
        shards, order, (tokens, turned), upper_cot, bias = gathered(
            weights, in_edge, cot_edge, prepare, bias
        )
        into = order ^ me
    else:
        weights = lax.all_gather(weights, "lat", axis=0, tiled=True)
        shards = tuple(weights.reshape(16, width // 16, 4 * width))
        into = to_slot[0]
        tokens, turned = prepare(passed_along(in_edge, "lat", -1))
        upper_cot = passed_along(cot_edge, "lat", -1)

    qkv_full, out_full, qkv, probs, mixed = call(
        forward_kernel,
        "forward",
        (
            shape(width, 3 * width),
            shape(width, width),
            shape(cells, 3 * width),
            shape(windows, HEADS // GROUP, GROUP * win, win),
            shape(cells, width),
        ),
        (into,),
        (tokens, bias, *shards),
        flops=2 * cells * width * width * 4,
        vmem=20,
    )
    (cot,) = call(
        shift_kernel,
        "shift",
        (shape(cells, width),),
        (),
        (cotangent, upper_cot, places),
        flops=2 * cells * width * lon_cells * WIN_R,
        vmem=16,
    )
    normed, grad_proj, grad_mix = call(
        norm_kernel,
        "norm",
        (shape(cells, width),) * 3,
        (),
        (mixed, out_full, cot, gain[None]),
        flops=2 * cells * width * width * 2,
        vmem=16,
    )
    (lower_out,) = call(
        edge_kernel,
        "edge",
        (shape(half_rows, lon_cells, width),),
        (),
        (normed, places),
        flops=2 * cells * width * lon_cells * half_rows,
        vmem=16,
    )
    lower_out = passed_along(lower_out, "lat", 1)
    grad_cells, *grads = call(
        backward_kernel,
        "backward",
        (
            shape(cells, 3 * width),
            *[shape(width // 2, CHUNKS[at // 2] * width, dtype=jnp.float32) for at in range(2 * len(CHUNKS))],
        ),
        (to_slot,),
        (qkv, probs, mixed, grad_proj, grad_mix, turned),
        flops=2 * cells * width * width * 6,
        vmem=30,
    )
    lower_out, grad_cells, *grads = lax.optimization_barrier((lower_out, grad_cells, *grads))

    def finish(normed, grad_cells):
        return call(
            finish_kernel,
            "finish",
            (shape(*inputs.shape), shape(*inputs.shape), shape(half_rows, lon_cells, width)),
            (),
            (grad_cells, qkv_full, normed, inputs, cotangent, places),
            (pltpu.VMEM((cells, width), jnp.bfloat16),),
            flops=2 * cells * width * (3 * width + 2 * lon_cells * WIN_R),
            vmem=24,
        )

    if direct:
        pairs = [(exchanged(sent, 1), kept) for sent, kept in zip(grads[::2], grads[1::2])]
        pairs = [fold(arrived, kept) for arrived, kept in pairs]
        kept, sent = pairs[-1]
        sent, normed, grad_cells = lax.optimization_barrier((sent, normed, grad_cells))
        pairs[-1] = (kept, sent)
        output, grad_in, lower = finish(normed, grad_cells)
        for step in (1, 2, 3):
            pairs = [
                (exchanged(sent, route[step]), kept) for route, (kept, sent) in zip(ROUTES, pairs)
            ]
            if step in (1, 3):
                arrived, kept = pairs[0]
                arrived, lower = lax.optimization_barrier((arrived, lower))
                pairs[0] = (arrived, kept)
            if step == 3:
                break
            pairs = [fold(arrived, kept) for arrived, kept in pairs]
            if step == 1:
                lower, _ = lax.optimization_barrier((lower, pairs[0][0]))
                lower = passed_along(lower, "lat", 1)
        grad_out, grad_qkv = call(
            last_kernel,
            "last",
            (
                shape(width // count, width, dtype=jnp.float32),
                shape(width // count, 3 * width, dtype=jnp.float32),
            ),
            (),
            [value for pair in pairs for value in pair],
            flops=8 * width * width,
            vmem=16,
        )
    else:
        whole = [jnp.concatenate([kept, sent]) for sent, kept in zip(grads[::2], grads[1::2])]
        both = lax.psum_scatter(jnp.concatenate(whole, axis=1), "lat", scatter_dimension=0, tiled=True)
        quarters = jnp.split(both, 4, axis=1)
        grad_out = quarters[0]
        grad_qkv = jnp.concatenate([quarters[place] for place in GRAD_PLACES], axis=1)
        output, grad_in, lower = finish(normed, grad_cells)
        lower = passed_along(lower, "lat", 1)

    def completed(result, lower):
        top = result[:half_rows].astype(jnp.float32) + lower.astype(jnp.float32)
        return result.at[:half_rows].set(top.astype(jnp.bfloat16))

    return (completed(output, lower_out), completed(grad_in, lower), grad_qkv, grad_out)


def solution(mesh):
    in_specs = (
        P(("grp", "lat"), None, None),
        P(("grp", "lat"), None, None),
        P(("grp", "lat"), None),
        P("lat", None),
        P("lat", None),
        P(),
    )
    out_specs = (
        P(("grp", "lat"), None, None),
        P(("grp", "lat"), None, None),
        P(("grp", "lat"), None),
        P(("grp", "lat"), None),
    )
    return jax.shard_map(
        per_device, mesh=mesh, in_specs=in_specs, out_specs=out_specs, check_vma=False
    )
```
